32 devices in a mesh: dp: 8 (over z, x), tensor: 4 (over y, core).
Axes of the slice: x: 2, y: 2, z: 4, core: 2. Of those that a mesh axis runs over, the one named last changes fastest.
Arguments:
- tokens: bfloat16 [9536, 768], P(('dp', 'tensor')), may hold values from -6 to 6
- lengths: int32 [8], P('dp'), may hold values from 397 to 1192, as said below
- ln1_gain: float32 [768], replicated, may hold values from 0.5 to 1.5
- ln1_shift: float32 [768], replicated, may hold values from -1.75 to 1.75
- qkv_weight: bfloat16 [768, 3, 768], P(None, None, 'tensor'), may hold values from -0.21875 to 0.21875
- qv_bias: float32 [2, 768], P(None, 'tensor'), may hold values from -1.75 to 1.75
- out_weight: bfloat16 [768, 768], P('tensor'), may hold values from -0.875 to 0.875
- out_bias: float32 [768], replicated, may hold values from -1.75 to 1.75
- ln2_gain: float32 [768], replicated, may hold values from 0.5 to 1.5
- ln2_shift: float32 [768], replicated, may hold values from -1.75 to 1.75
- up_weight: bfloat16 [768, 3072], P(None, 'tensor'), may hold values from -0.21875 to 0.21875
- up_bias: float32 [3072], P('tensor'), may hold values from -1.75 to 1.75
- down_weight: bfloat16 [3072, 768], P('tensor'), may hold values from -0.109375 to 0.109375
- down_bias: float32 [768], replicated, may hold values from -1.75 to 1.75
- cotangent: float32 [9536, 768], P(('dp', 'tensor')), may hold values from -6 to 6
Outputs:
- output: bfloat16 [9536, 768], P(('dp', 'tensor'))
- grad_tokens: float32 [9536, 768], P(('dp', 'tensor'))
- grad_ln1_gain: float32 [768], replicated
- grad_ln1_shift: float32 [768], replicated
- grad_qkv_weight: float32 [768, 3, 768], P(None, None, 'tensor')
- grad_qv_bias: float32 [2, 768], P(None, 'tensor')
- grad_out_weight: float32 [768, 768], P('tensor')
- grad_out_bias: float32 [768], replicated
- grad_ln2_gain: float32 [768], replicated
- grad_ln2_shift: float32 [768], replicated
- grad_up_weight: float32 [768, 3072], P(None, 'tensor')
- grad_up_bias: float32 [3072], P('tensor')
- grad_down_weight: float32 [3072, 768], P('tensor')
- grad_down_bias: float32 [768], replicated
The draws below stay inside these ranges and needn't reach their ends.
Inputs may be any that keep to these rules, and one draw needn't show every extreme that they name: `lengths`: keys of a clip at positions from its length on are padding.
All inputs are finite; a program needn't handle non-finite values.
Results may differ from the reference program's by a relative error of at most 0.02.
Values may be sent and summed in bfloat16 or wider, within the bound.
A program may use at most 192 MiB of HBM per device.

```python
import jax
import jax.numpy as jnp
from jax import lax

D = 768
HEADS = 12
HEAD_DIM = 64
FF = 3072
SEQ = 1192
CLIPS = 8
TOKENS = 9536


def draw_lengths(key, part):
    key = jax.random.fold_in(key, 11)
    flip_key, short_key = jax.random.split(key)
    coin_flip = jax.random.randint(flip_key, (CLIPS,), 0, 2)
    short = jax.random.randint(short_key, (CLIPS,), SEQ // 3, SEQ // 2 + 1)
    result = jnp.where(coin_flip == 1, SEQ, short)
    result = result.at[0].set(SEQ).at[1].set(SEQ // 3)
    return result.astype(jnp.int32)


def steps_of(key, shape, cuts, low, largest):
    level, own = 1.0, jax.random.fold_in(key, 6)
    for axis_at, blocks in cuts:
        heights = jnp.exp(jax.random.uniform(jax.random.fold_in(own, axis_at), (blocks,), jnp.float32, low / len(cuts), largest / len(cuts)))
        level = level * jnp.repeat(heights, shape[axis_at] // blocks).reshape([-1 if axis == axis_at else 1 for axis in range(len(shape))])
    return level


def centred(key, dims, scale, most, cuts=(), held_as=jnp.bfloat16):
    values = jax.random.normal(key, dims, jnp.float32) * scale
    if len(cuts) > 0:
        values = steps_of(key, dims, cuts, -0.22, 0.18) * values
    return jnp.clip(values, min=-most, max=most).astype(held_as)


def setup_inputs(seed: int = 0) -> dict:
    splits = jax.random.split(jax.random.key(seed), 16)
    return {
        "tokens": centred(splits[0], (TOKENS, D), 1.0, 6.0, ((0, 32),)),
        "lengths": draw_lengths(jax.random.fold_in(splits[15], 71), 0),
        "ln1_gain": jnp.clip(1.0 + 0.1 * jax.random.normal(splits[2], (D,), jnp.float32), 0.5, 1.5),
        "ln1_shift": centred(splits[3], (D,), 0.3, 1.75, (), jnp.float32),
        "qkv_weight": centred(splits[4], (D, 3, D), D ** -0.5, 0.21875, ((2, 4),)),
        "qv_bias": centred(splits[5], (2, D), 0.3, 1.75, ((1, 4),), jnp.float32),
        "out_weight": centred(splits[6], (D, D), (D // 16) ** -0.5, 0.875, ((0, 4),)),
        "out_bias": centred(splits[7], (D,), 0.3, 1.75, (), jnp.float32),
        "ln2_gain": jnp.clip(1.0 + 0.1 * jax.random.normal(splits[8], (D,), jnp.float32), 0.5, 1.5),
        "ln2_shift": centred(splits[9], (D,), 0.3, 1.75, (), jnp.float32),
        "up_weight": centred(splits[10], (D, FF), D ** -0.5, 0.21875, ((1, 4),)),
        "up_bias": centred(splits[11], (FF,), 0.3, 1.75, ((0, 4),), jnp.float32),
        "down_weight": centred(splits[12], (FF, D), FF ** -0.5, 0.109375, ((0, 4),)),
        "down_bias": centred(splits[13], (D,), 0.3, 1.75, (), jnp.float32),
        "cotangent": centred(splits[14], (TOKENS, D), 1.0, 6.0, ((0, 32),), jnp.float32),
    }


epsilon = 1e-06
highest = lax.Precision.HIGHEST

@jax.custom_vjp
def low(v):
    return lax.optimization_barrier(v.astype(jnp.bfloat16)).astype(jnp.float32)

@jax.custom_vjp
def low_back(v):
    return v

def low_keep(v):
    return (low(v), None)

def low_pass(kept, grad):
    return (grad,)

def back_keep(v):
    return (v, None)

def back_low(kept, grad):
    return (low(grad),)
low.defvjp(low_keep, low_pass)
low_back.defvjp(back_keep, back_low)

def layer_norm(values, gain, shift):
    center = values - lax.optimization_barrier(jnp.mean(values, -1, keepdims=True))
    spread = lax.optimization_barrier(jnp.mean(center * center, -1, keepdims=True))
    return center * lax.rsqrt(spread + epsilon) * gain + shift

def clip_forward(clip_in, length, ln1_gain, ln1_shift, qkv_weight, qv_bias, out_weight, out_bias, ln2_gain, ln2_shift, up_weight, up_bias, down_weight, down_bias):
    normed = low(layer_norm(clip_in, ln1_gain, ln1_shift))
    project = jnp.einsum('td,dcf->tcf', normed, qkv_weight, precision=highest)
    head_shape = (SEQ, HEADS, HEAD_DIM)
    query = low_back(low(project[:, 0] + qv_bias[0])).reshape(head_shape)
    keys = low_back(low(project[:, 1])).reshape(head_shape)
    values = low_back(low(project[:, 2] + qv_bias[1])).reshape(head_shape)
    scores = low_back(jnp.einsum('qhd,khd->hqk', query, keys, precision=highest) * HEAD_DIM ** (-0.5))
    valid = jnp.arange(SEQ) < length
    scores = jnp.where(valid[None, None, :], scores, -1e+30)
    row_top = lax.optimization_barrier(jnp.max(scores, -1, keepdims=True))
    exp_terms = jnp.exp(scores - row_top)
    probs = exp_terms / lax.optimization_barrier(jnp.sum(exp_terms, -1, keepdims=True))
    mixed = jnp.einsum('hqk,khd->qhd', low(probs), values, precision=highest).reshape(SEQ, D)
    mixed = low_back(low(mixed))
    hidden = clip_in + low_back(jnp.dot(mixed, out_weight, precision=highest) + out_bias)
    normed_two = low(layer_norm(hidden, ln2_gain, ln2_shift))
    upward = low_back(jnp.dot(normed_two, up_weight, precision=highest) + up_bias)
    active = low(jax.nn.gelu(upward))
    return hidden + low_back(jnp.dot(active, down_weight, precision=highest) + down_bias)

def reference(tokens, lengths, ln1_gain, ln1_shift, qkv_weight, qv_bias, out_weight, out_bias, ln2_gain, ln2_shift, up_weight, up_bias, down_weight, down_bias, cotangent):
    params = tuple((p.astype(jnp.float32) for p in (ln1_gain, ln1_shift, qkv_weight, qv_bias, out_weight, out_bias, ln2_gain, ln2_shift, up_weight, up_bias, down_weight, down_bias)))
    clips = tokens.astype(jnp.float32).reshape(CLIPS, SEQ, D)
    cotangents = cotangent.astype(jnp.float32).reshape(CLIPS, SEQ, D)

    def one_clip(sums, clip_item):
        clip_in, length, clip_cot = clip_item

        def forward(inputs, *weights):
            return clip_forward(inputs, length, *weights)
        result, pull = jax.vjp(forward, clip_in, *params)
        grads = pull(clip_cot)
        sums = tuple((total + grad for total, grad in zip(sums, grads[1:])))
        return (sums, (result.astype(jnp.bfloat16), grads[0]))
    zeros = tuple((jnp.zeros_like(p) for p in params))
    sums, (outputs, grad_in) = lax.scan(one_clip, zeros, (clips, lengths, cotangents))
    return (outputs.reshape(TOKENS, D), grad_in.reshape(TOKENS, D), sums[0], sums[1], sums[2], sums[3], sums[4], sums[5], sums[6], sums[7], sums[8], sums[9], sums[10], sums[11])
```

```python
import types

import jax
import jax.numpy as jnp
from jax import lax
from jax.experimental import pallas as pl
from jax.experimental.pallas import tpu as pltpu
from jax.sharding import PartitionSpec as P

HEAD_DIM = 64
MESH = pl.DeviceIdType.MESH
VMEM_BYTES = 62 * 2**20

epsilon = 1e-06
low = jnp.bfloat16
wide = jnp.float32


def round_up(amount, unit):
    return -(-amount // unit) * unit


def flipped(t, flip_chip, flip_core):
    return (t // 2 + flip_chip) % 2 * 2 + (t % 2 + flip_core) % 2


def dot(left, right):
    return jnp.dot(left, right, preferred_element_type=wide)


def dot_rows(left, right):
    return lax.dot_general(left, right, (((1,), (1,)), ((), ())), preferred_element_type=wide)


def dot_columns(left, right):
    return lax.dot_general(left, right, (((0,), (0,)), ((), ())), preferred_element_type=wide)


def standardize(values):
    center = values - jnp.mean(values, -1, keepdims=True)
    inverse = lax.rsqrt(jnp.mean(center * center, -1, keepdims=True) + epsilon)
    return center * inverse, inverse


def norm_back(grad, unit, inverse, gain):
    scaled = grad * gain
    return inverse * (
        scaled
        - jnp.mean(scaled, -1, keepdims=True)
        - unit * jnp.mean(scaled * unit, -1, keepdims=True)
    )


def flat(ref):
    a, b, c = ref.shape
    return ref[...].reshape(a * b, c)


class Links:
    def __init__(self, send, recv):
        self.send, self.recv, self.used, self.pending = send, recv, 0, []

    def take(self, amount=1):
        base = self.used
        self.used += amount
        assert self.used <= self.send.shape[0]
        return base

    def copy(self, src, dst, at, **where):
        return pltpu.make_async_remote_copy(
            src_ref=src,
            dst_ref=dst,
            send_sem=self.send.at[at],
            recv_sem=self.recv.at[at],
            device_id=where,
            device_id_type=MESH,
        )

    def start(self, src, dst, at, **where):
        copy = self.copy(src, dst, at, **where)
        copy.start()
        self.pending.append(copy)

    def arrived(self, dst, at, **where):
        self.copy(dst, dst, at, **where).wait_recv()

    def finish(self):
        for copy in self.pending:
            copy.wait_send()
        self.pending = []


class Gather:
    def __init__(self, links, buf, t, parts):
        self.links, self.buf, self.t, self.parts = links, buf, t, parts
        self.sib, self.cross, self.diag = flipped(t, 0, 1), flipped(t, 1, 0), flipped(t, 1, 1)
        self.base = links.take(3 * len(parts))

    def view(self, slot, part):
        start, size = self.parts[part]
        return self.buf.at[slot, pl.ds(start, size)]

    def _each(self):
        return range(len(self.parts))

    def start(self):
        for p in self._each():
            v = self.view(self.t, p)
            self.links.copy(v, v, self.base + 3 * p, tensor=self.cross).start()
        for p in self._each():
            v = self.view(self.t, p)
            self.links.copy(v, v, self.base + 3 * p + 1, tensor=self.sib).start()

    def wait_sib(self):
        for p in self._each():
            self.links.arrived(self.view(self.sib, p), self.base + 3 * p + 1, tensor=self.sib)

    def forward(self):
        for p in self._each():
            v = self.view(self.cross, p)
            self.links.arrived(v, self.base + 3 * p, tensor=self.cross)
            self.links.copy(v, v, self.base + 3 * p + 2, tensor=self.sib).start()

    def wait_diag(self):
        for p in self._each():
            self.links.arrived(self.view(self.diag, p), self.base + 3 * p + 2, tensor=self.sib)

    def finish(self):
        for p in self._each():
            v = self.view(self.t, p)
            self.links.copy(v, v, self.base + 3 * p, tensor=self.cross).wait_send()
            self.links.copy(v, v, self.base + 3 * p + 1, tensor=self.sib).wait_send()
            v = self.view(self.cross, p)
            self.links.copy(v, v, self.base + 3 * p + 2, tensor=self.sib).wait_send()


class Reduce:
    def __init__(self, links, part, pre, near, far, out, t):
        self.links, self.part, self.pre, self.near, self.far, self.out, self.t = (
            links, part, pre, near, far, out, t,
        )
        self.sib, self.cross, self.diag = flipped(t, 0, 1), flipped(t, 1, 0), flipped(t, 1, 1)
        self.base = links.take(3)

    def send_diag(self):
        self.links.copy(self.part.at[self.diag], self.pre, self.base, tensor=self.sib).start()

    def send_sib(self):
        self.links.copy(self.part.at[self.sib], self.near, self.base + 1, tensor=self.sib).start()

    def send_cross(self):
        self.links.arrived(self.pre, self.base, tensor=self.sib)
        total = self.part[self.cross].astype(wide) + self.pre[...].astype(wide)
        self.out[...] = total.astype(low)
        self.links.copy(self.out, self.far, self.base + 2, tensor=self.cross).start()

    def result(self):
        self.links.arrived(self.near, self.base + 1, tensor=self.sib)
        self.links.arrived(self.far, self.base + 2, tensor=self.cross)
        return (
            self.part[self.t].astype(wide) + self.near[...].astype(wide) + self.far[...].astype(wide)
        )

    def finish(self):
        self.links.copy(self.part.at[self.diag], self.pre, self.base, tensor=self.sib).wait_send()
        self.links.copy(self.part.at[self.sib], self.near, self.base + 1, tensor=self.sib).wait_send()
        self.links.copy(self.out, self.far, self.base + 2, tensor=self.cross).wait_send()


class DataReduce:
    def __init__(self, links, held, whole, boxes, first, rows, d, count, order):
        self.links, self.held, self.whole, self.boxes = links, held, whole, boxes
        bits = count.bit_length() - 1
        assert count == 1 << bits
        halving = [b for b in order if b < bits]
        self.d, self.rows = d, rows
        self.off = first
        self.halving, self.extra = halving, [b for b in range(bits) if b not in halving]
        self.steps = []
        self.trail = []
        for k, b in enumerate(halving):
            self.steps.append(lambda k=k, b=b: self._send_half(k, b))
            self.steps.append(lambda k=k, b=b: self._add_half(k, b, last=k == len(halving) - 1))
        for k, b in enumerate(self.extra):
            self.steps.append(lambda k=k, b=b: self._swap_send(k, b))
            self.steps.append(lambda k=k, b=b: self._swap_add(k, b))
        for k, b in reversed(list(enumerate(halving))):
            self.steps.append(lambda k=k, b=b: self._grow_send(k, b))
            self.steps.append(lambda k=k, b=b: self._grow_wait(k, b))
        self.size = rows
        self.base = links.take(2 * len(halving) + len(self.extra))
        self.sent = []

    def _bit(self, b):
        return self.d // (1 << b) % 2

    def _peer(self, b):
        return self.d + (1 - 2 * self._bit(b)) * (1 << b)

    def _send_half(self, k, b):
        half = self.size // 2
        bit = self._bit(b)
        keep = pl.multiple_of(self.off + bit * half, 16)
        give = pl.multiple_of(self.off + (1 - bit) * half, 16)
        self.trail.append(self.off)
        copy = self.links.copy(self.held.at[pl.ds(give, half)], self.boxes[k], self.base + k, dp=self._peer(b))
        copy.start()
        self.sent.append(copy)
        self.off, self.size = keep, half

    def _add_half(self, k, b, last):
        self.links.arrived(self.boxes[k], self.base + k, dp=self._peer(b))
        rows = pl.ds(self.off, self.size)
        total = (self.held[rows, :].astype(wide) + self.boxes[k][...].astype(wide)).astype(low)
        if last:
            self.whole[rows, :] = total
        else:
            self.held[rows, :] = total

    def _swap_send(self, k, b):
        n = len(self.halving)
        rows = pl.ds(self.off, self.size)
        self.held[rows, :] = self.whole[rows, :]
        at = self.base + 2 * n + k
        copy = self.links.copy(self.held.at[rows], self.boxes[n + k], at, dp=self._peer(b))
        copy.start()
        self.sent.append(copy)

    def _swap_add(self, k, b):
        n = len(self.halving)
        rows = pl.ds(self.off, self.size)
        self.links.arrived(self.boxes[n + k], self.base + 2 * n + k, dp=self._peer(b))
        self.sent[-1].wait_send()
        self.sent.pop()
        self.whole[rows, :] = (
            self.whole[rows, :].astype(wide) + self.boxes[n + k][...].astype(wide)
        ).astype(low)

    def _grow_send(self, k, b):
        view = self.whole.at[pl.ds(self.off, self.size)]
        copy = self.links.copy(view, view, self.base + len(self.halving) + k, dp=self._peer(b))
        copy.start()
        self.sent.append(copy)

    def _grow_wait(self, k, b):
        base = self.trail[k]
        other = pl.multiple_of(base + (1 - self._bit(b)) * self.size, 16)
        view = self.whole.at[pl.ds(other, self.size)]
        self.links.arrived(view, self.base + len(self.halving) + k, dp=self._peer(b))
        self.off, self.size = base, self.size * 2

    def step(self, amount=1):
        for _ in range(min(amount, len(self.steps))):
            self.steps.pop(0)()

    def finish(self):
        self.step(len(self.steps))
        for copy in self.sent:
            copy.wait_send()


def greet(axis, me, count):
    barrier = pltpu.get_barrier_semaphore()

    def one(j, carry):
        pl.semaphore_signal(
            barrier, inc=1, device_id={axis: lax.rem(me + j, count)}, device_id_type=MESH
        )
        return carry

    lax.fori_loop(1, count, one, 0)


def await_greetings(amount):
    pl.semaphore_wait(pltpu.get_barrier_semaphore(), amount)


def halves(rows):
    first = round_up(rows // 2, 16)
    return ((0, first), (first, rows - first))


def head_masks(shape, local_heads):
    lane = lax.broadcasted_iota(jnp.int32, shape, 1)
    return [
        jnp.where((lane >= h * HEAD_DIM) & (lane < (h + 1) * HEAD_DIM), 1.0, 0.0)
        for h in range(local_heads)
    ], lane


def first_kernel(n, *refs):
    S = types.SimpleNamespace(**dict(zip(FIRST, refs)))
    links = Links(S.send, S.recv)
    t = lax.axis_index("tensor")
    greet("tensor", t, 4)
    R, own, W, H = n.R, n.own, n.W, n.H

    S.xf[...] = jnp.zeros_like(S.xf)
    S.xf[0:own, :] = S.x[...].astype(wide)
    unit, _ = standardize(S.xf[...])
    S.a1[t] = (unit * S.g1[...] + S.b1[...]).astype(low)
    S.cot4[t] = jnp.zeros((R, n.D), low)
    S.cot4[t, 0:own, :] = S.cot[...].astype(low)
    S.ow4[t] = S.ow[...]
    await_greetings(3)
    rows_in = Gather(links, S.a1, t, halves(R))
    cot_in = Gather(links, S.cot4, t, halves(R))
    ow_in = Gather(links, S.ow4, t, ((0, W),))
    rows_in.start()
    S.k[...] = jnp.zeros_like(S.k)
    S.v[...] = jnp.zeros_like(S.v)
    length = S.lengths[0]

    def project(i, carry):
        s = flipped(t, i // 2, i % 2)

        @pl.when(i == 1)
        def _():
            rows_in.wait_sib()

        @pl.when(i == 2)
        def _():
            rows_in.forward()
            cot_in.start()
            ow_in.start()

        @pl.when(i == 3)
        def _():
            rows_in.wait_diag()

        out = dot(S.a1[s], S.wqkv[...]) + S.bqkv[...]
        S.q[s] = (out[:, :H].astype(low).astype(wide) * HEAD_DIM**-0.5).astype(low)
        row = lax.broadcasted_iota(jnp.int32, (R, H), 0)
        lane = lax.broadcasted_iota(jnp.int32, (R, H), 1)
        absent = (row >= own) | (row + s * own >= length)
        at = pl.ds(pl.multiple_of(s * R, 16), R)
        S.k[at, :] = jnp.where((lane == W) & absent, -8e30, out[:, H : 2 * H]).astype(low)
        S.v[at, :] = out[:, 2 * H :].astype(low)
        return carry

    lax.fori_loop(0, 4, project, 0)
    if n.K > 4 * R:
        lane = lax.broadcasted_iota(jnp.int32, (n.K - 4 * R, H), 1)
        S.k[4 * R :, :] = jnp.where(lane == W, -8e30, 0.0).astype(low)
    S.kt[...] = jnp.transpose(S.k[...])
    S.vt[...] = jnp.transpose(S.v[...])

    masks, lane = head_masks((1, H), n.heads)
    base = links.take(4)

    def attend(i, carry):
        s = flipped(t, 1 - i // 2, (i + i // 2) % 2)
        query = S.q[s]
        mixed = jnp.zeros((R, H), wide)
        inverse = jnp.zeros((R, H), wide)
        for h in range(n.heads):
            here = jnp.where(lane == W, 1.0, masks[h]).astype(low)
            scores = dot(query * here, S.kt[...])
            terms = jnp.exp(scores - jnp.max(scores, -1, keepdims=True)).astype(low)
            S.e[h, s] = terms
            part = dot(terms, S.v[...])
            scale = 1.0 / part[:, W : W + 1]
            mixed += part * (scale * masks[h])
            inverse += scale * masks[h]
        S.o[s] = mixed
        S.inv[s] = inverse
        S.mix[s] = mixed[:, :W].astype(low)

        @pl.when(i < 3)
        def _():
            links.copy(S.mix.at[s], S.mix4.at[t], base + i, tensor=s).start()

        @pl.when(i == 0)
        def _():
            cot_in.wait_sib()
            cot_in.forward()
            ow_in.wait_sib()

        @pl.when(i == 1)
        def _():
            ow_in.forward()
            cot_in.wait_diag()

        @pl.when(i == 2)
        def _():
            ow_in.wait_diag()

        return carry

    lax.fori_loop(0, 4, attend, 0)
    S.mix4[t] = S.mix[t]
    for i in range(3):
        s = flipped(t, 1 - i // 2, (i + i // 2) % 2)
        links.arrived(S.mix4.at[s], base + i, tensor=s)

    total = S.xf[...] + S.ob[...]
    for j in range(4):
        total += dot(S.mix4[j], S.ow4[j])
    S.hid[...] = total
    unit, _ = standardize(total)
    S.a2[...] = (unit * S.g2[...] + S.b2[...]).astype(low)
    for i in range(3):
        s = flipped(t, 1 - i // 2, (i + i // 2) % 2)
        links.copy(S.mix.at[s], S.mix4.at[t], base + i, tensor=s).wait_send()
    for gather in (rows_in, cot_in, ow_in):
        gather.finish()
    links.finish()


FIRST = (
    "x", "lengths", "g1", "b1", "wqkv", "bqkv", "ow", "ob", "g2", "b2", "cot", "a1", "cot4", "ow4", "q", "k",
    "vt", "e", "inv", "o", "mix", "hid", "a2", "xf", "v", "kt", "mix4", "send", "recv",
)


def second_kernel(n, *refs):
    S = types.SimpleNamespace(**dict(zip(SECOND, refs)))
    links = Links(S.send, S.recv)
    t = lax.axis_index("tensor")
    greet("tensor", t, 4)
    R, own = n.R, n.own
    S.a24[t] = S.a2[...]
    await_greetings(3)
    rows_in = Gather(links, S.a24, t, halves(R))
    rows_in.start()
    S.wupt[...] = jnp.transpose(S.wup[...])
    S.wdnt[...] = jnp.transpose(S.wdn[...])
    back = Reduce(links, S.ga2p, S.pre1, S.near1, S.far1, S.out1, t)
    ahead = Reduce(links, S.fop, S.pre2, S.near2, S.far2, S.out2, t)
    S.gub[...] = jnp.zeros_like(S.gub)

    def feed(i, carry):
        s = flipped(t, i // 2, i % 2)

        @pl.when(i == 1)
        def _():
            rows_in.wait_sib()

        @pl.when(i == 2)
        def _():
            rows_in.forward()

        @pl.when(i == 3)
        def _():
            rows_in.wait_diag()

        up = dot(S.a24[s], S.wup[...]) + S.bup[...]
        square = up * up
        c = 0.7978845608028654
        bend = jnp.tanh(c * up * (1.0 + 0.044715 * square))
        half = 0.5 * (1.0 + bend)
        slope = half + 0.5 * up * (1.0 - bend * bend) * (c + (3 * 0.044715 * c) * square)
        active = (up * half).astype(low)
        S.act[s] = active
        grad = (dot(S.cot4[s], S.wdnt[...]) * slope).astype(low)
        S.gup[s] = grad
        S.ga2p[s] = dot(grad, S.wupt[...]).astype(low)

        @pl.when(i == 1)
        def _():
            back.send_sib()

        @pl.when(i == 3)
        def _():
            back.send_diag()

        S.fop[s] = dot(active, S.wdn[...]).astype(low)

        @pl.when(i == 1)
        def _():
            ahead.send_sib()

        @pl.when(i == 3)
        def _():
            ahead.send_diag()

        S.gub[...] += jnp.sum(grad.astype(wide), 0, keepdims=True)
        return carry

    lax.fori_loop(0, 4, feed, 0)
    back.send_cross()
    tile = 256

    def weights(j, carry):
        at = pl.ds(pl.multiple_of(j * tile, tile), tile)
        left = S.a24[:, :, at].reshape(4 * R, tile)
        S.gw[at, :] = dot_columns(left, flat(S.gup)).astype(low)
        left = S.act[:, :, at].reshape(4 * R, tile)
        S.gw[pl.ds(pl.multiple_of(n.D + j * tile, tile), tile), :] = dot_columns(
            left, flat(S.cot4)
        ).astype(low)
        return carry

    lax.fori_loop(0, n.D // tile, weights, 0)
    ahead.send_cross()
    S.ga2[...] = back.result()
    result = S.hid[...] + (ahead.result() + S.db[...])
    S.output[...] = result[:own].astype(low)
    rows_in.finish()
    back.finish()
    ahead.finish()
    links.finish()


SECOND = (
    "a2", "cot4", "wup", "bup", "wdn", "db", "hid", "ga2", "output", "gw", "gub", "a24", "wupt", "wdnt",
    "act", "gup", "ga2p", "fop", "pre1", "near1", "far1", "out1", "pre2", "near2", "far2", "out2", "send",
    "recv",
)


def third_kernel(n, *refs):
    S = types.SimpleNamespace(**dict(zip(THIRD, refs)))
    links = Links(S.send, S.recv)
    t = lax.axis_index("tensor")
    d = lax.axis_index("dp")
    greet("tensor", t, 4)
    greet("dp", d, n.dp)
    R, own, W, H, D = n.R, n.own, n.W, n.H, n.D

    unit, inverse = standardize(S.hid[...])
    grad = S.ga2[...]
    S.small[...] = jnp.zeros_like(S.small)
    S.small[2:3, :] = jnp.sum(grad * unit, 0, keepdims=True)
    S.small[3:4, :] = jnp.sum(grad, 0, keepdims=True)
    S.gh[...] = norm_back(grad, unit, inverse, S.g2[...])
    S.gh[0:own, :] += S.cot[...]
    hidden_low = S.gh[...].astype(low)
    S.hl4[t] = hidden_low
    S.small[4:5, :] = jnp.sum(hidden_low.astype(wide), 0, keepdims=True)
    S.small[5:6, :] = jnp.sum(S.cot[...].astype(low).astype(wide), 0, keepdims=True)
    S.small[6:7, :] = S.gub[...]
    await_greetings(3 + n.dp - 1)

    base = links.take(4)

    def share(i, carry):
        s = flipped(t, 1 - i // 2, (i + i // 2) % 2)
        S.gms[s] = dot_rows(S.hl4[t], S.ow4[s]).astype(low)

        @pl.when(i < 3)
        def _():
            links.copy(S.gms.at[s], S.gm4.at[t], base + i, tensor=s).start()

        return carry

    lax.fori_loop(0, 4, share, 0)
    S.gm4[t] = S.gms[t]
    rows_in = Gather(links, S.hl4, t, halves(R))
    rows_in.start()
    sums = [
        DataReduce(links, S.gw, S.whole1, (S.b10, S.b11, S.b12) + S.spare[0], 0, D, d, n.dp, (0, 1, 2)),
        DataReduce(links, S.gw, S.whole1, (S.b20, S.b21, S.b22) + S.spare[1], D, D, d, n.dp, (1, 0, 2)),
    ]

    def tick(amount):
        for _ in range(amount):
            for r in sums:
                r.step()

    tick(1)
    S.dkt[...] = jnp.zeros_like(S.dkt)
    S.dvt[...] = jnp.zeros_like(S.dvt)
    S.do[...] = jnp.zeros_like(S.do)
    masks, lane = head_masks((1, H), n.heads)

    def pull(i):
        s = flipped(t, i // 2, i % 2)
        order = (3, 2, 0, 1)[i]
        if i > 0:
            links.arrived(S.gm4.at[s], base + order, tensor=s)
        S.do[:, :W] = S.gm4[s].astype(wide)
        scaled = (S.do[...] * S.inv[s]).astype(low)
        scaled_t = jnp.transpose(scaled)
        product = scaled.astype(wide) * S.o[s]
        query_t = jnp.transpose(S.q[s])
        dq = jnp.zeros((R, H), wide)
        for h in range(n.heads):
            inner = -jnp.sum(product * masks[h], -1, keepdims=True)
            upper = inner.astype(low).astype(wide)
            left = (
                scaled.astype(wide) * masks[h]
                + jnp.where(lane == W, upper, 0.0)
                + jnp.where(lane == W + 1, inner - upper, 0.0)
            ).astype(low)
            grad_p = dot(left, S.vt[...])
            terms = S.e[h, s]
            grad_s = (terms.astype(wide) * grad_p).astype(low)
            dq += dot(grad_s, S.k[...]) * masks[h]
            at = slice(h * HEAD_DIM, (h + 1) * HEAD_DIM)
            S.dkt[at, :] += dot(query_t[at, :], grad_s)
            S.dvt[at, :] += dot(scaled_t[at, :], terms)
        S.dqkv[s, :, 0:H] = (dq * HEAD_DIM**-0.5).astype(low)

    for i in range(4):
        pull(i)
        tick(2)
        if i == 0:
            rows_in.wait_sib()
        elif i == 1:
            rows_in.forward()
        elif i == 2:
            rows_in.wait_diag()

    S.dktl[...] = S.dkt[...].astype(low)
    S.dvtl[...] = S.dvt[...].astype(low)
    pad = jnp.zeros((R, H - W), low)
    for part, grad_t in ((1, S.dktl), (2, S.dvtl)):
        back = jnp.transpose(grad_t[...])
        for s in range(4):
            S.dqkv[s, :, part * H : part * H + W] = back[s * R : (s + 1) * R]
            S.dqkv[s, :, part * H + W : (part + 1) * H] = pad
    dqt = jnp.transpose(flat(S.dqkv.at[:, :, 0:H]))
    rows_all = flat(S.a1)
    S.gw2[0:W, :] = dot(dqt[:W], rows_all).astype(low)
    S.gw2[W : 2 * W, :] = dot(S.dktl[:, : 4 * R], rows_all).astype(low)
    S.gw2[2 * W : 3 * W, :] = dot(S.dvtl[:, : 4 * R], rows_all).astype(low)
    S.gw2[3 * W :, :] = dot_columns(flat(S.mix), flat(S.hl4)).astype(low)
    S.small[7:8, 0:H] = jnp.sum(flat(S.dqkv.at[:, :, 0:H]).astype(wide), 0, keepdims=True)
    S.small[7:8, H : 2 * H] = jnp.sum(
        flat(S.dqkv.at[:, :, 2 * H : 3 * H]).astype(wide), 0, keepdims=True
    )
    sums += [
        DataReduce(links, S.gw2, S.whole2, (S.b30, S.b31, S.b32) + S.spare[2], 0, D // 2, d, n.dp, (0, 1, 2)),
        DataReduce(links, S.gw2, S.whole2, (S.b40, S.b41, S.b42) + S.spare[3], D // 2, D // 2, d, n.dp, (1, 0, 2)),
    ]
    tick(1)

    down = Reduce(links, S.ga1p, S.pre, S.near, S.far, S.out, t)

    def lead(i, carry):
        s = flipped(t, 1 - i // 2, 1 - i % 2)
        S.ga1p[s] = dot_rows(S.dqkv[s], S.wqkv[...]).astype(low)

        @pl.when(i == 0)
        def _():
            down.send_diag()

        @pl.when(i == 2)
        def _():
            down.send_sib()

        return carry

    lax.fori_loop(0, 4, lead, 0)
    down.send_cross()
    tick(2)
    S.xf[...] = jnp.zeros_like(S.xf)
    S.xf[0:own, :] = S.x[...].astype(wide)
    unit, inverse = standardize(S.xf[...])
    grad = down.result()
    S.small[0:1, :] = jnp.sum(grad * unit, 0, keepdims=True)
    S.small[1:2, :] = jnp.sum(grad, 0, keepdims=True)
    S.small4[t] = S.small[...]
    base3 = links.take(3)
    for j in range(3):
        peer = lax.rem(t + j + 1, 4)
        links.start(S.small4.at[t], S.small4.at[t], base3 + j, tensor=peer)
    total = S.gh[...] + norm_back(grad, unit, inverse, S.g1[...])
    S.gt[...] = total[:own]
    for j in range(3):
        peer = lax.rem(t + 3 - j, 4)
        links.arrived(S.small4.at[peer], base3 + j, tensor=peer)
    over = S.small4[0] + S.small4[1] + S.small4[2] + S.small4[3]
    row = lax.broadcasted_iota(jnp.int32, over.shape, 0)
    S.smalls[d] = jnp.where(row < 6, over, S.small[...])
    base4 = links.take(n.dp)

    def tell(j, carry):
        links.copy(S.smalls.at[d], S.smalls.at[d], base4 + j, dp=lax.rem(d + j, n.dp)).start()
        return carry

    lax.fori_loop(1, n.dp, tell, 0)
    for r in sums:
        r.finish()

    def hear(j, carry):
        peer = lax.rem(d + n.dp - j, n.dp)
        links.arrived(S.smalls.at[peer], base4 + j, dp=peer)
        return carry

    lax.fori_loop(1, n.dp, hear, 0)
    S.small_sum[...] = lax.fori_loop(
        1, n.dp, lambda j, acc: acc + S.smalls[j], S.smalls[0]
    )

    def done(j, carry):
        links.copy(S.smalls.at[d], S.smalls.at[d], base4 + j, dp=lax.rem(d + j, n.dp)).wait_send()
        return carry

    lax.fori_loop(1, n.dp, done, 0)
    for i in range(3):
        s = flipped(t, 1 - i // 2, (i + i // 2) % 2)
        links.copy(S.gms.at[s], S.gm4.at[t], base + i, tensor=s).wait_send()
    rows_in.finish()
    down.finish()
    links.finish()


THIRD = (
    "ga2", "hid", "g2", "cot", "ow4", "q", "k", "vt", "e", "inv", "o", "mix", "a1", "wqkv", "x", "g1", "gw",
    "gub", "gt", "whole1", "whole2", "small_sum", "small", "gh", "hl4", "gms", "gm4", "dkt", "dvt", "do",
    "dqkv", "dktl", "dvtl", "gw2", "ga1p", "pre", "near", "far", "out", "xf", "small4", "smalls", "b10",
    "b11", "b12", "b20", "b21", "b22", "b30", "b31", "b32", "b40", "b41", "b42", "spare", "send", "recv",
)


def body(
    tokens,
    lengths,
    ln1_gain,
    ln1_shift,
    qkv_weight,
    qv_bias,
    out_weight,
    out_bias,
    ln2_gain,
    ln2_shift,
    up_weight,
    up_bias,
    down_weight,
    down_bias,
    cotangent,
):
    own, D = tokens.shape
    W = qkv_weight.shape[2]
    F = up_weight.shape[1]
    dp = lax.axis_size("dp")
    assert lax.axis_size("tensor") == 4 and lengths.shape[0] == 1 and F == D and 4 * W == D
    R = round_up(own, 16)
    H = round_up(W + 2, 128)
    K = round_up(4 * R, 256)
    n = types.SimpleNamespace(own=own, D=D, W=W, F=F, R=R, H=H, K=K, dp=dp, heads=W // HEAD_DIM)
    vmem, smem = pl.BlockSpec(memory_space=pltpu.VMEM), pl.BlockSpec(memory_space=pltpu.SMEM)
    row = lambda v: v.reshape(1, -1)

    def call(kernel, args, outs, scratch, number, sems, scalar=()):
        return pl.pallas_call(
            lambda *refs: kernel(n, *refs),
            out_shape=tuple(jax.ShapeDtypeStruct(s, ty) for s, ty in outs),
            in_specs=[smem if i in scalar else vmem for i in range(len(args))],
            out_specs=tuple(vmem for _ in outs),
            scratch_shapes=[pltpu.VMEM(s, ty) if not isinstance(s, list) else s for s, ty in scratch]
            + [pltpu.SemaphoreType.DMA((sems,)), pltpu.SemaphoreType.DMA((sems,))],
            compiler_params=pltpu.CompilerParams(
                collective_id=number, has_side_effects=True, vmem_limit_bytes=VMEM_BYTES
            ),
        )(*args)

    wqkv = jnp.pad(qkv_weight, ((0, 0), (0, 0), (0, H - W))).reshape(D, 3 * H)
    at = jnp.arange(H)
    bqkv = jnp.pad(qv_bias, ((0, 0), (0, H - W)))
    bqkv = jnp.concatenate(
        [
            jnp.where(at == W, 1.0, bqkv[0]),
            jnp.zeros((H,), wide),
            jnp.where((at == W) | (at == W + 1), 1.0, bqkv[1]),
        ]
    )
    rows4 = ((4, R, D), low)
    a1, cot4, ow4, q, k, vt, e, inv, o, mix, hid, a2 = call(
        first_kernel,
        (
            tokens, lengths, row(ln1_gain), row(ln1_shift), wqkv, row(bqkv), out_weight,
            row(out_bias), row(ln2_gain), row(ln2_shift), cotangent,
        ),
        (
            rows4, rows4, ((4, W, D), low), ((4, R, H), low), ((K, H), low), ((H, K), low),
            ((n.heads, 4, R, K), low), ((4, R, H), wide), ((4, R, H), wide), ((4, R, W), low),
            ((R, D), wide), ((R, D), low),
        ),
        (((R, D), wide), ((K, H), low), ((H, K), low), ((4, R, W), low)),
        0,
        32,
        (1,),
    )
    slab = ((R, D), low)
    ga2, output, gw, gub = call(
        second_kernel,
        (a2, cot4, up_weight, row(up_bias), down_weight, row(down_bias), hid),
        (((R, D), wide), ((own, D), low), ((2 * D, D), low), ((1, F), wide)),
        (rows4, ((D, D), low), ((D, D), low), rows4, rows4, rows4, rows4) + (slab,) * 8,
        1,
        32,
    )
    boxes = [((D // k, D), low) for k in (2, 4, 8)]
    extra = max(0, dp.bit_length() - 1 - 3)
    spare = [((D // 8, D), low)] * extra, [((D // 16, D), low)] * extra
    names = THIRD

    def third(n, *refs):
        refs = list(refs)
        cut = len(names) - 3
        flat_spare = refs[cut : cut + 4 * extra]
        groups = [tuple(flat_spare[g * extra : (g + 1) * extra]) for g in range(4)]
        third_kernel(n, *refs[:cut], groups, *refs[cut + 4 * extra :])

    gt, whole1, whole2, small = call(
        third,
        (
            ga2, hid, row(ln2_gain), cotangent, ow4, q, k, vt, e, inv, o, mix, a1, wqkv, tokens,
            row(ln1_gain), gw, gub,
        ),
        (((own, D), wide), ((2 * D, D), low), ((D, D), low), ((8, D), wide)),
        [
            ((8, D), wide), ((R, D), wide), rows4, ((4, R, W), low), ((4, R, W), low), ((W, K), wide),
            ((W, K), wide), ((R, H), wide), ((4, R, 3 * H), low), ((W, K), low), ((W, K), low),
            ((D, D), low), rows4, slab, slab, slab, slab, ((R, D), wide), ((4, 8, D), wide),
            ((dp, 8, D), wide),
        ]
        + boxes + boxes + [((D // k, D), low) for k in (4, 8, 16)] * 2
        + spare[0] * 2 + spare[1] * 2,
        2,
        96 + dp,
    )
    grad_qkv = jnp.transpose(whole2[: 3 * W].astype(wide).reshape(3, W, D), (2, 0, 1))
    return (
        output,
        gt,
        small[0],
        small[1],
        grad_qkv,
        jnp.stack([small[7, :W], small[7, H : H + W]]),
        whole2[3 * W :].astype(wide),
        small[4],
        small[2],
        small[3],
        whole1[:D].astype(wide),
        small[6],
        whole1[D:].astype(wide),
        small[5],
    )


def solution(mesh):
    placed = (
        P(("dp", "tensor"), None),
        P("dp"),
        P(),
        P(),
        P(None, None, "tensor"),
        P(None, "tensor"),
        P("tensor", None),
        P(),
        P(),
        P(),
        P(None, "tensor"),
        P("tensor"),
        P("tensor", None),
        P(),
        P(("dp", "tensor"), None),
    )
    return jax.shard_map(
        body,
        mesh=mesh,
        in_specs=placed,
        out_specs=(
            P(("dp", "tensor"), None),
            P(("dp", "tensor"), None),
            P(),
            P(),
            P(None, None, "tensor"),
            P(None, "tensor"),
            P("tensor", None),
            P(),
            P(),
            P(),
            P(None, "tensor"),
            P("tensor"),
            P("tensor", None),
            P(),
        ),
        check_vma=False,
    )
```

```python
import types

import jax
import jax.numpy as jnp
from jax import lax
from jax.experimental import pallas as pl
from jax.experimental.pallas import tpu as pltpu
from jax.sharding import PartitionSpec as P

HEAD_DIM = 64
MESH = pl.DeviceIdType.MESH
VMEM_BYTES = 62 * 2**20

epsilon = 1e-06
low = jnp.bfloat16
wide = jnp.float32


def round_up(amount, unit):
    return -(-amount // unit) * unit


def flipped(t, flip_chip, flip_core):
    return (t // 2 + flip_chip) % 2 * 2 + (t % 2 + flip_core) % 2


def dot(left, right):
    return jnp.dot(left, right, preferred_element_type=wide)


def dot_rows(left, right):
    return lax.dot_general(left, right, (((1,), (1,)), ((), ())), preferred_element_type=wide)


def dot_columns(left, right):
    return lax.dot_general(left, right, (((0,), (0,)), ((), ())), preferred_element_type=wide)


def standardize(values):
    center = values - jnp.mean(values, -1, keepdims=True)
    inverse = lax.rsqrt(jnp.mean(center * center, -1, keepdims=True) + epsilon)
    return center * inverse, inverse


def norm_back(grad, unit, inverse, gain):
    scaled = grad * gain
    return inverse * (
        scaled
        - jnp.mean(scaled, -1, keepdims=True)
        - unit * jnp.mean(scaled * unit, -1, keepdims=True)
    )


def flat(ref):
    a, b, c = ref.shape
    return ref[...].reshape(a * b, c)


class Links:
    def __init__(self, send, recv):
        self.send, self.recv, self.used, self.pending = send, recv, 0, []

    def take(self, amount=1):
        base = self.used
        self.used += amount
        assert self.used <= self.send.shape[0]
        return base

    def copy(self, src, dst, at, **where):
        return pltpu.make_async_remote_copy(
            src_ref=src,
            dst_ref=dst,
            send_sem=self.send.at[at],
            recv_sem=self.recv.at[at],
            device_id=where,
            device_id_type=MESH,
        )

    def start(self, src, dst, at, **where):
        copy = self.copy(src, dst, at, **where)
        copy.start()
        self.pending.append(copy)

    def arrived(self, dst, at, **where):
        self.copy(dst, dst, at, **where).wait_recv()

    def finish(self):
        for copy in self.pending:
            copy.wait_send()
        self.pending = []


class Gather:
    def __init__(self, links, buf, t, parts):
        self.links, self.buf, self.t, self.parts = links, buf, t, parts
        self.sib, self.cross, self.diag = flipped(t, 0, 1), flipped(t, 1, 0), flipped(t, 1, 1)
        self.base = links.take(3 * len(parts))

    def view(self, slot, part):
        start, size = self.parts[part]
        return self.buf.at[slot, pl.ds(start, size)]

    def _each(self):
        return range(len(self.parts))

    def start(self):
        for p in self._each():
            v = self.view(self.t, p)
            self.links.copy(v, v, self.base + 3 * p, tensor=self.cross).start()
        for p in self._each():
            v = self.view(self.t, p)
            self.links.copy(v, v, self.base + 3 * p + 1, tensor=self.sib).start()

    def wait_sib(self):
        for p in self._each():
            self.links.arrived(self.view(self.sib, p), self.base + 3 * p + 1, tensor=self.sib)

    def forward(self):
        for p in self._each():
            v = self.view(self.cross, p)
            self.links.arrived(v, self.base + 3 * p, tensor=self.cross)
            self.links.copy(v, v, self.base + 3 * p + 2, tensor=self.sib).start()

    def wait_diag(self):
        for p in self._each():
            self.links.arrived(self.view(self.diag, p), self.base + 3 * p + 2, tensor=self.sib)

    def finish(self):
        for p in self._each():
            v = self.view(self.t, p)
            self.links.copy(v, v, self.base + 3 * p, tensor=self.cross).wait_send()
            self.links.copy(v, v, self.base + 3 * p + 1, tensor=self.sib).wait_send()
            v = self.view(self.cross, p)
            self.links.copy(v, v, self.base + 3 * p + 2, tensor=self.sib).wait_send()


class Reduce:
    def __init__(self, links, part, pre, near, far, t):
        self.links, self.part, self.pre, self.near, self.far, self.t = links, part, pre, near, far, t
        self.sib, self.cross, self.diag = flipped(t, 0, 1), flipped(t, 1, 0), flipped(t, 1, 1)
        self.base = links.take(3)

    def send_diag(self):
        self.links.copy(self.part.at[self.diag], self.pre, self.base, tensor=self.sib).start()

    def send_sib(self):
        self.links.copy(self.part.at[self.sib], self.near, self.base + 1, tensor=self.sib).start()

    def send_cross(self):
        self.links.arrived(self.pre, self.base, tensor=self.sib)
        total = self.part[self.cross].astype(wide) + self.pre[...].astype(wide)
        self.part[self.cross] = total.astype(low)
        self.links.copy(self.part.at[self.cross], self.far, self.base + 2, tensor=self.cross).start()

    def result(self):
        self.links.arrived(self.near, self.base + 1, tensor=self.sib)
        self.links.arrived(self.far, self.base + 2, tensor=self.cross)
        return (
            self.part[self.t].astype(wide) + self.near[...].astype(wide) + self.far[...].astype(wide)
        )

    def finish(self):
        self.links.copy(self.part.at[self.diag], self.pre, self.base, tensor=self.sib).wait_send()
        self.links.copy(self.part.at[self.sib], self.near, self.base + 1, tensor=self.sib).wait_send()
        self.links.copy(self.part.at[self.cross], self.far, self.base + 2, tensor=self.cross).wait_send()


class DataReduce:
    def __init__(self, links, held, whole, share, box, box_at, first, rows, d, count, order):
        self.links, self.held, self.whole, self.share = links, held, whole, share
        bits = count.bit_length() - 1
        assert count == 1 << bits and bits >= 3 and rows % 128 == 0
        self.extra = [b for b in range(bits) if b not in order]
        self.d, self.off, self.size = d, first, rows
        self.trail, self.sent, self.boxes = [], [], []
        for size in [rows // 2, rows // 4, rows // 8] + [rows // 8] * len(self.extra):
            self.boxes.append(box.at[pl.ds(box_at, size)])
            box_at += size
        self.order = order
        self.base = links.take(7 + len(self.extra))
        self.steps = [lambda: self._send_half(0)]
        for k in (1, 2):
            self.steps.append(lambda k=k: (self._add_half(k - 1), self._send_half(k)))
        self.steps.append(lambda: (self._add_half(2), self._swap(), self._place(), self._grow_send(2)))
        for k in (2, 1):
            self.steps.append(lambda k=k: (self._grow_wait(k), self._grow_send(k - 1)))
        self.steps.append(lambda: self._grow_wait(0))

    @staticmethod
    def box_rows(rows, count):
        return rows // 8 * (7 + count.bit_length() - 1 - 3)

    def _bit(self, b):
        return self.d // (1 << b) % 2

    def _peer(self, b):
        return self.d + (1 - 2 * self._bit(b)) * (1 << b)

    def _start(self, copy):
        copy.start()
        self.sent.append(copy)

    def _send_half(self, k):
        b = self.order[k]
        half = self.size // 2
        bit = self._bit(b)
        keep = pl.multiple_of(self.off + bit * half, 16)
        give = pl.multiple_of(self.off + (1 - bit) * half, 16)
        self.trail.append(self.off)
        view = self.held.at[pl.ds(give, half)]
        self._start(self.links.copy(view, self.boxes[k], self.base + k, dp=self._peer(b)))
        self.off, self.size = keep, half

    def _add_half(self, k):
        self.links.arrived(self.boxes[k], self.base + k, dp=self._peer(self.order[k]))
        rows = pl.ds(self.off, self.size)
        total = (self.held[rows, :].astype(wide) + self.boxes[k][...].astype(wide)).astype(low)
        if k == 2:
            self.share[...] = total
        else:
            self.held[rows, :] = total

    def _swap(self):
        for k, b in enumerate(self.extra):
            box, at = self.boxes[3 + k], self.base + 7 + k
            copy = self.links.copy(self.share, box, at, dp=self._peer(b))
            copy.start()
            self.links.arrived(box, at, dp=self._peer(b))
            copy.wait_send()
            self.share[...] = (self.share[...].astype(wide) + box[...].astype(wide)).astype(low)

    def _place(self):
        self.placed = pltpu.make_async_copy(
            self.share, self.whole.at[pl.ds(self.off, self.size)], self.links.send.at[self.base + 6]
        )
        self.placed.start()

    def _grow_send(self, k):
        b = self.order[k]
        view = self.whole.at[pl.ds(self.off, self.size)]
        src = self.share if k == 2 else view
        self._start(self.links.copy(src, view, self.base + 3 + k, dp=self._peer(b)))

    def _grow_wait(self, k):
        base = self.trail[k]
        if k == 2:
            self.placed.wait()
        other = pl.multiple_of(base + (1 - self._bit(self.order[k])) * self.size, 16)
        view = self.whole.at[pl.ds(other, self.size)]
        self.links.arrived(view, self.base + 3 + k, dp=self._peer(self.order[k]))
        self.off, self.size = base, self.size * 2

    def step(self):
        if self.steps:
            self.steps.pop(0)()

    def finish(self):
        assert not self.steps
        for copy in self.sent:
            copy.wait_send()


class Pipeline:
    def __init__(self):
        self.members = []

    def add(self, member):
        self.members.append(member)
        member.step()

    def tick(self, amount=1):
        for _ in range(amount):
            left = [m for m in self.members if m.steps]
            if left:
                max(left, key=lambda m: len(m.steps)).step()

    def finish(self):
        while any(m.steps for m in self.members):
            self.tick()
        for m in self.members:
            m.finish()


def greet(axis, me, count):
    barrier = pltpu.get_barrier_semaphore()

    def one(j, carry):
        pl.semaphore_signal(
            barrier, inc=1, device_id={axis: lax.rem(me + j, count)}, device_id_type=MESH
        )
        return carry

    lax.fori_loop(1, count, one, 0)


def await_greetings(amount):
    pl.semaphore_wait(pltpu.get_barrier_semaphore(), amount)


def halves(rows):
    first = round_up(rows // 2, 16)
    return ((0, first), (first, rows - first))


def head_masks(shape, local_heads):
    lane = lax.broadcasted_iota(jnp.int32, shape, 1)
    return [
        jnp.where((lane >= h * HEAD_DIM) & (lane < (h + 1) * HEAD_DIM), 1.0, 0.0)
        for h in range(local_heads)
    ], lane


def kernel(n, S):
    links = Links(S.send, S.recv)
    t = lax.axis_index("tensor")
    d = lax.axis_index("dp")
    greet("tensor", t, 4)
    greet("dp", d, n.dp)
    R, own, W, H, D, K = n.R, n.own, n.W, n.H, n.D, n.K
    vector = lambda ref: ref[...].reshape(1, D)

    S.xf[...] = jnp.zeros_like(S.xf)
    S.xf[0:own, :] = S.x[...].astype(wide)
    unit, _ = standardize(S.xf[...])
    S.a1[t] = (unit * vector(S.g1) + vector(S.b1)).astype(low)
    S.cot4[t] = jnp.zeros((R, D), low)
    S.cot4[t, 0:own, :] = S.cot[...].astype(low)
    S.ow4[t] = S.ow[...]
    await_greetings(3 + n.dp - 1)
    rows_in = Gather(links, S.a1, t, halves(R))
    cot_in = Gather(links, S.cot4, t, halves(R))
    ow_in = Gather(links, S.ow4, t, ((0, W),))
    rows_in.start()
    S.gw[0:D, :] = jnp.transpose(S.wup[...])
    S.gw[D:, :] = jnp.transpose(S.wdn[...])
    S.v[4 * R :, :] = jnp.zeros((K - 4 * R, H), low)
    length = S.lengths[0]

    def project(i, carry):
        s = flipped(t, i // 2, i % 2)

        @pl.when(i == 1)
        def _():
            rows_in.wait_sib()

        @pl.when(i == 2)
        def _():
            rows_in.forward()
            cot_in.start()
            ow_in.start()

        @pl.when(i == 3)
        def _():
            rows_in.wait_diag()

        slab = S.a1[s]
        lane = lax.broadcasted_iota(jnp.int32, (R, H - W), 1)
        row = lax.broadcasted_iota(jnp.int32, (R, H - W), 0)
        absent = (row >= own) | (row + s * own >= length)
        at = pl.ds(pl.multiple_of(s * R, 16), R)
        out = dot(slab, S.wqkv[0]) + S.bq[0:1, :]
        S.q[s, :, :W] = (out.astype(low).astype(wide) * HEAD_DIM**-0.5).astype(low)
        S.q[s, :, W:] = jnp.where(lane == 0, HEAD_DIM**-0.5, 0.0).astype(low)
        S.k[at, :W] = dot(slab, S.wqkv[1]).astype(low)
        S.k[at, W:] = jnp.where((lane == 0) & absent, -8e30, 0.0).astype(low)
        S.v[at, :W] = (dot(slab, S.wqkv[2]) + S.bq[1:2, :]).astype(low)
        S.v[at, W:] = jnp.where(lane < 2, 1.0, 0.0).astype(low)
        return carry

    lax.fori_loop(0, 4, project, 0)
    if K > 4 * R:
        lane = lax.broadcasted_iota(jnp.int32, (K - 4 * R, H), 1)
        S.k[4 * R :, :] = jnp.where(lane == W, -8e30, 0.0).astype(low)
    S.kt[...] = jnp.transpose(S.k[...])
    S.vt[...] = jnp.transpose(S.v[...])

    masks, lane = head_masks((1, H), n.heads)
    mix_base = links.take(3)

    def attend(i, carry):
        s = flipped(t, 1 - i // 2, (i + i // 2) % 2)
        query = S.q[s]
        mixed = jnp.zeros((R, H), wide)
        inverse = jnp.zeros((R, H), wide)
        for h in range(n.heads):
            here = jnp.where(lane == W, 1.0, masks[h]).astype(low)
            scores = dot(query * here, S.kt[...])
            terms = jnp.exp(scores - jnp.max(scores, -1, keepdims=True)).astype(low)
            S.e[h, s] = terms
            part = dot(terms, S.v[...])
            scale = 1.0 / part[:, W : W + 1]
            mixed += part * (scale * masks[h])
            inverse += scale * masks[h]
        S.o[s] = mixed
        S.inv[s] = inverse
        S.mix[s] = mixed[:, :W].astype(low)

        @pl.when(i < 3)
        def _():
            links.copy(S.mix.at[s], S.mix4.at[t], mix_base + i, tensor=s).start()

        @pl.when(i == 0)
        def _():
            cot_in.wait_sib()
            ow_in.wait_sib()

        @pl.when(i == 1)
        def _():
            cot_in.forward()
            ow_in.forward()

        @pl.when(i == 2)
        def _():
            cot_in.wait_diag()
            ow_in.wait_diag()

        return carry

    lax.fori_loop(0, 4, attend, 0)
    S.mix4[t] = S.mix[t]
    for i in range(3):
        s = flipped(t, 1 - i // 2, (i + i // 2) % 2)
        links.arrived(S.mix4.at[s], mix_base + i, tensor=s)

    total = S.xf[...] + vector(S.ob)
    for j in range(4):
        total += dot(S.mix4[j], S.ow4[j])
    S.hid[...] = total
    unit, _ = standardize(total)
    S.a24[t] = (unit * vector(S.g2) + vector(S.b2)).astype(low)
    next_in = Gather(links, S.a24, t, halves(R))
    next_in.start()
    back = Reduce(links, S.part, S.pre1, S.near1, S.far1, t)
    ahead = Reduce(links, S.fop, S.pre2, S.near2, S.far2, t)
    S.gub[...] = jnp.zeros_like(S.gub)

    def feed(i, carry):
        s = flipped(t, i // 2, i % 2)

        @pl.when(i == 1)
        def _():
            next_in.wait_sib()

        @pl.when(i == 2)
        def _():
            next_in.forward()

        @pl.when(i == 3)
        def _():
            next_in.wait_diag()

        up = dot(S.a24[s], S.wup[...]) + vector(S.bup)
        square = up * up
        c = 0.7978845608028654
        bend = jnp.tanh(c * up * (1.0 + 0.044715 * square))
        half = 0.5 * (1.0 + bend)
        slope = half + 0.5 * up * (1.0 - bend * bend) * (c + (3 * 0.044715 * c) * square)
        active = (up * half).astype(low)
        S.act[s] = active
        grad = (dot(S.cot4[s], S.gw[D:, :]) * slope).astype(low)
        S.gup[s] = grad
        S.part[s] = dot(grad, S.gw[0:D, :]).astype(low)

        @pl.when(i == 1)
        def _():
            back.send_sib()

        @pl.when(i == 3)
        def _():
            back.send_diag()

        S.fop[s] = dot(active, S.wdn[...]).astype(low)

        @pl.when(i == 1)
        def _():
            ahead.send_sib()

        @pl.when(i == 3)
        def _():
            ahead.send_diag()

        S.gub[...] += jnp.sum(grad.astype(wide), 0, keepdims=True)
        return carry

    lax.fori_loop(0, 4, feed, 0)
    back.send_cross()

    sums = Pipeline()
    tile = D // 2
    box_at = 0

    def sum_over_dp(held, whole, first, rows, order):
        nonlocal box_at
        share = S.share.at[pl.ds(box_at // (7 + n.extra), rows // 8)]
        sums.add(DataReduce(links, held, whole, share, S.box, box_at, first, rows, d, n.dp, order))
        box_at += DataReduce.box_rows(rows, n.dp)

    for left, right, first in ((S.a24, S.gup, 0), (S.act, S.cot4, D)):
        for j in range(2):
            columns = left[:, :, j * tile : (j + 1) * tile].reshape(4 * R, tile)
            at = first + j * tile
            S.gw[at : at + tile, :] = dot_columns(columns, flat(right)).astype(low)
            sum_over_dp(S.gw, S.whole1, at, tile, (1, 0, 2) if at == tile else (0, 1, 2))
        if first == 0:
            ahead.send_cross()

    grad = back.result()
    unit, inverse = standardize(S.hid[...])
    S.small[...] = jnp.zeros_like(S.small)
    S.small[2:3, :] = jnp.sum(grad * unit, 0, keepdims=True)
    S.small[3:4, :] = jnp.sum(grad, 0, keepdims=True)
    S.gh[...] = norm_back(grad, unit, inverse, vector(S.g2))
    S.gh[0:own, :] += S.cot[...]
    hidden_low = S.gh[...].astype(low)
    S.hl4[t] = hidden_low
    S.small[4:5, :] = jnp.sum(hidden_low.astype(wide), 0, keepdims=True)
    S.small[5:6, :] = jnp.sum(S.cot4[t].astype(wide), 0, keepdims=True)
    S.small[6:7, :] = S.gub[...]
    gm_base = links.take(3)

    def share(i, carry):
        s = flipped(t, 1 - i // 2, (i + i // 2) % 2)
        S.mix4[s] = dot_rows(S.hl4[t], S.ow4[s]).astype(low)

        @pl.when(i < 3)
        def _():
            links.copy(S.mix4.at[s], S.gm4.at[t], gm_base + i, tensor=s).start()

        return carry

    lax.fori_loop(0, 4, share, 0)
    S.gm4[t] = S.mix4[t]
    hl_in = Gather(links, S.hl4, t, halves(R))
    hl_in.start()

    S.dkt[...] = jnp.zeros_like(S.dkt)
    S.dvt[...] = jnp.zeros_like(S.dvt)
    S.do[...] = jnp.zeros_like(S.do)
    sums.tick(2)

    for i in range(4):
        s = flipped(t, i // 2, i % 2)
        if i > 0:
            links.arrived(S.gm4.at[s], gm_base + (3, 2, 0, 1)[i], tensor=s)
        S.do[:, :W] = S.gm4[s].astype(wide)
        scaled = (S.do[...] * S.inv[s]).astype(low)
        scaled_t = jnp.transpose(scaled)
        product = scaled.astype(wide) * S.o[s]
        query_t = jnp.transpose(S.q[s])
        dq = jnp.zeros((R, H), wide)
        for h in range(n.heads):
            inner = -jnp.sum(product * masks[h], -1, keepdims=True)
            upper = inner.astype(low).astype(wide)
            left = (
                scaled.astype(wide) * masks[h]
                + jnp.where(lane == W, upper, 0.0)
                + jnp.where(lane == W + 1, inner - upper, 0.0)
            ).astype(low)
            grad_p = dot(left, S.vt[...])
            terms = S.e[h, s]
            grad_s = (terms.astype(wide) * grad_p).astype(low)
            dq += dot(grad_s, S.k[...]) * masks[h]
            at = slice(h * HEAD_DIM, (h + 1) * HEAD_DIM)
            S.dkt[at, :] += dot(query_t[at, :], grad_s)
            S.dvt[at, :] += dot(scaled_t[at, :], terms)
        S.gup[s, :, 0:H] = (dq * HEAD_DIM**-0.5).astype(low)
        sums.tick(5)
        if i == 0:
            hl_in.wait_sib()
        elif i == 1:
            hl_in.forward()
        elif i == 2:
            hl_in.wait_diag()
            S.gw2[3 * W :, :] = dot_columns(flat(S.mix), flat(S.hl4)).astype(low)

    S.kt[:W, :] = S.dkt[...].astype(low)
    S.vt[:W, :] = S.dvt[...].astype(low)
    pad = jnp.zeros((R, H - W), low)
    for part, grad_t in ((1, S.kt), (2, S.vt)):
        rows = jnp.transpose(grad_t[:W, :])
        for s in range(4):
            S.gup[s, :, part * H : part * H + W] = rows[s * R : (s + 1) * R]
            S.gup[s, :, part * H + W : (part + 1) * H] = pad
    dqt = jnp.transpose(flat(S.gup.at[:, :, 0:H]))
    rows_all = flat(S.a1)
    S.gw2[0:W, :] = dot(dqt[:W], rows_all).astype(low)
    S.gw2[W : 2 * W, :] = dot(S.kt[:W, : 4 * R], rows_all).astype(low)
    sum_over_dp(S.gw2, S.whole2, 0, D // 2, (0, 1, 2))
    S.gw2[2 * W : 3 * W, :] = dot(S.vt[:W, : 4 * R], rows_all).astype(low)
    sum_over_dp(S.gw2, S.whole2, D // 2, D // 2, (1, 0, 2))

    back.finish()
    down = Reduce(links, S.part, S.pre1, S.near1, S.far1, t)

    def lead(i, carry):
        s = flipped(t, 1 - i // 2, 1 - i % 2)
        out = dot_rows(S.gup[s, :, 0:W], S.wqkv[0])
        out += dot_rows(S.gup[s, :, H : H + W], S.wqkv[1])
        out += dot_rows(S.gup[s, :, 2 * H : 2 * H + W], S.wqkv[2])
        S.part[s] = out.astype(low)

        @pl.when(i == 0)
        def _():
            down.send_diag()

        @pl.when(i == 2)
        def _():
            down.send_sib()

        return carry

    lax.fori_loop(0, 4, lead, 0)
    down.send_cross()
    S.small[7:8, 0:H] = jnp.sum(flat(S.gup.at[:, :, 0:H]).astype(wide), 0, keepdims=True)
    S.small[7:8, H : 2 * H] = jnp.sum(
        flat(S.gup.at[:, :, 2 * H : 3 * H]).astype(wide), 0, keepdims=True
    )
    result = S.hid[...] + (ahead.result() + vector(S.db))
    S.output[...] = result[:own].astype(low)
    sums.tick(4)

    unit, inverse = standardize(S.xf[...])
    grad = down.result()
    S.small[0:1, :] = jnp.sum(grad * unit, 0, keepdims=True)
    S.small[1:2, :] = jnp.sum(grad, 0, keepdims=True)
    S.small4[t] = S.small[...]
    base3 = links.take(3)
    for j in range(3):
        peer = lax.rem(t + j + 1, 4)
        links.start(S.small4.at[t], S.small4.at[t], base3 + j, tensor=peer)
    total = S.gh[...] + norm_back(grad, unit, inverse, vector(S.g1))
    S.gt[...] = total[:own]
    for j in range(3):
        peer = lax.rem(t + 3 - j, 4)
        links.arrived(S.small4.at[peer], base3 + j, tensor=peer)
    over = S.small4[0] + S.small4[1] + S.small4[2] + S.small4[3]
    row = lax.broadcasted_iota(jnp.int32, over.shape, 0)
    S.smalls[d] = jnp.where(row < 6, over, S.small[...])
    base4 = links.take(n.dp)

    def tell(j, carry):
        links.copy(S.smalls.at[d], S.smalls.at[d], base4 + j, dp=lax.rem(d + j, n.dp)).start()
        return carry

    lax.fori_loop(1, n.dp, tell, 0)
    sums.finish()

    def hear(j, carry):
        peer = lax.rem(d + n.dp - j, n.dp)
        links.arrived(S.smalls.at[peer], base4 + j, dp=peer)
        return carry

    lax.fori_loop(1, n.dp, hear, 0)
    S.small_sum[...] = lax.fori_loop(
        1, n.dp, lambda j, acc: acc + S.smalls[j], S.smalls[0]
    )

    def done(j, carry):
        links.copy(S.smalls.at[d], S.smalls.at[d], base4 + j, dp=lax.rem(d + j, n.dp)).wait_send()
        return carry

    lax.fori_loop(1, n.dp, done, 0)
    for i in range(3):
        s = flipped(t, 1 - i // 2, (i + i // 2) % 2)
        links.copy(S.mix.at[s], S.mix4.at[t], mix_base + i, tensor=s).wait_send()
        links.copy(S.mix4.at[s], S.gm4.at[t], gm_base + i, tensor=s).wait_send()
    for transfer in (rows_in, cot_in, ow_in, next_in, hl_in, ahead, down):
        transfer.finish()
    links.finish()


def body(
    tokens,
    lengths,
    ln1_gain,
    ln1_shift,
    qkv_weight,
    qv_bias,
    out_weight,
    out_bias,
    ln2_gain,
    ln2_shift,
    up_weight,
    up_bias,
    down_weight,
    down_bias,
    cotangent,
):
    own, D = tokens.shape
    W = qkv_weight.shape[2]
    F = up_weight.shape[1]
    dp = lax.axis_size("dp")
    assert lax.axis_size("tensor") == 4 and lengths.shape[0] == 1 and F == D and 4 * W == D and 3 * round_up(W + 2, 128) == D
    R = round_up(own, 16)
    H = round_up(W + 2, 128)
    K = round_up(4 * R, 256)
    heads = W // HEAD_DIM
    extra = dp.bit_length() - 1 - 3
    n = types.SimpleNamespace(
        own=own, D=D, W=W, R=R, H=H, K=K, dp=dp, heads=heads, extra=extra
    )
    given = dict(
        x=tokens, lengths=lengths, g1=ln1_gain, b1=ln1_shift,
        wqkv=jnp.transpose(qkv_weight, (1, 0, 2)), bq=qv_bias, ow=out_weight, ob=out_bias,
        g2=ln2_gain, b2=ln2_shift, wup=up_weight, bup=up_bias, wdn=down_weight, db=down_bias,
        cot=cotangent,
    )
    outs = dict(
        output=((own, D), low), gt=((own, D), wide), small_sum=((8, D), wide),
        whole1=((2 * D, D), low), whole2=((D, D), low),
    )
    rows4 = ((4, R, D), low)
    slab = ((R, D), low)
    scratch = dict(
        a1=rows4, cot4=rows4, ow4=((4, W, D), low), q=((4, R, H), low), k=((K, H), low),
        v=((K, H), low), kt=((H, K), low), vt=((H, K), low), e=((heads, 4, R, K), low),
        o=((4, R, H), wide), inv=((4, R, H), wide), mix=((4, R, W), low), mix4=((4, R, W), low),
        xf=((R, D), wide), hid=((R, D), wide),
        a24=rows4, act=rows4, gup=rows4, part=rows4,
        fop=rows4, pre1=slab, near1=slab, far1=slab, pre2=slab, near2=slab, far2=slab,
        gw=((2 * D, D), low), gub=((1, D), wide),
        small=((8, D), wide), gh=((R, D), wide), hl4=rows4,
        gm4=((4, R, W), low), dkt=((W, K), wide), dvt=((W, K), wide), do=((R, H), wide),
        gw2=((D, D), low),
        small4=((4, 8, D), wide), smalls=((dp, 8, D), wide),
        box=((DataReduce.box_rows(3 * D, dp), D), low), share=((3 * D // 8, D), low),
    )
    sems = 112 + dp + 6 * extra
    names = list(given) + list(outs) + list(scratch) + ["send", "recv"]
    vmem = pl.BlockSpec(memory_space=pltpu.VMEM)
    smem = pl.BlockSpec(memory_space=pltpu.SMEM)
    hbm = pl.BlockSpec(memory_space=pl.ANY)
    output, gt, small, whole1, whole2 = pl.pallas_call(
        lambda *refs: kernel(n, types.SimpleNamespace(**dict(zip(names, refs)))),
        out_shape=tuple(jax.ShapeDtypeStruct(*spec) for spec in outs.values()),
        in_specs=[smem if name == "lengths" else vmem for name in given],
        out_specs=tuple(hbm if name in ("whole1", "whole2") else vmem for name in outs),
        scratch_shapes=[pltpu.VMEM(*spec) for spec in scratch.values()]
        + [pltpu.SemaphoreType.DMA((sems,))] * 2,
        compiler_params=pltpu.CompilerParams(
            collective_id=0, has_side_effects=True, vmem_limit_bytes=VMEM_BYTES
        ),
    )(*given.values())
    grad_qkv = jnp.transpose(whole2[: 3 * W].astype(wide).reshape(3, W, D), (2, 0, 1))
    return (
        output,
        gt,
        small[0],
        small[1],
        grad_qkv,
        jnp.stack([small[7, :W], small[7, H : H + W]]),
        whole2[3 * W :].astype(wide),
        small[4],
        small[2],
        small[3],
        whole1[:D].astype(wide),
        small[6],
        whole1[D:].astype(wide),
        small[5],
    )


def solution(mesh):
    placed = (
        P(("dp", "tensor"), None),
        P("dp"),
        P(),
        P(),
        P(None, None, "tensor"),
        P(None, "tensor"),
        P("tensor", None),
        P(),
        P(),
        P(),
        P(None, "tensor"),
        P("tensor"),
        P("tensor", None),
        P(),
        P(("dp", "tensor"), None),
    )
    return jax.shard_map(
        body,
        mesh=mesh,
        in_specs=placed,
        out_specs=(
            P(("dp", "tensor"), None),
            P(("dp", "tensor"), None),
            P(),
            P(),
            P(None, None, "tensor"),
            P(None, "tensor"),
            P("tensor", None),
            P(),
            P(),
            P(),
            P(None, "tensor"),
            P("tensor"),
            P("tensor", None),
            P(),
        ),
        check_vma=False,
    )
```

```python
import types

import jax
import jax.numpy as jnp
from jax import lax
from jax.experimental import pallas as pl
from jax.experimental.pallas import tpu as pltpu
from jax.sharding import PartitionSpec as P

HEAD_DIM = 64
MESH = pl.DeviceIdType.MESH
VMEM_BYTES = 62 * 2**20

epsilon = 1e-06
low = jnp.bfloat16
wide = jnp.float32


def round_up(amount, unit):
    return -(-amount // unit) * unit


def flipped(t, flip_chip, flip_core):
    return (t // 2 + flip_chip) % 2 * 2 + (t % 2 + flip_core) % 2


def dot(left, right):
    return jnp.dot(left, right, preferred_element_type=wide)


def dot_rows(left, right):
    return lax.dot_general(left, right, (((1,), (1,)), ((), ())), preferred_element_type=wide)


def dot_columns(left, right):
    return lax.dot_general(left, right, (((0,), (0,)), ((), ())), preferred_element_type=wide)


def standardize(values):
    center = values - jnp.mean(values, -1, keepdims=True)
    inverse = lax.rsqrt(jnp.mean(center * center, -1, keepdims=True) + epsilon)
    return center * inverse, inverse


def norm_back(grad, unit, inverse, gain):
    scaled = grad * gain
    return inverse * (
        scaled
        - jnp.mean(scaled, -1, keepdims=True)
        - unit * jnp.mean(scaled * unit, -1, keepdims=True)
    )


def flat(ref):
    a, b, c = ref.shape
    return ref[...].reshape(a * b, c)


class Links:
    def __init__(self, send, recv):
        self.send, self.recv, self.used, self.pending = send, recv, 0, []

    def take(self, amount=1):
        base = self.used
        self.used += amount
        assert self.used <= self.send.shape[0]
        return base

    def copy(self, src, dst, at, **where):
        return pltpu.make_async_remote_copy(
            src_ref=src,
            dst_ref=dst,
            send_sem=self.send.at[at],
            recv_sem=self.recv.at[at],
            device_id=where,
            device_id_type=MESH,
        )

    def start(self, src, dst, at, **where):
        copy = self.copy(src, dst, at, **where)
        copy.start()
        self.pending.append(copy)

    def arrived(self, dst, at, **where):
        self.copy(dst, dst, at, **where).wait_recv()

    def finish(self):
        for copy in self.pending:
            copy.wait_send()
        self.pending = []


class Gather:
    def __init__(self, links, buf, t, parts):
        self.links, self.buf, self.t, self.parts = links, buf, t, parts
        self.sib, self.cross, self.diag = flipped(t, 0, 1), flipped(t, 1, 0), flipped(t, 1, 1)
        self.base = links.take(3 * len(parts))

    def view(self, slot, part):
        start, size = self.parts[part]
        return self.buf.at[slot, pl.ds(start, size)]

    def _each(self):
        return range(len(self.parts))

    def start(self):
        for p in self._each():
            v = self.view(self.t, p)
            self.links.copy(v, v, self.base + 3 * p, tensor=self.cross).start()
        for p in self._each():
            v = self.view(self.t, p)
            self.links.copy(v, v, self.base + 3 * p + 1, tensor=self.sib).start()

    def wait_sib(self):
        for p in self._each():
            self.links.arrived(self.view(self.sib, p), self.base + 3 * p + 1, tensor=self.sib)

    def forward(self):
        for p in self._each():
            v = self.view(self.cross, p)
            self.links.arrived(v, self.base + 3 * p, tensor=self.cross)
            self.links.copy(v, v, self.base + 3 * p + 2, tensor=self.sib).start()

    def wait_diag(self):
        for p in self._each():
            self.links.arrived(self.view(self.diag, p), self.base + 3 * p + 2, tensor=self.sib)

    def finish(self):
        for p in self._each():
            v = self.view(self.t, p)
            self.links.copy(v, v, self.base + 3 * p, tensor=self.cross).wait_send()
            self.links.copy(v, v, self.base + 3 * p + 1, tensor=self.sib).wait_send()
            v = self.view(self.cross, p)
            self.links.copy(v, v, self.base + 3 * p + 2, tensor=self.sib).wait_send()


class Reduce:
    def __init__(self, links, part, pre, near, far, t):
        self.links, self.part, self.pre, self.near, self.far, self.t = links, part, pre, near, far, t
        self.sib, self.cross, self.diag = flipped(t, 0, 1), flipped(t, 1, 0), flipped(t, 1, 1)
        self.base = links.take(3)

    def send_diag(self):
        self.links.copy(self.part.at[self.diag], self.pre, self.base, tensor=self.sib).start()

    def send_sib(self):
        self.links.copy(self.part.at[self.sib], self.near, self.base + 1, tensor=self.sib).start()

    def send_cross(self):
        self.links.arrived(self.pre, self.base, tensor=self.sib)
        total = self.part[self.cross].astype(wide) + self.pre[...].astype(wide)
        self.part[self.cross] = total.astype(low)
        self.links.copy(self.part.at[self.cross], self.far, self.base + 2, tensor=self.cross).start()

    def result(self):
        self.links.arrived(self.near, self.base + 1, tensor=self.sib)
        self.links.arrived(self.far, self.base + 2, tensor=self.cross)
        return (
            self.part[self.t].astype(wide) + self.near[...].astype(wide) + self.far[...].astype(wide)
        )

    def finish(self):
        self.links.copy(self.part.at[self.diag], self.pre, self.base, tensor=self.sib).wait_send()
        self.links.copy(self.part.at[self.sib], self.near, self.base + 1, tensor=self.sib).wait_send()
        self.links.copy(self.part.at[self.cross], self.far, self.base + 2, tensor=self.cross).wait_send()


class DataReduce:
    def __init__(self, links, held, whole, share, box, box_at, first, rows, d, count, order):
        self.links, self.held, self.whole = links, held, whole
        bits = count.bit_length() - 1
        assert count == 1 << bits and bits >= 3
        self.extra = [b for b in range(bits) if b not in order]
        self.d, self.order = d, order
        self.region = (first, rows, 0, held.shape[1])
        self.trail, self.sent, self.boxes = [], [], []
        for tall, broad in self.sizes(rows, held.shape[1], count)[0]:
            self.boxes.append(box.at[pl.ds(box_at, tall), pl.ds(0, broad)])
            box_at += tall
        self.share = share.at[pl.ds(0, tall), pl.ds(0, broad)]
        self.base = links.take(7 + len(self.extra))
        self.steps = [lambda: self._send_half(0)]
        for k in (1, 2):
            self.steps.append(lambda k=k: (self._add_half(k - 1), self._send_half(k)))
        self.steps.append(lambda: (self._add_half(2), self._swap(), self._place(), self._grow_send(2)))
        for k in (2, 1):
            self.steps.append(lambda k=k: (self._grow_wait(k), self._grow_send(k - 1)))
        self.steps.append(lambda: self._grow_wait(0))

    @staticmethod
    def sizes(rows, columns, count):
        found = []
        for _ in range(3):
            if rows % 32 == 0:
                rows //= 2
            else:
                columns //= 2
            found.append((rows, columns))
        found += found[2:] * (count.bit_length() - 1 - 3)
        return found, sum(size[0] for size in found)

    def _bit(self, b):
        return self.d // (1 << b) % 2

    def _peer(self, b):
        return self.d + (1 - 2 * self._bit(b)) * (1 << b)

    def _start(self, copy):
        copy.start()
        self.sent.append(copy)

    @staticmethod
    def _view(ref, region):
        row, rows, column, columns = region
        if columns == ref.shape[1]:
            return ref.at[pl.ds(row, rows)]
        return ref.at[pl.ds(row, rows), pl.ds(column, columns)]

    @staticmethod
    def _part(region, bit):
        row, rows, column, columns = region
        if rows % 32 == 0:
            return (pl.multiple_of(row + bit * (rows // 2), 16), rows // 2, column, columns)
        return (row, rows, pl.multiple_of(column + bit * (columns // 2), 128), columns // 2)

    def _send_half(self, k):
        b = self.order[k]
        bit = self._bit(b)
        self.trail.append(self.region)
        view = self._view(self.held, self._part(self.region, 1 - bit))
        self._start(self.links.copy(view, self.boxes[k], self.base + k, dp=self._peer(b)))
        self.region = self._part(self.region, bit)

    def _add_half(self, k):
        self.links.arrived(self.boxes[k], self.base + k, dp=self._peer(self.order[k]))
        view = self._view(self.held, self.region)
        total = (view[...].astype(wide) + self.boxes[k][...].astype(wide)).astype(low)
        if k == 2:
            self.share[...] = total
        else:
            view[...] = total

    def _swap(self):
        for k, b in enumerate(self.extra):
            box, at = self.boxes[3 + k], self.base + 7 + k
            copy = self.links.copy(self.share, box, at, dp=self._peer(b))
            copy.start()
            self.links.arrived(box, at, dp=self._peer(b))
            copy.wait_send()
            self.share[...] = (self.share[...].astype(wide) + box[...].astype(wide)).astype(low)

    def _place(self):
        self.placed = pltpu.make_async_copy(
            self.share, self._view(self.whole, self.region), self.links.send.at[self.base + 6]
        )
        self.placed.start()

    def _grow_send(self, k):
        view = self._view(self.whole, self.region)
        src = self.share if k == 2 else view
        self._start(self.links.copy(src, view, self.base + 3 + k, dp=self._peer(self.order[k])))

    def _grow_wait(self, k):
        if k == 2:
            self.placed.wait()
        b = self.order[k]
        view = self._view(self.whole, self._part(self.trail[k], 1 - self._bit(b)))
        self.links.arrived(view, self.base + 3 + k, dp=self._peer(b))
        self.region = self.trail[k]

    def step(self):
        if self.steps:
            self.steps.pop(0)()

    def finish(self):
        assert not self.steps
        for copy in self.sent:
            copy.wait_send()


class Pipeline:
    def __init__(self):
        self.members, self.queue = [], []

    def add(self, member):
        self.members.append(member)
        member.step()
        self.queue.append(member)

    def tick(self, amount=1):
        for _ in range(min(amount, sum(len(m.steps) for m in self.queue))):
            member = self.queue.pop(0)
            member.step()
            if member.steps:
                self.queue.append(member)

    def finish(self):
        while self.queue:
            self.tick()
        for m in self.members:
            m.finish()


def greet(axis, me, count):
    barrier = pltpu.get_barrier_semaphore()

    def one(j, carry):
        pl.semaphore_signal(
            barrier, inc=1, device_id={axis: lax.rem(me + j, count)}, device_id_type=MESH
        )
        return carry

    lax.fori_loop(1, count, one, 0)


def await_greetings(amount):
    pl.semaphore_wait(pltpu.get_barrier_semaphore(), amount)


def halves(rows):
    first = round_up(rows // 2, 16)
    return ((0, first), (first, rows - first))


def head_masks(shape, local_heads):
    lane = lax.broadcasted_iota(jnp.int32, shape, 1)
    return [
        jnp.where((lane >= h * HEAD_DIM) & (lane < (h + 1) * HEAD_DIM), 1.0, 0.0)
        for h in range(local_heads)
    ], lane


def kernel(n, S):
    links = Links(S.send, S.recv)
    t = lax.axis_index("tensor")
    d = lax.axis_index("dp")
    greet("tensor", t, 4)
    greet("dp", d, n.dp)
    R, own, W, H, D, K = n.R, n.own, n.W, n.H, n.D, n.K
    vector = lambda ref: ref[...].reshape(1, D)

    S.xf[...] = jnp.zeros_like(S.xf)
    S.xf[0:own, :] = S.x[...].astype(wide)
    unit, _ = standardize(S.xf[...])
    S.a1[t] = (unit * vector(S.g1) + vector(S.b1)).astype(low)
    S.cot4[t] = jnp.zeros((R, D), low)
    S.cot4[t, 0:own, :] = S.cot[...].astype(low)
    S.ow4[t] = S.ow[...]
    await_greetings(3 + n.dp - 1)
    rows_in = Gather(links, S.a1, t, halves(R))
    cot_in = Gather(links, S.cot4, t, halves(R))
    ow_in = Gather(links, S.ow4, t, ((0, W),))
    rows_in.start()
    S.gw[0:D, :] = jnp.transpose(S.wup[...])
    S.gw[D:, :] = jnp.transpose(S.wdn[...])
    S.v[4 * R :, :] = jnp.zeros((K - 4 * R, H), low)
    length = S.lengths[0]

    def project(i, carry):
        s = flipped(t, i // 2, i % 2)

        @pl.when(i == 1)
        def _():
            rows_in.wait_sib()

        @pl.when(i == 2)
        def _():
            rows_in.forward()
            cot_in.start()
            ow_in.start()

        @pl.when(i == 3)
        def _():
            rows_in.wait_diag()

        slab = S.a1[s]
        lane = lax.broadcasted_iota(jnp.int32, (R, H - W), 1)
        row = lax.broadcasted_iota(jnp.int32, (R, H - W), 0)
        absent = (row >= own) | (row + s * own >= length)
        at = pl.ds(pl.multiple_of(s * R, 16), R)
        out = dot(slab, S.wqkv[0]) + S.bq[0:1, :]
        S.q[s, :, :W] = (out.astype(low).astype(wide) * HEAD_DIM**-0.5).astype(low)
        S.q[s, :, W:] = jnp.where(lane == 0, HEAD_DIM**-0.5, 0.0).astype(low)
        S.k[at, :W] = dot(slab, S.wqkv[1]).astype(low)
        S.k[at, W:] = jnp.where((lane == 0) & absent, -8e30, 0.0).astype(low)
        S.v[at, :W] = (dot(slab, S.wqkv[2]) + S.bq[1:2, :]).astype(low)
        S.v[at, W:] = jnp.where(lane < 2, 1.0, 0.0).astype(low)
        return carry

    lax.fori_loop(0, 4, project, 0)
    if K > 4 * R:
        lane = lax.broadcasted_iota(jnp.int32, (K - 4 * R, H), 1)
        S.k[4 * R :, :] = jnp.where(lane == W, -8e30, 0.0).astype(low)
    S.kt[...] = jnp.transpose(S.k[...])
    S.vt[...] = jnp.transpose(S.v[...])

    masks, lane = head_masks((1, H), n.heads)
    mix_base = links.take(3)

    def attend(i, carry):
        s = flipped(t, 1 - i // 2, (i + i // 2) % 2)
        query = S.q[s]
        mixed = jnp.zeros((R, H), wide)
        inverse = jnp.zeros((R, H), wide)
        for h in range(n.heads):
            here = jnp.where(lane == W, 1.0, masks[h]).astype(low)
            scores = dot(query * here, S.kt[...])
            terms = jnp.exp(scores - jnp.max(scores, -1, keepdims=True)).astype(low)
            S.e[h, s] = terms
            part = dot(terms, S.v[...])
            scale = 1.0 / part[:, W : W + 1]
            mixed += part * (scale * masks[h])
            inverse += scale * masks[h]
        S.o[s] = mixed
        S.inv[s] = inverse
        S.mix[s] = mixed[:, :W].astype(low)

        @pl.when(i < 3)
        def _():
            links.copy(S.mix.at[s], S.mix4.at[t], mix_base + i, tensor=s).start()

        @pl.when(i == 0)
        def _():
            cot_in.wait_sib()
            ow_in.wait_sib()

        @pl.when(i == 1)
        def _():
            cot_in.forward()
            ow_in.forward()

        @pl.when(i == 2)
        def _():
            cot_in.wait_diag()
            ow_in.wait_diag()

        return carry

    lax.fori_loop(0, 4, attend, 0)
    S.mix4[t] = S.mix[t]
    for i in range(3):
        s = flipped(t, 1 - i // 2, (i + i // 2) % 2)
        links.arrived(S.mix4.at[s], mix_base + i, tensor=s)

    total = S.xf[...] + vector(S.ob)
    for j in range(4):
        total += dot(S.mix4[j], S.ow4[j])
    S.hid[...] = total
    unit, _ = standardize(total)
    S.a24[t] = (unit * vector(S.g2) + vector(S.b2)).astype(low)
    next_in = Gather(links, S.a24, t, halves(R))
    next_in.start()
    back = Reduce(links, S.part, S.pre1, S.near1, S.far1, t)
    ahead = Reduce(links, S.fop, S.pre2, S.near2, S.far2, t)
    S.gub[...] = jnp.zeros_like(S.gub)

    def feed(i, carry):
        s = flipped(t, i // 2, i % 2)

        @pl.when(i == 1)
        def _():
            next_in.wait_sib()

        @pl.when(i == 2)
        def _():
            next_in.forward()

        @pl.when(i == 3)
        def _():
            next_in.wait_diag()

        up = dot(S.a24[s], S.wup[...]) + vector(S.bup)
        square = up * up
        c = 0.7978845608028654
        bend = jnp.tanh(c * up * (1.0 + 0.044715 * square))
        half = 0.5 * (1.0 + bend)
        slope = half + 0.5 * up * (1.0 - bend * bend) * (c + (3 * 0.044715 * c) * square)
        active = (up * half).astype(low)
        S.pool[s, :, 0:D] = active
        grad = (dot(S.cot4[s], S.gw[D:, :]) * slope).astype(low)
        S.gup[s] = grad
        S.part[s] = dot(grad, S.gw[0:D, :]).astype(low)

        @pl.when(i == 1)
        def _():
            back.send_sib()

        @pl.when(i == 3)
        def _():
            back.send_diag()

        S.fop[s] = dot(active, S.wdn[...]).astype(low)

        @pl.when(i == 1)
        def _():
            ahead.send_sib()

        @pl.when(i == 3)
        def _():
            ahead.send_diag()

        S.gub[...] += jnp.sum(grad.astype(wide), 0, keepdims=True)
        return carry

    lax.fori_loop(0, 4, feed, 0)
    back.send_cross()

    sums = Pipeline()
    tile = D // 2
    box_at = share_at = 0

    def sum_over_dp(held, whole, first, rows, order):
        nonlocal box_at, share_at
        sizes, taken = DataReduce.sizes(rows, D, n.dp)
        share = S.share.at[pl.ds(share_at, sizes[2][0])]
        sums.add(DataReduce(links, held, whole, share, S.box, box_at, first, rows, d, n.dp, order))
        box_at, share_at = box_at + taken, share_at + sizes[2][0]

    for left, right, first in ((S.a24, S.gup, 0), (S.pool, S.cot4, D)):
        for j in range(2):
            columns = left[:, :, j * tile : (j + 1) * tile].reshape(4 * R, tile)
            at = first + j * tile
            S.gw[at : at + tile, :] = dot_columns(columns, flat(right)).astype(low)
            sum_over_dp(S.gw, S.whole1, at, tile, (1, 0, 2) if at == tile else (0, 1, 2))
        if first == 0:
            ahead.send_cross()

    grad = back.result()
    unit, inverse = standardize(S.hid[...])
    S.small[...] = jnp.zeros_like(S.small)
    S.small[2:3, :] = jnp.sum(grad * unit, 0, keepdims=True)
    S.small[3:4, :] = jnp.sum(grad, 0, keepdims=True)
    S.gh[...] = norm_back(grad, unit, inverse, vector(S.g2))
    S.gh[0:own, :] += S.cot[...]
    hidden_low = S.gh[...].astype(low)
    S.hl4[t] = hidden_low
    S.small[4:5, :] = jnp.sum(hidden_low.astype(wide), 0, keepdims=True)
    S.small[5:6, :] = jnp.sum(S.cot4[t].astype(wide), 0, keepdims=True)
    S.small[6:7, :] = S.gub[...]
    gm_base = links.take(3)

    def share(i, carry):
        s = flipped(t, 1 - i // 2, (i + i // 2) % 2)
        S.mix4[s] = dot_rows(S.hl4[t], S.ow4[s]).astype(low)

        @pl.when(i < 3)
        def _():
            links.copy(S.mix4.at[s], S.gm4.at[t], gm_base + i, tensor=s).start()

        return carry

    lax.fori_loop(0, 4, share, 0)
    S.gm4[t] = S.mix4[t]
    hl_in = Gather(links, S.hl4, t, halves(R))
    hl_in.start()

    next_in.finish()
    S.do[...] = jnp.zeros_like(S.do)
    S.qt[...] = jnp.transpose(flat(S.q))
    sums.tick(2)

    def prepare(i, s):
        if i > 0:
            links.arrived(S.gm4.at[s], gm_base + (3, 2, 0, 1)[i], tensor=s)
        S.do[:, :W] = S.gm4[s].astype(wide)
        scaled = (S.do[...] * S.inv[s]).astype(low)
        S.v[pl.ds(pl.multiple_of(s * R, 16), R), :] = scaled
        scaled = scaled.astype(wide)
        product = scaled * S.o[s]
        for h in range(n.heads):
            inner = -jnp.sum(product * masks[h], -1, keepdims=True)
            upper = inner.astype(low).astype(wide)
            S.a24[s, :, h * H : (h + 1) * H] = (
                scaled * masks[h]
                + jnp.where(lane == W, upper, 0.0)
                + jnp.where(lane == W + 1, inner - upper, 0.0)
            ).astype(low)

    def pull(h, s):
        grad_p = dot(S.a24[s, :, h * H : (h + 1) * H], S.vt[...])
        grad_s = (S.e[h, s].astype(wide) * grad_p).astype(low)
        S.pool[s] = grad_s
        dq = dot(grad_s, S.k[...]) * (masks[h] * HEAD_DIM**-0.5)
        if h > 0:
            dq += S.gup[s, :, 0:H].astype(wide)
        S.gup[s, :, 0:H] = dq.astype(low)

    for h in range(n.heads):
        for i in range(4):
            s = flipped(t, i // 2, i % 2)
            if h == 0:
                prepare(i, s)
            pull(h, s)
            if i % 2 == 1:
                sums.tick(2)
        if h == 0:
            S.v[4 * R :, :] = jnp.zeros((K - 4 * R, H), low)
            S.kt[...] = jnp.transpose(S.v[...])
            hl_in.wait_sib()
            hl_in.forward()
        at = slice(h * HEAD_DIM, (h + 1) * HEAD_DIM)
        S.dk[at, :] = dot(S.qt[at, :], flat(S.pool)).astype(low)
        S.dv[at, :] = dot(S.kt[at, : 4 * R], flat(S.e.at[h])).astype(low)
        tile = h * HEAD_DIM // 128 * 128
        dqt = jnp.transpose(flat(S.gup.at[:, :, tile : tile + 128]))
        left = jnp.concatenate(
            [dqt[h * HEAD_DIM - tile : (h + 1) * HEAD_DIM - tile], S.dk[at, : 4 * R], S.dv[at, : 4 * R]], 0
        )
        S.gw2[h * W : (h + 1) * W, :] = dot(left, flat(S.a1)).astype(low)
        sum_over_dp(S.gw2, S.whole2, h * W, W, (0, 1, 2))
        if h == 0:
            hl_in.wait_diag()
            S.gw2[3 * W :, :] = dot_columns(flat(S.mix), flat(S.hl4)).astype(low)
            sum_over_dp(S.gw2, S.whole2, 3 * W, W, (1, 0, 2))

    pad = jnp.zeros((R, H - W), low)
    for part, grad_t in ((1, S.dk), (2, S.dv)):
        rows = jnp.transpose(grad_t[...])
        for s in range(4):
            S.gup[s, :, part * H : part * H + W] = rows[s * R : (s + 1) * R]
            S.gup[s, :, part * H + W : (part + 1) * H] = pad

    back.finish()
    down = Reduce(links, S.part, S.pre1, S.near1, S.far1, t)

    def lead(i, carry):
        s = flipped(t, 1 - i // 2, 1 - i % 2)
        out = dot_rows(S.gup[s, :, 0:W], S.wqkv[0])
        out += dot_rows(S.gup[s, :, H : H + W], S.wqkv[1])
        out += dot_rows(S.gup[s, :, 2 * H : 2 * H + W], S.wqkv[2])
        S.part[s] = out.astype(low)

        @pl.when(i == 0)
        def _():
            down.send_diag()

        @pl.when(i == 2)
        def _():
            down.send_sib()

        return carry

    lax.fori_loop(0, 4, lead, 0)
    down.send_cross()
    S.small[7:8, 0:H] = jnp.sum(flat(S.gup.at[:, :, 0:H]).astype(wide), 0, keepdims=True)
    S.small[7:8, H : 2 * H] = jnp.sum(
        flat(S.gup.at[:, :, 2 * H : 3 * H]).astype(wide), 0, keepdims=True
    )
    result = S.hid[...] + (ahead.result() + vector(S.db))
    S.output[...] = result[:own].astype(low)
    sums.tick(4)

    unit, inverse = standardize(S.xf[...])
    grad = down.result()
    S.small[0:1, :] = jnp.sum(grad * unit, 0, keepdims=True)
    S.small[1:2, :] = jnp.sum(grad, 0, keepdims=True)
    S.small4[t] = S.small[...]
    base3 = links.take(3)
    for j in range(3):
        peer = lax.rem(t + j + 1, 4)
        links.start(S.small4.at[t], S.small4.at[t], base3 + j, tensor=peer)
    total = S.gh[...] + norm_back(grad, unit, inverse, vector(S.g1))
    S.gt[...] = total[:own]
    for j in range(3):
        peer = lax.rem(t + 3 - j, 4)
        links.arrived(S.small4.at[peer], base3 + j, tensor=peer)
    over = S.small4[0] + S.small4[1] + S.small4[2] + S.small4[3]
    row = lax.broadcasted_iota(jnp.int32, over.shape, 0)
    S.smalls[d] = jnp.where(row < 6, over, S.small[...])
    base4 = links.take(n.dp)

    def tell(j, carry):
        links.copy(S.smalls.at[d], S.smalls.at[d], base4 + j, dp=lax.rem(d + j, n.dp)).start()
        return carry

    lax.fori_loop(1, n.dp, tell, 0)
    sums.finish()

    def hear(j, carry):
        peer = lax.rem(d + n.dp - j, n.dp)
        links.arrived(S.smalls.at[peer], base4 + j, dp=peer)
        return carry

    lax.fori_loop(1, n.dp, hear, 0)
    S.small_sum[...] = lax.fori_loop(
        1, n.dp, lambda j, acc: acc + S.smalls[j], S.smalls[0]
    )

    def done(j, carry):
        links.copy(S.smalls.at[d], S.smalls.at[d], base4 + j, dp=lax.rem(d + j, n.dp)).wait_send()
        return carry

    lax.fori_loop(1, n.dp, done, 0)
    for i in range(3):
        s = flipped(t, 1 - i // 2, (i + i // 2) % 2)
        links.copy(S.mix.at[s], S.mix4.at[t], mix_base + i, tensor=s).wait_send()
        links.copy(S.mix4.at[s], S.gm4.at[t], gm_base + i, tensor=s).wait_send()
    for transfer in (rows_in, cot_in, ow_in, hl_in, ahead, down):
        transfer.finish()
    links.finish()


def body(
    tokens,
    lengths,
    ln1_gain,
    ln1_shift,
    qkv_weight,
    qv_bias,
    out_weight,
    out_bias,
    ln2_gain,
    ln2_shift,
    up_weight,
    up_bias,
    down_weight,
    down_bias,
    cotangent,
):
    own, D = tokens.shape
    W = qkv_weight.shape[2]
    F = up_weight.shape[1]
    dp = lax.axis_size("dp")
    assert lax.axis_size("tensor") == 4 and lengths.shape[0] == 1 and F == D and 4 * W == D and 3 * round_up(W + 2, 128) == D
    R = round_up(own, 16)
    H = round_up(W + 2, 128)
    K = round_up(4 * R, 256)
    heads = W // HEAD_DIM
    extra = dp.bit_length() - 1 - 3
    n = types.SimpleNamespace(
        own=own, D=D, W=W, R=R, H=H, K=K, dp=dp, heads=heads, extra=extra
    )
    given = dict(
        x=tokens, lengths=lengths, g1=ln1_gain, b1=ln1_shift,
        wqkv=jnp.transpose(qkv_weight, (1, 0, 2)), bq=qv_bias, ow=out_weight, ob=out_bias,
        g2=ln2_gain, b2=ln2_shift, wup=up_weight, bup=up_bias, wdn=down_weight, db=down_bias,
        cot=cotangent,
    )
    outs = dict(
        output=((own, D), low), gt=((own, D), wide), small_sum=((8, D), wide),
        whole1=((2 * D, D), low), whole2=((D, D), low),
    )
    rows4 = ((4, R, D), low)
    slab = ((R, D), low)
    chunks = [D // 2] * 4 + [W] * 4
    scratch = dict(
        a1=rows4, cot4=rows4, ow4=((4, W, D), low), q=((4, R, H), low), k=((K, H), low),
        v=((K, H), low), kt=((H, K), low), vt=((H, K), low), e=((heads, 4, R, K), low),
        o=((4, R, H), wide), inv=((4, R, H), wide), mix=((4, R, W), low), mix4=((4, R, W), low),
        xf=((R, D), wide), hid=((R, D), wide),
        a24=rows4, pool=((4, R, K), low), gup=rows4, part=rows4,
        fop=rows4, pre1=slab, near1=slab, far1=slab, pre2=slab, near2=slab, far2=slab,
        gw=((2 * D, D), low), gub=((1, D), wide),
        small=((8, D), wide), gh=((R, D), wide), hl4=rows4,
        gm4=((4, R, W), low), dk=((W, K), low), dv=((W, K), low), qt=((H, 4 * R), low), do=((R, H), wide),
        gw2=((D, D), low),
        small4=((4, 8, D), wide), smalls=((dp, 8, D), wide),
        box=((sum(DataReduce.sizes(r, D, dp)[1] for r in chunks), D), low),
        share=((sum(DataReduce.sizes(r, D, dp)[0][2][0] for r in chunks), D), low),
    )
    sems = 140 + dp + 8 * extra
    names = list(given) + list(outs) + list(scratch) + ["send", "recv"]
    vmem = pl.BlockSpec(memory_space=pltpu.VMEM)
    smem = pl.BlockSpec(memory_space=pltpu.SMEM)
    hbm = pl.BlockSpec(memory_space=pl.ANY)
    output, gt, small, whole1, whole2 = pl.pallas_call(
        lambda *refs: kernel(n, types.SimpleNamespace(**dict(zip(names, refs)))),
        out_shape=tuple(jax.ShapeDtypeStruct(*spec) for spec in outs.values()),
        in_specs=[smem if name == "lengths" else vmem for name in given],
        out_specs=tuple(hbm if name in ("whole1", "whole2") else vmem for name in outs),
        scratch_shapes=[pltpu.VMEM(*spec) for spec in scratch.values()]
        + [pltpu.SemaphoreType.DMA((sems,))] * 2,
        compiler_params=pltpu.CompilerParams(
            collective_id=0, has_side_effects=True, vmem_limit_bytes=VMEM_BYTES
        ),
    )(*given.values())
    parts = whole2[: 3 * W].astype(wide).reshape(heads, 3, HEAD_DIM, D)
    grad_qkv = jnp.transpose(parts, (3, 1, 0, 2)).reshape(D, 3, W)
    return (
        output,
        gt,
        small[0],
        small[1],
        grad_qkv,
        jnp.stack([small[7, :W], small[7, H : H + W]]),
        whole2[3 * W :].astype(wide),
        small[4],
        small[2],
        small[3],
        whole1[:D].astype(wide),
        small[6],
        whole1[D:].astype(wide),
        small[5],
    )


def solution(mesh):
    placed = (
        P(("dp", "tensor"), None),
        P("dp"),
        P(),
        P(),
        P(None, None, "tensor"),
        P(None, "tensor"),
        P("tensor", None),
        P(),
        P(),
        P(),
        P(None, "tensor"),
        P("tensor"),
        P("tensor", None),
        P(),
        P(("dp", "tensor"), None),
    )
    return jax.shard_map(
        body,
        mesh=mesh,
        in_specs=placed,
        out_specs=(
            P(("dp", "tensor"), None),
            P(("dp", "tensor"), None),
            P(),
            P(),
            P(None, None, "tensor"),
            P(None, "tensor"),
            P("tensor", None),
            P(),
            P(),
            P(),
            P(None, "tensor"),
            P("tensor"),
            P("tensor", None),
            P(),
        ),
        check_vma=False,
    )
```

```python
import types

import jax
import jax.numpy as jnp
from jax import lax
from jax.experimental import pallas as pl
from jax.experimental.pallas import tpu as pltpu
from jax.sharding import PartitionSpec as P

HEAD_DIM = 64
MESH = pl.DeviceIdType.MESH
VMEM_BYTES = 62 * 2**20

epsilon = 1e-06
low = jnp.bfloat16
wide = jnp.float32


def round_up(amount, unit):
    return -(-amount // unit) * unit


def flipped(t, flip_chip, flip_core):
    return (t // 2 + flip_chip) % 2 * 2 + (t % 2 + flip_core) % 2


def dot(left, right):
    return jnp.dot(left, right, preferred_element_type=wide)


def dot_rows(left, right):
    return lax.dot_general(left, right, (((1,), (1,)), ((), ())), preferred_element_type=wide)


def dot_columns(left, right):
    return lax.dot_general(left, right, (((0,), (0,)), ((), ())), preferred_element_type=wide)


def standardize(values):
    center = values - jnp.mean(values, -1, keepdims=True)
    inverse = lax.rsqrt(jnp.mean(center * center, -1, keepdims=True) + epsilon)
    return center * inverse, inverse


def norm_back(grad, unit, inverse, gain):
    scaled = grad * gain
    return inverse * (
        scaled
        - jnp.mean(scaled, -1, keepdims=True)
        - unit * jnp.mean(scaled * unit, -1, keepdims=True)
    )


def flat(ref):
    a, b, c = ref.shape
    return ref[...].reshape(a * b, c)


class Links:
    def __init__(self, send, recv):
        self.send, self.recv, self.used, self.pending = send, recv, 0, []

    def take(self, amount=1):
        base = self.used
        self.used += amount
        assert self.used <= self.send.shape[0]
        return base

    def copy(self, src, dst, at, **where):
        return pltpu.make_async_remote_copy(
            src_ref=src,
            dst_ref=dst,
            send_sem=self.send.at[at],
            recv_sem=self.recv.at[at],
            device_id=where,
            device_id_type=MESH,
        )

    def start(self, src, dst, at, **where):
        copy = self.copy(src, dst, at, **where)
        copy.start()
        self.pending.append(copy)

    def arrived(self, dst, at, **where):
        self.copy(dst, dst, at, **where).wait_recv()

    def finish(self):
        for copy in self.pending:
            copy.wait_send()
        self.pending = []


class Gather:
    def __init__(self, links, buf, t, parts):
        self.links, self.buf, self.t, self.parts = links, buf, t, parts
        self.sib, self.cross, self.diag = flipped(t, 0, 1), flipped(t, 1, 0), flipped(t, 1, 1)
        self.base = links.take(3 * len(parts))

    def view(self, slot, part):
        start, size = self.parts[part]
        return self.buf.at[slot, pl.ds(start, size)]

    def _each(self):
        return range(len(self.parts))

    def start(self):
        for p in self._each():
            v = self.view(self.t, p)
            self.links.copy(v, v, self.base + 3 * p, tensor=self.cross).start()
        for p in self._each():
            v = self.view(self.t, p)
            self.links.copy(v, v, self.base + 3 * p + 1, tensor=self.sib).start()

    def wait_sib(self):
        for p in self._each():
            self.links.arrived(self.view(self.sib, p), self.base + 3 * p + 1, tensor=self.sib)

    def forward(self):
        for p in self._each():
            v = self.view(self.cross, p)
            self.links.arrived(v, self.base + 3 * p, tensor=self.cross)
            self.links.copy(v, v, self.base + 3 * p + 2, tensor=self.sib).start()

    def wait_diag(self):
        for p in self._each():
            self.links.arrived(self.view(self.diag, p), self.base + 3 * p + 2, tensor=self.sib)

    def finish(self):
        for p in self._each():
            v = self.view(self.t, p)
            self.links.copy(v, v, self.base + 3 * p, tensor=self.cross).wait_send()
            self.links.copy(v, v, self.base + 3 * p + 1, tensor=self.sib).wait_send()
            v = self.view(self.cross, p)
            self.links.copy(v, v, self.base + 3 * p + 2, tensor=self.sib).wait_send()


class Reduce:
    def __init__(self, links, part, pre, near, far, t):
        self.links, self.part, self.pre, self.near, self.far, self.t = links, part, pre, near, far, t
        self.sib, self.cross, self.diag = flipped(t, 0, 1), flipped(t, 1, 0), flipped(t, 1, 1)
        self.base = links.take(3)

    def send_diag(self):
        self.links.copy(self.part.at[self.diag], self.pre, self.base, tensor=self.sib).start()

    def send_sib(self):
        self.links.copy(self.part.at[self.sib], self.near, self.base + 1, tensor=self.sib).start()

    def send_cross(self):
        self.links.arrived(self.pre, self.base, tensor=self.sib)
        total = self.part[self.cross].astype(wide) + self.pre[...].astype(wide)
        self.part[self.cross] = total.astype(low)
        self.links.copy(self.part.at[self.cross], self.far, self.base + 2, tensor=self.cross).start()

    def result(self):
        self.links.arrived(self.near, self.base + 1, tensor=self.sib)
        self.links.arrived(self.far, self.base + 2, tensor=self.cross)
        return (
            self.part[self.t].astype(wide) + self.near[...].astype(wide) + self.far[...].astype(wide)
        )

    def finish(self):
        self.links.copy(self.part.at[self.diag], self.pre, self.base, tensor=self.sib).wait_send()
        self.links.copy(self.part.at[self.sib], self.near, self.base + 1, tensor=self.sib).wait_send()
        self.links.copy(self.part.at[self.cross], self.far, self.base + 2, tensor=self.cross).wait_send()


class DataReduce:
    def __init__(self, links, held, whole, share, box, box_at, first, rows, d, count, order):
        self.links, self.held, self.whole = links, held, whole
        bits = count.bit_length() - 1
        assert count == 1 << bits and bits >= 3
        self.extra = [b for b in range(bits) if b not in order]
        self.d, self.order = d, order
        self.region = (first, rows, 0, held.shape[1])
        self.trail, self.sent, self.boxes = [], [], []
        for tall, broad in self.sizes(rows, held.shape[1], count)[0]:
            self.boxes.append(box.at[pl.ds(box_at, tall), pl.ds(0, broad)])
            box_at += tall
        self.share = share.at[pl.ds(0, tall), pl.ds(0, broad)]
        self.base = links.take(7 + len(self.extra))
        self.steps = [lambda: self._send_half(0)]
        for k in (1, 2):
            self.steps.append(lambda k=k: (self._add_half(k - 1), self._send_half(k)))
        self.steps.append(lambda: (self._add_half(2), self._swap(), self._place(), self._grow_send(2)))
        for k in (2, 1):
            self.steps.append(lambda k=k: (self._grow_wait(k), self._grow_send(k - 1)))
        self.steps.append(lambda: self._grow_wait(0))

    @staticmethod
    def sizes(rows, columns, count):
        found = []
        for _ in range(3):
            if rows % 32 == 0:
                rows //= 2
            else:
                columns //= 2
            found.append((rows, columns))
        found += found[2:] * (count.bit_length() - 1 - 3)
        return found, sum(size[0] for size in found)

    def _bit(self, b):
        return self.d // (1 << b) % 2

    def _peer(self, b):
        return self.d + (1 - 2 * self._bit(b)) * (1 << b)

    def _start(self, copy):
        copy.start()
        self.sent.append(copy)

    @staticmethod
    def _view(ref, region):
        row, rows, column, columns = region
        if columns == ref.shape[1]:
            return ref.at[pl.ds(row, rows)]
        return ref.at[pl.ds(row, rows), pl.ds(column, columns)]

    @staticmethod
    def _part(region, bit):
        row, rows, column, columns = region
        if rows % 32 == 0:
            return (pl.multiple_of(row + bit * (rows // 2), 16), rows // 2, column, columns)
        return (row, rows, pl.multiple_of(column + bit * (columns // 2), 128), columns // 2)

    def _send_half(self, k):
        b = self.order[k]
        bit = self._bit(b)
        self.trail.append(self.region)
        view = self._view(self.held, self._part(self.region, 1 - bit))
        self._start(self.links.copy(view, self.boxes[k], self.base + k, dp=self._peer(b)))
        self.region = self._part(self.region, bit)

    def _add_half(self, k):
        self.links.arrived(self.boxes[k], self.base + k, dp=self._peer(self.order[k]))
        view = self._view(self.held, self.region)
        total = (view[...].astype(wide) + self.boxes[k][...].astype(wide)).astype(low)
        if k == 2:
            self.share[...] = total
        else:
            view[...] = total

    def _swap(self):
        for k, b in enumerate(self.extra):
            box, at = self.boxes[3 + k], self.base + 7 + k
            copy = self.links.copy(self.share, box, at, dp=self._peer(b))
            copy.start()
            self.links.arrived(box, at, dp=self._peer(b))
            copy.wait_send()
            self.share[...] = (self.share[...].astype(wide) + box[...].astype(wide)).astype(low)

    def _place(self):
        self.placed = pltpu.make_async_copy(
            self.share, self._view(self.whole, self.region), self.links.send.at[self.base + 6]
        )
        self.placed.start()

    def _grow_send(self, k):
        view = self._view(self.whole, self.region)
        src = self.share if k == 2 else view
        self._start(self.links.copy(src, view, self.base + 3 + k, dp=self._peer(self.order[k])))

    def _grow_wait(self, k):
        if k == 2:
            self.placed.wait()
        b = self.order[k]
        view = self._view(self.whole, self._part(self.trail[k], 1 - self._bit(b)))
        self.links.arrived(view, self.base + 3 + k, dp=self._peer(b))
        self.region = self.trail[k]

    def step(self):
        if self.steps:
            self.steps.pop(0)()

    def finish(self):
        assert not self.steps
        for copy in self.sent:
            copy.wait_send()


class Pipeline:
    def __init__(self):
        self.members, self.queue = [], []

    def add(self, member):
        self.members.append(member)
        member.step()
        self.queue.append(member)

    def tick(self, amount=1):
        for _ in range(min(amount, sum(len(m.steps) for m in self.queue))):
            member = self.queue.pop(0)
            member.step()
            if member.steps:
                self.queue.append(member)

    def finish(self):
        while self.queue:
            self.tick()
        for m in self.members:
            m.finish()


def greet(axis, me, count):
    barrier = pltpu.get_barrier_semaphore()

    def one(j, carry):
        pl.semaphore_signal(
            barrier, inc=1, device_id={axis: lax.rem(me + j, count)}, device_id_type=MESH
        )
        return carry

    lax.fori_loop(1, count, one, 0)


def await_greetings(amount):
    pl.semaphore_wait(pltpu.get_barrier_semaphore(), amount)


def halves(rows):
    first = round_up(rows // 2, 16)
    return ((0, first), (first, rows - first))


def head_masks(shape, local_heads):
    lane = lax.broadcasted_iota(jnp.int32, shape, 1)
    return [
        jnp.where((lane >= h * HEAD_DIM) & (lane < (h + 1) * HEAD_DIM), 1.0, 0.0)
        for h in range(local_heads)
    ], lane


def kernel(n, S):
    links = Links(S.send, S.recv)
    t = lax.axis_index("tensor")
    d = lax.axis_index("dp")
    greet("tensor", t, 4)
    greet("dp", d, n.dp)
    R, own, W, H, D, K = n.R, n.own, n.W, n.H, n.D, n.K
    vector = lambda ref: ref[...].reshape(1, D)

    S.xf[...] = jnp.zeros_like(S.xf)
    S.xf[0:own, :] = S.x[...].astype(wide)
    unit, _ = standardize(S.xf[...])
    S.a1[t] = (unit * vector(S.g1) + vector(S.b1)).astype(low)
    S.cot4[t] = jnp.zeros((R, D), low)
    S.cot4[t, 0:own, :] = S.cot[...].astype(low)
    S.ow4[t] = S.ow[...]
    await_greetings(3 + n.dp - 1)
    rows_in = Gather(links, S.a1, t, halves(R))
    cot_in = Gather(links, S.cot4, t, halves(R))
    ow_in = Gather(links, S.ow4, t, ((0, W),))
    rows_in.start()
    S.gw[0:D, :] = jnp.transpose(S.wup[...])
    S.gw[D:, :] = jnp.transpose(S.wdn[...])
    S.v[4 * R :, :] = jnp.zeros((K - 4 * R, H), low)
    length = S.lengths[0]

    def project(i, carry):
        s = flipped(t, i // 2, i % 2)

        @pl.when(i == 1)
        def _():
            rows_in.wait_sib()

        @pl.when(i == 2)
        def _():
            rows_in.forward()
            cot_in.start()
            ow_in.start()

        @pl.when(i == 3)
        def _():
            rows_in.wait_diag()

        slab = S.a1[s]
        lane = lax.broadcasted_iota(jnp.int32, (R, H - W), 1)
        row = lax.broadcasted_iota(jnp.int32, (R, H - W), 0)
        absent = (row >= own) | (row + s * own >= length)
        at = pl.ds(pl.multiple_of(s * R, 16), R)
        out = dot(slab, S.wqkv[0]) + S.bq[0:1, :]
        S.q[s, :, :W] = (out.astype(low).astype(wide) * HEAD_DIM**-0.5).astype(low)
        S.q[s, :, W:] = jnp.where(lane == 0, HEAD_DIM**-0.5, 0.0).astype(low)
        S.k[at, :W] = dot(slab, S.wqkv[1]).astype(low)
        S.k[at, W:] = jnp.where((lane == 0) & absent, -8e30, 0.0).astype(low)
        S.v[at, :W] = (dot(slab, S.wqkv[2]) + S.bq[1:2, :]).astype(low)
        S.v[at, W:] = jnp.where(lane < 2, 1.0, 0.0).astype(low)
        return carry

    lax.fori_loop(0, 4, project, 0)
    if K > 4 * R:
        lane = lax.broadcasted_iota(jnp.int32, (K - 4 * R, H), 1)
        S.k[4 * R :, :] = jnp.where(lane == W, -8e30, 0.0).astype(low)
    S.kt[...] = jnp.transpose(S.k[...])
    S.vt[...] = jnp.transpose(S.v[...])

    masks, lane = head_masks((1, H), n.heads)
    mix_base = links.take(3)

    def attend(i, carry):
        s = flipped(t, 1 - i // 2, (i + i // 2) % 2)
        query = S.q[s]
        mixed = jnp.zeros((R, H), wide)
        inverse = jnp.zeros((R, H), wide)
        for h in range(n.heads):
            here = jnp.where(lane == W, 1.0, masks[h]).astype(low)
            scores = dot(query * here, S.kt[...])
            terms = jnp.exp(scores - jnp.max(scores, -1, keepdims=True)).astype(low)
            S.e[h, s] = terms
            part = dot(terms, S.v[...])
            scale = 1.0 / part[:, W : W + 1]
            mixed += part * (scale * masks[h])
            inverse += scale * masks[h]
        S.o[s] = mixed
        S.inv[s] = inverse
        S.mix[s] = mixed[:, :W].astype(low)

        @pl.when(i < 3)
        def _():
            links.copy(S.mix.at[s], S.mix4.at[t], mix_base + i, tensor=s).start()

        @pl.when(i == 0)
        def _():
            cot_in.wait_sib()
            ow_in.wait_sib()

        @pl.when(i == 1)
        def _():
            cot_in.forward()
            ow_in.forward()

        @pl.when(i == 2)
        def _():
            cot_in.wait_diag()
            ow_in.wait_diag()

        return carry

    lax.fori_loop(0, 4, attend, 0)
    S.mix4[t] = S.mix[t]
    for i in range(3):
        s = flipped(t, 1 - i // 2, (i + i // 2) % 2)
        links.arrived(S.mix4.at[s], mix_base + i, tensor=s)

    total = S.xf[...] + vector(S.ob)
    for j in range(4):
        total += dot(S.mix4[j], S.ow4[j])
    S.hid[...] = total
    unit, _ = standardize(total)
    S.a24[t] = (unit * vector(S.g2) + vector(S.b2)).astype(low)
    next_in = Gather(links, S.a24, t, halves(R))
    next_in.start()
    back = Reduce(links, S.part, S.pre1, S.near1, S.far1, t)
    ahead = Reduce(links, S.fop, S.pre2, S.near2, S.far2, t)
    S.gub[...] = jnp.zeros_like(S.gub)

    def feed(i, carry):
        s = flipped(t, i // 2, i % 2)

        @pl.when(i == 1)
        def _():
            next_in.wait_sib()

        @pl.when(i == 2)
        def _():
            next_in.forward()

        @pl.when(i == 3)
        def _():
            next_in.wait_diag()

        up = dot(S.a24[s], S.wup[...]) + vector(S.bup)
        square = up * up
        c = 0.7978845608028654
        bend = jnp.tanh(c * up * (1.0 + 0.044715 * square))
        half = 0.5 * (1.0 + bend)
        slope = half + 0.5 * up * (1.0 - bend * bend) * (c + (3 * 0.044715 * c) * square)
        active = (up * half).astype(low)
        S.pool[s, :, 0:D] = active
        grad = (dot(S.cot4[s], S.gw[D:, :]) * slope).astype(low)
        S.gup[s] = grad
        S.part[s] = dot(grad, S.gw[0:D, :]).astype(low)

        @pl.when(i == 1)
        def _():
            back.send_sib()

        @pl.when(i == 3)
        def _():
            back.send_diag()

        S.fop[s] = dot(active, S.wdn[...]).astype(low)

        @pl.when(i == 1)
        def _():
            ahead.send_sib()

        @pl.when(i == 3)
        def _():
            ahead.send_diag()

        S.gub[...] += jnp.sum(grad.astype(wide), 0, keepdims=True)
        return carry

    lax.fori_loop(0, 4, feed, 0)
    back.send_cross()

    sums = Pipeline()
    tile = D // 2
    box_at = share_at = 0

    def sum_over_dp(held, whole, first, rows, order):
        nonlocal box_at, share_at
        sizes, taken = DataReduce.sizes(rows, D, n.dp)
        share = S.share.at[pl.ds(share_at, sizes[2][0])]
        sums.add(DataReduce(links, held, whole, share, S.box, box_at, first, rows, d, n.dp, order))
        box_at, share_at = box_at + taken, share_at + sizes[2][0]

    for left, right, first in ((S.a24, S.gup, 0), (S.pool, S.cot4, D)):
        for j in range(2):
            columns = left[:, :, j * tile : (j + 1) * tile].reshape(4 * R, tile)
            at = first + j * tile
            S.gw[at : at + tile, :] = dot_columns(columns, flat(right)).astype(low)
            sum_over_dp(S.gw, S.whole1, at, tile, (1, 0, 2) if at == tile else (0, 1, 2))
        if first == 0:
            ahead.send_cross()

    grad = back.result()
    unit, inverse = standardize(S.hid[...])
    S.small[...] = jnp.zeros_like(S.small)
    S.small[2:3, :] = jnp.sum(grad * unit, 0, keepdims=True)
    S.small[3:4, :] = jnp.sum(grad, 0, keepdims=True)
    S.gh[...] = norm_back(grad, unit, inverse, vector(S.g2))
    S.gh[0:own, :] += S.cot[...]
    hidden_low = S.gh[...].astype(low)
    S.hl4[t] = hidden_low
    S.small[4:5, :] = jnp.sum(hidden_low.astype(wide), 0, keepdims=True)
    S.small[5:6, :] = jnp.sum(S.cot4[t].astype(wide), 0, keepdims=True)
    S.small[6:7, :] = S.gub[...]
    gm_base = links.take(3)

    def share(i, carry):
        s = flipped(t, 1 - i // 2, (i + i // 2) % 2)
        S.mix4[s] = dot_rows(S.hl4[t], S.ow4[s]).astype(low)

        @pl.when(i < 3)
        def _():
            links.copy(S.mix4.at[s], S.gm4.at[t], gm_base + i, tensor=s).start()

        return carry

    lax.fori_loop(0, 4, share, 0)
    S.gm4[t] = S.mix4[t]
    sums.tick(2)
    hl_in = Gather(links, S.hl4, t, halves(R))
    hl_in.start()

    next_in.finish()
    S.do[...] = jnp.zeros_like(S.do)
    S.qt[...] = jnp.transpose(flat(S.q))
    sums.tick(2)

    def prepare(i, s):
        if i > 0:
            links.arrived(S.gm4.at[s], gm_base + (3, 2, 0, 1)[i], tensor=s)
        S.do[:, :W] = S.gm4[s].astype(wide)
        scaled = (S.do[...] * S.inv[s]).astype(low)
        S.v[pl.ds(pl.multiple_of(s * R, 16), R), :] = scaled
        scaled = scaled.astype(wide)
        product = scaled * S.o[s]
        for h in range(n.heads):
            inner = -jnp.sum(product * masks[h], -1, keepdims=True)
            upper = inner.astype(low).astype(wide)
            S.a24[s, :, h * H : (h + 1) * H] = (
                scaled * masks[h]
                + jnp.where(lane == W, upper, 0.0)
                + jnp.where(lane == W + 1, inner - upper, 0.0)
            ).astype(low)

    def pull(h, s):
        grad_p = dot(S.a24[s, :, h * H : (h + 1) * H], S.vt[...])
        grad_s = (S.e[h, s].astype(wide) * grad_p).astype(low)
        S.pool[s] = grad_s
        dq = dot(grad_s, S.k[...]) * (masks[h] * HEAD_DIM**-0.5)
        if h > 0:
            dq += S.gup[s, :, 0:H].astype(wide)
        S.gup[s, :, 0:H] = dq.astype(low)

    for h in range(n.heads):
        for i in range(4):
            s = flipped(t, i // 2, i % 2)
            if h == 0:
                prepare(i, s)
            pull(h, s)
            sums.tick(2)
        if h == 0:
            S.v[4 * R :, :] = jnp.zeros((K - 4 * R, H), low)
            S.kt[...] = jnp.transpose(S.v[...])
            hl_in.wait_sib()
            hl_in.forward()
        at = slice(h * HEAD_DIM, (h + 1) * HEAD_DIM)
        S.dk[at, :] = dot(S.qt[at, :], flat(S.pool)).astype(low)
        S.dv[at, :] = dot(S.kt[at, : 4 * R], flat(S.e.at[h])).astype(low)
        tile = h * HEAD_DIM // 128 * 128
        dqt = jnp.transpose(flat(S.gup.at[:, :, tile : tile + 128]))
        left = jnp.concatenate(
            [dqt[h * HEAD_DIM - tile : (h + 1) * HEAD_DIM - tile], S.dk[at, : 4 * R], S.dv[at, : 4 * R]], 0
        )
        S.gw2[h * W : (h + 1) * W, :] = dot(left, flat(S.a1)).astype(low)
        sum_over_dp(S.gw2, S.whole2, h * W, W, (0, 1, 2))
        if h == 0:
            hl_in.wait_diag()
            S.gw2[3 * W :, :] = dot_columns(flat(S.mix), flat(S.hl4)).astype(low)
            sum_over_dp(S.gw2, S.whole2, 3 * W, W, (1, 0, 2))

    pad = jnp.zeros((R, H - W), low)
    for part, grad_t in ((1, S.dk), (2, S.dv)):
        rows = jnp.transpose(grad_t[...])
        for s in range(4):
            S.gup[s, :, part * H : part * H + W] = rows[s * R : (s + 1) * R]
            S.gup[s, :, part * H + W : (part + 1) * H] = pad

    back.finish()
    down = Reduce(links, S.part, S.pre1, S.near1, S.far1, t)

    def lead(i, carry):
        s = flipped(t, 1 - i // 2, 1 - i % 2)
        out = dot_rows(S.gup[s, :, 0:W], S.wqkv[0])
        out += dot_rows(S.gup[s, :, H : H + W], S.wqkv[1])
        out += dot_rows(S.gup[s, :, 2 * H : 2 * H + W], S.wqkv[2])
        S.part[s] = out.astype(low)

        @pl.when(i == 0)
        def _():
            down.send_diag()

        @pl.when(i == 2)
        def _():
            down.send_sib()

        return carry

    lax.fori_loop(0, 4, lead, 0)
    down.send_cross()
    S.small[7:8, 0:H] = jnp.sum(flat(S.gup.at[:, :, 0:H]).astype(wide), 0, keepdims=True)
    S.small[7:8, H : 2 * H] = jnp.sum(
        flat(S.gup.at[:, :, 2 * H : 3 * H]).astype(wide), 0, keepdims=True
    )
    result = S.hid[...] + (ahead.result() + vector(S.db))
    S.output[...] = result[:own].astype(low)
    sums.tick(4)

    unit, inverse = standardize(S.xf[...])
    grad = down.result()
    S.small[0:1, :] = jnp.sum(grad * unit, 0, keepdims=True)
    S.small[1:2, :] = jnp.sum(grad, 0, keepdims=True)
    S.small4[t] = S.small[...]
    base3 = links.take(3)
    for j in range(3):
        peer = lax.rem(t + j + 1, 4)
        links.start(S.small4.at[t], S.small4.at[t], base3 + j, tensor=peer)
    total = S.gh[...] + norm_back(grad, unit, inverse, vector(S.g1))
    S.gt[...] = total[:own]
    for j in range(3):
        peer = lax.rem(t + 3 - j, 4)
        links.arrived(S.small4.at[peer], base3 + j, tensor=peer)
    over = S.small4[0] + S.small4[1] + S.small4[2] + S.small4[3]
    row = lax.broadcasted_iota(jnp.int32, over.shape, 0)
    S.smalls[d] = jnp.where(row < 6, over, S.small[...])
    base4 = links.take(n.dp)

    def tell(j, carry):
        links.copy(S.smalls.at[d], S.smalls.at[d], base4 + j, dp=lax.rem(d + j, n.dp)).start()
        return carry

    lax.fori_loop(1, n.dp, tell, 0)
    sums.finish()

    def hear(j, carry):
        peer = lax.rem(d + n.dp - j, n.dp)
        links.arrived(S.smalls.at[peer], base4 + j, dp=peer)
        return carry

    lax.fori_loop(1, n.dp, hear, 0)
    S.small_sum[...] = lax.fori_loop(
        1, n.dp, lambda j, acc: acc + S.smalls[j], S.smalls[0]
    )

    def done(j, carry):
        links.copy(S.smalls.at[d], S.smalls.at[d], base4 + j, dp=lax.rem(d + j, n.dp)).wait_send()
        return carry

    lax.fori_loop(1, n.dp, done, 0)
    for i in range(3):
        s = flipped(t, 1 - i // 2, (i + i // 2) % 2)
        links.copy(S.mix.at[s], S.mix4.at[t], mix_base + i, tensor=s).wait_send()
        links.copy(S.mix4.at[s], S.gm4.at[t], gm_base + i, tensor=s).wait_send()
    for transfer in (rows_in, cot_in, ow_in, hl_in, ahead, down):
        transfer.finish()
    links.finish()


def body(
    tokens,
    lengths,
    ln1_gain,
    ln1_shift,
    qkv_weight,
    qv_bias,
    out_weight,
    out_bias,
    ln2_gain,
    ln2_shift,
    up_weight,
    up_bias,
    down_weight,
    down_bias,
    cotangent,
):
    own, D = tokens.shape
    W = qkv_weight.shape[2]
    F = up_weight.shape[1]
    dp = lax.axis_size("dp")
    assert lax.axis_size("tensor") == 4 and lengths.shape[0] == 1 and F == D and 4 * W == D and 3 * round_up(W + 2, 128) == D
    R = round_up(own, 16)
    H = round_up(W + 2, 128)
    K = round_up(4 * R, 256)
    heads = W // HEAD_DIM
    extra = dp.bit_length() - 1 - 3
    n = types.SimpleNamespace(
        own=own, D=D, W=W, R=R, H=H, K=K, dp=dp, heads=heads, extra=extra
    )
    given = dict(
        x=tokens, lengths=lengths, g1=ln1_gain, b1=ln1_shift,
        wqkv=jnp.transpose(qkv_weight, (1, 0, 2)), bq=qv_bias, ow=out_weight, ob=out_bias,
        g2=ln2_gain, b2=ln2_shift, wup=up_weight, bup=up_bias, wdn=down_weight, db=down_bias,
        cot=cotangent,
    )
    outs = dict(
        output=((own, D), low), gt=((own, D), wide), small_sum=((8, D), wide),
        whole1=((2 * D, D), low), whole2=((D, D), low),
    )
    rows4 = ((4, R, D), low)
    slab = ((R, D), low)
    chunks = [D // 2] * 4 + [W] * 4
    scratch = dict(
        a1=rows4, cot4=rows4, ow4=((4, W, D), low), q=((4, R, H), low), k=((K, H), low),
        v=((K, H), low), kt=((H, K), low), vt=((H, K), low), e=((heads, 4, R, K), low),
        o=((4, R, H), wide), inv=((4, R, H), wide), mix=((4, R, W), low), mix4=((4, R, W), low),
        xf=((R, D), wide), hid=((R, D), wide),
        a24=rows4, pool=((4, R, K), low), gup=rows4, part=rows4,
        fop=rows4, pre1=slab, near1=slab, far1=slab, pre2=slab, near2=slab, far2=slab,
        gw=((2 * D, D), low), gub=((1, D), wide),
        small=((8, D), wide), gh=((R, D), wide), hl4=rows4,
        gm4=((4, R, W), low), dk=((W, K), low), dv=((W, K), low), qt=((H, 4 * R), low), do=((R, H), wide),
        gw2=((D, D), low),
        small4=((4, 8, D), wide), smalls=((dp, 8, D), wide),
        box=((sum(DataReduce.sizes(r, D, dp)[1] for r in chunks), D), low),
        share=((sum(DataReduce.sizes(r, D, dp)[0][2][0] for r in chunks), D), low),
    )
    sems = 140 + dp + 8 * extra
    names = list(given) + list(outs) + list(scratch) + ["send", "recv"]
    vmem = pl.BlockSpec(memory_space=pltpu.VMEM)
    smem = pl.BlockSpec(memory_space=pltpu.SMEM)
    hbm = pl.BlockSpec(memory_space=pl.ANY)
    output, gt, small, whole1, whole2 = pl.pallas_call(
        lambda *refs: kernel(n, types.SimpleNamespace(**dict(zip(names, refs)))),
        out_shape=tuple(jax.ShapeDtypeStruct(*spec) for spec in outs.values()),
        in_specs=[smem if name == "lengths" else vmem for name in given],
        out_specs=tuple(hbm if name in ("whole1", "whole2") else vmem for name in outs),
        scratch_shapes=[pltpu.VMEM(*spec) for spec in scratch.values()]
        + [pltpu.SemaphoreType.DMA((sems,))] * 2,
        compiler_params=pltpu.CompilerParams(
            collective_id=0, has_side_effects=True, vmem_limit_bytes=VMEM_BYTES
        ),
    )(*given.values())
    parts = whole2[: 3 * W].astype(wide).reshape(heads, 3, HEAD_DIM, D)
    grad_qkv = jnp.transpose(parts, (3, 1, 0, 2)).reshape(D, 3, W)
    return (
        output,
        gt,
        small[0],
        small[1],
        grad_qkv,
        jnp.stack([small[7, :W], small[7, H : H + W]]),
        whole2[3 * W :].astype(wide),
        small[4],
        small[2],
        small[3],
        whole1[:D].astype(wide),
        small[6],
        whole1[D:].astype(wide),
        small[5],
    )


def solution(mesh):
    placed = (
        P(("dp", "tensor"), None),
        P("dp"),
        P(),
        P(),
        P(None, None, "tensor"),
        P(None, "tensor"),
        P("tensor", None),
        P(),
        P(),
        P(),
        P(None, "tensor"),
        P("tensor"),
        P("tensor", None),
        P(),
        P(("dp", "tensor"), None),
    )
    return jax.shard_map(
        body,
        mesh=mesh,
        in_specs=placed,
        out_specs=(
            P(("dp", "tensor"), None),
            P(("dp", "tensor"), None),
            P(),
            P(),
            P(None, None, "tensor"),
            P(None, "tensor"),
            P("tensor", None),
            P(),
            P(),
            P(),
            P(None, "tensor"),
            P("tensor"),
            P("tensor", None),
            P(),
        ),
        check_vma=False,
    )
```

```python
import types

import jax
import jax.numpy as jnp
from jax import lax
from jax.experimental import pallas as pl
from jax.experimental.pallas import tpu as pltpu
from jax.sharding import PartitionSpec as P

HEAD_DIM = 64
MESH = pl.DeviceIdType.MESH
VMEM_BYTES = 62 * 2**20

epsilon = 1e-06
low = jnp.bfloat16
wide = jnp.float32


def round_up(amount, unit):
    return -(-amount // unit) * unit


def flipped(t, flip_chip, flip_core):
    return (t // 2 + flip_chip) % 2 * 2 + (t % 2 + flip_core) % 2


def dot(left, right):
    return jnp.dot(left, right, preferred_element_type=wide)


def dot_rows(left, right):
    return lax.dot_general(left, right, (((1,), (1,)), ((), ())), preferred_element_type=wide)


def dot_columns(left, right):
    return lax.dot_general(left, right, (((0,), (0,)), ((), ())), preferred_element_type=wide)


def standardize(values):
    center = values - jnp.mean(values, -1, keepdims=True)
    inverse = lax.rsqrt(jnp.mean(center * center, -1, keepdims=True) + epsilon)
    return center * inverse, inverse


def norm_back(grad, unit, inverse, gain):
    scaled = grad * gain
    return inverse * (
        scaled
        - jnp.mean(scaled, -1, keepdims=True)
        - unit * jnp.mean(scaled * unit, -1, keepdims=True)
    )


def flat(ref):
    a, b, c = ref.shape
    return ref[...].reshape(a * b, c)


class Links:
    def __init__(self, send, recv):
        self.send, self.recv, self.used, self.pending = send, recv, 0, []

    def take(self, amount=1):
        base = self.used
        self.used += amount
        assert self.used <= self.send.shape[0]
        return base

    def copy(self, src, dst, at, **where):
        return pltpu.make_async_remote_copy(
            src_ref=src,
            dst_ref=dst,
            send_sem=self.send.at[at],
            recv_sem=self.recv.at[at],
            device_id=where,
            device_id_type=MESH,
        )

    def start(self, src, dst, at, **where):
        copy = self.copy(src, dst, at, **where)
        copy.start()
        self.pending.append(copy)

    def arrived(self, dst, at, **where):
        self.copy(dst, dst, at, **where).wait_recv()

    def finish(self):
        for copy in self.pending:
            copy.wait_send()
        self.pending = []


class Gather:
    def __init__(self, links, buf, t, parts):
        self.links, self.buf, self.t, self.parts = links, buf, t, parts
        self.sib, self.cross, self.diag = flipped(t, 0, 1), flipped(t, 1, 0), flipped(t, 1, 1)
        self.base = links.take(3 * len(parts))

    def view(self, slot, part):
        start, size = self.parts[part]
        return self.buf.at[slot, pl.ds(start, size)]

    def _each(self):
        return range(len(self.parts))

    def start(self):
        for p in self._each():
            v = self.view(self.t, p)
            self.links.copy(v, v, self.base + 3 * p, tensor=self.cross).start()
        for p in self._each():
            v = self.view(self.t, p)
            self.links.copy(v, v, self.base + 3 * p + 1, tensor=self.sib).start()

    def wait_sib(self):
        for p in self._each():
            self.links.arrived(self.view(self.sib, p), self.base + 3 * p + 1, tensor=self.sib)

    def forward(self):
        for p in self._each():
            v = self.view(self.cross, p)
            self.links.arrived(v, self.base + 3 * p, tensor=self.cross)
            self.links.copy(v, v, self.base + 3 * p + 2, tensor=self.sib).start()

    def wait_diag(self):
        for p in self._each():
            self.links.arrived(self.view(self.diag, p), self.base + 3 * p + 2, tensor=self.sib)

    def finish(self):
        for p in self._each():
            v = self.view(self.t, p)
            self.links.copy(v, v, self.base + 3 * p, tensor=self.cross).wait_send()
            self.links.copy(v, v, self.base + 3 * p + 1, tensor=self.sib).wait_send()
            v = self.view(self.cross, p)
            self.links.copy(v, v, self.base + 3 * p + 2, tensor=self.sib).wait_send()


class Reduce:
    def __init__(self, links, part, pre, near, far, t):
        self.links, self.part, self.pre, self.near, self.far, self.t = links, part, pre, near, far, t
        self.sib, self.cross, self.diag = flipped(t, 0, 1), flipped(t, 1, 0), flipped(t, 1, 1)
        self.base = links.take(3)

    def send_diag(self):
        self.links.copy(self.part.at[self.diag], self.pre, self.base, tensor=self.sib).start()

    def send_sib(self):
        self.links.copy(self.part.at[self.sib], self.near, self.base + 1, tensor=self.sib).start()

    def send_cross(self):
        self.links.arrived(self.pre, self.base, tensor=self.sib)
        total = self.part[self.cross].astype(wide) + self.pre[...].astype(wide)
        self.part[self.cross] = total.astype(low)
        self.links.copy(self.part.at[self.cross], self.far, self.base + 2, tensor=self.cross).start()

    def result(self):
        self.links.arrived(self.near, self.base + 1, tensor=self.sib)
        self.links.arrived(self.far, self.base + 2, tensor=self.cross)
        return (
            self.part[self.t].astype(wide) + self.near[...].astype(wide) + self.far[...].astype(wide)
        )

    def finish(self):
        self.links.copy(self.part.at[self.diag], self.pre, self.base, tensor=self.sib).wait_send()
        self.links.copy(self.part.at[self.sib], self.near, self.base + 1, tensor=self.sib).wait_send()
        self.links.copy(self.part.at[self.cross], self.far, self.base + 2, tensor=self.cross).wait_send()


class DataReduce:
    def __init__(self, links, held, whole, share, box, box_at, first, rows, d, count, order):
        self.links, self.held, self.whole = links, held, whole
        bits = count.bit_length() - 1
        assert count == 1 << bits and bits >= 3
        self.extra = [b for b in range(bits) if b not in order]
        self.d, self.order = d, order
        self.region = (first, rows, 0, held.shape[1])
        self.trail, self.sent, self.boxes = [], [], []
        for tall, broad in self.sizes(rows, held.shape[1], count)[0]:
            self.boxes.append(box.at[pl.ds(box_at, tall), pl.ds(0, broad)])
            box_at += tall
        self.share = share.at[pl.ds(0, tall), pl.ds(0, broad)]
        self.base = links.take(7 + len(self.extra))
        self.steps = [lambda: self._send_half(0)]
        for k in (1, 2):
            self.steps.append(lambda k=k: (self._add_half(k - 1), self._send_half(k)))
        self.steps.append(lambda: (self._add_half(2), self._swap(), self._place(), self._grow_send(2)))
        for k in (2, 1):
            self.steps.append(lambda k=k: (self._grow_wait(k), self._grow_send(k - 1)))
        self.steps.append(lambda: self._grow_wait(0))

    @staticmethod
    def sizes(rows, columns, count):
        found = []
        for _ in range(3):
            if rows % 32 == 0:
                rows //= 2
            else:
                columns //= 2
            found.append((rows, columns))
        found += found[2:] * (count.bit_length() - 1 - 3)
        return found, sum(size[0] for size in found)

    def _bit(self, b):
        return self.d // (1 << b) % 2

    def _peer(self, b):
        return self.d + (1 - 2 * self._bit(b)) * (1 << b)

    def _start(self, copy):
        copy.start()
        self.sent.append(copy)

    @staticmethod
    def _view(ref, region):
        row, rows, column, columns = region
        if columns == ref.shape[1]:
            return ref.at[pl.ds(row, rows)]
        return ref.at[pl.ds(row, rows), pl.ds(column, columns)]

    @staticmethod
    def _part(region, bit):
        row, rows, column, columns = region
        if rows % 32 == 0:
            return (pl.multiple_of(row + bit * (rows // 2), 16), rows // 2, column, columns)
        return (row, rows, pl.multiple_of(column + bit * (columns // 2), 128), columns // 2)

    def _send_half(self, k):
        b = self.order[k]
        bit = self._bit(b)
        self.trail.append(self.region)
        view = self._view(self.held, self._part(self.region, 1 - bit))
        self._start(self.links.copy(view, self.boxes[k], self.base + k, dp=self._peer(b)))
        self.region = self._part(self.region, bit)

    def _add_half(self, k):
        self.links.arrived(self.boxes[k], self.base + k, dp=self._peer(self.order[k]))
        view = self._view(self.held, self.region)
        total = (view[...].astype(wide) + self.boxes[k][...].astype(wide)).astype(low)
        if k == 2:
            self.share[...] = total
        else:
            view[...] = total

    def _swap(self):
        for k, b in enumerate(self.extra):
            box, at = self.boxes[3 + k], self.base + 7 + k
            copy = self.links.copy(self.share, box, at, dp=self._peer(b))
            copy.start()
            self.links.arrived(box, at, dp=self._peer(b))
            copy.wait_send()
            self.share[...] = (self.share[...].astype(wide) + box[...].astype(wide)).astype(low)

    def _place(self):
        self.placed = pltpu.make_async_copy(
            self.share, self._view(self.whole, self.region), self.links.send.at[self.base + 6]
        )
        self.placed.start()

    def _grow_send(self, k):
        view = self._view(self.whole, self.region)
        src = self.share if k == 2 else view
        self._start(self.links.copy(src, view, self.base + 3 + k, dp=self._peer(self.order[k])))

    def _grow_wait(self, k):
        if k == 2:
            self.placed.wait()
        b = self.order[k]
        view = self._view(self.whole, self._part(self.trail[k], 1 - self._bit(b)))
        self.links.arrived(view, self.base + 3 + k, dp=self._peer(b))
        self.region = self.trail[k]

    def step(self):
        if self.steps:
            self.steps.pop(0)()

    def finish(self):
        assert not self.steps
        for copy in self.sent:
            copy.wait_send()


class Pipeline:
    def __init__(self):
        self.members, self.queue = [], []

    def add(self, member):
        self.members.append(member)
        member.step()
        self.queue.append(member)

    def tick(self, amount=1):
        for _ in range(min(amount, sum(len(m.steps) for m in self.queue))):
            member = self.queue.pop(0)
            member.step()
            if member.steps:
                self.queue.append(member)

    def finish(self):
        while self.queue:
            self.tick()
        for m in self.members:
            m.finish()


def greet(axis, me, count):
    barrier = pltpu.get_barrier_semaphore()

    def one(j, carry):
        pl.semaphore_signal(
            barrier, inc=1, device_id={axis: lax.rem(me + j, count)}, device_id_type=MESH
        )
        return carry

    lax.fori_loop(1, count, one, 0)


def await_greetings(amount):
    pl.semaphore_wait(pltpu.get_barrier_semaphore(), amount)


def halves(rows):
    first = round_up(rows // 2, 16)
    return ((0, first), (first, rows - first))


def head_masks(shape, local_heads):
    lane = lax.broadcasted_iota(jnp.int32, shape, 1)
    return [
        jnp.where((lane >= h * HEAD_DIM) & (lane < (h + 1) * HEAD_DIM), 1.0, 0.0)
        for h in range(local_heads)
    ], lane


def kernel(n, S):
    links = Links(S.send, S.recv)
    t = lax.axis_index("tensor")
    d = lax.axis_index("dp")
    greet("tensor", t, 4)
    greet("dp", d, n.dp)
    R, own, W, H, D, K = n.R, n.own, n.W, n.H, n.D, n.K
    vector = lambda ref: ref[...].reshape(1, D)

    S.xf[...] = jnp.zeros_like(S.xf)
    S.xf[0:own, :] = S.x[...].astype(wide)
    unit, _ = standardize(S.xf[...])
    S.a1[t] = (unit * vector(S.g1) + vector(S.b1)).astype(low)
    S.cot4[t] = jnp.zeros((R, D), low)
    S.cot4[t, 0:own, :] = S.cot[...].astype(low)
    S.ow4[t] = S.ow[...]
    await_greetings(3 + n.dp - 1)
    rows_in = Gather(links, S.a1, t, halves(R))
    cot_in = Gather(links, S.cot4, t, halves(R))
    ow_in = Gather(links, S.ow4, t, ((0, W),))
    rows_in.start()
    S.gw[0:D, :] = jnp.transpose(S.wup[...])
    S.gw[D:, :] = jnp.transpose(S.wdn[...])
    S.v[4 * R :, :] = jnp.zeros((K - 4 * R, H), low)
    length = S.lengths[0]

    def project(i, carry):
        s = flipped(t, i // 2, i % 2)

        @pl.when(i == 1)
        def _():
            rows_in.wait_sib()

        @pl.when(i == 2)
        def _():
            rows_in.forward()
            cot_in.start()
            ow_in.start()

        @pl.when(i == 3)
        def _():
            rows_in.wait_diag()

        slab = S.a1[s]
        lane = lax.broadcasted_iota(jnp.int32, (R, H - W), 1)
        row = lax.broadcasted_iota(jnp.int32, (R, H - W), 0)
        absent = (row >= own) | (row + s * own >= length)
        at = pl.ds(pl.multiple_of(s * R, 16), R)
        out = dot(slab, S.wqkv[0]) + S.bq[0:1, :]
        S.q[s, :, :W] = (out.astype(low).astype(wide) * HEAD_DIM**-0.5).astype(low)
        S.q[s, :, W:] = jnp.where(lane == 0, HEAD_DIM**-0.5, 0.0).astype(low)
        S.k[at, :W] = dot(slab, S.wqkv[1]).astype(low)
        S.k[at, W:] = jnp.where((lane == 0) & absent, -8e30, 0.0).astype(low)
        S.v[at, :W] = (dot(slab, S.wqkv[2]) + S.bq[1:2, :]).astype(low)
        S.v[at, W:] = jnp.where(lane < 2, 1.0, 0.0).astype(low)
        return carry

    lax.fori_loop(0, 4, project, 0)
    if K > 4 * R:
        lane = lax.broadcasted_iota(jnp.int32, (K - 4 * R, H), 1)
        S.k[4 * R :, :] = jnp.where(lane == W, -8e30, 0.0).astype(low)
    S.kt[...] = jnp.transpose(S.k[...])
    S.vt[...] = jnp.transpose(S.v[...])

    masks, lane = head_masks((1, H), n.heads)
    mix_base = links.take(3)

    def attend(i, carry):
        s = flipped(t, 1 - i // 2, (i + i // 2) % 2)
        query = S.q[s]
        mixed = jnp.zeros((R, H), wide)
        inverse = jnp.zeros((R, H), wide)
        for h in range(n.heads):
            here = jnp.where(lane == W, 1.0, masks[h]).astype(low)
            scores = dot(query * here, S.kt[...])
            terms = jnp.exp(scores - jnp.max(scores, -1, keepdims=True)).astype(low)
            S.e[h, s] = terms
            part = dot(terms, S.v[...])
            scale = 1.0 / part[:, W : W + 1]
            mixed += part * (scale * masks[h])
            inverse += scale * masks[h]
        S.o[s] = mixed
        S.inv[s] = inverse
        S.mix[s] = mixed[:, :W].astype(low)

        @pl.when(i < 3)
        def _():
            links.copy(S.mix.at[s], S.mix4.at[t], mix_base + i, tensor=s).start()

        @pl.when(i == 0)
        def _():
            cot_in.wait_sib()
            ow_in.wait_sib()

        @pl.when(i == 1)
        def _():
            cot_in.forward()
            ow_in.forward()

        @pl.when(i == 2)
        def _():
            cot_in.wait_diag()
            ow_in.wait_diag()

        return carry

    lax.fori_loop(0, 4, attend, 0)
    S.mix4[t] = S.mix[t]
    for i in range(3):
        s = flipped(t, 1 - i // 2, (i + i // 2) % 2)
        links.arrived(S.mix4.at[s], mix_base + i, tensor=s)

    total = S.xf[...] + vector(S.ob)
    for j in range(4):
        total += dot(S.mix4[j], S.ow4[j])
    S.hid[...] = total
    unit, _ = standardize(total)
    S.a24[t] = (unit * vector(S.g2) + vector(S.b2)).astype(low)
    next_in = Gather(links, S.a24, t, halves(R))
    next_in.start()
    back = Reduce(links, S.part, S.pre1, S.near1, S.far1, t)
    ahead = Reduce(links, S.fop, S.pre2, S.near2, S.far2, t)
    S.gub[...] = jnp.zeros_like(S.gub)

    def feed(i, carry):
        s = flipped(t, i // 2, i % 2)

        @pl.when(i == 1)
        def _():
            next_in.wait_sib()

        @pl.when(i == 2)
        def _():
            next_in.forward()

        @pl.when(i == 3)
        def _():
            next_in.wait_diag()

        up = dot(S.a24[s], S.wup[...]) + vector(S.bup)
        square = up * up
        c = 0.7978845608028654
        bend = jnp.tanh(c * up * (1.0 + 0.044715 * square))
        half = 0.5 * (1.0 + bend)
        slope = half + 0.5 * up * (1.0 - bend * bend) * (c + (3 * 0.044715 * c) * square)
        active = (up * half).astype(low)
        S.pool[s, :, 0:D] = active
        grad = (dot(S.cot4[s], S.gw[D:, :]) * slope).astype(low)
        S.gup[s] = grad
        S.part[s] = dot(grad, S.gw[0:D, :]).astype(low)

        @pl.when(i == 1)
        def _():
            back.send_sib()

        @pl.when(i == 3)
        def _():
            back.send_diag()

        S.fop[s] = dot(active, S.wdn[...]).astype(low)

        @pl.when(i == 1)
        def _():
            ahead.send_sib()

        @pl.when(i == 3)
        def _():
            ahead.send_diag()

        S.gub[...] += jnp.sum(grad.astype(wide), 0, keepdims=True)
        return carry

    lax.fori_loop(0, 4, feed, 0)
    back.send_cross()

    sums = Pipeline()
    tile = D // 2
    box_at = share_at = 0

    def sum_over_dp(held, whole, first, rows, order):
        nonlocal box_at, share_at
        sizes, taken = DataReduce.sizes(rows, D, n.dp)
        share = S.share.at[pl.ds(share_at, sizes[2][0])]
        sums.add(DataReduce(links, held, whole, share, S.box, box_at, first, rows, d, n.dp, order))
        box_at, share_at = box_at + taken, share_at + sizes[2][0]

    for left, right, first in ((S.a24, S.gup, 0), (S.pool, S.cot4, D)):
        for j in range(2):
            columns = left[:, :, j * tile : (j + 1) * tile].reshape(4 * R, tile)
            at = first + j * tile
            S.gw[at : at + tile, :] = dot_columns(columns, flat(right)).astype(low)
            sum_over_dp(S.gw, S.whole1, at, tile, (1, 0, 2) if at == tile else (0, 1, 2))

    sums.tick(1)
    grad = back.result()
    unit, inverse = standardize(S.hid[...])
    S.small[...] = jnp.zeros_like(S.small)
    S.small[2:3, :] = jnp.sum(grad * unit, 0, keepdims=True)
    S.small[3:4, :] = jnp.sum(grad, 0, keepdims=True)
    S.gh[...] = norm_back(grad, unit, inverse, vector(S.g2))
    S.gh[0:own, :] += S.cot[...]
    hidden_low = S.gh[...].astype(low)
    S.hl4[t] = hidden_low
    S.small[4:5, :] = jnp.sum(hidden_low.astype(wide), 0, keepdims=True)
    S.small[5:6, :] = jnp.sum(S.cot4[t].astype(wide), 0, keepdims=True)
    S.small[6:7, :] = S.gub[...]
    gm_base = links.take(3)

    def share(i, carry):
        s = flipped(t, 1 - i // 2, (i + i // 2) % 2)
        S.mix4[s] = dot_rows(S.hl4[t], S.ow4[s]).astype(low)

        @pl.when(i < 3)
        def _():
            links.copy(S.mix4.at[s], S.gm4.at[t], gm_base + i, tensor=s).start()

        return carry

    lax.fori_loop(0, 4, share, 0)
    S.gm4[t] = S.mix4[t]
    hl_in = Gather(links, S.hl4, t, halves(R))
    sums.tick(1)

    next_in.finish()
    S.do[...] = jnp.zeros_like(S.do)
    S.qt[...] = jnp.transpose(flat(S.q))
    sums.tick(2)

    def prepare(i, s):
        if i > 0:
            links.arrived(S.gm4.at[s], gm_base + (3, 2, 0, 1)[i], tensor=s)
        S.do[:, :W] = S.gm4[s].astype(wide)
        scaled = (S.do[...] * S.inv[s]).astype(low)
        S.v[pl.ds(pl.multiple_of(s * R, 16), R), :] = scaled
        scaled = scaled.astype(wide)
        product = scaled * S.o[s]
        for h in range(n.heads):
            inner = -jnp.sum(product * masks[h], -1, keepdims=True)
            upper = inner.astype(low).astype(wide)
            S.a24[s, :, h * H : (h + 1) * H] = (
                scaled * masks[h]
                + jnp.where(lane == W, upper, 0.0)
                + jnp.where(lane == W + 1, inner - upper, 0.0)
            ).astype(low)

    def pull(h, s):
        grad_p = dot(S.a24[s, :, h * H : (h + 1) * H], S.vt[...])
        grad_s = (S.e[h, s].astype(wide) * grad_p).astype(low)
        S.pool[s] = grad_s
        dq = dot(grad_s, S.k[...]) * (masks[h] * HEAD_DIM**-0.5)
        if h > 0:
            dq += S.gup[s, :, 0:H].astype(wide)
        S.gup[s, :, 0:H] = dq.astype(low)

    for h in range(n.heads):
        for i in range(4):
            s = flipped(t, i // 2, i % 2)
            if h == 0:
                prepare(i, s)
            pull(h, s)
            sums.tick(1)
            if (h, i) == (0, 3):
                hl_in.start()
            elif (h, i) == (1, 1):
                hl_in.wait_sib()
                hl_in.forward()
                ahead.send_cross()
            elif (h, i) == (1, 3):
                hl_in.wait_diag()
                S.gw2[3 * W :, :] = dot_columns(flat(S.mix), flat(S.hl4)).astype(low)
                sum_over_dp(S.gw2, S.whole2, 3 * W, W, (1, 0, 2))
        if h == 0:
            S.v[4 * R :, :] = jnp.zeros((K - 4 * R, H), low)
            S.kt[...] = jnp.transpose(S.v[...])
        at = slice(h * HEAD_DIM, (h + 1) * HEAD_DIM)
        S.dk[at, :] = dot(S.qt[at, :], flat(S.pool)).astype(low)
        S.dv[at, :] = dot(S.kt[at, : 4 * R], flat(S.e.at[h])).astype(low)
        tile = h * HEAD_DIM // 128 * 128
        dqt = jnp.transpose(flat(S.gup.at[:, :, tile : tile + 128]))
        left = jnp.concatenate(
            [dqt[h * HEAD_DIM - tile : (h + 1) * HEAD_DIM - tile], S.dk[at, : 4 * R], S.dv[at, : 4 * R]], 0
        )
        S.gw2[h * W : (h + 1) * W, :] = dot(left, flat(S.a1)).astype(low)
        sum_over_dp(S.gw2, S.whole2, h * W, W, (0, 1, 2))
        sums.tick(2)

    pad = jnp.zeros((R, H - W), low)
    for part, grad_t in ((1, S.dk), (2, S.dv)):
        rows = jnp.transpose(grad_t[...])
        for s in range(4):
            S.gup[s, :, part * H : part * H + W] = rows[s * R : (s + 1) * R]
            S.gup[s, :, part * H + W : (part + 1) * H] = pad

    back.finish()
    down = Reduce(links, S.part, S.pre1, S.near1, S.far1, t)

    def lead(i, carry):
        s = flipped(t, 1 - i // 2, 1 - i % 2)
        out = dot_rows(S.gup[s, :, 0:W], S.wqkv[0])
        out += dot_rows(S.gup[s, :, H : H + W], S.wqkv[1])
        out += dot_rows(S.gup[s, :, 2 * H : 2 * H + W], S.wqkv[2])
        S.part[s] = out.astype(low)

        @pl.when(i == 0)
        def _():
            down.send_diag()

        @pl.when(i == 2)
        def _():
            down.send_sib()

        return carry

    lax.fori_loop(0, 4, lead, 0)
    down.send_cross()
    S.small[7:8, 0:H] = jnp.sum(flat(S.gup.at[:, :, 0:H]).astype(wide), 0, keepdims=True)
    S.small[7:8, H : 2 * H] = jnp.sum(
        flat(S.gup.at[:, :, 2 * H : 3 * H]).astype(wide), 0, keepdims=True
    )
    result = S.hid[...] + (ahead.result() + vector(S.db))
    S.output[...] = result[:own].astype(low)
    sums.tick(4)

    unit, inverse = standardize(S.xf[...])
    grad = down.result()
    S.small[0:1, :] = jnp.sum(grad * unit, 0, keepdims=True)
    S.small[1:2, :] = jnp.sum(grad, 0, keepdims=True)
    S.small4[t] = S.small[...]
    base3 = links.take(3)
    for j in range(3):
        peer = lax.rem(t + j + 1, 4)
        links.start(S.small4.at[t], S.small4.at[t], base3 + j, tensor=peer)
    total = S.gh[...] + norm_back(grad, unit, inverse, vector(S.g1))
    S.gt[...] = total[:own]
    for j in range(3):
        peer = lax.rem(t + 3 - j, 4)
        links.arrived(S.small4.at[peer], base3 + j, tensor=peer)
    over = S.small4[0] + S.small4[1] + S.small4[2] + S.small4[3]
    row = lax.broadcasted_iota(jnp.int32, over.shape, 0)
    S.smalls[d] = jnp.where(row < 6, over, S.small[...])
    base4 = links.take(n.dp)

    def tell(j, carry):
        links.copy(S.smalls.at[d], S.smalls.at[d], base4 + j, dp=lax.rem(d + j, n.dp)).start()
        return carry

    lax.fori_loop(1, n.dp, tell, 0)
    sums.finish()

    def hear(j, carry):
        peer = lax.rem(d + n.dp - j, n.dp)
        links.arrived(S.smalls.at[peer], base4 + j, dp=peer)
        return carry

    lax.fori_loop(1, n.dp, hear, 0)
    S.small_sum[...] = lax.fori_loop(
        1, n.dp, lambda j, acc: acc + S.smalls[j], S.smalls[0]
    )

    def done(j, carry):
        links.copy(S.smalls.at[d], S.smalls.at[d], base4 + j, dp=lax.rem(d + j, n.dp)).wait_send()
        return carry

    lax.fori_loop(1, n.dp, done, 0)
    for i in range(3):
        s = flipped(t, 1 - i // 2, (i + i // 2) % 2)
        links.copy(S.mix.at[s], S.mix4.at[t], mix_base + i, tensor=s).wait_send()
        links.copy(S.mix4.at[s], S.gm4.at[t], gm_base + i, tensor=s).wait_send()
    for transfer in (rows_in, cot_in, ow_in, hl_in, ahead, down):
        transfer.finish()
    links.finish()


def body(
    tokens,
    lengths,
    ln1_gain,
    ln1_shift,
    qkv_weight,
    qv_bias,
    out_weight,
    out_bias,
    ln2_gain,
    ln2_shift,
    up_weight,
    up_bias,
    down_weight,
    down_bias,
    cotangent,
):
    own, D = tokens.shape
    W = qkv_weight.shape[2]
    F = up_weight.shape[1]
    dp = lax.axis_size("dp")
    assert lax.axis_size("tensor") == 4 and lengths.shape[0] == 1 and F == D and 4 * W == D and 3 * round_up(W + 2, 128) == D
    R = round_up(own, 16)
    H = round_up(W + 2, 128)
    K = round_up(4 * R, 256)
    heads = W // HEAD_DIM
    extra = dp.bit_length() - 1 - 3
    n = types.SimpleNamespace(
        own=own, D=D, W=W, R=R, H=H, K=K, dp=dp, heads=heads, extra=extra
    )
    given = dict(
        x=tokens, lengths=lengths, g1=ln1_gain, b1=ln1_shift,
        wqkv=jnp.transpose(qkv_weight, (1, 0, 2)), bq=qv_bias, ow=out_weight, ob=out_bias,
        g2=ln2_gain, b2=ln2_shift, wup=up_weight, bup=up_bias, wdn=down_weight, db=down_bias,
        cot=cotangent,
    )
    outs = dict(
        output=((own, D), low), gt=((own, D), wide), small_sum=((8, D), wide),
        whole1=((2 * D, D), low), whole2=((D, D), low),
    )
    rows4 = ((4, R, D), low)
    slab = ((R, D), low)
    chunks = [D // 2] * 4 + [W] * 4
    scratch = dict(
        a1=rows4, cot4=rows4, ow4=((4, W, D), low), q=((4, R, H), low), k=((K, H), low),
        v=((K, H), low), kt=((H, K), low), vt=((H, K), low), e=((heads, 4, R, K), low),
        o=((4, R, H), wide), inv=((4, R, H), wide), mix=((4, R, W), low), mix4=((4, R, W), low),
        xf=((R, D), wide), hid=((R, D), wide),
        a24=rows4, pool=((4, R, K), low), gup=rows4, part=rows4,
        fop=rows4, pre1=slab, near1=slab, far1=slab, pre2=slab, near2=slab, far2=slab,
        gw=((2 * D, D), low), gub=((1, D), wide),
        small=((8, D), wide), gh=((R, D), wide), hl4=rows4,
        gm4=((4, R, W), low), dk=((W, K), low), dv=((W, K), low), qt=((H, 4 * R), low), do=((R, H), wide),
        gw2=((D, D), low),
        small4=((4, 8, D), wide), smalls=((dp, 8, D), wide),
        box=((sum(DataReduce.sizes(r, D, dp)[1] for r in chunks), D), low),
        share=((sum(DataReduce.sizes(r, D, dp)[0][2][0] for r in chunks), D), low),
    )
    sems = 140 + dp + 8 * extra
    names = list(given) + list(outs) + list(scratch) + ["send", "recv"]
    vmem = pl.BlockSpec(memory_space=pltpu.VMEM)
    smem = pl.BlockSpec(memory_space=pltpu.SMEM)
    hbm = pl.BlockSpec(memory_space=pl.ANY)
    output, gt, small, whole1, whole2 = pl.pallas_call(
        lambda *refs: kernel(n, types.SimpleNamespace(**dict(zip(names, refs)))),
        out_shape=tuple(jax.ShapeDtypeStruct(*spec) for spec in outs.values()),
        in_specs=[smem if name == "lengths" else vmem for name in given],
        out_specs=tuple(hbm if name in ("whole1", "whole2") else vmem for name in outs),
        scratch_shapes=[pltpu.VMEM(*spec) for spec in scratch.values()]
        + [pltpu.SemaphoreType.DMA((sems,))] * 2,
        compiler_params=pltpu.CompilerParams(
            collective_id=0, has_side_effects=True, vmem_limit_bytes=VMEM_BYTES
        ),
    )(*given.values())
    parts = whole2[: 3 * W].astype(wide).reshape(heads, 3, HEAD_DIM, D)
    grad_qkv = jnp.transpose(parts, (3, 1, 0, 2)).reshape(D, 3, W)
    return (
        output,
        gt,
        small[0],
        small[1],
        grad_qkv,
        jnp.stack([small[7, :W], small[7, H : H + W]]),
        whole2[3 * W :].astype(wide),
        small[4],
        small[2],
        small[3],
        whole1[:D].astype(wide),
        small[6],
        whole1[D:].astype(wide),
        small[5],
    )


def solution(mesh):
    placed = (
        P(("dp", "tensor"), None),
        P("dp"),
        P(),
        P(),
        P(None, None, "tensor"),
        P(None, "tensor"),
        P("tensor", None),
        P(),
        P(),
        P(),
        P(None, "tensor"),
        P("tensor"),
        P("tensor", None),
        P(),
        P(("dp", "tensor"), None),
    )
    return jax.shard_map(
        body,
        mesh=mesh,
        in_specs=placed,
        out_specs=(
            P(("dp", "tensor"), None),
            P(("dp", "tensor"), None),
            P(),
            P(),
            P(None, None, "tensor"),
            P(None, "tensor"),
            P("tensor", None),
            P(),
            P(),
            P(),
            P(None, "tensor"),
            P("tensor"),
            P("tensor", None),
            P(),
        ),
        check_vma=False,
    )
```

```python
import types

import jax
import jax.numpy as jnp
from jax import lax
from jax.experimental import pallas as pl
from jax.experimental.pallas import tpu as pltpu
from jax.sharding import PartitionSpec as P

HEAD_DIM = 64
MESH = pl.DeviceIdType.MESH
VMEM_BYTES = 62 * 2**20

epsilon = 1e-06
low = jnp.bfloat16
wide = jnp.float32


def round_up(amount, unit):
    return -(-amount // unit) * unit


def flipped(t, flip_chip, flip_core):
    return (t // 2 + flip_chip) % 2 * 2 + (t % 2 + flip_core) % 2


def dot(left, right):
    return jnp.dot(left, right, preferred_element_type=wide)


def dot_rows(left, right):
    return lax.dot_general(left, right, (((1,), (1,)), ((), ())), preferred_element_type=wide)


def dot_columns(left, right):
    return lax.dot_general(left, right, (((0,), (0,)), ((), ())), preferred_element_type=wide)


def standardize(values):
    center = values - jnp.mean(values, -1, keepdims=True)
    inverse = lax.rsqrt(jnp.mean(center * center, -1, keepdims=True) + epsilon)
    return center * inverse, inverse


def norm_back(grad, unit, inverse, gain):
    scaled = grad * gain
    return inverse * (
        scaled
        - jnp.mean(scaled, -1, keepdims=True)
        - unit * jnp.mean(scaled * unit, -1, keepdims=True)
    )


def flat(ref):
    a, b, c = ref.shape
    return ref[...].reshape(a * b, c)


class Links:
    def __init__(self, send, recv):
        self.send, self.recv, self.used, self.pending = send, recv, 0, []

    def take(self, amount=1):
        base = self.used
        self.used += amount
        assert self.used <= self.send.shape[0]
        return base

    def copy(self, src, dst, at, **where):
        return pltpu.make_async_remote_copy(
            src_ref=src,
            dst_ref=dst,
            send_sem=self.send.at[at],
            recv_sem=self.recv.at[at],
            device_id=where,
            device_id_type=MESH,
        )

    def start(self, src, dst, at, **where):
        copy = self.copy(src, dst, at, **where)
        copy.start()
        self.pending.append(copy)

    def arrived(self, dst, at, **where):
        self.copy(dst, dst, at, **where).wait_recv()

    def finish(self):
        for copy in self.pending:
            copy.wait_send()
        self.pending = []


class Gather:
    def __init__(self, links, buf, t, parts):
        self.links, self.buf, self.t, self.parts = links, buf, t, parts
        self.sib, self.cross, self.diag = flipped(t, 0, 1), flipped(t, 1, 0), flipped(t, 1, 1)
        self.base = links.take(3 * len(parts))

    def view(self, slot, part):
        start, size = self.parts[part]
        return self.buf.at[slot, pl.ds(start, size)]

    def _each(self):
        return range(len(self.parts))

    def start(self):
        for p in self._each():
            v = self.view(self.t, p)
            self.links.copy(v, v, self.base + 3 * p, tensor=self.cross).start()
        for p in self._each():
            v = self.view(self.t, p)
            self.links.copy(v, v, self.base + 3 * p + 1, tensor=self.sib).start()

    def wait_sib(self):
        for p in self._each():
            self.links.arrived(self.view(self.sib, p), self.base + 3 * p + 1, tensor=self.sib)

    def forward(self):
        for p in self._each():
            v = self.view(self.cross, p)
            self.links.arrived(v, self.base + 3 * p, tensor=self.cross)
            self.links.copy(v, v, self.base + 3 * p + 2, tensor=self.sib).start()

    def wait_diag(self):
        for p in self._each():
            self.links.arrived(self.view(self.diag, p), self.base + 3 * p + 2, tensor=self.sib)

    def finish(self):
        for p in self._each():
            v = self.view(self.t, p)
            self.links.copy(v, v, self.base + 3 * p, tensor=self.cross).wait_send()
            self.links.copy(v, v, self.base + 3 * p + 1, tensor=self.sib).wait_send()
            v = self.view(self.cross, p)
            self.links.copy(v, v, self.base + 3 * p + 2, tensor=self.sib).wait_send()


class Reduce:
    def __init__(self, links, part, pre, near, far, t):
        self.links, self.part, self.pre, self.near, self.far, self.t = links, part, pre, near, far, t
        self.sib, self.cross, self.diag = flipped(t, 0, 1), flipped(t, 1, 0), flipped(t, 1, 1)
        self.base = links.take(3)

    def send_diag(self):
        self.links.copy(self.part.at[self.diag], self.pre, self.base, tensor=self.sib).start()

    def send_sib(self):
        self.links.copy(self.part.at[self.sib], self.near, self.base + 1, tensor=self.sib).start()

    def send_cross(self):
        self.links.arrived(self.pre, self.base, tensor=self.sib)
        total = self.part[self.cross].astype(wide) + self.pre[...].astype(wide)
        self.part[self.cross] = total.astype(low)
        self.links.copy(self.part.at[self.cross], self.far, self.base + 2, tensor=self.cross).start()

    def result(self):
        self.links.arrived(self.near, self.base + 1, tensor=self.sib)
        self.links.arrived(self.far, self.base + 2, tensor=self.cross)
        return (
            self.part[self.t].astype(wide) + self.near[...].astype(wide) + self.far[...].astype(wide)
        )

    def finish(self):
        self.links.copy(self.part.at[self.diag], self.pre, self.base, tensor=self.sib).wait_send()
        self.links.copy(self.part.at[self.sib], self.near, self.base + 1, tensor=self.sib).wait_send()
        self.links.copy(self.part.at[self.cross], self.far, self.base + 2, tensor=self.cross).wait_send()


class DataReduce:
    def __init__(self, links, held, whole, share, box, box_at, first, rows, d, count, order):
        self.links, self.held, self.whole = links, held, whole
        bits = count.bit_length() - 1
        assert count == 1 << bits and bits >= 3
        self.extra = [b for b in range(bits) if b not in order]
        self.d, self.order = d, order
        self.region = (first, rows, 0, held.shape[1])
        self.trail, self.sent, self.boxes = [], [], []
        for tall, broad in self.sizes(rows, held.shape[1], count)[0]:
            self.boxes.append(box.at[pl.ds(box_at, tall), pl.ds(0, broad)])
            box_at += tall
        self.share = share.at[pl.ds(0, tall), pl.ds(0, broad)]
        self.base = links.take(7 + len(self.extra))
        self.steps = [lambda: self._send_half(0)]
        for k in (1, 2):
            self.steps.append(lambda k=k: (self._add_half(k - 1), self._send_half(k)))
        self.steps.append(lambda: (self._add_half(2), self._swap(), self._place(), self._grow_send(2)))
        for k in (2, 1):
            self.steps.append(lambda k=k: (self._grow_wait(k), self._grow_send(k - 1)))
        self.steps.append(lambda: self._grow_wait(0))

    @staticmethod
    def sizes(rows, columns, count):
        found = []
        for _ in range(3):
            if rows % 32 == 0:
                rows //= 2
            else:
                columns //= 2
            found.append((rows, columns))
        found += found[2:] * (count.bit_length() - 1 - 3)
        return found, sum(size[0] for size in found)

    def _bit(self, b):
        return self.d // (1 << b) % 2

    def _peer(self, b):
        return self.d + (1 - 2 * self._bit(b)) * (1 << b)

    def _start(self, copy):
        copy.start()
        self.sent.append(copy)

    @staticmethod
    def _view(ref, region):
        row, rows, column, columns = region
        if columns == ref.shape[1]:
            return ref.at[pl.ds(row, rows)]
        return ref.at[pl.ds(row, rows), pl.ds(column, columns)]

    @staticmethod
    def _part(region, bit):
        row, rows, column, columns = region
        if rows % 32 == 0:
            return (pl.multiple_of(row + bit * (rows // 2), 16), rows // 2, column, columns)
        return (row, rows, pl.multiple_of(column + bit * (columns // 2), 128), columns // 2)

    def _send_half(self, k):
        b = self.order[k]
        bit = self._bit(b)
        self.trail.append(self.region)
        view = self._view(self.held, self._part(self.region, 1 - bit))
        self._start(self.links.copy(view, self.boxes[k], self.base + k, dp=self._peer(b)))
        self.region = self._part(self.region, bit)

    def _add_half(self, k):
        self.links.arrived(self.boxes[k], self.base + k, dp=self._peer(self.order[k]))
        view = self._view(self.held, self.region)
        total = (view[...].astype(wide) + self.boxes[k][...].astype(wide)).astype(low)
        if k == 2:
            self.share[...] = total
        else:
            view[...] = total

    def _swap(self):
        for k, b in enumerate(self.extra):
            box, at = self.boxes[3 + k], self.base + 7 + k
            copy = self.links.copy(self.share, box, at, dp=self._peer(b))
            copy.start()
            self.links.arrived(box, at, dp=self._peer(b))
            copy.wait_send()
            self.share[...] = (self.share[...].astype(wide) + box[...].astype(wide)).astype(low)

    def _place(self):
        self.placed = pltpu.make_async_copy(
            self.share, self._view(self.whole, self.region), self.links.send.at[self.base + 6]
        )
        self.placed.start()

    def _grow_send(self, k):
        view = self._view(self.whole, self.region)
        src = self.share if k == 2 else view
        self._start(self.links.copy(src, view, self.base + 3 + k, dp=self._peer(self.order[k])))

    def _grow_wait(self, k):
        if k == 2:
            self.placed.wait()
        b = self.order[k]
        view = self._view(self.whole, self._part(self.trail[k], 1 - self._bit(b)))
        self.links.arrived(view, self.base + 3 + k, dp=self._peer(b))
        self.region = self.trail[k]

    def step(self):
        if self.steps:
            self.steps.pop(0)()

    def finish(self):
        assert not self.steps
        for copy in self.sent:
            copy.wait_send()


class Pipeline:
    def __init__(self):
        self.members, self.queue = [], []

    def add(self, member):
        self.members.append(member)
        member.step()
        self.queue.append(member)

    def tick(self, amount=1):
        for _ in range(min(amount, sum(len(m.steps) for m in self.queue))):
            member = self.queue.pop(0)
            member.step()
            if member.steps:
                self.queue.append(member)

    def finish(self):
        while self.queue:
            self.tick()
        for m in self.members:
            m.finish()


def greet(axis, me, count):
    barrier = pltpu.get_barrier_semaphore()

    def one(j, carry):
        pl.semaphore_signal(
            barrier, inc=1, device_id={axis: lax.rem(me + j, count)}, device_id_type=MESH
        )
        return carry

    lax.fori_loop(1, count, one, 0)


def await_greetings(amount):
    pl.semaphore_wait(pltpu.get_barrier_semaphore(), amount)


def halves(rows):
    first = round_up(rows // 2, 16)
    return ((0, first), (first, rows - first))


def head_masks(shape, local_heads):
    lane = lax.broadcasted_iota(jnp.int32, shape, 1)
    return [
        jnp.where((lane >= h * HEAD_DIM) & (lane < (h + 1) * HEAD_DIM), 1.0, 0.0)
        for h in range(local_heads)
    ], lane


def kernel(n, S):
    links = Links(S.send, S.recv)
    t = lax.axis_index("tensor")
    d = lax.axis_index("dp")
    greet("tensor", t, 4)
    greet("dp", d, n.dp)
    R, own, W, H, D, K = n.R, n.own, n.W, n.H, n.D, n.K
    vector = lambda ref: ref[...].reshape(1, D)

    S.xf[...] = jnp.zeros_like(S.xf)
    S.xf[0:own, :] = S.x[...].astype(wide)
    unit, _ = standardize(S.xf[...])
    S.a1[t] = (unit * vector(S.g1) + vector(S.b1)).astype(low)
    S.cot4[t] = jnp.zeros((R, D), low)
    S.cot4[t, 0:own, :] = S.cot[...].astype(low)
    S.ow4[t] = S.ow[...]
    await_greetings(3 + n.dp - 1)
    rows_in = Gather(links, S.a1, t, halves(R))
    cot_in = Gather(links, S.cot4, t, halves(R))
    ow_in = Gather(links, S.ow4, t, ((0, W),))
    rows_in.start()
    S.gw[0:D, :] = jnp.transpose(S.wup[...])
    S.gw[D:, :] = jnp.transpose(S.wdn[...])
    S.v[4 * R :, :] = jnp.zeros((K - 4 * R, H), low)
    length = S.lengths[0]

    def project(i, carry):
        s = flipped(t, i // 2, i % 2)

        @pl.when(i == 1)
        def _():
            rows_in.wait_sib()

        @pl.when(i == 2)
        def _():
            rows_in.forward()
            cot_in.start()
            ow_in.start()

        @pl.when(i == 3)
        def _():
            rows_in.wait_diag()

        slab = S.a1[s]
        lane = lax.broadcasted_iota(jnp.int32, (R, H - W), 1)
        row = lax.broadcasted_iota(jnp.int32, (R, H - W), 0)
        absent = (row >= own) | (row + s * own >= length)
        at = pl.ds(pl.multiple_of(s * R, 16), R)
        out = dot(slab, S.wqkv[0]) + S.bq[0:1, :]
        S.q[s, :, :W] = (out.astype(low).astype(wide) * HEAD_DIM**-0.5).astype(low)
        S.q[s, :, W:] = jnp.where(lane == 0, HEAD_DIM**-0.5, 0.0).astype(low)
        S.k[at, :W] = dot(slab, S.wqkv[1]).astype(low)
        S.k[at, W:] = jnp.where((lane == 0) & absent, -8e30, 0.0).astype(low)
        S.v[at, :W] = (dot(slab, S.wqkv[2]) + S.bq[1:2, :]).astype(low)
        S.v[at, W:] = jnp.where(lane < 2, 1.0, 0.0).astype(low)
        return carry

    lax.fori_loop(0, 4, project, 0)
    if K > 4 * R:
        lane = lax.broadcasted_iota(jnp.int32, (K - 4 * R, H), 1)
        S.k[4 * R :, :] = jnp.where(lane == W, -8e30, 0.0).astype(low)
    S.kt[...] = jnp.transpose(S.k[...])
    S.vt[...] = jnp.transpose(S.v[...])

    masks, lane = head_masks((1, H), n.heads)
    mix_base = links.take(3)

    def attend(i, carry):
        s = flipped(t, 1 - i // 2, (i + i // 2) % 2)
        query = S.q[s]
        mixed = jnp.zeros((R, H), wide)
        inverse = jnp.zeros((R, H), wide)

        def score(h):
            here = jnp.where(lane == W, 1.0, masks[h]).astype(low)
            return dot(query * here, S.kt[...])

        ready = score(0)
        for h in range(n.heads):
            scores = ready
            if h + 1 < n.heads:
                ready = score(h + 1)
            terms = jnp.exp(scores - jnp.max(scores, -1, keepdims=True)).astype(low)
            S.e[h, s] = terms
            part = dot(terms, S.v[...])
            scale = 1.0 / part[:, W : W + 1]
            mixed += part * (scale * masks[h])
            inverse += scale * masks[h]
        S.o[s] = mixed
        S.inv[s] = inverse
        S.mix[s] = mixed[:, :W].astype(low)

        @pl.when(i < 3)
        def _():
            links.copy(S.mix.at[s], S.mix4.at[t], mix_base + i, tensor=s).start()

        @pl.when(i == 0)
        def _():
            cot_in.wait_sib()
            ow_in.wait_sib()

        @pl.when(i == 1)
        def _():
            cot_in.forward()
            ow_in.forward()

        @pl.when(i == 2)
        def _():
            cot_in.wait_diag()
            ow_in.wait_diag()

        return carry

    lax.fori_loop(0, 4, attend, 0)
    S.mix4[t] = S.mix[t]
    for i in range(3):
        s = flipped(t, 1 - i // 2, (i + i // 2) % 2)
        links.arrived(S.mix4.at[s], mix_base + i, tensor=s)

    total = S.xf[...] + vector(S.ob)
    for j in range(4):
        total += dot(S.mix4[j], S.ow4[j])
    S.hid[...] = total
    unit, _ = standardize(total)
    S.a24[t] = (unit * vector(S.g2) + vector(S.b2)).astype(low)
    next_in = Gather(links, S.a24, t, halves(R))
    next_in.start()
    back = Reduce(links, S.part, S.pre1, S.near1, S.far1, t)
    ahead = Reduce(links, S.fop, S.pre2, S.near2, S.far2, t)
    S.gub[...] = jnp.zeros_like(S.gub)

    def feed(i, carry):
        s = flipped(t, i // 2, i % 2)

        @pl.when(i == 1)
        def _():
            next_in.wait_sib()

        @pl.when(i == 2)
        def _():
            next_in.forward()

        @pl.when(i == 3)
        def _():
            next_in.wait_diag()

        up = dot(S.a24[s], S.wup[...]) + vector(S.bup)
        square = up * up
        c = 0.7978845608028654
        bend = jnp.tanh(c * up * (1.0 + 0.044715 * square))
        half = 0.5 * (1.0 + bend)
        slope = half + 0.5 * up * (1.0 - bend * bend) * (c + (3 * 0.044715 * c) * square)
        active = (up * half).astype(low)
        S.pool[s, :, 0:D] = active
        grad = (dot(S.cot4[s], S.gw[D:, :]) * slope).astype(low)
        S.gup[s] = grad
        S.part[s] = dot(grad, S.gw[0:D, :]).astype(low)

        @pl.when(i == 1)
        def _():
            back.send_sib()

        @pl.when(i == 3)
        def _():
            back.send_diag()

        S.fop[s] = dot(active, S.wdn[...]).astype(low)

        @pl.when(i == 1)
        def _():
            ahead.send_sib()

        @pl.when(i == 3)
        def _():
            ahead.send_diag()

        S.gub[...] += jnp.sum(grad.astype(wide), 0, keepdims=True)
        return carry

    lax.fori_loop(0, 4, feed, 0)
    back.send_cross()

    sums = Pipeline()
    tile = D // 2
    box_at = share_at = 0

    def sum_over_dp(held, whole, first, rows, order):
        nonlocal box_at, share_at
        sizes, taken = DataReduce.sizes(rows, D, n.dp)
        share = S.share.at[pl.ds(share_at, sizes[2][0])]
        sums.add(DataReduce(links, held, whole, share, S.box, box_at, first, rows, d, n.dp, order))
        box_at, share_at = box_at + taken, share_at + sizes[2][0]

    for left, right, first in ((S.a24, S.gup, 0), (S.pool, S.cot4, D)):
        for j in range(2):
            columns = left[:, :, j * tile : (j + 1) * tile].reshape(4 * R, tile)
            at = first + j * tile
            S.gw[at : at + tile, :] = dot_columns(columns, flat(right)).astype(low)
            sum_over_dp(S.gw, S.whole1, at, tile, (1, 0, 2) if at == tile else (0, 1, 2))

    sums.tick(1)
    grad = back.result()
    unit, inverse = standardize(S.hid[...])
    S.small[...] = jnp.zeros_like(S.small)
    S.small[2:3, :] = jnp.sum(grad * unit, 0, keepdims=True)
    S.small[3:4, :] = jnp.sum(grad, 0, keepdims=True)
    S.gt[...] = norm_back(grad, unit, inverse, vector(S.g2))[:own] + S.cot[...]
    S.hl4[t] = jnp.zeros((R, D), low)
    S.hl4[t, 0:own, :] = S.gt[...].astype(low)
    S.small[4:5, :] = jnp.sum(S.hl4[t].astype(wide), 0, keepdims=True)
    S.small[5:6, :] = jnp.sum(S.cot4[t].astype(wide), 0, keepdims=True)
    S.small[6:7, :] = S.gub[...]
    gm_base = links.take(3)

    def share(i, carry):
        s = flipped(t, 1 - i // 2, (i + i // 2) % 2)
        S.mix4[s] = dot_rows(S.hl4[t], S.ow4[s]).astype(low)

        @pl.when(i < 3)
        def _():
            links.copy(S.mix4.at[s], S.gm4.at[t], gm_base + i, tensor=s).start()

        return carry

    lax.fori_loop(0, 4, share, 0)
    S.gm4[t] = S.mix4[t]
    hl_in = Gather(links, S.hl4, t, halves(R))
    sums.tick(1)

    next_in.finish()
    S.do[...] = jnp.zeros_like(S.do)
    S.qt[...] = jnp.transpose(flat(S.q))
    sums.tick(2)

    def prepare(i, s):
        if i > 0:
            links.arrived(S.gm4.at[s], gm_base + (3, 2, 0, 1)[i], tensor=s)
        S.do[:, :W] = S.gm4[s].astype(wide)
        scaled = (S.do[...] * S.inv[s]).astype(low)
        S.v[pl.ds(pl.multiple_of(s * R, 16), R), :] = scaled
        scaled = scaled.astype(wide)
        product = scaled * S.o[s]
        for h in range(n.heads):
            inner = -jnp.sum(product * masks[h], -1, keepdims=True)
            upper = inner.astype(low).astype(wide)
            S.a24[s, :, h * H : (h + 1) * H] = (
                scaled * masks[h]
                + jnp.where(lane == W, upper, 0.0)
                + jnp.where(lane == W + 1, inner - upper, 0.0)
            ).astype(low)

    def pull(h, slabs):
        grads = [dot(S.a24[s, :, h * H : (h + 1) * H], S.vt[...]) for s in slabs]
        for s, grad_p in zip(slabs, grads):
            grad_s = (S.e[h, s].astype(wide) * grad_p).astype(low)
            S.pool[s] = grad_s
            dq = dot(grad_s, S.k[...]) * (masks[h] * HEAD_DIM**-0.5)
            if h > 0:
                dq += S.gup[s, :, 0:H].astype(wide)
            S.gup[s, :, 0:H] = dq.astype(low)

    for h in range(n.heads):
        for i in (0, 2):
            slabs = [flipped(t, i // 2, 0), flipped(t, i // 2, 1)]
            if h == 0:
                prepare(i, slabs[0])
                prepare(i + 1, slabs[1])
            if (h, i) == (0, 2):
                hl_in.start()
            pull(h, slabs)
            sums.tick(2)
            if (h, i) == (1, 0):
                hl_in.wait_sib()
                hl_in.forward()
                ahead.send_cross()
            elif (h, i) == (1, 2):
                hl_in.wait_diag()
                S.gw2[3 * W :, :] = dot_columns(flat(S.mix), flat(S.hl4)).astype(low)
                sum_over_dp(S.gw2, S.whole2, 3 * W, W, (1, 0, 2))
        if h == 0:
            S.v[4 * R :, :] = jnp.zeros((K - 4 * R, H), low)
            S.kt[...] = jnp.transpose(S.v[...])
        at = slice(h * HEAD_DIM, (h + 1) * HEAD_DIM)
        S.dk[at, :] = dot(S.qt[at, :], flat(S.pool)).astype(low)
        S.dv[at, :] = dot(S.kt[at, : 4 * R], flat(S.e.at[h])).astype(low)
        tile = h * HEAD_DIM // 128 * 128
        dqt = jnp.transpose(flat(S.gup.at[:, :, tile : tile + 128]))
        left = jnp.concatenate(
            [dqt[h * HEAD_DIM - tile : (h + 1) * HEAD_DIM - tile], S.dk[at, : 4 * R], S.dv[at, : 4 * R]], 0
        )
        S.gw2[h * W : (h + 1) * W, :] = dot(left, flat(S.a1)).astype(low)
        sum_over_dp(S.gw2, S.whole2, h * W, W, (0, 1, 2))
        if h + 1 < n.heads:
            sums.tick(2)

    pad = jnp.zeros((R, H - W), low)
    for part, grad_t in ((1, S.dk), (2, S.dv)):
        rows = jnp.transpose(grad_t[...])
        for s in range(4):
            S.gup[s, :, part * H : part * H + W] = rows[s * R : (s + 1) * R]
            S.gup[s, :, part * H + W : (part + 1) * H] = pad

    back.finish()
    down = Reduce(links, S.part, S.pre1, S.near1, S.far1, t)

    def lead(i, carry):
        s = flipped(t, 1 - i // 2, 1 - i % 2)
        out = dot_rows(S.gup[s, :, 0:W], S.wqkv[0])
        out += dot_rows(S.gup[s, :, H : H + W], S.wqkv[1])
        out += dot_rows(S.gup[s, :, 2 * H : 2 * H + W], S.wqkv[2])
        S.part[s] = out.astype(low)

        @pl.when(i == 0)
        def _():
            down.send_diag()

        @pl.when(i == 2)
        def _():
            down.send_sib()

        return carry

    lax.fori_loop(0, 4, lead, 0)
    down.send_cross()
    sums.tick(6)
    S.small[7:8, 0:H] = jnp.sum(flat(S.gup.at[:, :, 0:H]).astype(wide), 0, keepdims=True)
    S.small[7:8, H : 2 * H] = jnp.sum(
        flat(S.gup.at[:, :, 2 * H : 3 * H]).astype(wide), 0, keepdims=True
    )
    result = S.hid[...] + (ahead.result() + vector(S.db))
    S.output[...] = result[:own].astype(low)
    sums.tick(4)

    unit, inverse = standardize(S.xf[...])
    grad = down.result()
    S.small[0:1, :] = jnp.sum(grad * unit, 0, keepdims=True)
    S.small[1:2, :] = jnp.sum(grad, 0, keepdims=True)
    S.small4[t] = S.small[...]
    base3 = links.take(3)
    for j in range(3):
        peer = lax.rem(t + j + 1, 4)
        links.start(S.small4.at[t], S.small4.at[t], base3 + j, tensor=peer)
    S.gt[...] += norm_back(grad, unit, inverse, vector(S.g1))[:own]
    for j in range(3):
        peer = lax.rem(t + 3 - j, 4)
        links.arrived(S.small4.at[peer], base3 + j, tensor=peer)
    over = S.small4[0] + S.small4[1] + S.small4[2] + S.small4[3]
    row = lax.broadcasted_iota(jnp.int32, over.shape, 0)
    S.smalls[d] = jnp.where(row < 6, over, S.small[...])
    base4 = links.take(n.dp)

    def tell(j, carry):
        links.copy(S.smalls.at[d], S.smalls.at[d], base4 + j, dp=lax.rem(d + j, n.dp)).start()
        return carry

    lax.fori_loop(1, n.dp, tell, 0)
    sums.finish()

    def hear(j, carry):
        peer = lax.rem(d + n.dp - j, n.dp)
        links.arrived(S.smalls.at[peer], base4 + j, dp=peer)
        return carry

    lax.fori_loop(1, n.dp, hear, 0)
    S.small_sum[...] = lax.fori_loop(
        1, n.dp, lambda j, acc: acc + S.smalls[j], S.smalls[0]
    )

    def done(j, carry):
        links.copy(S.smalls.at[d], S.smalls.at[d], base4 + j, dp=lax.rem(d + j, n.dp)).wait_send()
        return carry

    lax.fori_loop(1, n.dp, done, 0)
    for i in range(3):
        s = flipped(t, 1 - i // 2, (i + i // 2) % 2)
        links.copy(S.mix.at[s], S.mix4.at[t], mix_base + i, tensor=s).wait_send()
        links.copy(S.mix4.at[s], S.gm4.at[t], gm_base + i, tensor=s).wait_send()
    for transfer in (rows_in, cot_in, ow_in, hl_in, ahead, down):
        transfer.finish()
    links.finish()


def body(
    tokens,
    lengths,
    ln1_gain,
    ln1_shift,
    qkv_weight,
    qv_bias,
    out_weight,
    out_bias,
    ln2_gain,
    ln2_shift,
    up_weight,
    up_bias,
    down_weight,
    down_bias,
    cotangent,
):
    own, D = tokens.shape
    W = qkv_weight.shape[2]
    F = up_weight.shape[1]
    dp = lax.axis_size("dp")
    assert lax.axis_size("tensor") == 4 and lengths.shape[0] == 1 and F == D and 4 * W == D and 3 * round_up(W + 2, 128) == D
    R = round_up(own, 16)
    H = round_up(W + 2, 128)
    K = round_up(4 * R, 256)
    heads = W // HEAD_DIM
    extra = dp.bit_length() - 1 - 3
    n = types.SimpleNamespace(
        own=own, D=D, W=W, R=R, H=H, K=K, dp=dp, heads=heads, extra=extra
    )
    given = dict(
        x=tokens, lengths=lengths, g1=ln1_gain, b1=ln1_shift,
        wqkv=jnp.transpose(qkv_weight, (1, 0, 2)), bq=qv_bias, ow=out_weight, ob=out_bias,
        g2=ln2_gain, b2=ln2_shift, wup=up_weight, bup=up_bias, wdn=down_weight, db=down_bias,
        cot=cotangent,
    )
    outs = dict(
        output=((own, D), low), gt=((own, D), wide), small_sum=((8, D), wide),
        whole1=((2 * D, D), low), whole2=((D, D), low),
    )
    rows4 = ((4, R, D), low)
    slab = ((R, D), low)
    chunks = [D // 2] * 4 + [W] * 4
    scratch = dict(
        a1=rows4, cot4=rows4, ow4=((4, W, D), low), q=((4, R, H), low), k=((K, H), low),
        v=((K, H), low), kt=((H, K), low), vt=((H, K), low), e=((heads, 4, R, K), low),
        o=((4, R, H), wide), inv=((4, R, H), wide), mix=((4, R, W), low), mix4=((4, R, W), low),
        xf=((R, D), wide), hid=((R, D), wide),
        a24=rows4, pool=((4, R, K), low), gup=rows4, part=rows4,
        fop=rows4, pre1=slab, near1=slab, far1=slab, pre2=slab, near2=slab, far2=slab,
        gw=((2 * D, D), low), gub=((1, D), wide),
        small=((8, D), wide), hl4=rows4,
        gm4=((4, R, W), low), dk=((W, K), low), dv=((W, K), low), qt=((H, 4 * R), low), do=((R, H), wide),
        gw2=((D, D), low),
        small4=((4, 8, D), wide), smalls=((dp, 8, D), wide),
        box=((sum(DataReduce.sizes(r, D, dp)[1] for r in chunks), D), low),
        share=((sum(DataReduce.sizes(r, D, dp)[0][2][0] for r in chunks), D), low),
    )
    sems = 140 + dp + 8 * extra
    names = list(given) + list(outs) + list(scratch) + ["send", "recv"]
    vmem = pl.BlockSpec(memory_space=pltpu.VMEM)
    smem = pl.BlockSpec(memory_space=pltpu.SMEM)
    hbm = pl.BlockSpec(memory_space=pl.ANY)
    output, gt, small, whole1, whole2 = pl.pallas_call(
        lambda *refs: kernel(n, types.SimpleNamespace(**dict(zip(names, refs)))),
        out_shape=tuple(jax.ShapeDtypeStruct(*spec) for spec in outs.values()),
        in_specs=[smem if name == "lengths" else vmem for name in given],
        out_specs=tuple(hbm if name in ("whole1", "whole2") else vmem for name in outs),
        scratch_shapes=[pltpu.VMEM(*spec) for spec in scratch.values()]
        + [pltpu.SemaphoreType.DMA((sems,))] * 2,
        compiler_params=pltpu.CompilerParams(
            collective_id=0, has_side_effects=True, vmem_limit_bytes=VMEM_BYTES
        ),
    )(*given.values())
    parts = whole2[: 3 * W].astype(wide).reshape(heads, 3, HEAD_DIM, D)
    grad_qkv = jnp.transpose(parts, (3, 1, 0, 2)).reshape(D, 3, W)
    return (
        output,
        gt,
        small[0],
        small[1],
        grad_qkv,
        jnp.stack([small[7, :W], small[7, H : H + W]]),
        whole2[3 * W :].astype(wide),
        small[4],
        small[2],
        small[3],
        whole1[:D].astype(wide),
        small[6],
        whole1[D:].astype(wide),
        small[5],
    )


def solution(mesh):
    placed = (
        P(("dp", "tensor"), None),
        P("dp"),
        P(),
        P(),
        P(None, None, "tensor"),
        P(None, "tensor"),
        P("tensor", None),
        P(),
        P(),
        P(),
        P(None, "tensor"),
        P("tensor"),
        P("tensor", None),
        P(),
        P(("dp", "tensor"), None),
    )
    return jax.shard_map(
        body,
        mesh=mesh,
        in_specs=placed,
        out_specs=(
            P(("dp", "tensor"), None),
            P(("dp", "tensor"), None),
            P(),
            P(),
            P(None, None, "tensor"),
            P(None, "tensor"),
            P("tensor", None),
            P(),
            P(),
            P(),
            P(None, "tensor"),
            P("tensor"),
            P("tensor", None),
            P(),
        ),
        check_vma=False,
    )
```

```python
import types

import jax
import jax.numpy as jnp
from jax import lax
from jax.experimental import pallas as pl
from jax.experimental.pallas import tpu as pltpu
from jax.sharding import PartitionSpec as P

HEAD_DIM = 64
MESH = pl.DeviceIdType.MESH
VMEM_BYTES = 62 * 2**20

epsilon = 1e-06
low = jnp.bfloat16
wide = jnp.float32


def round_up(amount, unit):
    return -(-amount // unit) * unit


def flipped(t, flip_chip, flip_core):
    return (t // 2 + flip_chip) % 2 * 2 + (t % 2 + flip_core) % 2


def dot(left, right):
    return jnp.dot(left, right, preferred_element_type=wide)


def dot_rows(left, right):
    return lax.dot_general(left, right, (((1,), (1,)), ((), ())), preferred_element_type=wide)


def dot_columns(left, right):
    return lax.dot_general(left, right, (((0,), (0,)), ((), ())), preferred_element_type=wide)


def standardize(values):
    center = values - jnp.mean(values, -1, keepdims=True)
    inverse = lax.rsqrt(jnp.mean(center * center, -1, keepdims=True) + epsilon)
    return center * inverse, inverse


def norm_back(grad, unit, inverse, gain):
    scaled = grad * gain
    return inverse * (
        scaled
        - jnp.mean(scaled, -1, keepdims=True)
        - unit * jnp.mean(scaled * unit, -1, keepdims=True)
    )


def pair(ref, p):
    _, rows, columns = ref.shape
    return ref[pl.ds(2 * p, 2)].reshape(2 * rows, columns)


def set_pair(ref, p, values):
    ref[pl.ds(2 * p, 2)] = values.reshape(2, -1, values.shape[1])


def flat(ref):
    a, b, c = ref.shape
    return ref[...].reshape(a * b, c)


class Links:
    def __init__(self, send, recv):
        self.send, self.recv, self.used, self.pending = send, recv, 0, []

    def take(self, amount=1):
        base = self.used
        self.used += amount
        assert self.used <= self.send.shape[0]
        return base

    def copy(self, src, dst, at, **where):
        return pltpu.make_async_remote_copy(
            src_ref=src,
            dst_ref=dst,
            send_sem=self.send.at[at],
            recv_sem=self.recv.at[at],
            device_id=where,
            device_id_type=MESH,
        )

    def start(self, src, dst, at, **where):
        copy = self.copy(src, dst, at, **where)
        copy.start()
        self.pending.append(copy)

    def arrived(self, dst, at, **where):
        self.copy(dst, dst, at, **where).wait_recv()

    def finish(self):
        for copy in self.pending:
            copy.wait_send()
        self.pending = []


class Gather:
    def __init__(self, links, buf, t, parts):
        self.links, self.buf, self.t, self.parts = links, buf, t, parts
        self.sib, self.cross, self.diag = flipped(t, 0, 1), flipped(t, 1, 0), flipped(t, 1, 1)
        self.base = links.take(3 * len(parts))

    def view(self, slot, part):
        start, size = self.parts[part]
        return self.buf.at[slot, pl.ds(start, size)]

    def _each(self):
        return range(len(self.parts))

    def start(self):
        for p in self._each():
            v = self.view(self.t, p)
            self.links.copy(v, v, self.base + 3 * p, tensor=self.cross).start()
        for p in self._each():
            v = self.view(self.t, p)
            self.links.copy(v, v, self.base + 3 * p + 1, tensor=self.sib).start()

    def wait_sib(self):
        for p in self._each():
            self.links.arrived(self.view(self.sib, p), self.base + 3 * p + 1, tensor=self.sib)

    def forward(self):
        for p in self._each():
            v = self.view(self.cross, p)
            self.links.arrived(v, self.base + 3 * p, tensor=self.cross)
            self.links.copy(v, v, self.base + 3 * p + 2, tensor=self.sib).start()

    def wait_diag(self):
        for p in self._each():
            self.links.arrived(self.view(self.diag, p), self.base + 3 * p + 2, tensor=self.sib)

    def finish(self):
        for p in self._each():
            v = self.view(self.t, p)
            self.links.copy(v, v, self.base + 3 * p, tensor=self.cross).wait_send()
            self.links.copy(v, v, self.base + 3 * p + 1, tensor=self.sib).wait_send()
            v = self.view(self.cross, p)
            self.links.copy(v, v, self.base + 3 * p + 2, tensor=self.sib).wait_send()


class Reduce:
    def __init__(self, links, part, pre, near, far, t):
        self.links, self.part, self.pre, self.near, self.far, self.t = links, part, pre, near, far, t
        self.sib, self.cross, self.diag = flipped(t, 0, 1), flipped(t, 1, 0), flipped(t, 1, 1)
        self.base = links.take(3)

    def send_diag(self):
        self.links.copy(self.part.at[self.diag], self.pre, self.base, tensor=self.sib).start()

    def send_sib(self):
        self.links.copy(self.part.at[self.sib], self.near, self.base + 1, tensor=self.sib).start()

    def send_cross(self):
        self.links.arrived(self.pre, self.base, tensor=self.sib)
        total = self.part[self.cross].astype(wide) + self.pre[...].astype(wide)
        self.part[self.cross] = total.astype(low)
        self.links.copy(self.part.at[self.cross], self.far, self.base + 2, tensor=self.cross).start()

    def result(self):
        self.links.arrived(self.near, self.base + 1, tensor=self.sib)
        self.links.arrived(self.far, self.base + 2, tensor=self.cross)
        return (
            self.part[self.t].astype(wide) + self.near[...].astype(wide) + self.far[...].astype(wide)
        )

    def finish(self):
        self.links.copy(self.part.at[self.diag], self.pre, self.base, tensor=self.sib).wait_send()
        self.links.copy(self.part.at[self.sib], self.near, self.base + 1, tensor=self.sib).wait_send()
        self.links.copy(self.part.at[self.cross], self.far, self.base + 2, tensor=self.cross).wait_send()


class DataReduce:
    def __init__(self, links, held, whole, share, box, box_at, first, rows, d, count, order):
        self.links, self.held, self.whole = links, held, whole
        bits = count.bit_length() - 1
        assert count == 1 << bits and bits >= 3
        self.extra = [b for b in range(bits) if b not in order]
        self.d, self.order = d, order
        self.region = (first, rows, 0, held.shape[1])
        self.trail, self.sent, self.boxes = [], [], []
        for tall, broad in self.sizes(rows, held.shape[1], count)[0]:
            self.boxes.append(box.at[pl.ds(box_at, tall), pl.ds(0, broad)])
            box_at += tall
        self.share = share.at[pl.ds(0, tall), pl.ds(0, broad)]
        self.base = links.take(7 + len(self.extra))
        self.steps = [lambda: self._send_half(0)]
        for k in (1, 2):
            self.steps.append(lambda k=k: (self._add_half(k - 1), self._send_half(k)))
        self.steps.append(lambda: (self._add_half(2), self._swap(), self._place(), self._grow_send(2)))
        for k in (2, 1):
            self.steps.append(lambda k=k: (self._grow_wait(k), self._grow_send(k - 1)))
        self.steps.append(lambda: self._grow_wait(0))

    @staticmethod
    def sizes(rows, columns, count):
        found = []
        for _ in range(3):
            if rows % 32 == 0:
                rows //= 2
            else:
                columns //= 2
            found.append((rows, columns))
        found += found[2:] * (count.bit_length() - 1 - 3)
        return found, sum(size[0] for size in found)

    def _bit(self, b):
        return self.d // (1 << b) % 2

    def _peer(self, b):
        return self.d + (1 - 2 * self._bit(b)) * (1 << b)

    def _start(self, copy):
        copy.start()
        self.sent.append(copy)

    @staticmethod
    def _view(ref, region):
        row, rows, column, columns = region
        if columns == ref.shape[1]:
            return ref.at[pl.ds(row, rows)]
        return ref.at[pl.ds(row, rows), pl.ds(column, columns)]

    @staticmethod
    def _part(region, bit):
        row, rows, column, columns = region
        if rows % 32 == 0:
            return (pl.multiple_of(row + bit * (rows // 2), 16), rows // 2, column, columns)
        return (row, rows, pl.multiple_of(column + bit * (columns // 2), 128), columns // 2)

    def _send_half(self, k):
        b = self.order[k]
        bit = self._bit(b)
        self.trail.append(self.region)
        view = self._view(self.held, self._part(self.region, 1 - bit))
        self._start(self.links.copy(view, self.boxes[k], self.base + k, dp=self._peer(b)))
        self.region = self._part(self.region, bit)

    def _add_half(self, k):
        self.links.arrived(self.boxes[k], self.base + k, dp=self._peer(self.order[k]))
        view = self._view(self.held, self.region)
        total = (view[...].astype(wide) + self.boxes[k][...].astype(wide)).astype(low)
        if k == 2:
            self.share[...] = total
        else:
            view[...] = total

    def _swap(self):
        for k, b in enumerate(self.extra):
            box, at = self.boxes[3 + k], self.base + 7 + k
            copy = self.links.copy(self.share, box, at, dp=self._peer(b))
            copy.start()
            self.links.arrived(box, at, dp=self._peer(b))
            copy.wait_send()
            self.share[...] = (self.share[...].astype(wide) + box[...].astype(wide)).astype(low)

    def _place(self):
        self.placed = pltpu.make_async_copy(
            self.share, self._view(self.whole, self.region), self.links.send.at[self.base + 6]
        )
        self.placed.start()

    def _grow_send(self, k):
        view = self._view(self.whole, self.region)
        src = self.share if k == 2 else view
        self._start(self.links.copy(src, view, self.base + 3 + k, dp=self._peer(self.order[k])))

    def _grow_wait(self, k):
        if k == 2:
            self.placed.wait()
        b = self.order[k]
        view = self._view(self.whole, self._part(self.trail[k], 1 - self._bit(b)))
        self.links.arrived(view, self.base + 3 + k, dp=self._peer(b))
        self.region = self.trail[k]

    def step(self):
        if self.steps:
            self.steps.pop(0)()

    def finish(self):
        assert not self.steps
        for copy in self.sent:
            copy.wait_send()


class Pipeline:
    def __init__(self):
        self.members, self.queue = [], []

    def add(self, member):
        self.members.append(member)
        member.step()
        self.queue.append(member)

    def tick(self, amount=1):
        for _ in range(min(amount, sum(len(m.steps) for m in self.queue))):
            member = self.queue.pop(0)
            member.step()
            if member.steps:
                self.queue.append(member)

    def finish(self):
        while self.queue:
            self.tick()
        for m in self.members:
            m.finish()


class Everyone:
    def __init__(self, links, buf, me, count, device):
        self.links, self.buf, self.me, self.count, self.device = links, buf, me, count, device
        self.base = links.take(count)

    def _copy(self, j):
        slot = self.buf.at[self.me]
        peer = self.device(lax.rem(self.me + j, self.count))
        return self.links.copy(slot, slot, self.base + j, dp=peer)

    def _loop(self, act):
        def one(j, carry):
            act(j)
            return carry

        lax.fori_loop(1, self.count, one, 0)

    def start(self, values):
        self.buf[self.me] = values
        self._loop(lambda j: self._copy(j).start())

    def _hear(self, j):
        peer = lax.rem(self.me + self.count - j, self.count)
        self.links.arrived(self.buf.at[peer], self.base + j, dp=self.device(peer))

    def result(self):
        self._loop(self._hear)
        return lax.fori_loop(1, self.count, lambda j, acc: acc + self.buf[j], self.buf[0])

    def finish(self):
        self._loop(lambda j: self._copy(j).wait_send())


def greet(axis, me, count):
    barrier = pltpu.get_barrier_semaphore()

    def one(j, carry):
        pl.semaphore_signal(
            barrier, inc=1, device_id={axis: lax.rem(me + j, count)}, device_id_type=MESH
        )
        return carry

    lax.fori_loop(1, count, one, 0)


def await_greetings(amount):
    pl.semaphore_wait(pltpu.get_barrier_semaphore(), amount)


def halves(rows):
    first = round_up(rows // 2, 16)
    return ((0, first), (first, rows - first))


def head_masks(shape, local_heads):
    lane = lax.broadcasted_iota(jnp.int32, shape, 1)
    return [
        jnp.where((lane >= h * HEAD_DIM) & (lane < (h + 1) * HEAD_DIM), 1.0, 0.0)
        for h in range(local_heads)
    ], lane


def kernel(n, S):
    links = Links(S.send, S.recv)
    t = lax.axis_index("tensor")
    d = lax.axis_index("dp")
    greet("tensor", t, 4)
    greet("dp", d, n.dp)
    R, own, W, H, D, K = n.R, n.own, n.W, n.H, n.D, n.K
    vector = lambda ref: ref[...].reshape(1, D)

    fetch = pltpu.make_async_copy(S.cot, S.gt, S.local)
    fetch.start()
    S.a1[t] = jnp.zeros((R, D), low)
    S.cot4[t] = jnp.zeros((R, D), low)
    S.a24[t] = jnp.zeros((R, D), low)
    S.hl4[t] = jnp.zeros((R, D), low)
    unit, _ = standardize(S.x[...].astype(wide))
    S.a1[t, 0:own, :] = (unit * vector(S.g1) + vector(S.b1)).astype(low)
    fetch.wait()
    S.cot4[t, 0:own, :] = S.gt[...].astype(low)
    S.ow4[t] = S.ow[...]
    await_greetings(3 + n.dp - 1)
    rows_in = Gather(links, S.a1, t, halves(R))
    cot_in = Gather(links, S.cot4, t, halves(R))
    ow_in = Gather(links, S.ow4, t, ((0, W),))
    rows_in.start()
    S.gw[0:D, :] = jnp.transpose(S.wup[...])
    S.gw[D:, :] = jnp.transpose(S.wdn[...])
    S.v[4 * R :, :] = jnp.zeros((K - 4 * R, H), low)
    length = S.lengths[0]

    chip = t // 2

    def project(i, carry):
        p = (chip + i) % 2

        @pl.when(i == 0)
        def _():
            rows_in.wait_sib()

        @pl.when(i == 1)
        def _():
            rows_in.forward()
            cot_in.start()
            ow_in.start()
            rows_in.wait_diag()

        rows = pair(S.a1, p)
        lane = lax.broadcasted_iota(jnp.int32, (2 * R, H - W), 1)
        row = lax.broadcasted_iota(jnp.int32, (2 * R, H - W), 0)
        second = row >= R
        row = row - jnp.where(second, R, 0)
        absent = (row >= own) | (row + (2 * p + jnp.where(second, 1, 0)) * own >= length)
        at = pl.ds(pl.multiple_of(2 * p * R, 16), 2 * R)
        out = dot(rows, S.wqkv[0]) + S.bq[0:1, :]
        out = (out.astype(low).astype(wide) * HEAD_DIM**-0.5).astype(low)
        S.q[pl.ds(2 * p, 2), :, :W] = out.reshape(2, R, W)
        unmasked = jnp.where(lane == 0, HEAD_DIM**-0.5, 0.0).astype(low)
        S.q[pl.ds(2 * p, 2), :, W:] = unmasked.reshape(2, R, H - W)
        S.k[at, :W] = dot(rows, S.wqkv[1]).astype(low)
        S.k[at, W:] = jnp.where((lane == 0) & absent, -8e30, 0.0).astype(low)
        S.v[at, :W] = (dot(rows, S.wqkv[2]) + S.bq[1:2, :]).astype(low)
        S.v[at, W:] = jnp.where(lane < 2, 1.0, 0.0).astype(low)
        return carry

    lax.fori_loop(0, 2, project, 0)
    if K > 4 * R:
        lane = lax.broadcasted_iota(jnp.int32, (K - 4 * R, H), 1)
        S.k[4 * R :, :] = jnp.where(lane == W, -8e30, 0.0).astype(low)
    S.kt[...] = jnp.transpose(S.k[...])
    S.vt[...] = jnp.transpose(S.v[...])

    masks, lane = head_masks((1, H), n.heads)
    mix_base = links.take(3)

    peers = [flipped(t, 1, 0), flipped(t, 1, 1), flipped(t, 0, 1)]

    def attend(i, carry):
        p = (chip + 1 + i) % 2
        query = pair(S.q, p)
        mixed = jnp.zeros((2 * R, H), wide)
        inverse = jnp.zeros((2 * R, 128), wide)
        first = lax.broadcasted_iota(jnp.int32, (1, 128), 1)
        for h in range(n.heads):
            here = jnp.where(lane == W, 1.0, masks[h]).astype(low)
            scores = dot(query * here, S.kt[...])
            terms = jnp.exp(scores - jnp.max(scores, -1, keepdims=True)).astype(low)
            set_pair(S.e.at[h], p, terms)
            part = dot(terms, S.v[...])
            scale = 1.0 / part[:, W : W + 1]
            mixed += part * (scale * masks[h])
            inverse = jnp.where(first == h, scale, inverse)
        set_pair(S.o, p, mixed)
        set_pair(S.inv, p, inverse)
        set_pair(S.mix, p, mixed[:, :W].astype(low))

        @pl.when(i == 0)
        def _():
            for j in (0, 1):
                s = peers[j]
                links.copy(S.mix.at[s], S.mix4.at[t], mix_base + j, tensor=s).start()
            cot_in.wait_sib()
            ow_in.wait_sib()
            cot_in.forward()
            ow_in.forward()

        @pl.when(i == 1)
        def _():
            links.copy(S.mix.at[peers[2]], S.mix4.at[t], mix_base + 2, tensor=peers[2]).start()
            cot_in.wait_diag()
            ow_in.wait_diag()

        return carry

    lax.fori_loop(0, 2, attend, 0)
    S.mix4[t] = S.mix[t]
    for j, s in enumerate(peers):
        links.arrived(S.mix4.at[s], mix_base + j, tensor=s)

    total = dot(S.mix4[0], S.ow4[0])
    for j in range(1, 4):
        total += dot(S.mix4[j], S.ow4[j])
    total = S.x[...].astype(wide) + (total[:own] + vector(S.ob))
    S.hid[...] = total
    unit, _ = standardize(total)
    S.a24[t, 0:own, :] = (unit * vector(S.g2) + vector(S.b2)).astype(low)
    next_in = Gather(links, S.a24, t, halves(R))
    next_in.start()
    back = Reduce(links, S.part, S.pre1, S.near1, S.far1, t)
    ahead = Reduce(links, S.fop, S.pre2, S.near2, S.far2, t)
    S.gub[...] = jnp.zeros_like(S.gub)

    def feed(i, carry):
        p = (chip + i) % 2

        @pl.when(i == 0)
        def _():
            next_in.wait_sib()

        @pl.when(i == 1)
        def _():
            next_in.forward()
            next_in.wait_diag()

        up = dot(pair(S.a24, p), S.wup[...]) + vector(S.bup)
        square = up * up
        c = 0.7978845608028654
        bend = jnp.tanh(c * up * (1.0 + 0.044715 * square))
        half = 0.5 * (1.0 + bend)
        slope = half + 0.5 * up * (1.0 - bend * bend) * (c + (3 * 0.044715 * c) * square)
        active = (up * half).astype(low)
        S.pool[pl.ds(2 * p, 2), :, 0:D] = active.reshape(2, R, D)
        grad = (dot(pair(S.cot4, p), S.gw[D:, :]) * slope).astype(low)
        set_pair(S.gup, p, grad)
        set_pair(S.part, p, dot(grad, S.gw[0:D, :]).astype(low))

        @pl.when(i == 0)
        def _():
            back.send_sib()

        @pl.when(i == 1)
        def _():
            back.send_diag()

        set_pair(S.fop, p, dot(active, S.wdn[...]).astype(low))

        @pl.when(i == 0)
        def _():
            ahead.send_sib()

        @pl.when(i == 1)
        def _():
            ahead.send_diag()

        S.gub[...] += jnp.sum(grad.astype(wide), 0, keepdims=True)
        return carry

    lax.fori_loop(0, 2, feed, 0)
    back.send_cross()

    sums = Pipeline()
    tile = D // 2
    box_at = share_at = 0

    def sum_over_dp(held, whole, first, rows, order):
        nonlocal box_at, share_at
        sizes, taken = DataReduce.sizes(rows, D, n.dp)
        share = S.share.at[pl.ds(share_at, sizes[2][0])]
        sums.add(DataReduce(links, held, whole, share, S.box, box_at, first, rows, d, n.dp, order))
        box_at, share_at = box_at + taken, share_at + sizes[2][0]

    for left, right, first in ((S.a24, S.gup, 0), (S.pool, S.cot4, D)):
        rows = left[:, :, 0:D].reshape(4 * R, D)
        S.gw[first : first + D, :] = dot_columns(rows, flat(right)).astype(low)
        for at in (first, first + tile):
            sum_over_dp(S.gw, S.whole1, at, tile, (1, 0, 2) if at == tile else (0, 1, 2))

    sums.tick(1)
    grad = back.result()[:own]
    unit, inverse = standardize(S.hid[...])
    S.small[...] = jnp.zeros_like(S.small)
    S.small[2:3, :] = jnp.sum(grad * unit, 0, keepdims=True)
    S.small[3:4, :] = jnp.sum(grad, 0, keepdims=True)
    S.gt[...] += norm_back(grad, unit, inverse, vector(S.g2))
    S.hl4[t, 0:own, :] = S.gt[...].astype(low)
    S.small[4:5, :] = jnp.sum(S.hl4[t].astype(wide), 0, keepdims=True)
    S.small[5:6, :] = jnp.sum(S.cot4[t].astype(wide), 0, keepdims=True)
    S.small[6:7, :] = S.gub[...]
    gm_base = links.take(3)

    for j, s in enumerate(peers + [t]):
        S.mix4[s] = dot_rows(S.hl4[t], S.ow4[s]).astype(low)
        if j < 3:
            links.copy(S.mix4.at[s], S.gm4.at[t], gm_base + j, tensor=s).start()
    S.gm4[t] = S.mix4[t]
    hl_in = Gather(links, S.hl4, t, halves(R))
    sums.tick(1)

    next_in.finish()
    S.do[...] = jnp.zeros_like(S.do)
    S.qt[...] = jnp.transpose(flat(S.q))
    sums.tick(2)

    def prepare(i, s):
        if i > 0:
            j = (None, 2, 0, 1)[i]
            links.arrived(S.gm4.at[s], gm_base + j, tensor=peers[j])
        S.do[:, :W] = S.gm4[s].astype(wide)
        inverse = sum(S.inv[s, :, h : h + 1] * masks[h] for h in range(n.heads))
        scaled = (S.do[...] * inverse).astype(low)
        S.v[pl.ds(pl.multiple_of(s * R, 16), R), :] = scaled
        scaled = scaled.astype(wide)
        product = scaled * S.o[s]
        for h in range(n.heads):
            inner = -jnp.sum(product * masks[h], -1, keepdims=True)
            upper = inner.astype(low).astype(wide)
            S.a24[s, :, h * H : (h + 1) * H] = (
                scaled * masks[h]
                + jnp.where(lane == W, upper, 0.0)
                + jnp.where(lane == W + 1, inner - upper, 0.0)
            ).astype(low)

    def pull(h, p):
        grad_p = dot(pair(S.a24.at[:, :, h * H : (h + 1) * H], p), S.vt[...])
        grad_s = (pair(S.e.at[h], p).astype(wide) * grad_p).astype(low)
        set_pair(S.pool, p, grad_s)
        dq = dot(grad_s, S.k[...]) * (masks[h] * HEAD_DIM**-0.5)
        if h > 0:
            dq += pair(S.gup.at[:, :, 0:H], p).astype(wide)
        S.gup[pl.ds(2 * p, 2), :, 0:H] = dq.astype(low).reshape(2, R, H)

    for h in range(n.heads):
        for i in (0, 2):
            if h == 0:
                prepare(i, flipped(t, i // 2, 0))
                prepare(i + 1, flipped(t, i // 2, 1))
            if (h, i) == (0, 2):
                hl_in.start()
            pull(h, (chip + i // 2) % 2)
            sums.tick(2)
            if (h, i) == (1, 0):
                hl_in.wait_sib()
                hl_in.forward()
                ahead.send_cross()
            elif (h, i) == (1, 2):
                hl_in.wait_diag()
                S.gw2[3 * W :, :] = dot_columns(flat(S.mix), flat(S.hl4)).astype(low)
                sum_over_dp(S.gw2, S.whole2, 3 * W, W, (1, 0, 2))
        if h == 0:
            S.v[4 * R :, :] = jnp.zeros((K - 4 * R, H), low)
            S.kt[...] = jnp.transpose(S.v[...])
        at = slice(h * HEAD_DIM, (h + 1) * HEAD_DIM)
        S.dk[at, :] = dot(S.qt[at, :], flat(S.pool)).astype(low)
        S.dv[at, :] = dot(S.kt[at, : 4 * R], flat(S.e.at[h])).astype(low)
        tile = h * HEAD_DIM // 128 * 128
        dqt = jnp.transpose(flat(S.gup.at[:, :, tile : tile + 128]))
        left = jnp.concatenate(
            [dqt[h * HEAD_DIM - tile : (h + 1) * HEAD_DIM - tile], S.dk[at, : 4 * R], S.dv[at, : 4 * R]], 0
        )
        S.gw2[h * W : (h + 1) * W, :] = dot(left, flat(S.a1)).astype(low)
        sum_over_dp(S.gw2, S.whole2, h * W, W, (0, 1, 2))
        if h + 1 < n.heads:
            sums.tick(2)

    pad = jnp.zeros((R, H - W), low)
    for part, grad_t in ((1, S.dk), (2, S.dv)):
        rows = jnp.transpose(grad_t[...])
        for s in range(4):
            S.gup[s, :, part * H : part * H + W] = rows[s * R : (s + 1) * R]
            S.gup[s, :, part * H + W : (part + 1) * H] = pad

    back.finish()
    down = Reduce(links, S.part, S.pre1, S.near1, S.far1, t)

    def lead(i, carry):
        p = (chip + 1 + i) % 2
        rows = pair(S.gup, p)
        out = dot_rows(rows[:, 0:W], S.wqkv[0])
        out += dot_rows(rows[:, H : H + W], S.wqkv[1])
        out += dot_rows(rows[:, 2 * H : 2 * H + W], S.wqkv[2])
        set_pair(S.part, p, out.astype(low))

        @pl.when(i == 0)
        def _():
            down.send_diag()

        @pl.when(i == 1)
        def _():
            down.send_sib()

        return carry

    lax.fori_loop(0, 2, lead, 0)
    down.send_cross()
    sums.tick(6)
    S.small[7:8, 0:H] = jnp.sum(flat(S.gup.at[:, :, 0:H]).astype(wide), 0, keepdims=True)
    S.small[7:8, H : 2 * H] = jnp.sum(
        flat(S.gup.at[:, :, 2 * H : 3 * H]).astype(wide), 0, keepdims=True
    )
    S.output[...] = (S.hid[...] + (ahead.result()[:own] + vector(S.db))).astype(low)
    sums.tick(4)

    unit, inverse = standardize(S.x[...].astype(wide))
    grad = down.result()[:own]
    S.small[0:1, :] = jnp.sum(grad * unit, 0, keepdims=True)
    S.small[1:2, :] = jnp.sum(grad, 0, keepdims=True)
    S.small4[t] = S.small[...]
    base3 = links.take(3)
    for j in range(3):
        peer = lax.rem(t + j + 1, 4)
        links.start(S.small4.at[t], S.small4.at[t], base3 + j, tensor=peer)
    S.gt[...] += norm_back(grad, unit, inverse, vector(S.g1))
    for j in range(3):
        peer = lax.rem(t + 3 - j, 4)
        links.arrived(S.small4.at[peer], base3 + j, tensor=peer)
    over = S.small4[0] + S.small4[1] + S.small4[2] + S.small4[3]
    row = lax.broadcasted_iota(jnp.int32, over.shape, 0)
    near = min(8, n.dp)
    inner = Everyone(links, S.smalls, d % near, near, lambda j: d // near * near + j)
    inner.start(jnp.where(row < 6, over, S.small[...]))
    sums.finish()
    total = inner.result()
    inner.finish()
    if n.dp > near:
        outer = Everyone(links, S.smalls2, d // near, n.dp // near, lambda j: j * near + d % near)
        outer.start(total)
        total = outer.result()
        outer.finish()
    S.small_sum[...] = total
    for j, s in enumerate(peers):
        links.copy(S.mix.at[s], S.mix4.at[t], mix_base + j, tensor=s).wait_send()
        links.copy(S.mix4.at[s], S.gm4.at[t], gm_base + j, tensor=s).wait_send()
    for transfer in (rows_in, cot_in, ow_in, hl_in, ahead, down):
        transfer.finish()
    links.finish()


def body(
    tokens,
    lengths,
    ln1_gain,
    ln1_shift,
    qkv_weight,
    qv_bias,
    out_weight,
    out_bias,
    ln2_gain,
    ln2_shift,
    up_weight,
    up_bias,
    down_weight,
    down_bias,
    cotangent,
):
    own, D = tokens.shape
    W = qkv_weight.shape[2]
    F = up_weight.shape[1]
    dp = lax.axis_size("dp")
    assert lax.axis_size("tensor") == 4 and lengths.shape[0] == 1 and F == D and 4 * W == D and 3 * round_up(W + 2, 128) == D
    R = round_up(own, 16)
    H = round_up(W + 2, 128)
    K = round_up(4 * R, 256)
    heads = W // HEAD_DIM
    extra = dp.bit_length() - 1 - 3
    n = types.SimpleNamespace(
        own=own, D=D, W=W, R=R, H=H, K=K, dp=dp, heads=heads, extra=extra
    )
    given = dict(
        x=tokens, lengths=lengths, g1=ln1_gain, b1=ln1_shift,
        wqkv=jnp.transpose(qkv_weight, (1, 0, 2)), bq=qv_bias, ow=out_weight, ob=out_bias,
        g2=ln2_gain, b2=ln2_shift, wup=up_weight, bup=up_bias, wdn=down_weight, db=down_bias,
        cot=cotangent,
    )
    outs = dict(
        output=((own, D), low), gt=((own, D), wide), small_sum=((8, D), wide),
        whole1=((2 * D, D), low), whole2=((D, D), low),
    )
    rows4 = ((4, R, D), low)
    slab = ((R, D), low)
    chunks = [D // 2] * 4 + [W] * 4
    scratch = dict(
        a1=rows4, cot4=rows4, ow4=((4, W, D), low), q=((4, R, H), low), k=((K, H), low),
        v=((K, H), low), kt=((H, K), low), vt=((H, K), low), e=((heads, 4, R, K), low),
        o=((4, R, H), wide), inv=((4, R, 128), wide), mix=((4, R, W), low), mix4=((4, R, W), low),
        hid=((own, D), wide),
        a24=rows4, pool=((4, R, K), low), gup=rows4, part=rows4,
        fop=rows4, pre1=slab, near1=slab, far1=slab, pre2=slab, near2=slab, far2=slab,
        gw=((2 * D, D), low), gub=((1, D), wide),
        small=((8, D), wide), hl4=rows4,
        gm4=((4, R, W), low), dk=((W, K), low), dv=((W, K), low), qt=((H, 4 * R), low), do=((R, H), wide),
        gw2=((D, D), low),
        small4=((4, 8, D), wide), smalls=((min(8, dp), 8, D), wide),
        box=((sum(DataReduce.sizes(r, D, dp)[1] for r in chunks), D), low),
        share=((sum(DataReduce.sizes(r, D, dp)[0][2][0] for r in chunks), D), low),
    )
    if dp > 8:
        scratch["smalls2"] = ((dp // 8, 8, D), wide)
    sems = 140 + dp + 8 * extra
    names = list(given) + list(outs) + list(scratch) + ["local", "send", "recv"]
    vmem = pl.BlockSpec(memory_space=pltpu.VMEM)
    smem = pl.BlockSpec(memory_space=pltpu.SMEM)
    hbm = pl.BlockSpec(memory_space=pl.ANY)
    output, gt, small, whole1, whole2 = pl.pallas_call(
        lambda *refs: kernel(n, types.SimpleNamespace(**dict(zip(names, refs)))),
        out_shape=tuple(jax.ShapeDtypeStruct(*spec) for spec in outs.values()),
        in_specs=[dict(lengths=smem, cot=hbm).get(name, vmem) for name in given],
        out_specs=tuple(hbm if name in ("whole1", "whole2") else vmem for name in outs),
        scratch_shapes=[pltpu.VMEM(*spec) for spec in scratch.values()]
        + [pltpu.SemaphoreType.DMA] + [pltpu.SemaphoreType.DMA((sems,))] * 2,
        compiler_params=pltpu.CompilerParams(
            collective_id=0, has_side_effects=True, vmem_limit_bytes=VMEM_BYTES
        ),
    )(*given.values())
    parts = whole2[: 3 * W].astype(wide).reshape(heads, 3, HEAD_DIM, D)
    grad_qkv = jnp.transpose(parts, (3, 1, 0, 2)).reshape(D, 3, W)
    return (
        output,
        gt,
        small[0],
        small[1],
        grad_qkv,
        jnp.stack([small[7, :W], small[7, H : H + W]]),
        whole2[3 * W :].astype(wide),
        small[4],
        small[2],
        small[3],
        whole1[:D].astype(wide),
        small[6],
        whole1[D:].astype(wide),
        small[5],
    )


def solution(mesh):
    placed = (
        P(("dp", "tensor"), None),
        P("dp"),
        P(),
        P(),
        P(None, None, "tensor"),
        P(None, "tensor"),
        P("tensor", None),
        P(),
        P(),
        P(),
        P(None, "tensor"),
        P("tensor"),
        P("tensor", None),
        P(),
        P(("dp", "tensor"), None),
    )
    return jax.shard_map(
        body,
        mesh=mesh,
        in_specs=placed,
        out_specs=(
            P(("dp", "tensor"), None),
            P(("dp", "tensor"), None),
            P(),
            P(),
            P(None, None, "tensor"),
            P(None, "tensor"),
            P("tensor", None),
            P(),
            P(),
            P(),
            P(None, "tensor"),
            P("tensor"),
            P("tensor", None),
            P(),
        ),
        check_vma=False,
    )
```

```python
import types

import jax
import jax.numpy as jnp
from jax import lax
from jax.experimental import pallas as pl
from jax.experimental.pallas import tpu as pltpu
from jax.sharding import PartitionSpec as P

HEAD_DIM = 64
MESH = pl.DeviceIdType.MESH
VMEM_BYTES = 62 * 2**20

epsilon = 1e-06
low = jnp.bfloat16
wide = jnp.float32


def round_up(amount, unit):
    return -(-amount // unit) * unit


def flipped(t, flip_chip, flip_core):
    return (t // 2 + flip_chip) % 2 * 2 + (t % 2 + flip_core) % 2


def dot(left, right):
    return jnp.dot(left, right, preferred_element_type=wide)


def dot_rows(left, right):
    return lax.dot_general(left, right, (((1,), (1,)), ((), ())), preferred_element_type=wide)


def dot_columns(left, right):
    return lax.dot_general(left, right, (((0,), (0,)), ((), ())), preferred_element_type=wide)


def standardize(values):
    center = values - jnp.mean(values, -1, keepdims=True)
    inverse = lax.rsqrt(jnp.mean(center * center, -1, keepdims=True) + epsilon)
    return center * inverse, inverse


def norm_back(grad, unit, inverse, gain):
    scaled = grad * gain
    return inverse * (
        scaled
        - jnp.mean(scaled, -1, keepdims=True)
        - unit * jnp.mean(scaled * unit, -1, keepdims=True)
    )


def pair(ref, p):
    _, rows, columns = ref.shape
    return ref[pl.ds(2 * p, 2)].reshape(2 * rows, columns)


def set_pair(ref, p, values):
    ref[pl.ds(2 * p, 2)] = values.reshape(2, -1, values.shape[1])


def flat(ref):
    a, b, c = ref.shape
    return ref[...].reshape(a * b, c)


class Links:
    def __init__(self, send, recv):
        self.send, self.recv, self.used, self.pending = send, recv, 0, []

    def take(self, amount=1):
        base = self.used
        self.used += amount
        assert self.used <= self.send.shape[0]
        return base

    def copy(self, src, dst, at, **where):
        return pltpu.make_async_remote_copy(
            src_ref=src,
            dst_ref=dst,
            send_sem=self.send.at[at],
            recv_sem=self.recv.at[at],
            device_id=where,
            device_id_type=MESH,
        )

    def start(self, src, dst, at, **where):
        copy = self.copy(src, dst, at, **where)
        copy.start()
        self.pending.append(copy)

    def arrived(self, dst, at, **where):
        self.copy(dst, dst, at, **where).wait_recv()

    def finish(self):
        for copy in self.pending:
            copy.wait_send()
        self.pending = []


class Gather:
    def __init__(self, links, buf, t, parts):
        self.links, self.buf, self.t, self.parts = links, buf, t, parts
        self.sib, self.cross, self.diag = flipped(t, 0, 1), flipped(t, 1, 0), flipped(t, 1, 1)
        self.base = links.take(3 * len(parts))

    def view(self, slot, part):
        start, size = self.parts[part]
        return self.buf.at[slot, pl.ds(start, size)]

    def _each(self):
        return range(len(self.parts))

    def start(self):
        for p in self._each():
            v = self.view(self.t, p)
            self.links.copy(v, v, self.base + 3 * p, tensor=self.cross).start()
        for p in self._each():
            v = self.view(self.t, p)
            self.links.copy(v, v, self.base + 3 * p + 1, tensor=self.sib).start()

    def wait_sib(self):
        for p in self._each():
            self.links.arrived(self.view(self.sib, p), self.base + 3 * p + 1, tensor=self.sib)

    def forward(self):
        for p in self._each():
            v = self.view(self.cross, p)
            self.links.arrived(v, self.base + 3 * p, tensor=self.cross)
            self.links.copy(v, v, self.base + 3 * p + 2, tensor=self.sib).start()

    def wait_diag(self):
        for p in self._each():
            self.links.arrived(self.view(self.diag, p), self.base + 3 * p + 2, tensor=self.sib)

    def finish(self):
        for p in self._each():
            v = self.view(self.t, p)
            self.links.copy(v, v, self.base + 3 * p, tensor=self.cross).wait_send()
            self.links.copy(v, v, self.base + 3 * p + 1, tensor=self.sib).wait_send()
            v = self.view(self.cross, p)
            self.links.copy(v, v, self.base + 3 * p + 2, tensor=self.sib).wait_send()


class Reduce:
    def __init__(self, links, part, pre, near, far, t):
        self.links, self.part, self.pre, self.near, self.far, self.t = links, part, pre, near, far, t
        self.sib, self.cross, self.diag = flipped(t, 0, 1), flipped(t, 1, 0), flipped(t, 1, 1)
        self.base = links.take(3)

    def send_diag(self):
        self.links.copy(self.part.at[self.diag], self.pre, self.base, tensor=self.sib).start()

    def send_sib(self):
        self.links.copy(self.part.at[self.sib], self.near, self.base + 1, tensor=self.sib).start()

    def send_cross(self):
        self.links.arrived(self.pre, self.base, tensor=self.sib)
        total = self.part[self.cross].astype(wide) + self.pre[...].astype(wide)
        self.part[self.cross] = total.astype(low)
        self.links.copy(self.part.at[self.cross], self.far, self.base + 2, tensor=self.cross).start()

    def result(self):
        self.links.arrived(self.near, self.base + 1, tensor=self.sib)
        self.links.arrived(self.far, self.base + 2, tensor=self.cross)
        return (
            self.part[self.t].astype(wide) + self.near[...].astype(wide) + self.far[...].astype(wide)
        )

    def finish(self):
        self.links.copy(self.part.at[self.diag], self.pre, self.base, tensor=self.sib).wait_send()
        self.links.copy(self.part.at[self.sib], self.near, self.base + 1, tensor=self.sib).wait_send()
        self.links.copy(self.part.at[self.cross], self.far, self.base + 2, tensor=self.cross).wait_send()


class DataReduce:
    def __init__(self, links, held, whole, share, box, box_at, first, rows, d, count, order):
        self.links, self.held, self.whole = links, held, whole
        bits = count.bit_length() - 1
        assert count == 1 << bits and bits >= 3
        self.extra = [b for b in range(bits) if b not in order]
        self.d, self.order = d, order
        self.region = (first, rows, 0, held.shape[1])
        self.trail, self.sent, self.boxes = [], [], []
        for tall, broad in self.sizes(rows, held.shape[1], count)[0]:
            self.boxes.append(box.at[pl.ds(box_at, tall), pl.ds(0, broad)])
            box_at += tall
        self.share = share.at[pl.ds(0, tall), pl.ds(0, broad)]
        self.base = links.take(7 + len(self.extra))
        self.steps = [lambda: self._send_half(0)]
        for k in (1, 2):
            self.steps.append(lambda k=k: (self._add_half(k - 1), self._send_half(k)))
        self.steps.append(lambda: (self._add_half(2), self._swap(), self._place(), self._grow_send(2)))
        for k in (2, 1):
            self.steps.append(lambda k=k: (self._grow_wait(k), self._grow_send(k - 1)))
        self.steps.append(lambda: self._grow_wait(0))

    @staticmethod
    def sizes(rows, columns, count):
        found = []
        for _ in range(3):
            if rows % 32 == 0:
                rows //= 2
            else:
                columns //= 2
            found.append((rows, columns))
        found += found[2:] * (count.bit_length() - 1 - 3)
        return found, sum(size[0] for size in found)

    def _bit(self, b):
        return self.d // (1 << b) % 2

    def _peer(self, b):
        return self.d + (1 - 2 * self._bit(b)) * (1 << b)

    def _start(self, copy):
        copy.start()
        self.sent.append(copy)

    @staticmethod
    def _view(ref, region):
        row, rows, column, columns = region
        if columns == ref.shape[1]:
            return ref.at[pl.ds(row, rows)]
        return ref.at[pl.ds(row, rows), pl.ds(column, columns)]

    @staticmethod
    def _part(region, bit):
        row, rows, column, columns = region
        if rows % 32 == 0:
            return (pl.multiple_of(row + bit * (rows // 2), 16), rows // 2, column, columns)
        return (row, rows, pl.multiple_of(column + bit * (columns // 2), 128), columns // 2)

    def _send_half(self, k):
        b = self.order[k]
        bit = self._bit(b)
        self.trail.append(self.region)
        view = self._view(self.held, self._part(self.region, 1 - bit))
        self._start(self.links.copy(view, self.boxes[k], self.base + k, dp=self._peer(b)))
        self.region = self._part(self.region, bit)

    def _add_half(self, k):
        self.links.arrived(self.boxes[k], self.base + k, dp=self._peer(self.order[k]))
        view = self._view(self.held, self.region)
        total = (view[...].astype(wide) + self.boxes[k][...].astype(wide)).astype(low)
        if k == 2:
            self.share[...] = total
        else:
            view[...] = total

    def _swap(self):
        for k, b in enumerate(self.extra):
            box, at = self.boxes[3 + k], self.base + 7 + k
            copy = self.links.copy(self.share, box, at, dp=self._peer(b))
            copy.start()
            self.links.arrived(box, at, dp=self._peer(b))
            copy.wait_send()
            self.share[...] = (self.share[...].astype(wide) + box[...].astype(wide)).astype(low)

    def _place(self):
        self.placed = pltpu.make_async_copy(
            self.share, self._view(self.whole, self.region), self.links.send.at[self.base + 6]
        )
        self.placed.start()

    def _grow_send(self, k):
        view = self._view(self.whole, self.region)
        src = self.share if k == 2 else view
        self._start(self.links.copy(src, view, self.base + 3 + k, dp=self._peer(self.order[k])))

    def _grow_wait(self, k):
        if k == 2:
            self.placed.wait()
        b = self.order[k]
        view = self._view(self.whole, self._part(self.trail[k], 1 - self._bit(b)))
        self.links.arrived(view, self.base + 3 + k, dp=self._peer(b))
        self.region = self.trail[k]

    def step(self):
        if self.steps:
            self.steps.pop(0)()

    def finish(self):
        assert not self.steps
        for copy in self.sent:
            copy.wait_send()


class Pipeline:
    def __init__(self, plan):
        self.plan, self.members = plan, []

    def add(self, member):
        self.members.append(member)
        member.step()

    def at(self, place):
        for number in self.plan[place]:
            self.members[number].step()

    def finish(self):
        self.at("end")
        for m in self.members:
            while m.steps:
                m.step()
            m.finish()


PLAN = dict(
    waiting=(),
    shared=(0, 1),
    h0p0=(2, 3),
    h0p2=(0, 1),
    h0=(2, 3),
    h1p0=(0,),
    h1p2=(1, 4, 2),
    h1=(3,),
    h2p0=(4, 0),
    h2p2=(),
    h2=(5, 1, 6),
    led=(2, 0),
    crossing=(3, 7, 6, 4, 5, 1, 2, 7, 6, 4, 5, 0),
    told=(3, 1, 7, 6),
    end=(5, 2, 4, 3, 7, 6, 5, 4, 7, 6, 5, 7),
)


class Everyone:
    def __init__(self, links, buf, me, count, device):
        self.links, self.buf, self.me, self.count, self.device = links, buf, me, count, device
        self.base = links.take(count)

    def _copy(self, j):
        slot = self.buf.at[self.me]
        peer = self.device(lax.rem(self.me + j, self.count))
        return self.links.copy(slot, slot, self.base + j, dp=peer)

    def _loop(self, act):
        def one(j, carry):
            act(j)
            return carry

        lax.fori_loop(1, self.count, one, 0)

    def start(self, values):
        self.buf[self.me] = values
        self._loop(lambda j: self._copy(j).start())

    def _hear(self, j):
        peer = lax.rem(self.me + self.count - j, self.count)
        self.links.arrived(self.buf.at[peer], self.base + j, dp=self.device(peer))

    def result(self):
        self._loop(self._hear)
        return lax.fori_loop(1, self.count, lambda j, acc: acc + self.buf[j], self.buf[0])

    def finish(self):
        self._loop(lambda j: self._copy(j).wait_send())


def greet(axis, me, count):
    barrier = pltpu.get_barrier_semaphore()

    def one(j, carry):
        pl.semaphore_signal(
            barrier, inc=1, device_id={axis: lax.rem(me + j, count)}, device_id_type=MESH
        )
        return carry

    lax.fori_loop(1, count, one, 0)


def await_greetings(amount):
    pl.semaphore_wait(pltpu.get_barrier_semaphore(), amount)


def halves(rows):
    first = round_up(rows // 2, 16)
    return ((0, first), (first, rows - first))


def head_masks(shape, local_heads):
    lane = lax.broadcasted_iota(jnp.int32, shape, 1)
    return [
        jnp.where((lane >= h * HEAD_DIM) & (lane < (h + 1) * HEAD_DIM), 1.0, 0.0)
        for h in range(local_heads)
    ], lane


def kernel(n, S):
    links = Links(S.send, S.recv)
    t = lax.axis_index("tensor")
    d = lax.axis_index("dp")
    greet("tensor", t, 4)
    greet("dp", d, n.dp)
    R, own, W, H, D, K = n.R, n.own, n.W, n.H, n.D, n.K
    vector = lambda ref: ref[...].reshape(1, D)

    fetch = pltpu.make_async_copy(S.cot, S.gt, S.local)
    fetch.start()
    S.a1[t] = jnp.zeros((R, D), low)
    S.cot4[t] = jnp.zeros((R, D), low)
    S.a24[t] = jnp.zeros((R, D), low)
    S.hl4[t] = jnp.zeros((R, D), low)
    unit, _ = standardize(S.x[...].astype(wide))
    S.a1[t, 0:own, :] = (unit * vector(S.g1) + vector(S.b1)).astype(low)
    fetch.wait()
    S.cot4[t, 0:own, :] = S.gt[...].astype(low)
    S.ow4[t] = S.ow[...]
    await_greetings(3 + n.dp - 1)
    rows_in = Gather(links, S.a1, t, halves(R))
    cot_in = Gather(links, S.cot4, t, halves(R))
    ow_in = Gather(links, S.ow4, t, ((0, W),))
    rows_in.start()
    S.gw[0:D, :] = jnp.transpose(S.wup[...])
    S.gw[D:, :] = jnp.transpose(S.wdn[...])
    S.v[4 * R :, :] = jnp.zeros((K - 4 * R, H), low)
    length = S.lengths[0]

    chip = t // 2

    def project(i, carry):
        s = flipped(t, i // 2, i % 2)

        @pl.when(i == 1)
        def _():
            rows_in.wait_sib()

        @pl.when(i == 2)
        def _():
            rows_in.forward()
            ow_in.start()

        @pl.when(i == 3)
        def _():
            rows_in.wait_diag()

        slab = S.a1[s]
        lane = lax.broadcasted_iota(jnp.int32, (R, H - W), 1)
        row = lax.broadcasted_iota(jnp.int32, (R, H - W), 0)
        absent = (row >= own) | (row + s * own >= length)
        at = pl.ds(pl.multiple_of(s * R, 16), R)
        out = dot(slab, S.wqkv[0]) + S.bq[0:1, :]
        S.q[s, :, :W] = (out.astype(low).astype(wide) * HEAD_DIM**-0.5).astype(low)
        S.q[s, :, W:] = jnp.where(lane == 0, HEAD_DIM**-0.5, 0.0).astype(low)
        S.k[at, :W] = dot(slab, S.wqkv[1]).astype(low)
        S.k[at, W:] = jnp.where((lane == 0) & absent, -8e30, 0.0).astype(low)
        S.v[at, :W] = (dot(slab, S.wqkv[2]) + S.bq[1:2, :]).astype(low)
        S.v[at, W:] = jnp.where(lane < 2, 1.0, 0.0).astype(low)
        return carry

    lax.fori_loop(0, 4, project, 0)
    if K > 4 * R:
        lane = lax.broadcasted_iota(jnp.int32, (K - 4 * R, H), 1)
        S.k[4 * R :, :] = jnp.where(lane == W, -8e30, 0.0).astype(low)
    S.kt[...] = jnp.transpose(S.k[...])
    S.vt[...] = jnp.transpose(S.v[...])

    masks, lane = head_masks((1, H), n.heads)
    mix_base = links.take(3)

    peers = [flipped(t, 1, 0), flipped(t, 1, 1), flipped(t, 0, 1)]

    def attend(i, carry):
        s = flipped(t, 1 - i // 2, (i + i // 2) % 2)
        query = S.q[s]
        mixed = jnp.zeros((R, H), wide)
        inverse = jnp.zeros((R, 128), wide)
        first = lax.broadcasted_iota(jnp.int32, (1, 128), 1)

        def score(h):
            here = jnp.where(lane == W, 1.0, masks[h]).astype(low)
            return dot(query * here, S.kt[...])

        ready = score(0)
        for h in range(n.heads):
            scores = ready
            if h + 1 < n.heads:
                ready = score(h + 1)
            terms = jnp.exp(scores - jnp.max(scores, -1, keepdims=True)).astype(low)
            S.e[h, s] = terms
            part = dot(terms, S.v[...])
            scale = 1.0 / part[:, W : W + 1]
            mixed += part * (scale * masks[h])
            inverse = jnp.where(first == h, scale, inverse)
        S.o[s] = mixed
        S.inv[s] = inverse
        S.mix[s] = mixed[:, :W].astype(low)

        @pl.when(i < 3)
        def _():
            links.copy(S.mix.at[s], S.mix4.at[t], mix_base + i, tensor=s).start()

        @pl.when(i == 1)
        def _():
            cot_in.start()

        @pl.when(i == 2)
        def _():
            ow_in.wait_sib()
            ow_in.forward()

        return carry

    lax.fori_loop(0, 4, attend, 0)
    ow_in.wait_diag()
    S.mix4[t] = S.mix[t]
    for j, s in enumerate(peers):
        links.arrived(S.mix4.at[s], mix_base + j, tensor=s)

    total = dot(S.mix4[0], S.ow4[0])
    for j in range(1, 4):
        total += dot(S.mix4[j], S.ow4[j])
    total = S.x[...].astype(wide) + (total[:own] + vector(S.ob))
    S.hid[...] = total
    unit, _ = standardize(total)
    S.a24[t, 0:own, :] = (unit * vector(S.g2) + vector(S.b2)).astype(low)
    next_in = Gather(links, S.a24, t, halves(R))
    next_in.start()
    back = Reduce(links, S.part, S.pre1, S.near1, S.far1, t)
    ahead = Reduce(links, S.fop, S.pre2, S.near2, S.far2, t)
    S.gub[...] = jnp.zeros_like(S.gub)

    def feed(i, carry):
        s = flipped(t, i // 2, i % 2)

        @pl.when(i == 1)
        def _():
            next_in.wait_sib()
            cot_in.wait_sib()

        @pl.when(i == 2)
        def _():
            cot_in.forward()
            next_in.forward()

        @pl.when(i == 3)
        def _():
            next_in.wait_diag()
            cot_in.wait_diag()

        up = dot(S.a24[s], S.wup[...]) + vector(S.bup)
        square = up * up
        c = 0.7978845608028654
        bend = jnp.tanh(c * up * (1.0 + 0.044715 * square))
        half = 0.5 * (1.0 + bend)
        slope = half + 0.5 * up * (1.0 - bend * bend) * (c + (3 * 0.044715 * c) * square)
        active = (up * half).astype(low)
        S.pool[s, :, 0:D] = active
        grad = (dot(S.cot4[s], S.gw[D:, :]) * slope).astype(low)
        S.gup[s] = grad
        S.part[s] = dot(grad, S.gw[0:D, :]).astype(low)

        @pl.when(i == 1)
        def _():
            back.send_sib()

        @pl.when(i == 3)
        def _():
            back.send_diag()

        S.fop[s] = dot(active, S.wdn[...]).astype(low)

        @pl.when(i == 1)
        def _():
            ahead.send_sib()

        @pl.when(i == 3)
        def _():
            ahead.send_diag()

        S.gub[...] += jnp.sum(grad.astype(wide), 0, keepdims=True)
        return carry

    lax.fori_loop(0, 4, feed, 0)
    back.send_cross()

    sums = Pipeline(PLAN)
    tile = D // 2
    box_at = share_at = 0

    def sum_over_dp(held, whole, first, rows, order):
        nonlocal box_at, share_at
        sizes, taken = DataReduce.sizes(rows, D, n.dp)
        share = S.share.at[pl.ds(share_at, sizes[2][0])]
        sums.add(DataReduce(links, held, whole, share, S.box, box_at, first, rows, d, n.dp, order))
        box_at, share_at = box_at + taken, share_at + sizes[2][0]

    for left, right, first in ((S.a24, S.gup, 0), (S.pool, S.cot4, D)):
        rows = left[:, :, 0:D].reshape(4 * R, D)
        S.gw[first : first + D, :] = dot_columns(rows, flat(right)).astype(low)
        for at in (first, first + tile):
            sum_over_dp(S.gw, S.whole1, at, tile, (0, 1, 2) if at == first else (1, 0, 2))

    sums.at("waiting")
    grad = back.result()[:own]
    unit, inverse = standardize(S.hid[...])
    S.small[...] = jnp.zeros_like(S.small)
    S.small[2:3, :] = jnp.sum(grad * unit, 0, keepdims=True)
    S.small[3:4, :] = jnp.sum(grad, 0, keepdims=True)
    S.gt[...] += norm_back(grad, unit, inverse, vector(S.g2))
    S.hl4[t, 0:own, :] = S.gt[...].astype(low)
    S.small[4:5, :] = jnp.sum(S.hl4[t].astype(wide), 0, keepdims=True)
    S.small[5:6, :] = jnp.sum(S.cot4[t].astype(wide), 0, keepdims=True)
    S.small[6:7, :] = S.gub[...]
    gm_base = links.take(3)

    for j, s in enumerate(peers + [t]):
        S.mix4[s] = dot_rows(S.hl4[t], S.ow4[s]).astype(low)
        if j < 3:
            links.copy(S.mix4.at[s], S.gm4.at[t], gm_base + j, tensor=s).start()
    S.gm4[t] = S.mix4[t]
    hl_in = Gather(links, S.hl4, t, halves(R))

    next_in.finish()
    S.do[...] = jnp.zeros_like(S.do)
    S.qt[...] = jnp.transpose(flat(S.q))
    sums.at("shared")

    def prepare(i, s):
        if i > 0:
            j = (None, 2, 0, 1)[i]
            links.arrived(S.gm4.at[s], gm_base + j, tensor=peers[j])
        S.do[:, :W] = S.gm4[s].astype(wide)
        inverse = sum(S.inv[s, :, h : h + 1] * masks[h] for h in range(n.heads))
        scaled = (S.do[...] * inverse).astype(low)
        S.v[pl.ds(pl.multiple_of(s * R, 16), R), :] = scaled
        scaled = scaled.astype(wide)
        product = scaled * S.o[s]
        for h in range(n.heads):
            inner = -jnp.sum(product * masks[h], -1, keepdims=True)
            upper = inner.astype(low).astype(wide)
            S.a24[s, :, h * H : (h + 1) * H] = (
                scaled * masks[h]
                + jnp.where(lane == W, upper, 0.0)
                + jnp.where(lane == W + 1, inner - upper, 0.0)
            ).astype(low)

    def pull(h, p):
        grad_p = dot(pair(S.a24.at[:, :, h * H : (h + 1) * H], p), S.vt[...])
        grad_s = (pair(S.e.at[h], p).astype(wide) * grad_p).astype(low)
        set_pair(S.pool, p, grad_s)
        dq = dot(grad_s, S.k[...]) * (masks[h] * HEAD_DIM**-0.5)
        if h > 0:
            dq += pair(S.gup.at[:, :, 0:H], p).astype(wide)
        S.gup[pl.ds(2 * p, 2), :, 0:H] = dq.astype(low).reshape(2, R, H)

    for h in range(n.heads):
        for i in (0, 2):
            if h == 0:
                prepare(i, flipped(t, i // 2, 0))
                prepare(i + 1, flipped(t, i // 2, 1))
            if (h, i) == (0, 2):
                hl_in.start()
            pull(h, (chip + i // 2) % 2)
            sums.at(f"h{h}p{i}")
            if (h, i) == (1, 0):
                hl_in.wait_sib()
                hl_in.forward()
                ahead.send_cross()
            elif (h, i) == (1, 2):
                hl_in.wait_diag()
                S.gw2[3 * W :, :] = dot_columns(flat(S.mix), flat(S.hl4)).astype(low)
                sum_over_dp(S.gw2, S.whole2, 3 * W, W, (1, 0, 2))
        if h == 0:
            S.v[4 * R :, :] = jnp.zeros((K - 4 * R, H), low)
            S.kt[...] = jnp.transpose(S.v[...])
        at = slice(h * HEAD_DIM, (h + 1) * HEAD_DIM)
        S.dk[at, :] = dot(S.qt[at, :], flat(S.pool)).astype(low)
        S.dv[at, :] = dot(S.kt[at, : 4 * R], flat(S.e.at[h])).astype(low)
        tile = h * HEAD_DIM // 128 * 128
        dqt = jnp.transpose(flat(S.gup.at[:, :, tile : tile + 128]))
        left = jnp.concatenate(
            [dqt[h * HEAD_DIM - tile : (h + 1) * HEAD_DIM - tile], S.dk[at, : 4 * R], S.dv[at, : 4 * R]], 0
        )
        S.gw2[h * W : (h + 1) * W, :] = dot(left, flat(S.a1)).astype(low)
        sum_over_dp(S.gw2, S.whole2, h * W, W, (0, 1, 2) if h in (1, 2) else (1, 0, 2))
        sums.at(f"h{h}")

    pad = jnp.zeros((R, H - W), low)
    for part, grad_t in ((1, S.dk), (2, S.dv)):
        rows = jnp.transpose(grad_t[...])
        for s in range(4):
            S.gup[s, :, part * H : part * H + W] = rows[s * R : (s + 1) * R]
            S.gup[s, :, part * H + W : (part + 1) * H] = pad

    back.finish()
    down = Reduce(links, S.part, S.pre1, S.near1, S.far1, t)

    def lead(i, carry):
        s = flipped(t, 1 - i // 2, 1 - i % 2)
        out = dot_rows(S.gup[s, :, 0:W], S.wqkv[0])
        out += dot_rows(S.gup[s, :, H : H + W], S.wqkv[1])
        out += dot_rows(S.gup[s, :, 2 * H : 2 * H + W], S.wqkv[2])
        S.part[s] = out.astype(low)

        @pl.when(i == 0)
        def _():
            down.send_diag()

        @pl.when(i == 2)
        def _():
            down.send_sib()
            down.send_cross()

        return carry

    lax.fori_loop(0, 4, lead, 0)
    sums.at("led")
    S.small[7:8, 0:H] = jnp.sum(flat(S.gup.at[:, :, 0:H]).astype(wide), 0, keepdims=True)
    S.small[7:8, H : 2 * H] = jnp.sum(
        flat(S.gup.at[:, :, 2 * H : 3 * H]).astype(wide), 0, keepdims=True
    )
    S.output[...] = (S.hid[...] + (ahead.result()[:own] + vector(S.db))).astype(low)
    sums.at("crossing")

    unit, inverse = standardize(S.x[...].astype(wide))
    grad = down.result()[:own]
    S.small[0:1, :] = jnp.sum(grad * unit, 0, keepdims=True)
    S.small[1:2, :] = jnp.sum(grad, 0, keepdims=True)
    S.small4[t] = S.small[...]
    base3 = links.take(3)
    for j in range(3):
        peer = lax.rem(t + j + 1, 4)
        links.start(S.small4.at[t], S.small4.at[t], base3 + j, tensor=peer)
    S.gt[...] += norm_back(grad, unit, inverse, vector(S.g1))
    sums.at("told")
    for j in range(3):
        peer = lax.rem(t + 3 - j, 4)
        links.arrived(S.small4.at[peer], base3 + j, tensor=peer)
    over = S.small4[0] + S.small4[1] + S.small4[2] + S.small4[3]
    row = lax.broadcasted_iota(jnp.int32, over.shape, 0)
    near = min(8, n.dp)
    inner = Everyone(links, S.smalls, d % near, near, lambda j: d // near * near + j)
    inner.start(jnp.where(row < 6, over, S.small[...]))
    sums.finish()
    total = inner.result()
    inner.finish()
    if n.dp > near:
        outer = Everyone(links, S.smalls2, d // near, n.dp // near, lambda j: j * near + d % near)
        outer.start(total)
        total = outer.result()
        outer.finish()
    S.small_sum[...] = total
    for j, s in enumerate(peers):
        links.copy(S.mix.at[s], S.mix4.at[t], mix_base + j, tensor=s).wait_send()
        links.copy(S.mix4.at[s], S.gm4.at[t], gm_base + j, tensor=s).wait_send()
    for transfer in (rows_in, cot_in, ow_in, hl_in, ahead, down):
        transfer.finish()
    links.finish()


def body(
    tokens,
    lengths,
    ln1_gain,
    ln1_shift,
    qkv_weight,
    qv_bias,
    out_weight,
    out_bias,
    ln2_gain,
    ln2_shift,
    up_weight,
    up_bias,
    down_weight,
    down_bias,
    cotangent,
):
    own, D = tokens.shape
    W = qkv_weight.shape[2]
    F = up_weight.shape[1]
    dp = lax.axis_size("dp")
    assert lax.axis_size("tensor") == 4 and lengths.shape[0] == 1 and F == D and 4 * W == D and 3 * round_up(W + 2, 128) == D
    R = round_up(own, 16)
    H = round_up(W + 2, 128)
    K = round_up(4 * R, 256)
    heads = W // HEAD_DIM
    extra = dp.bit_length() - 1 - 3
    n = types.SimpleNamespace(
        own=own, D=D, W=W, R=R, H=H, K=K, dp=dp, heads=heads, extra=extra
    )
    given = dict(
        x=tokens, lengths=lengths, g1=ln1_gain, b1=ln1_shift,
        wqkv=jnp.transpose(qkv_weight, (1, 0, 2)), bq=qv_bias, ow=out_weight, ob=out_bias,
        g2=ln2_gain, b2=ln2_shift, wup=up_weight, bup=up_bias, wdn=down_weight, db=down_bias,
        cot=cotangent,
    )
    outs = dict(
        output=((own, D), low), gt=((own, D), wide), small_sum=((8, D), wide),
        whole1=((2 * D, D), low), whole2=((D, D), low),
    )
    rows4 = ((4, R, D), low)
    slab = ((R, D), low)
    chunks = [D // 2] * 4 + [W] * 4
    scratch = dict(
        a1=rows4, cot4=rows4, ow4=((4, W, D), low), q=((4, R, H), low), k=((K, H), low),
        v=((K, H), low), kt=((H, K), low), vt=((H, K), low), e=((heads, 4, R, K), low),
        o=((4, R, H), wide), inv=((4, R, 128), wide), mix=((4, R, W), low), mix4=((4, R, W), low),
        hid=((own, D), wide),
        a24=rows4, pool=((4, R, K), low), gup=rows4, part=rows4,
        fop=rows4, pre1=slab, near1=slab, far1=slab, pre2=slab, near2=slab, far2=slab,
        gw=((2 * D, D), low), gub=((1, D), wide),
        small=((8, D), wide), hl4=rows4,
        gm4=((4, R, W), low), dk=((W, K), low), dv=((W, K), low), qt=((H, 4 * R), low), do=((R, H), wide),
        gw2=((D, D), low),
        small4=((4, 8, D), wide), smalls=((min(8, dp), 8, D), wide),
        box=((sum(DataReduce.sizes(r, D, dp)[1] for r in chunks), D), low),
        share=((sum(DataReduce.sizes(r, D, dp)[0][2][0] for r in chunks), D), low),
    )
    if dp > 8:
        scratch["smalls2"] = ((dp // 8, 8, D), wide)
    sems = 140 + dp + 8 * extra
    names = list(given) + list(outs) + list(scratch) + ["local", "send", "recv"]
    vmem = pl.BlockSpec(memory_space=pltpu.VMEM)
    smem = pl.BlockSpec(memory_space=pltpu.SMEM)
    hbm = pl.BlockSpec(memory_space=pl.ANY)
    output, gt, small, whole1, whole2 = pl.pallas_call(
        lambda *refs: kernel(n, types.SimpleNamespace(**dict(zip(names, refs)))),
        out_shape=tuple(jax.ShapeDtypeStruct(*spec) for spec in outs.values()),
        in_specs=[dict(lengths=smem, cot=hbm).get(name, vmem) for name in given],
        out_specs=tuple(hbm if name in ("whole1", "whole2") else vmem for name in outs),
        scratch_shapes=[pltpu.VMEM(*spec) for spec in scratch.values()]
        + [pltpu.SemaphoreType.DMA] + [pltpu.SemaphoreType.DMA((sems,))] * 2,
        compiler_params=pltpu.CompilerParams(
            collective_id=0, has_side_effects=True, vmem_limit_bytes=VMEM_BYTES
        ),
    )(*given.values())
    parts = whole2[: 3 * W].astype(wide).reshape(heads, 3, HEAD_DIM, D)
    grad_qkv = jnp.transpose(parts, (3, 1, 0, 2)).reshape(D, 3, W)
    return (
        output,
        gt,
        small[0],
        small[1],
        grad_qkv,
        jnp.stack([small[7, :W], small[7, H : H + W]]),
        whole2[3 * W :].astype(wide),
        small[4],
        small[2],
        small[3],
        whole1[:D].astype(wide),
        small[6],
        whole1[D:].astype(wide),
        small[5],
    )


def solution(mesh):
    placed = (
        P(("dp", "tensor"), None),
        P("dp"),
        P(),
        P(),
        P(None, None, "tensor"),
        P(None, "tensor"),
        P("tensor", None),
        P(),
        P(),
        P(),
        P(None, "tensor"),
        P("tensor"),
        P("tensor", None),
        P(),
        P(("dp", "tensor"), None),
    )
    return jax.shard_map(
        body,
        mesh=mesh,
        in_specs=placed,
        out_specs=(
            P(("dp", "tensor"), None),
            P(("dp", "tensor"), None),
            P(),
            P(),
            P(None, None, "tensor"),
            P(None, "tensor"),
            P("tensor", None),
            P(),
            P(),
            P(),
            P(None, "tensor"),
            P("tensor"),
            P("tensor", None),
            P(),
        ),
        check_vma=False,
    )
```

```python
import types

import jax
import jax.numpy as jnp
from jax import lax
from jax.experimental import pallas as pl
from jax.experimental.pallas import tpu as pltpu
from jax.sharding import PartitionSpec as P

HEAD_DIM = 64
MESH = pl.DeviceIdType.MESH
VMEM_BYTES = 62 * 2**20

epsilon = 1e-06
low = jnp.bfloat16
wide = jnp.float32


def round_up(amount, unit):
    return -(-amount // unit) * unit


def flipped(t, flip_chip, flip_core):
    return (t // 2 + flip_chip) % 2 * 2 + (t % 2 + flip_core) % 2


def dot(left, right):
    return jnp.dot(left, right, preferred_element_type=wide)


def dot_rows(left, right):
    return lax.dot_general(left, right, (((1,), (1,)), ((), ())), preferred_element_type=wide)


def dot_columns(left, right):
    return lax.dot_general(left, right, (((0,), (0,)), ((), ())), preferred_element_type=wide)


def standardize(values):
    center = values - jnp.mean(values, -1, keepdims=True)
    inverse = lax.rsqrt(jnp.mean(center * center, -1, keepdims=True) + epsilon)
    return center * inverse, inverse


def norm_back(grad, unit, inverse, gain):
    scaled = grad * gain
    return inverse * (
        scaled
        - jnp.mean(scaled, -1, keepdims=True)
        - unit * jnp.mean(scaled * unit, -1, keepdims=True)
    )


def pair(ref, p):
    _, rows, columns = ref.shape
    return ref[pl.ds(2 * p, 2)].reshape(2 * rows, columns)


def set_pair(ref, p, values):
    ref[pl.ds(2 * p, 2)] = values.reshape(2, -1, values.shape[1])


def flat(ref):
    a, b, c = ref.shape
    return ref[...].reshape(a * b, c)


class Links:
    def __init__(self, send, recv):
        self.send, self.recv, self.used, self.pending = send, recv, 0, []

    def take(self, amount=1):
        base = self.used
        self.used += amount
        assert self.used <= self.send.shape[0]
        return base

    def copy(self, src, dst, at, **where):
        return pltpu.make_async_remote_copy(
            src_ref=src,
            dst_ref=dst,
            send_sem=self.send.at[at],
            recv_sem=self.recv.at[at],
            device_id=where,
            device_id_type=MESH,
        )

    def start(self, src, dst, at, **where):
        copy = self.copy(src, dst, at, **where)
        copy.start()
        self.pending.append(copy)

    def arrived(self, dst, at, **where):
        self.copy(dst, dst, at, **where).wait_recv()

    def finish(self):
        for copy in self.pending:
            copy.wait_send()
        self.pending = []


class Gather:
    def __init__(self, links, buf, t, parts):
        self.links, self.buf, self.t, self.parts = links, buf, t, parts
        self.sib, self.cross, self.diag = flipped(t, 0, 1), flipped(t, 1, 0), flipped(t, 1, 1)
        self.base = links.take(3 * len(parts))

    def view(self, slot, part):
        start, size = self.parts[part]
        return self.buf.at[slot, pl.ds(start, size)]

    def _each(self):
        return range(len(self.parts))

    def start(self):
        for p in self._each():
            v = self.view(self.t, p)
            self.links.copy(v, v, self.base + 3 * p, tensor=self.cross).start()
        for p in self._each():
            v = self.view(self.t, p)
            self.links.copy(v, v, self.base + 3 * p + 1, tensor=self.sib).start()

    def wait_sib(self):
        for p in self._each():
            self.links.arrived(self.view(self.sib, p), self.base + 3 * p + 1, tensor=self.sib)

    def forward(self):
        for p in self._each():
            v = self.view(self.cross, p)
            self.links.arrived(v, self.base + 3 * p, tensor=self.cross)
            self.links.copy(v, v, self.base + 3 * p + 2, tensor=self.sib).start()

    def wait_diag(self):
        for p in self._each():
            self.links.arrived(self.view(self.diag, p), self.base + 3 * p + 2, tensor=self.sib)

    def finish(self):
        for p in self._each():
            v = self.view(self.t, p)
            self.links.copy(v, v, self.base + 3 * p, tensor=self.cross).wait_send()
            self.links.copy(v, v, self.base + 3 * p + 1, tensor=self.sib).wait_send()
            v = self.view(self.cross, p)
            self.links.copy(v, v, self.base + 3 * p + 2, tensor=self.sib).wait_send()


class Reduce:
    def __init__(self, links, part, pre, near, far, t):
        self.links, self.part, self.pre, self.near, self.far, self.t = links, part, pre, near, far, t
        self.sib, self.cross, self.diag = flipped(t, 0, 1), flipped(t, 1, 0), flipped(t, 1, 1)
        self.base = links.take(3)

    def send_diag(self):
        self.links.copy(self.part.at[self.diag], self.pre, self.base, tensor=self.sib).start()

    def send_sib(self):
        self.links.copy(self.part.at[self.sib], self.near, self.base + 1, tensor=self.sib).start()

    def send_cross(self):
        self.links.arrived(self.pre, self.base, tensor=self.sib)
        total = self.part[self.cross].astype(wide) + self.pre[...].astype(wide)
        self.part[self.cross] = total.astype(low)
        self.links.copy(self.part.at[self.cross], self.far, self.base + 2, tensor=self.cross).start()

    def result(self):
        self.links.arrived(self.near, self.base + 1, tensor=self.sib)
        self.links.arrived(self.far, self.base + 2, tensor=self.cross)
        return (
            self.part[self.t].astype(wide) + self.near[...].astype(wide) + self.far[...].astype(wide)
        )

    def finish(self):
        self.links.copy(self.part.at[self.diag], self.pre, self.base, tensor=self.sib).wait_send()
        self.links.copy(self.part.at[self.sib], self.near, self.base + 1, tensor=self.sib).wait_send()
        self.links.copy(self.part.at[self.cross], self.far, self.base + 2, tensor=self.cross).wait_send()


class DataReduce:
    def __init__(self, links, held, whole, share, box, box_at, first, rows, d, count, order):
        self.links, self.held, self.whole = links, held, whole
        bits = count.bit_length() - 1
        assert count == 1 << bits and bits >= 3
        self.extra = [b for b in range(bits) if b not in order]
        self.d, self.order = d, order
        self.region = (first, rows, 0, held.shape[1])
        self.trail, self.sent, self.boxes = [], [], []
        for tall, broad in self.sizes(rows, held.shape[1], count)[0]:
            self.boxes.append(box.at[pl.ds(box_at, tall), pl.ds(0, broad)])
            box_at += tall
        self.share = share.at[pl.ds(0, tall), pl.ds(0, broad)]
        self.base = links.take(7 + len(self.extra))
        self.steps = [lambda: self._send_half(0)]
        for k in (1, 2):
            self.steps.append(lambda k=k: (self._add_half(k - 1), self._send_half(k)))
        self.steps.append(lambda: (self._add_half(2), self._swap(), self._place(), self._grow_send(2)))
        for k in (2, 1):
            self.steps.append(lambda k=k: (self._grow_wait(k), self._grow_send(k - 1)))
        self.steps.append(lambda: self._grow_wait(0))

    @staticmethod
    def sizes(rows, columns, count):
        found = []
        for _ in range(3):
            if rows % 32 == 0:
                rows //= 2
            else:
                columns //= 2
            found.append((rows, columns))
        found += found[2:] * (count.bit_length() - 1 - 3)
        return found, sum(size[0] for size in found)

    def _bit(self, b):
        return self.d // (1 << b) % 2

    def _peer(self, b):
        return self.d + (1 - 2 * self._bit(b)) * (1 << b)

    def _start(self, copy):
        copy.start()
        self.sent.append(copy)

    @staticmethod
    def _view(ref, region):
        row, rows, column, columns = region
        if columns == ref.shape[1]:
            return ref.at[pl.ds(row, rows)]
        return ref.at[pl.ds(row, rows), pl.ds(column, columns)]

    @staticmethod
    def _part(region, bit):
        row, rows, column, columns = region
        if rows % 32 == 0:
            return (pl.multiple_of(row + bit * (rows // 2), 16), rows // 2, column, columns)
        return (row, rows, pl.multiple_of(column + bit * (columns // 2), 128), columns // 2)

    def _send_half(self, k):
        b = self.order[k]
        bit = self._bit(b)
        self.trail.append(self.region)
        view = self._view(self.held, self._part(self.region, 1 - bit))
        self._start(self.links.copy(view, self.boxes[k], self.base + k, dp=self._peer(b)))
        self.region = self._part(self.region, bit)

    def _add_half(self, k):
        self.links.arrived(self.boxes[k], self.base + k, dp=self._peer(self.order[k]))
        view = self._view(self.held, self.region)
        total = (view[...].astype(wide) + self.boxes[k][...].astype(wide)).astype(low)
        if k == 2:
            self.share[...] = total
        else:
            view[...] = total

    def _swap(self):
        for k, b in enumerate(self.extra):
            box, at = self.boxes[3 + k], self.base + 7 + k
            copy = self.links.copy(self.share, box, at, dp=self._peer(b))
            copy.start()
            self.links.arrived(box, at, dp=self._peer(b))
            copy.wait_send()
            self.share[...] = (self.share[...].astype(wide) + box[...].astype(wide)).astype(low)

    def _place(self):
        self.placed = pltpu.make_async_copy(
            self.share, self._view(self.whole, self.region), self.links.send.at[self.base + 6]
        )
        self.placed.start()

    def _grow_send(self, k):
        view = self._view(self.whole, self.region)
        src = self.share if k == 2 else view
        self._start(self.links.copy(src, view, self.base + 3 + k, dp=self._peer(self.order[k])))

    def _grow_wait(self, k):
        if k == 2:
            self.placed.wait()
        b = self.order[k]
        view = self._view(self.whole, self._part(self.trail[k], 1 - self._bit(b)))
        self.links.arrived(view, self.base + 3 + k, dp=self._peer(b))
        self.region = self.trail[k]

    def step(self):
        if self.steps:
            self.steps.pop(0)()

    def finish(self):
        assert not self.steps
        for copy in self.sent:
            copy.wait_send()


class Pipeline:
    def __init__(self, plan):
        self.plan, self.members = plan, []

    def add(self, member):
        self.members.append(member)
        member.step()

    def at(self, place):
        for number in self.plan[place]:
            self.members[number].step()

    def finish(self):
        self.at("end")
        for m in self.members:
            while m.steps:
                m.step()
            m.finish()


PLAN = dict(
    waiting=(),
    shared=(0, 1),
    h0p0=(2, 3),
    h0p2=(0, 1),
    h0=(2, 3),
    h1p0=(0,),
    h1p2=(1, 4, 2),
    h1=(3,),
    h2p0=(4, 0),
    h2p2=(),
    h2=(5, 1, 6),
    led=(2, 0),
    crossing=(3, 7, 6, 4, 5, 1, 2, 7, 6, 4, 5, 0),
    told=(3, 1, 7, 6),
    end=(5, 2, 4, 3, 7, 6, 5, 4, 7, 6, 5, 7),
)


class Everyone:
    def __init__(self, links, buf, me, count, device):
        self.links, self.buf, self.me, self.count, self.device = links, buf, me, count, device
        self.base = links.take(count)

    def _copy(self, j):
        slot = self.buf.at[self.me]
        peer = self.device(lax.rem(self.me + j, self.count))
        return self.links.copy(slot, slot, self.base + j, dp=peer)

    def _loop(self, act):
        def one(j, carry):
            act(j)
            return carry

        lax.fori_loop(1, self.count, one, 0)

    def start(self, values):
        self.buf[self.me] = values
        self._loop(lambda j: self._copy(j).start())

    def _hear(self, j):
        peer = lax.rem(self.me + self.count - j, self.count)
        self.links.arrived(self.buf.at[peer], self.base + j, dp=self.device(peer))

    def result(self):
        self._loop(self._hear)
        return lax.fori_loop(1, self.count, lambda j, acc: acc + self.buf[j], self.buf[0])

    def finish(self):
        self._loop(lambda j: self._copy(j).wait_send())


def greet(axis, me, count):
    barrier = pltpu.get_barrier_semaphore()

    def one(j, carry):
        pl.semaphore_signal(
            barrier, inc=1, device_id={axis: lax.rem(me + j, count)}, device_id_type=MESH
        )
        return carry

    lax.fori_loop(1, count, one, 0)


def await_greetings(amount):
    pl.semaphore_wait(pltpu.get_barrier_semaphore(), amount)


def halves(rows):
    first = round_up(rows // 2, 16)
    return ((0, first), (first, rows - first))


def head_masks(shape, local_heads):
    lane = lax.broadcasted_iota(jnp.int32, shape, 1)
    return [
        jnp.where((lane >= h * HEAD_DIM) & (lane < (h + 1) * HEAD_DIM), 1.0, 0.0)
        for h in range(local_heads)
    ], lane


def kernel(n, S):
    links = Links(S.send, S.recv)
    t = lax.axis_index("tensor")
    d = lax.axis_index("dp")
    greet("tensor", t, 4)
    greet("dp", d, n.dp)
    R, own, W, H, D, K = n.R, n.own, n.W, n.H, n.D, n.K
    vector = lambda ref: ref[...].reshape(1, D)

    fetch = pltpu.make_async_copy(S.cot, S.gt, S.local)
    fetch.start()
    S.a1[t] = jnp.zeros((R, D), low)
    S.cot4[t] = jnp.zeros((R, D), low)
    S.a24[t] = jnp.zeros((R, D), low)
    S.hl4[t] = jnp.zeros((R, D), low)
    unit, _ = standardize(S.x[...].astype(wide))
    S.a1[t, 0:own, :] = (unit * vector(S.g1) + vector(S.b1)).astype(low)
    fetch.wait()
    S.cot4[t, 0:own, :] = S.gt[...].astype(low)
    S.ow4[t] = S.ow[...]
    await_greetings(3 + n.dp - 1)
    rows_in = Gather(links, S.a1, t, halves(R))
    cot_in = Gather(links, S.cot4, t, halves(R))
    ow_in = Gather(links, S.ow4, t, ((0, W),))
    rows_in.start()
    S.gw[0:D, :] = jnp.transpose(S.wup[...])
    S.gw[D:, :] = jnp.transpose(S.wdn[...])
    S.v[4 * R :, :] = jnp.zeros((K - 4 * R, H), low)
    length = S.lengths[0]

    chip = t // 2

    def project(i, carry):
        s = flipped(t, i // 2, i % 2)

        @pl.when(i == 1)
        def _():
            rows_in.wait_sib()

        @pl.when(i == 2)
        def _():
            rows_in.forward()
            ow_in.start()

        @pl.when(i == 3)
        def _():
            rows_in.wait_diag()

        slab = S.a1[s]
        lane = lax.broadcasted_iota(jnp.int32, (R, H - W), 1)
        row = lax.broadcasted_iota(jnp.int32, (R, H - W), 0)
        absent = (row >= own) | (row + s * own >= length)
        at = pl.ds(pl.multiple_of(s * R, 16), R)
        out = dot_rows(slab, S.wqkv[0]) + S.bq[0:1, :]
        S.q[s, :, :W] = (out.astype(low).astype(wide) * HEAD_DIM**-0.5).astype(low)
        S.q[s, :, W:] = jnp.where(lane == 0, HEAD_DIM**-0.5, 0.0).astype(low)
        S.k[at, :W] = dot_rows(slab, S.wqkv[1]).astype(low)
        S.k[at, W:] = jnp.where((lane == 0) & absent, -8e30, 0.0).astype(low)
        S.v[at, :W] = (dot_rows(slab, S.wqkv[2]) + S.bq[1:2, :]).astype(low)
        S.v[at, W:] = jnp.where(lane < 2, 1.0, 0.0).astype(low)
        return carry

    lax.fori_loop(0, 4, project, 0)
    if K > 4 * R:
        lane = lax.broadcasted_iota(jnp.int32, (K - 4 * R, H), 1)
        S.k[4 * R :, :] = jnp.where(lane == W, -8e30, 0.0).astype(low)
    S.kt[...] = jnp.transpose(S.k[...])
    S.vt[...] = jnp.transpose(S.v[...])

    masks, lane = head_masks((1, H), n.heads)
    mix_base = links.take(3)

    peers = [flipped(t, 1, 0), flipped(t, 1, 1), flipped(t, 0, 1)]

    def attend(i, carry):
        s = flipped(t, 1 - i // 2, (i + i // 2) % 2)
        query = S.q[s]
        mixed = jnp.zeros((R, H), wide)
        inverse = jnp.zeros((R, 128), wide)
        first = lax.broadcasted_iota(jnp.int32, (1, 128), 1)

        def score(h):
            here = jnp.where(lane == W, 1.0, masks[h]).astype(low)
            return dot(query * here, S.kt[...])

        ready = score(0)
        for h in range(n.heads):
            scores = ready
            if h + 1 < n.heads:
                ready = score(h + 1)
            terms = jnp.exp(scores - jnp.max(scores, -1, keepdims=True)).astype(low)
            S.e[h, s] = terms
            part = dot(terms, S.v[...])
            scale = 1.0 / part[:, W : W + 1]
            mixed += part * (scale * masks[h])
            inverse = jnp.where(first == h, scale, inverse)
        S.o[s] = mixed
        S.inv[s] = inverse
        S.mix[s] = mixed[:, :W].astype(low)

        @pl.when(i < 3)
        def _():
            links.copy(S.mix.at[s], S.mix4.at[t], mix_base + i, tensor=s).start()

        @pl.when(i == 1)
        def _():
            cot_in.start()

        @pl.when(i == 2)
        def _():
            ow_in.wait_sib()
            ow_in.forward()

        return carry

    lax.fori_loop(0, 4, attend, 0)
    ow_in.wait_diag()
    S.mix4[t] = S.mix[t]
    for j, s in enumerate(peers):
        links.arrived(S.mix4.at[s], mix_base + j, tensor=s)

    total = dot(S.mix4[0], S.ow4[0])
    for j in range(1, 4):
        total += dot(S.mix4[j], S.ow4[j])
    total = S.x[...].astype(wide) + (total[:own] + vector(S.ob))
    S.hid[...] = total
    unit, _ = standardize(total)
    S.a24[t, 0:own, :] = (unit * vector(S.g2) + vector(S.b2)).astype(low)
    next_in = Gather(links, S.a24, t, halves(R))
    next_in.start()
    back = Reduce(links, S.part, S.pre1, S.near1, S.far1, t)
    ahead = Reduce(links, S.fop, S.pre2, S.near2, S.far2, t)
    S.gub[...] = jnp.zeros_like(S.gub)

    def feed(i, carry):
        s = flipped(t, i // 2, i % 2)

        @pl.when(i == 1)
        def _():
            next_in.wait_sib()
            cot_in.wait_sib()

        @pl.when(i == 2)
        def _():
            cot_in.forward()
            next_in.forward()

        @pl.when(i == 3)
        def _():
            next_in.wait_diag()
            cot_in.wait_diag()

        up = dot(S.a24[s], S.wup[...]) + vector(S.bup)
        square = up * up
        c = 0.7978845608028654
        bend = jnp.tanh(c * up * (1.0 + 0.044715 * square))
        half = 0.5 * (1.0 + bend)
        slope = half + 0.5 * up * (1.0 - bend * bend) * (c + (3 * 0.044715 * c) * square)
        active = (up * half).astype(low)
        S.pool[s, :, 0:D] = active
        grad = (dot(S.cot4[s], S.gw[D:, :]) * slope).astype(low)
        S.gup[s] = grad
        S.part[s] = dot(grad, S.gw[0:D, :]).astype(low)

        @pl.when(i == 1)
        def _():
            back.send_sib()

        @pl.when(i == 3)
        def _():
            back.send_diag()

        S.fop[s] = dot(active, S.wdn[...]).astype(low)

        @pl.when(i == 1)
        def _():
            ahead.send_sib()

        @pl.when(i == 3)
        def _():
            ahead.send_diag()

        S.gub[...] += jnp.sum(grad.astype(wide), 0, keepdims=True)
        return carry

    lax.fori_loop(0, 4, feed, 0)
    back.send_cross()

    sums = Pipeline(PLAN)
    tile = D // 2
    box_at = share_at = 0

    def sum_over_dp(held, whole, first, rows, order):
        nonlocal box_at, share_at
        sizes, taken = DataReduce.sizes(rows, D, n.dp)
        share = S.share.at[pl.ds(share_at, sizes[2][0])]
        sums.add(DataReduce(links, held, whole, share, S.box, box_at, first, rows, d, n.dp, order))
        box_at, share_at = box_at + taken, share_at + sizes[2][0]

    for left, right, first in ((S.a24, S.gup, 0), (S.pool, S.cot4, D)):
        rows = left[:, :, 0:D].reshape(4 * R, D)
        S.gw[first : first + D, :] = dot_columns(rows, flat(right)).astype(low)
        for at in (first, first + tile):
            sum_over_dp(S.gw, S.whole1, at, tile, (0, 1, 2) if at == first else (1, 0, 2))

    sums.at("waiting")
    grad = back.result()[:own]
    unit, inverse = standardize(S.hid[...])
    S.small[...] = jnp.zeros_like(S.small)
    S.small[2:3, :] = jnp.sum(grad * unit, 0, keepdims=True)
    S.small[3:4, :] = jnp.sum(grad, 0, keepdims=True)
    S.gt[...] += norm_back(grad, unit, inverse, vector(S.g2))
    S.hl4[t, 0:own, :] = S.gt[...].astype(low)
    S.small[4:5, :] = jnp.sum(S.hl4[t].astype(wide), 0, keepdims=True)
    S.small[5:6, :] = jnp.sum(S.cot4[t].astype(wide), 0, keepdims=True)
    S.small[6:7, :] = S.gub[...]
    gm_base = links.take(3)

    for j, s in enumerate(peers + [t]):
        S.mix4[s] = dot_rows(S.hl4[t], S.ow4[s]).astype(low)
        if j < 3:
            links.copy(S.mix4.at[s], S.gm4.at[t], gm_base + j, tensor=s).start()
    S.gm4[t] = S.mix4[t]
    hl_in = Gather(links, S.hl4, t, halves(R))

    next_in.finish()
    S.do[...] = jnp.zeros_like(S.do)
    S.qt[...] = jnp.transpose(flat(S.q))
    sums.at("shared")

    def prepare(i, s):
        if i > 0:
            j = (None, 2, 0, 1)[i]
            links.arrived(S.gm4.at[s], gm_base + j, tensor=peers[j])
        S.do[:, :W] = S.gm4[s].astype(wide)
        inverse = sum(S.inv[s, :, h : h + 1] * masks[h] for h in range(n.heads))
        scaled = (S.do[...] * inverse).astype(low)
        S.v[pl.ds(pl.multiple_of(s * R, 16), R), :] = scaled
        scaled = scaled.astype(wide)
        product = scaled * S.o[s]
        for h in range(n.heads):
            inner = -jnp.sum(product * masks[h], -1, keepdims=True)
            upper = inner.astype(low).astype(wide)
            S.a24[s, :, h * H : (h + 1) * H] = (
                scaled * masks[h]
                + jnp.where(lane == W, upper, 0.0)
                + jnp.where(lane == W + 1, inner - upper, 0.0)
            ).astype(low)

    def pull(h, p):
        grad_p = dot(pair(S.a24.at[:, :, h * H : (h + 1) * H], p), S.vt[...])
        grad_s = (pair(S.e.at[h], p).astype(wide) * grad_p).astype(low)
        set_pair(S.pool, p, grad_s)
        dq = dot(grad_s, S.k[...]) * (masks[h] * HEAD_DIM**-0.5)
        if h > 0:
            dq += pair(S.gup.at[:, :, 0:H], p).astype(wide)
        S.gup[pl.ds(2 * p, 2), :, 0:H] = dq.astype(low).reshape(2, R, H)

    for h in range(n.heads):
        for i in (0, 2):
            if h == 0:
                prepare(i, flipped(t, i // 2, 0))
                prepare(i + 1, flipped(t, i // 2, 1))
            if (h, i) == (0, 2):
                hl_in.start()
            pull(h, (chip + i // 2) % 2)
            sums.at(f"h{h}p{i}")
            if (h, i) == (1, 0):
                hl_in.wait_sib()
                hl_in.forward()
                ahead.send_cross()
            elif (h, i) == (1, 2):
                hl_in.wait_diag()
                S.gw2[3 * W :, :] = dot_columns(flat(S.mix), flat(S.hl4)).astype(low)
                sum_over_dp(S.gw2, S.whole2, 3 * W, W, (1, 0, 2))
        if h == 0:
            S.v[4 * R :, :] = jnp.zeros((K - 4 * R, H), low)
            S.kt[...] = jnp.transpose(S.v[...])
        at = slice(h * HEAD_DIM, (h + 1) * HEAD_DIM)
        S.dk[at, :] = dot(S.qt[at, :], flat(S.pool)).astype(low)
        S.dv[at, :] = dot(S.kt[at, : 4 * R], flat(S.e.at[h])).astype(low)
        tile = h * HEAD_DIM // 128 * 128
        dqt = jnp.transpose(flat(S.gup.at[:, :, tile : tile + 128]))
        left = jnp.concatenate(
            [dqt[h * HEAD_DIM - tile : (h + 1) * HEAD_DIM - tile], S.dk[at, : 4 * R], S.dv[at, : 4 * R]], 0
        )
        S.gw2[h * W : (h + 1) * W, :] = dot(left, flat(S.a1)).astype(low)
        sum_over_dp(S.gw2, S.whole2, h * W, W, (0, 1, 2) if h in (1, 2) else (1, 0, 2))
        sums.at(f"h{h}")

    pad = jnp.zeros((R, H - W), low)
    for part, grad_t in ((1, S.dk), (2, S.dv)):
        rows = jnp.transpose(grad_t[...])
        for s in range(4):
            S.gup[s, :, part * H : part * H + W] = rows[s * R : (s + 1) * R]
            S.gup[s, :, part * H + W : (part + 1) * H] = pad

    back.finish()
    down = Reduce(links, S.part, S.pre1, S.near1, S.far1, t)

    def lead(i, carry):
        s = flipped(t, 1 - i // 2, 1 - i % 2)
        out = dot(S.gup[s, :, 0:W], S.wqkv[0])
        out += dot(S.gup[s, :, H : H + W], S.wqkv[1])
        out += dot(S.gup[s, :, 2 * H : 2 * H + W], S.wqkv[2])
        S.part[s] = out.astype(low)

        @pl.when(i == 0)
        def _():
            down.send_diag()

        @pl.when(i == 2)
        def _():
            down.send_sib()
            down.send_cross()

        return carry

    lax.fori_loop(0, 4, lead, 0)
    sums.at("led")
    S.small[7:8, 0:H] = jnp.sum(flat(S.gup.at[:, :, 0:H]).astype(wide), 0, keepdims=True)
    S.small[7:8, H : 2 * H] = jnp.sum(
        flat(S.gup.at[:, :, 2 * H : 3 * H]).astype(wide), 0, keepdims=True
    )
    S.output[...] = (S.hid[...] + (ahead.result()[:own] + vector(S.db))).astype(low)
    sums.at("crossing")

    unit, inverse = standardize(S.x[...].astype(wide))
    grad = down.result()[:own]
    S.small[0:1, :] = jnp.sum(grad * unit, 0, keepdims=True)
    S.small[1:2, :] = jnp.sum(grad, 0, keepdims=True)
    S.small4[t] = S.small[...]
    base3 = links.take(3)
    for j in range(3):
        peer = lax.rem(t + j + 1, 4)
        links.start(S.small4.at[t], S.small4.at[t], base3 + j, tensor=peer)
    S.gt[...] += norm_back(grad, unit, inverse, vector(S.g1))
    sums.at("told")
    for j in range(3):
        peer = lax.rem(t + 3 - j, 4)
        links.arrived(S.small4.at[peer], base3 + j, tensor=peer)
    over = S.small4[0] + S.small4[1] + S.small4[2] + S.small4[3]
    row = lax.broadcasted_iota(jnp.int32, over.shape, 0)
    near = min(8, n.dp)
    inner = Everyone(links, S.smalls, d % near, near, lambda j: d // near * near + j)
    inner.start(jnp.where(row < 6, over, S.small[...]))
    sums.finish()
    total = inner.result()
    inner.finish()
    if n.dp > near:
        outer = Everyone(links, S.smalls2, d // near, n.dp // near, lambda j: j * near + d % near)
        outer.start(total)
        total = outer.result()
        outer.finish()
    S.small_sum[...] = total
    for j, s in enumerate(peers):
        links.copy(S.mix.at[s], S.mix4.at[t], mix_base + j, tensor=s).wait_send()
        links.copy(S.mix4.at[s], S.gm4.at[t], gm_base + j, tensor=s).wait_send()
    for transfer in (rows_in, cot_in, ow_in, hl_in, ahead, down):
        transfer.finish()
    links.finish()


SMALL = ("gain1", "shift1", "gain2", "shift2", "bias_out", "bias_down", "bias_up", "bias_qv")


def finish(n, output, gt, small, whole1, whole2):
    D, W, H = n.D, n.W, n.H
    steps = 2 * n.heads
    rows1, rows2 = D // steps, HEAD_DIM // 2

    def spread(output, gt, small, up, down, q, k, v, out, *refs):
        to_output, to_gt, to_up, to_down, to_qkv, to_out = refs[:6]
        vectors, sems = refs[6:14], refs[14]
        i = pl.program_id(0)
        passed = [
            pltpu.make_async_copy(output, to_output, sems.at[0]),
            pltpu.make_async_copy(gt, to_gt, sems.at[1]),
        ]

        @pl.when(i == 0)
        def _():
            for copy in passed:
                copy.start()
            for j in range(7):
                vectors[j][...] = small[j : j + 1, :].reshape(D)
            vectors[7][0:1, :] = small[7:8, :W]
            vectors[7][1:2, :] = small[7:8, H : H + W]

        to_up[...] = up[...].astype(wide)
        to_down[...] = down[...].astype(wide)
        for j, part in enumerate((q, k, v)):
            to_qkv[j] = part[...].astype(wide)
        to_out[...] = out[...].astype(wide)

        @pl.when(i == steps - 1)
        def _():
            for copy in passed:
                copy.wait()

    hbm = pl.BlockSpec(memory_space=pl.ANY)
    whole = pl.BlockSpec(memory_space=pltpu.VMEM)
    at_row = lambda rows, index: pl.BlockSpec((rows, D), lambda i: (index(i), 0))
    of_part = lambda j: at_row(rows2, lambda i: i // 2 * 6 + j * 2 + i % 2)
    shape = jax.ShapeDtypeStruct
    return pl.pallas_call(
        spread,
        grid=(steps,),
        out_shape=[shape(output.shape, low), shape(gt.shape, wide)]
        + [shape((D, D), wide)] * 2
        + [shape((3, W, D), wide), shape((W, D), wide)]
        + [shape((D,), wide)] * 7
        + [shape((2, W), wide)],
        in_specs=[hbm, hbm, whole, at_row(rows1, lambda i: i), at_row(rows1, lambda i: i + steps)]
        + [of_part(j) for j in range(3)]
        + [at_row(rows2, lambda i: 3 * steps + i)],
        out_specs=[hbm, hbm]
        + [at_row(rows1, lambda i: i)] * 2
        + [pl.BlockSpec((3, rows2, D), lambda i: (0, i, 0)), at_row(rows2, lambda i: i)]
        + [whole] * 8,
        scratch_shapes=[pltpu.SemaphoreType.DMA((2,))],
    )(output, gt, small, whole1, whole1, whole2, whole2, whole2, whole2)


def body(
    tokens,
    lengths,
    ln1_gain,
    ln1_shift,
    qkv_weight,
    qv_bias,
    out_weight,
    out_bias,
    ln2_gain,
    ln2_shift,
    up_weight,
    up_bias,
    down_weight,
    down_bias,
    cotangent,
):
    own, D = tokens.shape
    W = qkv_weight.shape[2]
    F = up_weight.shape[1]
    dp = lax.axis_size("dp")
    assert lax.axis_size("tensor") == 4 and lengths.shape[0] == 1 and F == D and 4 * W == D and 3 * round_up(W + 2, 128) == D
    R = round_up(own, 16)
    H = round_up(W + 2, 128)
    K = round_up(4 * R, 256)
    heads = W // HEAD_DIM
    extra = dp.bit_length() - 1 - 3
    n = types.SimpleNamespace(
        own=own, D=D, W=W, R=R, H=H, K=K, dp=dp, heads=heads, extra=extra
    )
    given = dict(
        x=tokens, lengths=lengths, g1=ln1_gain, b1=ln1_shift,
        wqkv=jnp.transpose(qkv_weight, (1, 2, 0)), bq=qv_bias, ow=out_weight, ob=out_bias,
        g2=ln2_gain, b2=ln2_shift, wup=up_weight, bup=up_bias, wdn=down_weight, db=down_bias,
        cot=cotangent,
    )
    outs = dict(
        output=((own, D), low), gt=((own, D), wide), small_sum=((8, D), wide),
        whole1=((2 * D, D), low), whole2=((D, D), low),
    )
    rows4 = ((4, R, D), low)
    slab = ((R, D), low)
    chunks = [D // 2] * 4 + [W] * 4
    scratch = dict(
        a1=rows4, cot4=rows4, ow4=((4, W, D), low), q=((4, R, H), low), k=((K, H), low),
        v=((K, H), low), kt=((H, K), low), vt=((H, K), low), e=((heads, 4, R, K), low),
        o=((4, R, H), wide), inv=((4, R, 128), wide), mix=((4, R, W), low), mix4=((4, R, W), low),
        hid=((own, D), wide),
        a24=rows4, pool=((4, R, K), low), gup=rows4, part=rows4,
        fop=rows4, pre1=slab, near1=slab, far1=slab, pre2=slab, near2=slab, far2=slab,
        gw=((2 * D, D), low), gub=((1, D), wide),
        small=((8, D), wide), hl4=rows4,
        gm4=((4, R, W), low), dk=((W, K), low), dv=((W, K), low), qt=((H, 4 * R), low), do=((R, H), wide),
        gw2=((D, D), low),
        small4=((4, 8, D), wide), smalls=((min(8, dp), 8, D), wide),
        box=((sum(DataReduce.sizes(r, D, dp)[1] for r in chunks), D), low),
        share=((sum(DataReduce.sizes(r, D, dp)[0][2][0] for r in chunks), D), low),
    )
    if dp > 8:
        scratch["smalls2"] = ((dp // 8, 8, D), wide)
    sems = 140 + dp + 8 * extra
    names = list(given) + list(outs) + list(scratch) + ["local", "send", "recv"]
    vmem = pl.BlockSpec(memory_space=pltpu.VMEM)
    smem = pl.BlockSpec(memory_space=pltpu.SMEM)
    hbm = pl.BlockSpec(memory_space=pl.ANY)
    output, gt, small, whole1, whole2 = pl.pallas_call(
        lambda *refs: kernel(n, types.SimpleNamespace(**dict(zip(names, refs)))),
        out_shape=tuple(jax.ShapeDtypeStruct(*spec) for spec in outs.values()),
        in_specs=[dict(lengths=smem, cot=hbm).get(name, vmem) for name in given],
        out_specs=tuple(hbm if name in ("whole1", "whole2") else vmem for name in outs),
        scratch_shapes=[pltpu.VMEM(*spec) for spec in scratch.values()]
        + [pltpu.SemaphoreType.DMA] + [pltpu.SemaphoreType.DMA((sems,))] * 2,
        compiler_params=pltpu.CompilerParams(
            collective_id=0, has_side_effects=True, vmem_limit_bytes=VMEM_BYTES
        ),
    )(*given.values())
    finished = finish(n, output, gt, small, whole1, whole2)
    small_rows = dict(zip(SMALL, finished[6:]))
    return (
        finished[0],
        finished[1],
        small_rows["gain1"],
        small_rows["shift1"],
        jnp.transpose(finished[4], (2, 0, 1)),
        small_rows["bias_qv"],
        finished[5],
        small_rows["bias_out"],
        small_rows["gain2"],
        small_rows["shift2"],
        finished[2],
        small_rows["bias_up"],
        finished[3],
        small_rows["bias_down"],
    )


def solution(mesh):
    placed = (
        P(("dp", "tensor"), None),
        P("dp"),
        P(),
        P(),
        P(None, None, "tensor"),
        P(None, "tensor"),
        P("tensor", None),
        P(),
        P(),
        P(),
        P(None, "tensor"),
        P("tensor"),
        P("tensor", None),
        P(),
        P(("dp", "tensor"), None),
    )
    return jax.shard_map(
        body,
        mesh=mesh,
        in_specs=placed,
        out_specs=(
            P(("dp", "tensor"), None),
            P(("dp", "tensor"), None),
            P(),
            P(),
            P(None, None, "tensor"),
            P(None, "tensor"),
            P("tensor", None),
            P(),
            P(),
            P(),
            P(None, "tensor"),
            P("tensor"),
            P("tensor", None),
            P(),
        ),
        check_vma=False,
    )
```

```python
import types

import jax
import jax.numpy as jnp
from jax import lax
from jax.experimental import pallas as pl
from jax.experimental.pallas import tpu as pltpu
from jax.sharding import PartitionSpec as P

HEAD_DIM = 64
MESH = pl.DeviceIdType.MESH
VMEM_BYTES = 62 * 2**20

epsilon = 1e-06
low = jnp.bfloat16
wide = jnp.float32


def round_up(amount, unit):
    return -(-amount // unit) * unit


def flipped(t, flip_chip, flip_core):
    return (t // 2 + flip_chip) % 2 * 2 + (t % 2 + flip_core) % 2


def dot(left, right):
    return jnp.dot(left, right, preferred_element_type=wide)


def dot_rows(left, right):
    return lax.dot_general(left, right, (((1,), (1,)), ((), ())), preferred_element_type=wide)


def dot_columns(left, right):
    return lax.dot_general(left, right, (((0,), (0,)), ((), ())), preferred_element_type=wide)


def standardize(values):
    center = values - jnp.mean(values, -1, keepdims=True)
    inverse = lax.rsqrt(jnp.mean(center * center, -1, keepdims=True) + epsilon)
    return center * inverse, inverse


def norm_back(grad, unit, inverse, gain):
    scaled = grad * gain
    return inverse * (
        scaled
        - jnp.mean(scaled, -1, keepdims=True)
        - unit * jnp.mean(scaled * unit, -1, keepdims=True)
    )


def pair(ref, p):
    _, rows, columns = ref.shape
    return ref[pl.ds(2 * p, 2)].reshape(2 * rows, columns)


def set_pair(ref, p, values):
    ref[pl.ds(2 * p, 2)] = values.reshape(2, -1, values.shape[1])


def flat(ref):
    a, b, c = ref.shape
    return ref[...].reshape(a * b, c)


class Links:
    def __init__(self, send, recv):
        self.send, self.recv, self.used, self.pending = send, recv, 0, []

    def take(self, amount=1):
        base = self.used
        self.used += amount
        assert self.used <= self.send.shape[0]
        return base

    def copy(self, src, dst, at, **where):
        return pltpu.make_async_remote_copy(
            src_ref=src,
            dst_ref=dst,
            send_sem=self.send.at[at],
            recv_sem=self.recv.at[at],
            device_id=where,
            device_id_type=MESH,
        )

    def start(self, src, dst, at, **where):
        copy = self.copy(src, dst, at, **where)
        copy.start()
        self.pending.append(copy)

    def arrived(self, dst, at, **where):
        self.copy(dst, dst, at, **where).wait_recv()

    def finish(self):
        for copy in self.pending:
            copy.wait_send()
        self.pending = []


class Gather:
    def __init__(self, links, buf, t, parts):
        self.links, self.buf, self.t, self.parts = links, buf, t, parts
        self.sib, self.cross, self.diag = flipped(t, 0, 1), flipped(t, 1, 0), flipped(t, 1, 1)
        self.base = links.take(3 * len(parts))

    def view(self, slot, part):
        start, size = self.parts[part]
        return self.buf.at[slot, pl.ds(start, size)]

    def _each(self):
        return range(len(self.parts))

    def start(self):
        for p in self._each():
            v = self.view(self.t, p)
            self.links.copy(v, v, self.base + 3 * p, tensor=self.cross).start()
        for p in self._each():
            v = self.view(self.t, p)
            self.links.copy(v, v, self.base + 3 * p + 1, tensor=self.sib).start()

    def wait_sib(self):
        for p in self._each():
            self.links.arrived(self.view(self.sib, p), self.base + 3 * p + 1, tensor=self.sib)

    def forward(self):
        for p in self._each():
            v = self.view(self.cross, p)
            self.links.arrived(v, self.base + 3 * p, tensor=self.cross)
            self.links.copy(v, v, self.base + 3 * p + 2, tensor=self.sib).start()

    def wait_diag(self):
        for p in self._each():
            self.links.arrived(self.view(self.diag, p), self.base + 3 * p + 2, tensor=self.sib)

    def finish(self):
        for p in self._each():
            v = self.view(self.t, p)
            self.links.copy(v, v, self.base + 3 * p, tensor=self.cross).wait_send()
            self.links.copy(v, v, self.base + 3 * p + 1, tensor=self.sib).wait_send()
            v = self.view(self.cross, p)
            self.links.copy(v, v, self.base + 3 * p + 2, tensor=self.sib).wait_send()


class Reduce:
    def __init__(self, links, part, pre, near, far, t):
        self.links, self.part, self.pre, self.near, self.far, self.t = links, part, pre, near, far, t
        self.sib, self.cross, self.diag = flipped(t, 0, 1), flipped(t, 1, 0), flipped(t, 1, 1)
        self.base = links.take(3)

    def send_diag(self):
        self.links.copy(self.part.at[self.diag], self.pre, self.base, tensor=self.sib).start()

    def send_sib(self):
        self.links.copy(self.part.at[self.sib], self.near, self.base + 1, tensor=self.sib).start()

    def send_cross(self):
        self.links.arrived(self.pre, self.base, tensor=self.sib)
        total = self.part[self.cross].astype(wide) + self.pre[...].astype(wide)
        self.part[self.cross] = total.astype(low)
        self.links.copy(self.part.at[self.cross], self.far, self.base + 2, tensor=self.cross).start()

    def result(self):
        self.links.arrived(self.near, self.base + 1, tensor=self.sib)
        self.links.arrived(self.far, self.base + 2, tensor=self.cross)
        return (
            self.part[self.t].astype(wide) + self.near[...].astype(wide) + self.far[...].astype(wide)
        )

    def finish(self):
        self.links.copy(self.part.at[self.diag], self.pre, self.base, tensor=self.sib).wait_send()
        self.links.copy(self.part.at[self.sib], self.near, self.base + 1, tensor=self.sib).wait_send()
        self.links.copy(self.part.at[self.cross], self.far, self.base + 2, tensor=self.cross).wait_send()


class DataReduce:
    def __init__(self, links, held, whole, out, box, box_at, first, rows, d, count, order):
        self.links, self.held, self.whole, self.out = links, held, whole, out
        bits = count.bit_length() - 1
        assert count == 1 << bits and bits >= 3
        self.extra = [b for b in range(bits) if b not in order]
        self.d, self.order = d, order
        self.region = (first, rows, 0, held.shape[1])
        self.trail, self.sent, self.boxes = [], [], []
        for tall, broad in self.sizes(rows, held.shape[1], count)[0]:
            self.boxes.append(box.at[pl.ds(box_at, tall), pl.ds(0, broad)])
            box_at += tall
        self.base = links.take(7 + len(self.extra))
        self.steps = [lambda: self._send_half(0)]
        for k in (1, 2):
            self.steps.append(lambda k=k: (self._add_half(k - 1), self._send_half(k)))
        self.steps.append(lambda: (self._add_half(2), self._swap(), self._grow_send(2)))
        for k in (2, 1):
            self.steps.append(lambda k=k: (self._grow_wait(k), self._grow_send(k - 1)))
        self.steps.append(lambda: (self._grow_wait(0), self._leave()))

    @staticmethod
    def sizes(rows, columns, count):
        found = []
        for _ in range(3):
            if rows % 32 == 0:
                rows //= 2
            else:
                columns //= 2
            found.append((rows, columns))
        found += found[2:] * (count.bit_length() - 1 - 3)
        return found, sum(size[0] for size in found)

    def _bit(self, b):
        return self.d // (1 << b) % 2

    def _peer(self, b):
        return self.d + (1 - 2 * self._bit(b)) * (1 << b)

    def _start(self, copy):
        copy.start()
        self.sent.append(copy)

    @staticmethod
    def _view(ref, region):
        row, rows, column, columns = region
        if columns == ref.shape[1]:
            return ref.at[pl.ds(row, rows)]
        return ref.at[pl.ds(row, rows), pl.ds(column, columns)]

    @staticmethod
    def _part(region, bit):
        row, rows, column, columns = region
        if rows % 32 == 0:
            return (pl.multiple_of(row + bit * (rows // 2), 16), rows // 2, column, columns)
        return (row, rows, pl.multiple_of(column + bit * (columns // 2), 128), columns // 2)

    def _send_half(self, k):
        b = self.order[k]
        bit = self._bit(b)
        self.trail.append(self.region)
        view = self._view(self.held, self._part(self.region, 1 - bit))
        self._start(self.links.copy(view, self.boxes[k], self.base + k, dp=self._peer(b)))
        self.region = self._part(self.region, bit)

    def _add_half(self, k):
        self.links.arrived(self.boxes[k], self.base + k, dp=self._peer(self.order[k]))
        view = self._view(self.held, self.region)
        total = (view[...].astype(wide) + self.boxes[k][...].astype(wide)).astype(low)
        if k == 2:
            view = self._view(self.whole, self.region)
        view[...] = total

    def _swap(self):
        view = self._view(self.whole, self.region)
        for k, b in enumerate(self.extra):
            box, at = self.boxes[3 + k], self.base + 7 + k
            copy = self.links.copy(view, box, at, dp=self._peer(b))
            copy.start()
            self.links.arrived(box, at, dp=self._peer(b))
            copy.wait_send()
            view[...] = (view[...].astype(wide) + box[...].astype(wide)).astype(low)

    def _grow_send(self, k):
        view = self._view(self.whole, self.region)
        self._start(self.links.copy(view, view, self.base + 3 + k, dp=self._peer(self.order[k])))

    def _grow_wait(self, k):
        b = self.order[k]
        view = self._view(self.whole, self._part(self.trail[k], 1 - self._bit(b)))
        self.links.arrived(view, self.base + 3 + k, dp=self._peer(b))
        self.region = self.trail[k]

    def _leave(self):
        rows = pl.ds(self.region[0], self.region[1])
        self.left = pltpu.make_async_copy(
            self.whole.at[rows], self.out.at[rows], self.links.send.at[self.base + 6]
        )
        self.left.start()

    def step(self):
        if self.steps:
            self.steps.pop(0)()

    def finish(self):
        assert not self.steps
        self.left.wait()
        for copy in self.sent:
            copy.wait_send()


class Pipeline:
    def __init__(self, plan):
        self.plan, self.members = plan, []

    def add(self, member):
        self.members.append(member)
        member.step()

    def at(self, place):
        for number in self.plan[place]:
            self.members[number].step()

    def finish(self):
        self.at("end")
        for m in self.members:
            while m.steps:
                m.step()
            m.finish()


PLAN = dict(
    waiting=(),
    shared=(0, 1),
    h0p0=(2, 3),
    h0p2=(0, 1),
    h0=(2, 3),
    h1p0=(0,),
    h1p2=(1, 4, 2),
    h1=(3,),
    h2p0=(4, 0),
    h2p2=(),
    h2=(5, 1, 6),
    led=(2, 0),
    crossing=(3, 7, 6, 4, 5, 1, 2, 7, 6, 4, 5, 0),
    told=(3, 1, 7, 6),
    end=(5, 2, 4, 3, 7, 6, 5, 4, 7, 6, 5, 7),
)


class Everyone:
    def __init__(self, links, buf, me, count, device):
        self.links, self.buf, self.me, self.count, self.device = links, buf, me, count, device
        self.base = links.take(count)

    def _copy(self, j):
        slot = self.buf.at[self.me]
        peer = self.device(lax.rem(self.me + j, self.count))
        return self.links.copy(slot, slot, self.base + j, dp=peer)

    def _loop(self, act):
        def one(j, carry):
            act(j)
            return carry

        lax.fori_loop(1, self.count, one, 0)

    def start(self, values):
        self.buf[self.me] = values
        self._loop(lambda j: self._copy(j).start())

    def _hear(self, j):
        peer = lax.rem(self.me + self.count - j, self.count)
        self.links.arrived(self.buf.at[peer], self.base + j, dp=self.device(peer))

    def result(self):
        self._loop(self._hear)
        return lax.fori_loop(1, self.count, lambda j, acc: acc + self.buf[j], self.buf[0])

    def finish(self):
        self._loop(lambda j: self._copy(j).wait_send())


def greet(axis, me, count):
    barrier = pltpu.get_barrier_semaphore()

    def one(j, carry):
        pl.semaphore_signal(
            barrier, inc=1, device_id={axis: lax.rem(me + j, count)}, device_id_type=MESH
        )
        return carry

    lax.fori_loop(1, count, one, 0)


def await_greetings(amount):
    pl.semaphore_wait(pltpu.get_barrier_semaphore(), amount)


def halves(rows):
    first = round_up(rows // 2, 16)
    return ((0, first), (first, rows - first))


def head_masks(shape, local_heads):
    lane = lax.broadcasted_iota(jnp.int32, shape, 1)
    return [
        jnp.where((lane >= h * HEAD_DIM) & (lane < (h + 1) * HEAD_DIM), 1.0, 0.0)
        for h in range(local_heads)
    ], lane


def kernel(n, S):
    links = Links(S.send, S.recv)
    t = lax.axis_index("tensor")
    d = lax.axis_index("dp")
    greet("tensor", t, 4)
    greet("dp", d, n.dp)
    R, own, W, H, D, K = n.R, n.own, n.W, n.H, n.D, n.K
    vector = lambda ref: ref[...].reshape(1, D)

    fetch = pltpu.make_async_copy(S.cot, S.gt, S.local)
    fetch.start()
    S.a1[t] = jnp.zeros((R, D), low)
    S.cot4[t] = jnp.zeros((R, D), low)
    S.a24[t] = jnp.zeros((R, D), low)
    S.hl4[t] = jnp.zeros((R, D), low)
    unit, _ = standardize(S.x[...].astype(wide))
    S.a1[t, 0:own, :] = (unit * vector(S.g1) + vector(S.b1)).astype(low)
    fetch.wait()
    S.cot4[t, 0:own, :] = S.gt[...].astype(low)
    S.ow4[t] = S.ow[...]
    await_greetings(3 + n.dp - 1)
    rows_in = Gather(links, S.a1, t, halves(R))
    cot_in = Gather(links, S.cot4, t, halves(R))
    ow_in = Gather(links, S.ow4, t, ((0, W),))
    rows_in.start()
    S.gw[0:D, :] = jnp.transpose(S.wup[...])
    S.gw[D:, :] = jnp.transpose(S.wdn[...])
    S.v[4 * R :, :] = jnp.zeros((K - 4 * R, H), low)
    length = S.lengths[0]

    chip = t // 2

    def project(i, carry):
        s = flipped(t, i // 2, i % 2)

        @pl.when(i == 1)
        def _():
            rows_in.wait_sib()

        @pl.when(i == 2)
        def _():
            rows_in.forward()
            ow_in.start()

        @pl.when(i == 3)
        def _():
            rows_in.wait_diag()

        slab = S.a1[s]
        lane = lax.broadcasted_iota(jnp.int32, (R, H - W), 1)
        row = lax.broadcasted_iota(jnp.int32, (R, H - W), 0)
        absent = (row >= own) | (row + s * own >= length)
        at = pl.ds(pl.multiple_of(s * R, 16), R)
        out = dot_rows(slab, S.wqkv[0]) + S.bq[0:1, :]
        S.q[s, :, :W] = (out.astype(low).astype(wide) * HEAD_DIM**-0.5).astype(low)
        S.q[s, :, W:] = jnp.where(lane == 0, HEAD_DIM**-0.5, 0.0).astype(low)
        S.k[at, :W] = dot_rows(slab, S.wqkv[1]).astype(low)
        S.k[at, W:] = jnp.where((lane == 0) & absent, -8e30, 0.0).astype(low)
        S.v[at, :W] = (dot_rows(slab, S.wqkv[2]) + S.bq[1:2, :]).astype(low)
        S.v[at, W:] = jnp.where(lane < 2, 1.0, 0.0).astype(low)
        return carry

    lax.fori_loop(0, 4, project, 0)
    if K > 4 * R:
        lane = lax.broadcasted_iota(jnp.int32, (K - 4 * R, H), 1)
        S.k[4 * R :, :] = jnp.where(lane == W, -8e30, 0.0).astype(low)
    S.kt[...] = jnp.transpose(S.k[...])
    S.vt[...] = jnp.transpose(S.v[...])

    masks, lane = head_masks((1, H), n.heads)
    mix_base = links.take(3)

    peers = [flipped(t, 1, 0), flipped(t, 1, 1), flipped(t, 0, 1)]

    def attend(i, carry):
        s = flipped(t, 1 - i // 2, (i + i // 2) % 2)
        query = S.q[s]
        mixed = jnp.zeros((R, H), wide)
        inverse = jnp.zeros((R, 128), wide)
        first = lax.broadcasted_iota(jnp.int32, (1, 128), 1)

        def score(h):
            here = jnp.where(lane == W, 1.0, masks[h]).astype(low)
            return dot(query * here, S.kt[...])

        ready = score(0)
        for h in range(n.heads):
            scores = ready
            if h + 1 < n.heads:
                ready = score(h + 1)
            terms = jnp.exp(scores - jnp.max(scores, -1, keepdims=True)).astype(low)
            S.e[h, s] = terms
            part = dot(terms, S.v[...])
            scale = 1.0 / part[:, W : W + 1]
            mixed += part * (scale * masks[h])
            inverse = jnp.where(first == h, scale, inverse)
        S.o[s] = mixed
        S.inv[s] = inverse
        S.mix[s] = mixed[:, :W].astype(low)

        @pl.when(i < 3)
        def _():
            links.copy(S.mix.at[s], S.mix4.at[t], mix_base + i, tensor=s).start()

        @pl.when(i == 1)
        def _():
            cot_in.start()

        @pl.when(i == 2)
        def _():
            ow_in.wait_sib()
            ow_in.forward()

        return carry

    lax.fori_loop(0, 4, attend, 0)
    ow_in.wait_diag()
    S.mix4[t] = S.mix[t]
    for j, s in enumerate(peers):
        links.arrived(S.mix4.at[s], mix_base + j, tensor=s)

    total = dot(S.mix4[0], S.ow4[0])
    for j in range(1, 4):
        total += dot(S.mix4[j], S.ow4[j])
    total = S.x[...].astype(wide) + (total[:own] + vector(S.ob))
    S.hid[...] = total
    unit, _ = standardize(total)
    S.a24[t, 0:own, :] = (unit * vector(S.g2) + vector(S.b2)).astype(low)
    next_in = Gather(links, S.a24, t, halves(R))
    next_in.start()
    back = Reduce(links, S.part, S.pre1, S.near1, S.far1, t)
    ahead = Reduce(links, S.fop, S.pre2, S.near2, S.far2, t)
    S.gub[...] = jnp.zeros_like(S.gub)

    def feed(i, carry):
        s = flipped(t, i // 2, i % 2)

        @pl.when(i == 1)
        def _():
            next_in.wait_sib()
            cot_in.wait_sib()

        @pl.when(i == 2)
        def _():
            cot_in.forward()
            next_in.forward()

        @pl.when(i == 3)
        def _():
            next_in.wait_diag()
            cot_in.wait_diag()

        up = dot(S.a24[s], S.wup[...]) + vector(S.bup)
        square = up * up
        c = 0.7978845608028654
        bend = jnp.tanh(c * up * (1.0 + 0.044715 * square))
        half = 0.5 * (1.0 + bend)
        slope = half + 0.5 * up * (1.0 - bend * bend) * (c + (3 * 0.044715 * c) * square)
        active = (up * half).astype(low)
        S.pool[s, :, 0:D] = active
        grad = (dot(S.cot4[s], S.gw[D:, :]) * slope).astype(low)
        S.gup[s] = grad
        S.part[s] = dot(grad, S.gw[0:D, :]).astype(low)

        @pl.when(i == 1)
        def _():
            back.send_sib()

        @pl.when(i == 3)
        def _():
            back.send_diag()

        S.fop[s] = dot(active, S.wdn[...]).astype(low)

        @pl.when(i == 1)
        def _():
            ahead.send_sib()

        @pl.when(i == 3)
        def _():
            ahead.send_diag()

        S.gub[...] += jnp.sum(grad.astype(wide), 0, keepdims=True)
        return carry

    lax.fori_loop(0, 4, feed, 0)
    back.send_cross()

    sums = Pipeline(PLAN)
    tile = D // 2
    box_at = 0

    def sum_over_dp(held, whole, out, first, rows, order):
        nonlocal box_at
        sums.add(DataReduce(links, held, whole, out, S.box, box_at, first, rows, d, n.dp, order))
        box_at += DataReduce.sizes(rows, D, n.dp)[1]

    for left, right, first in ((S.a24, S.gup, 0), (S.pool, S.cot4, D)):
        rows = left[:, :, 0:D].reshape(4 * R, D)
        S.gw[first : first + D, :] = dot_columns(rows, flat(right)).astype(low)
        for at in (first, first + tile):
            sum_over_dp(S.gw, S.sum1, S.whole1, at, tile, (0, 1, 2) if at == first else (1, 0, 2))

    sums.at("waiting")
    grad = back.result()[:own]
    unit, inverse = standardize(S.hid[...])
    S.small[...] = jnp.zeros_like(S.small)
    S.small[2:3, :] = jnp.sum(grad * unit, 0, keepdims=True)
    S.small[3:4, :] = jnp.sum(grad, 0, keepdims=True)
    S.gt[...] += norm_back(grad, unit, inverse, vector(S.g2))
    S.hl4[t, 0:own, :] = S.gt[...].astype(low)
    S.small[4:5, :] = jnp.sum(S.hl4[t].astype(wide), 0, keepdims=True)
    S.small[5:6, :] = jnp.sum(S.cot4[t].astype(wide), 0, keepdims=True)
    S.small[6:7, :] = S.gub[...]
    gm_base = links.take(3)

    for j, s in enumerate(peers + [t]):
        S.mix4[s] = dot_rows(S.hl4[t], S.ow4[s]).astype(low)
        if j < 3:
            links.copy(S.mix4.at[s], S.gm4.at[t], gm_base + j, tensor=s).start()
    S.gm4[t] = S.mix4[t]
    hl_in = Gather(links, S.hl4, t, halves(R))

    next_in.finish()
    S.do[...] = jnp.zeros_like(S.do)
    S.qt[...] = jnp.transpose(flat(S.q))
    sums.at("shared")

    def prepare(i, s):
        if i > 0:
            j = (None, 2, 0, 1)[i]
            links.arrived(S.gm4.at[s], gm_base + j, tensor=peers[j])
        S.do[:, :W] = S.gm4[s].astype(wide)
        inverse = sum(S.inv[s, :, h : h + 1] * masks[h] for h in range(n.heads))
        scaled = (S.do[...] * inverse).astype(low)
        S.v[pl.ds(pl.multiple_of(s * R, 16), R), :] = scaled
        scaled = scaled.astype(wide)
        product = scaled * S.o[s]
        for h in range(n.heads):
            inner = -jnp.sum(product * masks[h], -1, keepdims=True)
            upper = inner.astype(low).astype(wide)
            S.a24[s, :, h * H : (h + 1) * H] = (
                scaled * masks[h]
                + jnp.where(lane == W, upper, 0.0)
                + jnp.where(lane == W + 1, inner - upper, 0.0)
            ).astype(low)

    def pull(h, p):
        grad_p = dot(pair(S.a24.at[:, :, h * H : (h + 1) * H], p), S.vt[...])
        grad_s = (pair(S.e.at[h], p).astype(wide) * grad_p).astype(low)
        set_pair(S.pool, p, grad_s)
        dq = dot(grad_s, S.k[...]) * (masks[h] * HEAD_DIM**-0.5)
        if h > 0:
            dq += pair(S.gup.at[:, :, 0:H], p).astype(wide)
        S.gup[pl.ds(2 * p, 2), :, 0:H] = dq.astype(low).reshape(2, R, H)

    for h in range(n.heads):
        for i in (0, 2):
            if h == 0:
                prepare(i, flipped(t, i // 2, 0))
                prepare(i + 1, flipped(t, i // 2, 1))
            if (h, i) == (0, 2):
                hl_in.start()
            pull(h, (chip + i // 2) % 2)
            sums.at(f"h{h}p{i}")
            if (h, i) == (1, 0):
                hl_in.wait_sib()
                hl_in.forward()
                ahead.send_cross()
            elif (h, i) == (1, 2):
                hl_in.wait_diag()
                S.gw2[3 * W :, :] = dot_columns(flat(S.mix), flat(S.hl4)).astype(low)
                sum_over_dp(S.gw2, S.sum2, S.whole2, 3 * W, W, (1, 0, 2))
        if h == 0:
            S.v[4 * R :, :] = jnp.zeros((K - 4 * R, H), low)
            S.kt[...] = jnp.transpose(S.v[...])
        at = slice(h * HEAD_DIM, (h + 1) * HEAD_DIM)
        S.qt[at, :] = dot(S.qt[at, :], flat(S.pool))[:, : 4 * R].astype(low)
        S.kt[at, : 4 * R] = dot(S.kt[at, : 4 * R], flat(S.e.at[h]))[:, : 4 * R].astype(low)
        tile = h * HEAD_DIM // 128 * 128
        dqt = jnp.transpose(flat(S.gup.at[:, :, tile : tile + 128]))
        left = jnp.concatenate(
            [dqt[h * HEAD_DIM - tile : (h + 1) * HEAD_DIM - tile], S.qt[at, :], S.kt[at, : 4 * R]], 0
        )
        S.gw2[h * W : (h + 1) * W, :] = dot(left, flat(S.a1)).astype(low)
        sum_over_dp(S.gw2, S.sum2, S.whole2, h * W, W, (0, 1, 2) if h in (1, 2) else (1, 0, 2))
        sums.at(f"h{h}")

    pad = jnp.zeros((R, H - W), low)
    for part, grad_t in ((1, S.qt), (2, S.kt)):
        rows = jnp.transpose(grad_t[:W, : 4 * R])
        for s in range(4):
            S.gup[s, :, part * H : part * H + W] = rows[s * R : (s + 1) * R]
            S.gup[s, :, part * H + W : (part + 1) * H] = pad

    back.finish()
    down = Reduce(links, S.part, S.pre1, S.near1, S.far1, t)

    def lead(i, carry):
        s = flipped(t, 1 - i // 2, 1 - i % 2)
        out = dot(S.gup[s, :, 0:W], S.wqkv[0])
        out += dot(S.gup[s, :, H : H + W], S.wqkv[1])
        out += dot(S.gup[s, :, 2 * H : 2 * H + W], S.wqkv[2])
        S.part[s] = out.astype(low)

        @pl.when(i == 0)
        def _():
            down.send_diag()

        @pl.when(i == 2)
        def _():
            down.send_sib()
            down.send_cross()

        return carry

    lax.fori_loop(0, 4, lead, 0)
    sums.at("led")
    S.small[7:8, 0:H] = jnp.sum(flat(S.gup.at[:, :, 0:H]).astype(wide), 0, keepdims=True)
    S.small[7:8, H : 2 * H] = jnp.sum(
        flat(S.gup.at[:, :, 2 * H : 3 * H]).astype(wide), 0, keepdims=True
    )
    S.output[...] = (S.hid[...] + (ahead.result()[:own] + vector(S.db))).astype(low)
    sums.at("crossing")

    unit, inverse = standardize(S.x[...].astype(wide))
    grad = down.result()[:own]
    S.small[0:1, :] = jnp.sum(grad * unit, 0, keepdims=True)
    S.small[1:2, :] = jnp.sum(grad, 0, keepdims=True)
    S.small4[t] = S.small[...]
    base3 = links.take(3)
    for j in range(3):
        peer = lax.rem(t + j + 1, 4)
        links.start(S.small4.at[t], S.small4.at[t], base3 + j, tensor=peer)
    S.gt[...] += norm_back(grad, unit, inverse, vector(S.g1))
    sums.at("told")
    for j in range(3):
        peer = lax.rem(t + 3 - j, 4)
        links.arrived(S.small4.at[peer], base3 + j, tensor=peer)
    over = S.small4[0] + S.small4[1] + S.small4[2] + S.small4[3]
    row = lax.broadcasted_iota(jnp.int32, over.shape, 0)
    near = min(8, n.dp)
    inner = Everyone(links, S.smalls, d % near, near, lambda j: d // near * near + j)
    inner.start(jnp.where(row < 6, over, S.small[...]))
    sums.finish()
    total = inner.result()
    inner.finish()
    if n.dp > near:
        outer = Everyone(links, S.smalls2, d // near, n.dp // near, lambda j: j * near + d % near)
        outer.start(total)
        total = outer.result()
        outer.finish()
    S.small_sum[...] = total
    for j, s in enumerate(peers):
        links.copy(S.mix.at[s], S.mix4.at[t], mix_base + j, tensor=s).wait_send()
        links.copy(S.mix4.at[s], S.gm4.at[t], gm_base + j, tensor=s).wait_send()
    for transfer in (rows_in, cot_in, ow_in, hl_in, ahead, down):
        transfer.finish()
    links.finish()


SMALL = ("gain1", "shift1", "gain2", "shift2", "bias_out", "bias_down", "bias_up", "bias_qv")


def finish(n, output, gt, small, whole1, whole2):
    D, W, H = n.D, n.W, n.H
    steps = 2 * n.heads
    rows1, rows2 = D // steps, HEAD_DIM // 2

    def spread(output, gt, small, up, down, q, k, v, out, *refs):
        to_output, to_gt, to_up, to_down, to_qkv, to_out = refs[:6]
        vectors, sems = refs[6:14], refs[14]
        i = pl.program_id(0)
        held = refs[15:]
        come = [pltpu.make_async_copy(a, b, sems.at[j]) for j, (a, b) in enumerate(zip((output, gt), held))]
        go = [
            pltpu.make_async_copy(a, b, sems.at[2 + j])
            for j, (a, b) in enumerate(zip(held, (to_output, to_gt)))
        ]

        @pl.when(i == 0)
        def _():
            for copy in come:
                copy.start()
            for j in range(7):
                vectors[j][...] = small[j : j + 1, :].reshape(D)
            vectors[7][0:1, :] = small[7:8, :W]
            vectors[7][1:2, :] = small[7:8, H : H + W]

        to_up[...] = up[...].astype(wide)
        to_down[...] = down[...].astype(wide)
        for j, part in enumerate((q, k, v)):
            to_qkv[j] = part[...].astype(wide)
        to_out[...] = out[...].astype(wide)

        @pl.when(i == 1)
        def _():
            for first, second in zip(come, go):
                first.wait()
                second.start()

        @pl.when(i == steps - 1)
        def _():
            for copy in go:
                copy.wait()

    hbm = pl.BlockSpec(memory_space=pl.ANY)
    whole = pl.BlockSpec(memory_space=pltpu.VMEM)
    at_row = lambda rows, index: pl.BlockSpec((rows, D), lambda i: (index(i), 0))
    of_part = lambda j: at_row(rows2, lambda i: i // 2 * 6 + j * 2 + i % 2)
    shape = jax.ShapeDtypeStruct
    return pl.pallas_call(
        spread,
        grid=(steps,),
        out_shape=[shape(output.shape, low), shape(gt.shape, wide)]
        + [shape((D, D), wide)] * 2
        + [shape((3, W, D), wide), shape((W, D), wide)]
        + [shape((D,), wide)] * 7
        + [shape((2, W), wide)],
        in_specs=[hbm, hbm, whole, at_row(rows1, lambda i: i), at_row(rows1, lambda i: i + steps)]
        + [of_part(j) for j in range(3)]
        + [at_row(rows2, lambda i: 3 * steps + i)],
        out_specs=[hbm, hbm]
        + [at_row(rows1, lambda i: i)] * 2
        + [pl.BlockSpec((3, rows2, D), lambda i: (0, i, 0)), at_row(rows2, lambda i: i)]
        + [whole] * 8,
        scratch_shapes=[
            pltpu.SemaphoreType.DMA((4,)),
            pltpu.VMEM(output.shape, low),
            pltpu.VMEM(gt.shape, wide),
        ],
    )(output, gt, small, whole1, whole1, whole2, whole2, whole2, whole2)


def body(
    tokens,
    lengths,
    ln1_gain,
    ln1_shift,
    qkv_weight,
    qv_bias,
    out_weight,
    out_bias,
    ln2_gain,
    ln2_shift,
    up_weight,
    up_bias,
    down_weight,
    down_bias,
    cotangent,
):
    own, D = tokens.shape
    W = qkv_weight.shape[2]
    F = up_weight.shape[1]
    dp = lax.axis_size("dp")
    assert lax.axis_size("tensor") == 4 and lengths.shape[0] == 1 and F == D and 4 * W == D and 3 * round_up(W + 2, 128) == D
    R = round_up(own, 16)
    H = round_up(W + 2, 128)
    K = round_up(4 * R, 256)
    heads = W // HEAD_DIM
    extra = dp.bit_length() - 1 - 3
    n = types.SimpleNamespace(
        own=own, D=D, W=W, R=R, H=H, K=K, dp=dp, heads=heads, extra=extra
    )
    given = dict(
        x=tokens, lengths=lengths, g1=ln1_gain, b1=ln1_shift,
        wqkv=jnp.transpose(qkv_weight, (1, 2, 0)), bq=qv_bias, ow=out_weight, ob=out_bias,
        g2=ln2_gain, b2=ln2_shift, wup=up_weight, bup=up_bias, wdn=down_weight, db=down_bias,
        cot=cotangent,
    )
    outs = dict(
        output=((own, D), low), gt=((own, D), wide), small_sum=((8, D), wide),
        whole1=((2 * D, D), low), whole2=((D, D), low),
    )
    rows4 = ((4, R, D), low)
    slab = ((R, D), low)
    chunks = [D // 2] * 4 + [W] * 4
    scratch = dict(
        a1=rows4, cot4=rows4, ow4=((4, W, D), low), q=((4, R, H), low), k=((K, H), low),
        v=((K, H), low), kt=((H, K), low), vt=((H, K), low), e=((heads, 4, R, K), low),
        o=((4, R, H), wide), inv=((4, R, 128), wide), mix=((4, R, W), low), mix4=((4, R, W), low),
        hid=((own, D), wide),
        a24=rows4, pool=((4, R, K), low), gup=rows4, part=rows4,
        fop=rows4, pre1=slab, near1=slab, far1=slab, pre2=slab, near2=slab, far2=slab,
        gw=((2 * D, D), low), gub=((1, D), wide),
        small=((8, D), wide), hl4=rows4,
        gm4=((4, R, W), low), qt=((H, 4 * R), low), do=((R, H), wide),
        gw2=((D, D), low),
        small4=((4, 8, D), wide), smalls=((min(8, dp), 8, D), wide),
        box=((sum(DataReduce.sizes(r, D, dp)[1] for r in chunks), D), low),
        sum1=((2 * D, D), low), sum2=((D, D), low),
    )
    if dp > 8:
        scratch["smalls2"] = ((dp // 8, 8, D), wide)
    sems = 140 + dp + 8 * extra
    names = list(given) + list(outs) + list(scratch) + ["local", "send", "recv"]
    vmem = pl.BlockSpec(memory_space=pltpu.VMEM)
    smem = pl.BlockSpec(memory_space=pltpu.SMEM)
    hbm = pl.BlockSpec(memory_space=pl.ANY)
    output, gt, small, whole1, whole2 = pl.pallas_call(
        lambda *refs: kernel(n, types.SimpleNamespace(**dict(zip(names, refs)))),
        out_shape=tuple(jax.ShapeDtypeStruct(*spec) for spec in outs.values()),
        in_specs=[dict(lengths=smem, cot=hbm).get(name, vmem) for name in given],
        out_specs=tuple(hbm if name in ("whole1", "whole2") else vmem for name in outs),
        scratch_shapes=[pltpu.VMEM(*spec) for spec in scratch.values()]
        + [pltpu.SemaphoreType.DMA] + [pltpu.SemaphoreType.DMA((sems,))] * 2,
        compiler_params=pltpu.CompilerParams(
            collective_id=0, has_side_effects=True, vmem_limit_bytes=VMEM_BYTES
        ),
    )(*given.values())
    finished = finish(n, output, gt, small, whole1, whole2)
    small_rows = dict(zip(SMALL, finished[6:]))
    return (
        finished[0],
        finished[1],
        small_rows["gain1"],
        small_rows["shift1"],
        jnp.transpose(finished[4], (2, 0, 1)),
        small_rows["bias_qv"],
        finished[5],
        small_rows["bias_out"],
        small_rows["gain2"],
        small_rows["shift2"],
        finished[2],
        small_rows["bias_up"],
        finished[3],
        small_rows["bias_down"],
    )


def solution(mesh):
    placed = (
        P(("dp", "tensor"), None),
        P("dp"),
        P(),
        P(),
        P(None, None, "tensor"),
        P(None, "tensor"),
        P("tensor", None),
        P(),
        P(),
        P(),
        P(None, "tensor"),
        P("tensor"),
        P("tensor", None),
        P(),
        P(("dp", "tensor"), None),
    )
    return jax.shard_map(
        body,
        mesh=mesh,
        in_specs=placed,
        out_specs=(
            P(("dp", "tensor"), None),
            P(("dp", "tensor"), None),
            P(),
            P(),
            P(None, None, "tensor"),
            P(None, "tensor"),
            P("tensor", None),
            P(),
            P(),
            P(),
            P(None, "tensor"),
            P("tensor"),
            P("tensor", None),
            P(),
        ),
        check_vma=False,
    )
```

```python
import types

import jax
import jax.numpy as jnp
from jax import lax
from jax.experimental import pallas as pl
from jax.experimental.pallas import tpu as pltpu
from jax.sharding import PartitionSpec as P

HEAD_DIM = 64
MESH = pl.DeviceIdType.MESH
VMEM_BYTES = 62 * 2**20

epsilon = 1e-06
low = jnp.bfloat16
wide = jnp.float32


def round_up(amount, unit):
    return -(-amount // unit) * unit


def flipped(t, flip_chip, flip_core):
    return (t // 2 + flip_chip) % 2 * 2 + (t % 2 + flip_core) % 2


def dot(left, right):
    return jnp.dot(left, right, preferred_element_type=wide)


def dot_rows(left, right):
    return lax.dot_general(left, right, (((1,), (1,)), ((), ())), preferred_element_type=wide)


def dot_columns(left, right):
    return lax.dot_general(left, right, (((0,), (0,)), ((), ())), preferred_element_type=wide)


def standardize(values):
    center = values - jnp.mean(values, -1, keepdims=True)
    inverse = lax.rsqrt(jnp.mean(center * center, -1, keepdims=True) + epsilon)
    return center * inverse, inverse


def norm_back(grad, unit, inverse, gain):
    scaled = grad * gain
    return inverse * (
        scaled
        - jnp.mean(scaled, -1, keepdims=True)
        - unit * jnp.mean(scaled * unit, -1, keepdims=True)
    )


def pair(ref, p):
    _, rows, columns = ref.shape
    return ref[pl.ds(2 * p, 2)].reshape(2 * rows, columns)


def set_pair(ref, p, values):
    ref[pl.ds(2 * p, 2)] = values.reshape(2, -1, values.shape[1])


def flat(ref):
    a, b, c = ref.shape
    return ref[...].reshape(a * b, c)


class Links:
    def __init__(self, send, recv):
        self.send, self.recv, self.used, self.pending = send, recv, 0, []

    def take(self, amount=1):
        base = self.used
        self.used += amount
        assert self.used <= self.send.shape[0]
        return base

    def copy(self, src, dst, at, **where):
        return pltpu.make_async_remote_copy(
            src_ref=src,
            dst_ref=dst,
            send_sem=self.send.at[at],
            recv_sem=self.recv.at[at],
            device_id=where,
            device_id_type=MESH,
        )

    def start(self, src, dst, at, **where):
        copy = self.copy(src, dst, at, **where)
        copy.start()
        self.pending.append(copy)

    def arrived(self, dst, at, **where):
        self.copy(dst, dst, at, **where).wait_recv()

    def finish(self):
        for copy in self.pending:
            copy.wait_send()
        self.pending = []


class Gather:
    def __init__(self, links, buf, t, parts):
        self.links, self.buf, self.t, self.parts = links, buf, t, parts
        self.sib, self.cross, self.diag = flipped(t, 0, 1), flipped(t, 1, 0), flipped(t, 1, 1)
        self.base = links.take(3 * len(parts))

    def view(self, slot, part):
        start, size = self.parts[part]
        return self.buf.at[slot, pl.ds(start, size)]

    def _each(self):
        return range(len(self.parts))

    def start(self):
        for p in self._each():
            v = self.view(self.t, p)
            self.links.copy(v, v, self.base + 3 * p, tensor=self.cross).start()
        for p in self._each():
            v = self.view(self.t, p)
            self.links.copy(v, v, self.base + 3 * p + 1, tensor=self.sib).start()

    def wait_sib(self):
        for p in self._each():
            self.links.arrived(self.view(self.sib, p), self.base + 3 * p + 1, tensor=self.sib)

    def forward(self):
        for p in self._each():
            v = self.view(self.cross, p)
            self.links.arrived(v, self.base + 3 * p, tensor=self.cross)
            self.links.copy(v, v, self.base + 3 * p + 2, tensor=self.sib).start()

    def wait_diag(self):
        for p in self._each():
            self.links.arrived(self.view(self.diag, p), self.base + 3 * p + 2, tensor=self.sib)

    def finish(self):
        for p in self._each():
            v = self.view(self.t, p)
            self.links.copy(v, v, self.base + 3 * p, tensor=self.cross).wait_send()
            self.links.copy(v, v, self.base + 3 * p + 1, tensor=self.sib).wait_send()
            v = self.view(self.cross, p)
            self.links.copy(v, v, self.base + 3 * p + 2, tensor=self.sib).wait_send()


class Reduce:
    def __init__(self, links, part, pre, near, far, t):
        self.links, self.part, self.pre, self.near, self.far, self.t = links, part, pre, near, far, t
        self.sib, self.cross, self.diag = flipped(t, 0, 1), flipped(t, 1, 0), flipped(t, 1, 1)
        self.base = links.take(3)

    def send_diag(self):
        self.links.copy(self.part.at[self.diag], self.pre, self.base, tensor=self.sib).start()

    def send_sib(self):
        self.links.copy(self.part.at[self.sib], self.near, self.base + 1, tensor=self.sib).start()

    def send_cross(self):
        self.links.arrived(self.pre, self.base, tensor=self.sib)
        total = self.part[self.cross].astype(wide) + self.pre[...].astype(wide)
        self.part[self.cross] = total.astype(low)
        self.links.copy(self.part.at[self.cross], self.far, self.base + 2, tensor=self.cross).start()

    def result(self):
        self.links.arrived(self.near, self.base + 1, tensor=self.sib)
        self.links.arrived(self.far, self.base + 2, tensor=self.cross)
        return (
            self.part[self.t].astype(wide) + self.near[...].astype(wide) + self.far[...].astype(wide)
        )

    def finish(self):
        self.links.copy(self.part.at[self.diag], self.pre, self.base, tensor=self.sib).wait_send()
        self.links.copy(self.part.at[self.sib], self.near, self.base + 1, tensor=self.sib).wait_send()
        self.links.copy(self.part.at[self.cross], self.far, self.base + 2, tensor=self.cross).wait_send()


class DataReduce:
    def __init__(self, links, held, whole, out, box, box_at, first, rows, d, count):
        self.links, self.held, self.whole, self.out, self.d = links, held, whole, out, d
        bits = count.bit_length() - 1
        assert count == 1 << bits and bits >= 3
        self.extra = list(range(3, bits))
        self.region = (first, rows, 0, held.shape[1])
        self.trail, self.sent, self.boxes = [], [], []
        for tall, broad in self.sizes(rows, held.shape[1], count)[0]:
            self.boxes.append(box.at[pl.ds(box_at, tall), pl.ds(0, broad)])
            box_at += tall
        self.base = links.take(9 + len(self.extra))
        self.plan()

    @classmethod
    def sizes(cls, rows, columns, count):
        found = cls.boxes_of(rows, columns)
        found += found[-1:] * (count.bit_length() - 1 - 3)
        return found, sum(size[0] for size in found)

    def _bit(self, b):
        return self.d // (1 << b) % 2

    def _peer(self, b):
        return self.d + (1 - 2 * self._bit(b)) * (1 << b)

    def _send(self, src, dst, at, peer):
        copy = self.links.copy(src, dst, self.base + at, dp=peer)
        copy.start()
        self.sent.append(copy)

    def _wait(self, dst, at, peer):
        self.links.arrived(dst, self.base + at, dp=peer)

    @staticmethod
    def _view(ref, region):
        row, rows, column, columns = region
        if columns == ref.shape[1]:
            return ref.at[pl.ds(row, rows)]
        return ref.at[pl.ds(row, rows), pl.ds(column, columns)]

    @staticmethod
    def _part(region, bit):
        row, rows, column, columns = region
        if rows % 32 == 0:
            return (pl.multiple_of(row + bit * (rows // 2), 16), rows // 2, column, columns)
        return (row, rows, pl.multiple_of(column + bit * (columns // 2), 128), columns // 2)

    def _give_half(self, b, box, at):
        bit = self._bit(b)
        self.trail.append(self.region)
        self._send(self._view(self.held, self._part(self.region, 1 - bit)), self.boxes[box], at, self._peer(b))
        self.region = self._part(self.region, bit)

    def _add(self, boxes, last):
        view = self._view(self.held, self.region)
        total = view[...].astype(wide)
        for box in boxes:
            total += self.boxes[box][...].astype(wide)
        if last:
            view = self._view(self.whole, self.region)
        view[...] = total.astype(low)
        if last:
            self._swap()

    def _swap(self):
        view = self._view(self.whole, self.region)
        for k, b in enumerate(self.extra):
            box, at = self.boxes[k - len(self.extra)], 9 + k
            copy = self.links.copy(view, box, self.base + at, dp=self._peer(b))
            copy.start()
            self._wait(box, at, self._peer(b))
            copy.wait_send()
            view[...] = (view[...].astype(wide) + box[...].astype(wide)).astype(low)

    def _give_whole(self, b, at):
        view = self._view(self.whole, self.region)
        self._send(view, view, at, self._peer(b))

    def _take_half(self, b, at):
        outer = self.trail.pop()
        view = self._view(self.whole, self._part(outer, 1 - self._bit(b)))
        self._wait(view, at, self._peer(b))
        self.region = outer

    def _leave(self):
        rows = pl.ds(self.region[0], self.region[1])
        self.left = pltpu.make_async_copy(
            self.whole.at[rows], self.out.at[rows], self.links.send.at[self.base + 8]
        )
        self.left.start()

    def step(self):
        if self.steps:
            self.steps.pop(0)()

    def finish(self):
        assert not self.steps
        self.left.wait()
        for copy in self.sent:
            copy.wait_send()


class Halves(DataReduce):
    order = (1, 0, 2)

    @staticmethod
    def boxes_of(rows, columns):
        found = []
        for _ in range(3):
            if rows % 32 == 0:
                rows //= 2
            else:
                columns //= 2
            found.append((rows, columns))
        return found

    def plan(self):
        low_bit, x, high = self.order
        self.steps = [
            lambda: self._give_half(low_bit, 0, 0),
            lambda: (self._wait_box(low_bit, 0), self._add((0,), False), self._give_half(x, 1, 1)),
            lambda: (self._wait_box(x, 1), self._add((1,), False), self._give_half(high, 2, 2)),
            lambda: (self._wait_box(high, 2), self._add((2,), True), self._give_whole(high, 3)),
            lambda: (self._take_half(high, 3), self._give_whole(x, 4)),
            lambda: (self._take_half(x, 4), self._give_whole(low_bit, 5)),
            lambda: (self._take_half(low_bit, 5), self._leave()),
        ]

    def _wait_box(self, b, box):
        self._wait(self.boxes[box], box, self._peer(b))


class Quarters(DataReduce):
    @staticmethod
    def boxes_of(rows, columns):
        tall, broad = rows // 8, columns
        if tall % 16:
            tall, broad = rows // 4, columns // 2
        return [(rows // 2, columns)] + [(tall, broad)] * 3

    def plan(self):
        self.steps = [
            lambda: self._give_half(0, 0, 0),
            lambda: (self._wait(self.boxes[0], 0, self._peer(0)), self._add((0,), False), self._give_quarters()),
            lambda: (self._take_boxes(), self._add((1, 2, 3), True), self._give_quarter()),
            lambda: (self._take_quarters(), self._give_whole(0, 7)),
            lambda: (self._take_half(0, 7), self._leave()),
        ]

    def _z(self, j):
        low_bit = (self._bit(1) + j % 2) % 2
        high = (self._bit(2) + j // 2) % 2
        return low_bit, high, self.d // 8 * 8 + high * 4 + low_bit * 2 + self._bit(0)

    def _quarter(self, j):
        low_bit, high, peer = self._z(j)
        return self._part(self._part(self.trail[-1], high), low_bit), peer

    def _give_quarters(self):
        self.trail.append(self.region)
        for j in (1, 2, 3):
            part, peer = self._quarter(j)
            self._send(self._view(self.held, part), self.boxes[j], j, peer)
        self.region = self._quarter(0)[0]

    def _take_boxes(self):
        for j in (1, 2, 3):
            self._wait(self.boxes[j], j, self._z(j)[2])

    def _give_quarter(self):
        view = self._view(self.whole, self.region)
        for j in (1, 2, 3):
            self._send(view, view, 3 + j, self._z(j)[2])

    def _take_quarters(self):
        for j in (1, 2, 3):
            part, peer = self._quarter(j)
            self._wait(self._view(self.whole, part), 3 + j, peer)
        self.region = self.trail.pop()


class Pipeline:
    def __init__(self, plan):
        self.plan, self.members = plan, []

    def add(self, member):
        self.members.append(member)
        member.step()

    def at(self, place):
        for number in self.plan[place]:
            self.members[number].step()

    def finish(self):
        self.at("end")
        for m in self.members:
            while m.steps:
                m.step()
            m.finish()


PLAN = dict(
    waiting=(0,),
    shared=(1, 3),
    arriving=(1,),
    h0p0=(),
    h0p2=(0,),
    h0=(),
    h1p0=(3, 2, 4),
    h1p2=(1,),
    h1=(),
    h2p0=(2, 0),
    h2p2=(5, 1, 6),
    h2=(2, 3, 4, 5, 1),
    led=(2, 7, 6, 4, 5),
    crossing=(1, 7, 3, 2, 6, 4),
    told=(7,),
    end=(5, 0, 2, 6, 7),
)


class Everyone:
    def __init__(self, links, buf, me, count, device):
        self.links, self.buf, self.me, self.count, self.device = links, buf, me, count, device
        self.base = links.take(count)

    def _copy(self, j):
        slot = self.buf.at[self.me]
        peer = self.device(lax.rem(self.me + j, self.count))
        return self.links.copy(slot, slot, self.base + j, dp=peer)

    def _loop(self, act):
        def one(j, carry):
            act(j)
            return carry

        lax.fori_loop(1, self.count, one, 0)

    def start(self, values):
        self.buf[self.me] = values
        self._loop(lambda j: self._copy(j).start())

    def _hear(self, j):
        peer = lax.rem(self.me + self.count - j, self.count)
        self.links.arrived(self.buf.at[peer], self.base + j, dp=self.device(peer))

    def result(self):
        self._loop(self._hear)
        return lax.fori_loop(1, self.count, lambda j, acc: acc + self.buf[j], self.buf[0])

    def finish(self):
        self._loop(lambda j: self._copy(j).wait_send())


def greet(axis, me, count):
    barrier = pltpu.get_barrier_semaphore()

    def one(j, carry):
        pl.semaphore_signal(
            barrier, inc=1, device_id={axis: lax.rem(me + j, count)}, device_id_type=MESH
        )
        return carry

    lax.fori_loop(1, count, one, 0)


def await_greetings(amount):
    pl.semaphore_wait(pltpu.get_barrier_semaphore(), amount)


def halves(rows):
    first = round_up(rows // 2, 16)
    return ((0, first), (first, rows - first))


def head_masks(shape, local_heads):
    lane = lax.broadcasted_iota(jnp.int32, shape, 1)
    return [
        jnp.where((lane >= h * HEAD_DIM) & (lane < (h + 1) * HEAD_DIM), 1.0, 0.0)
        for h in range(local_heads)
    ], lane


def kernel(n, S):
    links = Links(S.send, S.recv)
    t = lax.axis_index("tensor")
    d = lax.axis_index("dp")
    greet("tensor", t, 4)
    greet("dp", d, n.dp)
    R, own, W, H, D, K = n.R, n.own, n.W, n.H, n.D, n.K
    vector = lambda ref: ref[...].reshape(1, D)

    fetch = pltpu.make_async_copy(S.cot, S.gt, S.local)
    fetch.start()
    S.a1[t] = jnp.zeros((R, D), low)
    S.cot4[t] = jnp.zeros((R, D), low)
    S.a24[t] = jnp.zeros((R, D), low)
    S.hl4[t] = jnp.zeros((R, D), low)
    unit, _ = standardize(S.x[...].astype(wide))
    S.a1[t, 0:own, :] = (unit * vector(S.g1) + vector(S.b1)).astype(low)
    fetch.wait()
    S.cot4[t, 0:own, :] = S.gt[...].astype(low)
    S.ow4[t] = S.ow[...]
    await_greetings(3 + n.dp - 1)
    rows_in = Gather(links, S.a1, t, halves(R))
    cot_in = Gather(links, S.cot4, t, halves(R))
    ow_in = Gather(links, S.ow4, t, ((0, W),))
    rows_in.start()
    S.gw[0:D, :] = jnp.transpose(S.wup[...])
    S.gw[D:, :] = jnp.transpose(S.wdn[...])
    S.v[4 * R :, :] = jnp.zeros((K - 4 * R, H), low)
    length = S.lengths[0]

    chip = t // 2

    def project(i, carry):
        s = flipped(t, i // 2, i % 2)

        @pl.when(i == 1)
        def _():
            rows_in.wait_sib()

        @pl.when(i == 2)
        def _():
            rows_in.forward()
            ow_in.start()

        @pl.when(i == 3)
        def _():
            rows_in.wait_diag()

        slab = S.a1[s]
        lane = lax.broadcasted_iota(jnp.int32, (R, H - W), 1)
        row = lax.broadcasted_iota(jnp.int32, (R, H - W), 0)
        absent = (row >= own) | (row + s * own >= length)
        at = pl.ds(pl.multiple_of(s * R, 16), R)
        out = dot_rows(slab, S.wqkv[0]) + S.bq[0:1, :]
        S.q[s, :, :W] = (out.astype(low).astype(wide) * HEAD_DIM**-0.5).astype(low)
        S.q[s, :, W:] = jnp.where(lane == 0, HEAD_DIM**-0.5, 0.0).astype(low)
        S.k[at, :W] = dot_rows(slab, S.wqkv[1]).astype(low)
        S.k[at, W:] = jnp.where((lane == 0) & absent, -8e30, 0.0).astype(low)
        S.v[at, :W] = (dot_rows(slab, S.wqkv[2]) + S.bq[1:2, :]).astype(low)
        S.v[at, W:] = jnp.where(lane < 2, 1.0, 0.0).astype(low)
        return carry

    lax.fori_loop(0, 4, project, 0)
    if K > 4 * R:
        lane = lax.broadcasted_iota(jnp.int32, (K - 4 * R, H), 1)
        S.k[4 * R :, :] = jnp.where(lane == W, -8e30, 0.0).astype(low)
    S.kt[...] = jnp.transpose(S.k[...])
    S.vt[...] = jnp.transpose(S.v[...])

    masks, lane = head_masks((1, H), n.heads)
    mix_base = links.take(3)

    peers = [flipped(t, 1, 0), flipped(t, 1, 1), flipped(t, 0, 1)]

    def attend(i, carry):
        s = flipped(t, 1 - i // 2, (i + i // 2) % 2)
        query = S.q[s]
        mixed = jnp.zeros((R, H), wide)
        inverse = jnp.zeros((R, 128), wide)
        first = lax.broadcasted_iota(jnp.int32, (1, 128), 1)

        def score(h):
            here = jnp.where(lane == W, 1.0, masks[h]).astype(low)
            return dot(query * here, S.kt[...])

        ready = score(0)
        for h in range(n.heads):
            scores = ready
            if h + 1 < n.heads:
                ready = score(h + 1)
            terms = jnp.exp(scores - jnp.max(scores, -1, keepdims=True)).astype(low)
            S.e[h, s] = terms
            part = dot(terms, S.v[...])
            scale = 1.0 / part[:, W : W + 1]
            mixed += part * (scale * masks[h])
            inverse = jnp.where(first == h, scale, inverse)
        S.o[s] = mixed
        S.inv[s] = inverse
        S.mix[s] = mixed[:, :W].astype(low)

        @pl.when(i < 3)
        def _():
            links.copy(S.mix.at[s], S.mix4.at[t], mix_base + i, tensor=s).start()

        @pl.when(i == 1)
        def _():
            cot_in.start()

        @pl.when(i == 2)
        def _():
            ow_in.wait_sib()
            ow_in.forward()

        return carry

    lax.fori_loop(0, 4, attend, 0)
    ow_in.wait_diag()
    S.mix4[t] = S.mix[t]
    for j, s in enumerate(peers):
        links.arrived(S.mix4.at[s], mix_base + j, tensor=s)

    total = dot(S.mix4[0], S.ow4[0])
    for j in range(1, 4):
        total += dot(S.mix4[j], S.ow4[j])
    total = S.x[...].astype(wide) + (total[:own] + vector(S.ob))
    S.hid[...] = total
    unit, _ = standardize(total)
    S.a24[t, 0:own, :] = (unit * vector(S.g2) + vector(S.b2)).astype(low)
    next_in = Gather(links, S.a24, t, halves(R))
    next_in.start()
    back = Reduce(links, S.part, S.pre1, S.near1, S.far1, t)
    ahead = Reduce(links, S.fop, S.pre2, S.near2, S.far2, t)
    S.gub[...] = jnp.zeros_like(S.gub)

    def feed(i, carry):
        s = flipped(t, i // 2, i % 2)

        @pl.when(i == 1)
        def _():
            next_in.wait_sib()
            cot_in.wait_sib()

        @pl.when(i == 2)
        def _():
            cot_in.forward()
            next_in.forward()

        @pl.when(i == 3)
        def _():
            next_in.wait_diag()
            cot_in.wait_diag()

        up = dot(S.a24[s], S.wup[...]) + vector(S.bup)
        square = up * up
        c = 0.7978845608028654
        bend = jnp.tanh(c * up * (1.0 + 0.044715 * square))
        half = 0.5 * (1.0 + bend)
        slope = half + 0.5 * up * (1.0 - bend * bend) * (c + (3 * 0.044715 * c) * square)
        active = (up * half).astype(low)
        S.pool[s, :, 0:D] = active
        grad = (dot(S.cot4[s], S.gw[D:, :]) * slope).astype(low)
        S.gup[s] = grad
        S.part[s] = dot(grad, S.gw[0:D, :]).astype(low)

        @pl.when(i == 1)
        def _():
            back.send_sib()

        @pl.when(i == 3)
        def _():
            back.send_diag()

        S.fop[s] = dot(active, S.wdn[...]).astype(low)

        @pl.when(i == 1)
        def _():
            ahead.send_sib()

        @pl.when(i == 3)
        def _():
            ahead.send_diag()

        S.gub[...] += jnp.sum(grad.astype(wide), 0, keepdims=True)
        return carry

    lax.fori_loop(0, 4, feed, 0)
    back.send_cross()

    sums = Pipeline(PLAN)
    tile = D // 2
    box_at = 0

    def sum_over_dp(kind, held, whole, out, first, rows):
        nonlocal box_at
        sums.add(kind(links, held, whole, out, S.box, box_at, first, rows, d, n.dp))
        box_at += kind.sizes(rows, D, n.dp)[1]

    for left, right, first in ((S.a24, S.gup, 0), (S.pool, S.cot4, D)):
        rows = left[:, :, 0:D].reshape(4 * R, D)
        S.gw[first : first + D, :] = dot_columns(rows, flat(right)).astype(low)
        for at in (first, first + tile):
            kind = Quarters if at in (0, D + tile) else Halves
            sum_over_dp(kind, S.gw, S.sum1, S.whole1, at, tile)

    sums.at("waiting")
    grad = back.result()[:own]
    unit, inverse = standardize(S.hid[...])
    S.small[...] = jnp.zeros_like(S.small)
    S.small[2:3, :] = jnp.sum(grad * unit, 0, keepdims=True)
    S.small[3:4, :] = jnp.sum(grad, 0, keepdims=True)
    S.gt[...] += norm_back(grad, unit, inverse, vector(S.g2))
    S.hl4[t, 0:own, :] = S.gt[...].astype(low)
    S.small[4:5, :] = jnp.sum(S.hl4[t].astype(wide), 0, keepdims=True)
    S.small[5:6, :] = jnp.sum(S.cot4[t].astype(wide), 0, keepdims=True)
    S.small[6:7, :] = S.gub[...]
    gm_base = links.take(3)

    for j, s in enumerate(peers + [t]):
        S.mix4[s] = dot_rows(S.hl4[t], S.ow4[s]).astype(low)
        if j < 3:
            links.copy(S.mix4.at[s], S.gm4.at[t], gm_base + j, tensor=s).start()
    S.gm4[t] = S.mix4[t]
    hl_in = Gather(links, S.hl4, t, halves(R))

    next_in.finish()
    S.do[...] = jnp.zeros_like(S.do)
    S.qt[...] = jnp.transpose(flat(S.q))
    sums.at("shared")

    def prepare(i, s):
        if i > 0:
            j = (None, 2, 0, 1)[i]
            links.arrived(S.gm4.at[s], gm_base + j, tensor=peers[j])
        S.do[:, :W] = S.gm4[s].astype(wide)
        inverse = sum(S.inv[s, :, h : h + 1] * masks[h] for h in range(n.heads))
        scaled = (S.do[...] * inverse).astype(low)
        S.v[pl.ds(pl.multiple_of(s * R, 16), R), :] = scaled
        scaled = scaled.astype(wide)
        product = scaled * S.o[s]
        for h in range(n.heads):
            inner = -jnp.sum(product * masks[h], -1, keepdims=True)
            upper = inner.astype(low).astype(wide)
            S.a24[s, :, h * H : (h + 1) * H] = (
                scaled * masks[h]
                + jnp.where(lane == W, upper, 0.0)
                + jnp.where(lane == W + 1, inner - upper, 0.0)
            ).astype(low)

    def pull(h, p):
        grad_p = dot(pair(S.a24.at[:, :, h * H : (h + 1) * H], p), S.vt[...])
        grad_s = (pair(S.e.at[h], p).astype(wide) * grad_p).astype(low)
        set_pair(S.pool, p, grad_s)
        dq = dot(grad_s, S.k[...]) * (masks[h] * HEAD_DIM**-0.5)
        if h > 0:
            dq += pair(S.gup.at[:, :, 0:H], p).astype(wide)
        S.gup[pl.ds(2 * p, 2), :, 0:H] = dq.astype(low).reshape(2, R, H)

    for h in range(n.heads):
        for i in (0, 2):
            if (h, i) == (0, 2):
                sums.at("arriving")
            if h == 0:
                prepare(i, flipped(t, i // 2, 0))
                prepare(i + 1, flipped(t, i // 2, 1))
            if (h, i) == (0, 2):
                hl_in.start()
            pull(h, (chip + i // 2) % 2)
            sums.at(f"h{h}p{i}")
            if (h, i) == (1, 0):
                hl_in.wait_sib()
                hl_in.forward()
                ahead.send_cross()
            elif (h, i) == (1, 2):
                hl_in.wait_diag()
                S.gw2[3 * W :, :] = dot_columns(flat(S.mix), flat(S.hl4)).astype(low)
                sum_over_dp(Quarters, S.gw2, S.sum2, S.whole2, 3 * W, W)
        if h == 0:
            S.v[4 * R :, :] = jnp.zeros((K - 4 * R, H), low)
            S.kt[...] = jnp.transpose(S.v[...])
        at = slice(h * HEAD_DIM, (h + 1) * HEAD_DIM)
        S.qt[at, :] = dot(S.qt[at, :], flat(S.pool))[:, : 4 * R].astype(low)
        S.kt[at, : 4 * R] = dot(S.kt[at, : 4 * R], flat(S.e.at[h]))[:, : 4 * R].astype(low)
        tile = h * HEAD_DIM // 128 * 128
        dqt = jnp.transpose(flat(S.gup.at[:, :, tile : tile + 128]))
        left = jnp.concatenate(
            [dqt[h * HEAD_DIM - tile : (h + 1) * HEAD_DIM - tile], S.qt[at, :], S.kt[at, : 4 * R]], 0
        )
        S.gw2[h * W : (h + 1) * W, :] = dot(left, flat(S.a1)).astype(low)
        sum_over_dp(Quarters, S.gw2, S.sum2, S.whole2, h * W, W)
        sums.at(f"h{h}")

    pad = jnp.zeros((R, H - W), low)
    for part, grad_t in ((1, S.qt), (2, S.kt)):
        rows = jnp.transpose(grad_t[:W, : 4 * R])
        for s in range(4):
            S.gup[s, :, part * H : part * H + W] = rows[s * R : (s + 1) * R]
            S.gup[s, :, part * H + W : (part + 1) * H] = pad

    back.finish()
    down = Reduce(links, S.part, S.pre1, S.near1, S.far1, t)

    def lead(i, carry):
        s = flipped(t, 1 - i // 2, 1 - i % 2)
        out = dot(S.gup[s, :, 0:W], S.wqkv[0])
        out += dot(S.gup[s, :, H : H + W], S.wqkv[1])
        out += dot(S.gup[s, :, 2 * H : 2 * H + W], S.wqkv[2])
        S.part[s] = out.astype(low)

        @pl.when(i == 0)
        def _():
            down.send_diag()

        @pl.when(i == 2)
        def _():
            down.send_sib()
            down.send_cross()

        return carry

    lax.fori_loop(0, 4, lead, 0)
    sums.at("led")
    S.small[7:8, 0:H] = jnp.sum(flat(S.gup.at[:, :, 0:H]).astype(wide), 0, keepdims=True)
    S.small[7:8, H : 2 * H] = jnp.sum(
        flat(S.gup.at[:, :, 2 * H : 3 * H]).astype(wide), 0, keepdims=True
    )
    S.output[...] = (S.hid[...] + (ahead.result()[:own] + vector(S.db))).astype(low)
    sums.at("crossing")

    unit, inverse = standardize(S.x[...].astype(wide))
    grad = down.result()[:own]
    S.small[0:1, :] = jnp.sum(grad * unit, 0, keepdims=True)
    S.small[1:2, :] = jnp.sum(grad, 0, keepdims=True)
    S.small4[t] = S.small[...]
    base3 = links.take(3)
    for j in range(3):
        peer = lax.rem(t + j + 1, 4)
        links.start(S.small4.at[t], S.small4.at[t], base3 + j, tensor=peer)
    S.gt[...] += norm_back(grad, unit, inverse, vector(S.g1))
    sums.at("told")
    for j in range(3):
        peer = lax.rem(t + 3 - j, 4)
        links.arrived(S.small4.at[peer], base3 + j, tensor=peer)
    over = S.small4[0] + S.small4[1] + S.small4[2] + S.small4[3]
    row = lax.broadcasted_iota(jnp.int32, over.shape, 0)
    near = min(8, n.dp)
    inner = Everyone(links, S.smalls, d % near, near, lambda j: d // near * near + j)
    inner.start(jnp.where(row < 6, over, S.small[...]))
    sums.finish()
    total = inner.result()
    inner.finish()
    if n.dp > near:
        outer = Everyone(links, S.smalls2, d // near, n.dp // near, lambda j: j * near + d % near)
        outer.start(total)
        total = outer.result()
        outer.finish()
    S.small_sum[...] = total
    for j, s in enumerate(peers):
        links.copy(S.mix.at[s], S.mix4.at[t], mix_base + j, tensor=s).wait_send()
        links.copy(S.mix4.at[s], S.gm4.at[t], gm_base + j, tensor=s).wait_send()
    for transfer in (rows_in, cot_in, ow_in, hl_in, ahead, down):
        transfer.finish()
    links.finish()


SMALL = ("gain1", "shift1", "gain2", "shift2", "bias_out", "bias_down", "bias_up", "bias_qv")


def finish(n, output, gt, small, whole1, whole2):
    D, W, H = n.D, n.W, n.H
    steps = n.heads
    rows1 = D // steps

    def spread(output, gt, small, up, down, head, out, *refs):
        to_output, to_gt, to_up, to_down, to_qkv, to_out = refs[:6]
        vectors, sems = refs[6:14], refs[14]
        i = pl.program_id(0)
        held = refs[15:]
        come = [pltpu.make_async_copy(a, b, sems.at[j]) for j, (a, b) in enumerate(zip((output, gt), held))]
        go = [
            pltpu.make_async_copy(a, b, sems.at[2 + j])
            for j, (a, b) in enumerate(zip(held, (to_output, to_gt)))
        ]

        @pl.when(i == 0)
        def _():
            for copy in come:
                copy.start()
            for j in range(7):
                vectors[j][...] = small[j : j + 1, :].reshape(D)
            vectors[7][0:1, :] = small[7:8, :W]
            vectors[7][1:2, :] = small[7:8, H : H + W]

        to_up[...] = up[...].astype(wide)
        to_down[...] = down[...].astype(wide)
        for j in range(3):
            to_qkv[j] = head[j * HEAD_DIM : (j + 1) * HEAD_DIM, :].astype(wide)
        to_out[...] = out[...].astype(wide)

        @pl.when(i == 1)
        def _():
            for first, second in zip(come, go):
                first.wait()
                second.start()

        @pl.when(i == steps - 1)
        def _():
            for copy in go:
                copy.wait()

    hbm = pl.BlockSpec(memory_space=pl.ANY)
    whole = pl.BlockSpec(memory_space=pltpu.VMEM)
    at_row = lambda rows, index: pl.BlockSpec((rows, D), lambda i: (index(i), 0))
    shape = jax.ShapeDtypeStruct
    return pl.pallas_call(
        spread,
        grid=(steps,),
        out_shape=[shape(output.shape, low), shape(gt.shape, wide)]
        + [shape((D, D), wide)] * 2
        + [shape((3, W, D), wide), shape((W, D), wide)]
        + [shape((D,), wide)] * 7
        + [shape((2, W), wide)],
        in_specs=[hbm, hbm, whole, at_row(rows1, lambda i: i), at_row(rows1, lambda i: i + steps)]
        + [at_row(W, lambda i: i), at_row(HEAD_DIM, lambda i: 3 * steps + i)],
        out_specs=[hbm, hbm]
        + [at_row(rows1, lambda i: i)] * 2
        + [pl.BlockSpec((3, HEAD_DIM, D), lambda i: (0, i, 0)), at_row(HEAD_DIM, lambda i: i)]
        + [whole] * 8,
        scratch_shapes=[
            pltpu.SemaphoreType.DMA((4,)),
            pltpu.VMEM(output.shape, low),
            pltpu.VMEM(gt.shape, wide),
        ],
    )(output, gt, small, whole1, whole1, whole2, whole2)


def body(
    tokens,
    lengths,
    ln1_gain,
    ln1_shift,
    qkv_weight,
    qv_bias,
    out_weight,
    out_bias,
    ln2_gain,
    ln2_shift,
    up_weight,
    up_bias,
    down_weight,
    down_bias,
    cotangent,
):
    own, D = tokens.shape
    W = qkv_weight.shape[2]
    F = up_weight.shape[1]
    dp = lax.axis_size("dp")
    assert lax.axis_size("tensor") == 4 and lengths.shape[0] == 1 and F == D and 4 * W == D and 3 * round_up(W + 2, 128) == D
    R = round_up(own, 16)
    H = round_up(W + 2, 128)
    K = round_up(4 * R, 256)
    heads = W // HEAD_DIM
    extra = dp.bit_length() - 1 - 3
    n = types.SimpleNamespace(
        own=own, D=D, W=W, R=R, H=H, K=K, dp=dp, heads=heads, extra=extra
    )
    given = dict(
        x=tokens, lengths=lengths, g1=ln1_gain, b1=ln1_shift,
        wqkv=jnp.transpose(qkv_weight, (1, 2, 0)), bq=qv_bias, ow=out_weight, ob=out_bias,
        g2=ln2_gain, b2=ln2_shift, wup=up_weight, bup=up_bias, wdn=down_weight, db=down_bias,
        cot=cotangent,
    )
    outs = dict(
        output=((own, D), low), gt=((own, D), wide), small_sum=((8, D), wide),
        whole1=((2 * D, D), low), whole2=((D, D), low),
    )
    rows4 = ((4, R, D), low)
    slab = ((R, D), low)
    chunks = [(Quarters, D // 2), (Halves, D // 2)] * 2 + [(Quarters, W)] * 4
    scratch = dict(
        a1=rows4, cot4=rows4, ow4=((4, W, D), low), q=((4, R, H), low), k=((K, H), low),
        v=((K, H), low), kt=((H, K), low), vt=((H, K), low), e=((heads, 4, R, K), low),
        o=((4, R, H), wide), inv=((4, R, 128), wide), mix=((4, R, W), low), mix4=((4, R, W), low),
        hid=((own, D), wide),
        a24=rows4, pool=((4, R, K), low), gup=rows4, part=rows4,
        fop=rows4, pre1=slab, near1=slab, far1=slab, pre2=slab, near2=slab, far2=slab,
        gw=((2 * D, D), low), gub=((1, D), wide),
        small=((8, D), wide), hl4=rows4,
        gm4=((4, R, W), low), qt=((H, 4 * R), low), do=((R, H), wide),
        gw2=((D, D), low),
        small4=((4, 8, D), wide), smalls=((min(8, dp), 8, D), wide),
        box=((sum(kind.sizes(r, D, dp)[1] for kind, r in chunks), D), low),
        sum1=((2 * D, D), low), sum2=((D, D), low),
    )
    if dp > 8:
        scratch["smalls2"] = ((dp // 8, 8, D), wide)
    sems = 150 + dp + 8 * extra
    names = list(given) + list(outs) + list(scratch) + ["local", "send", "recv"]
    vmem = pl.BlockSpec(memory_space=pltpu.VMEM)
    smem = pl.BlockSpec(memory_space=pltpu.SMEM)
    hbm = pl.BlockSpec(memory_space=pl.ANY)
    output, gt, small, whole1, whole2 = pl.pallas_call(
        lambda *refs: kernel(n, types.SimpleNamespace(**dict(zip(names, refs)))),
        out_shape=tuple(jax.ShapeDtypeStruct(*spec) for spec in outs.values()),
        in_specs=[dict(lengths=smem, cot=hbm).get(name, vmem) for name in given],
        out_specs=tuple(hbm if name in ("whole1", "whole2") else vmem for name in outs),
        scratch_shapes=[pltpu.VMEM(*spec) for spec in scratch.values()]
        + [pltpu.SemaphoreType.DMA] + [pltpu.SemaphoreType.DMA((sems,))] * 2,
        compiler_params=pltpu.CompilerParams(
            collective_id=0, has_side_effects=True, vmem_limit_bytes=VMEM_BYTES
        ),
    )(*given.values())
    finished = finish(n, output, gt, small, whole1, whole2)
    small_rows = dict(zip(SMALL, finished[6:]))
    return (
        finished[0],
        finished[1],
        small_rows["gain1"],
        small_rows["shift1"],
        jnp.transpose(finished[4], (2, 0, 1)),
        small_rows["bias_qv"],
        finished[5],
        small_rows["bias_out"],
        small_rows["gain2"],
        small_rows["shift2"],
        finished[2],
        small_rows["bias_up"],
        finished[3],
        small_rows["bias_down"],
    )


def solution(mesh):
    placed = (
        P(("dp", "tensor"), None),
        P("dp"),
        P(),
        P(),
        P(None, None, "tensor"),
        P(None, "tensor"),
        P("tensor", None),
        P(),
        P(),
        P(),
        P(None, "tensor"),
        P("tensor"),
        P("tensor", None),
        P(),
        P(("dp", "tensor"), None),
    )
    return jax.shard_map(
        body,
        mesh=mesh,
        in_specs=placed,
        out_specs=(
            P(("dp", "tensor"), None),
            P(("dp", "tensor"), None),
            P(),
            P(),
            P(None, None, "tensor"),
            P(None, "tensor"),
            P("tensor", None),
            P(),
            P(),
            P(),
            P(None, "tensor"),
            P("tensor"),
            P("tensor", None),
            P(),
        ),
        check_vma=False,
    )
```

```python
import types

import jax
import jax.numpy as jnp
from jax import lax
from jax.experimental import pallas as pl
from jax.experimental.pallas import tpu as pltpu
from jax.sharding import PartitionSpec as P

HEAD_DIM = 64
MESH = pl.DeviceIdType.MESH
VMEM_BYTES = 62 * 2**20

epsilon = 1e-06
low = jnp.bfloat16
wide = jnp.float32


def round_up(amount, unit):
    return -(-amount // unit) * unit


def flipped(t, flip_chip, flip_core):
    return (t // 2 + flip_chip) % 2 * 2 + (t % 2 + flip_core) % 2


def dot(left, right):
    return jnp.dot(left, right, preferred_element_type=wide)


def dot_rows(left, right):
    return lax.dot_general(left, right, (((1,), (1,)), ((), ())), preferred_element_type=wide)


def dot_columns(left, right):
    return lax.dot_general(left, right, (((0,), (0,)), ((), ())), preferred_element_type=wide)


def standardize(values):
    center = values - jnp.mean(values, -1, keepdims=True)
    inverse = lax.rsqrt(jnp.mean(center * center, -1, keepdims=True) + epsilon)
    return center * inverse, inverse


def norm_back(grad, unit, inverse, gain):
    scaled = grad * gain
    return inverse * (
        scaled
        - jnp.mean(scaled, -1, keepdims=True)
        - unit * jnp.mean(scaled * unit, -1, keepdims=True)
    )


def pair(ref, p):
    _, rows, columns = ref.shape
    return ref[pl.ds(2 * p, 2)].reshape(2 * rows, columns)


def set_pair(ref, p, values):
    ref[pl.ds(2 * p, 2)] = values.reshape(2, -1, values.shape[1])


def flat(ref):
    a, b, c = ref.shape
    return ref[...].reshape(a * b, c)


class Links:
    def __init__(self, send, recv):
        self.send, self.recv, self.used, self.pending = send, recv, 0, []

    def take(self, amount=1):
        base = self.used
        self.used += amount
        assert self.used <= self.send.shape[0]
        return base

    def copy(self, src, dst, at, **where):
        return pltpu.make_async_remote_copy(
            src_ref=src,
            dst_ref=dst,
            send_sem=self.send.at[at],
            recv_sem=self.recv.at[at],
            device_id=where,
            device_id_type=MESH,
        )

    def start(self, src, dst, at, **where):
        copy = self.copy(src, dst, at, **where)
        copy.start()
        self.pending.append(copy)

    def arrived(self, dst, at, **where):
        self.copy(dst, dst, at, **where).wait_recv()

    def finish(self):
        for copy in self.pending:
            copy.wait_send()
        self.pending = []


class Gather:
    def __init__(self, links, buf, t, parts):
        self.links, self.buf, self.t, self.parts = links, buf, t, parts
        self.sib, self.cross, self.diag = flipped(t, 0, 1), flipped(t, 1, 0), flipped(t, 1, 1)
        self.base = links.take(3 * len(parts))

    def view(self, slot, part):
        start, size = self.parts[part]
        return self.buf.at[slot, pl.ds(start, size)]

    def _each(self):
        return range(len(self.parts))

    def start(self):
        for p in self._each():
            v = self.view(self.t, p)
            self.links.copy(v, v, self.base + 3 * p, tensor=self.cross).start()
        for p in self._each():
            v = self.view(self.t, p)
            self.links.copy(v, v, self.base + 3 * p + 1, tensor=self.sib).start()

    def wait_sib(self):
        for p in self._each():
            self.links.arrived(self.view(self.sib, p), self.base + 3 * p + 1, tensor=self.sib)

    def forward(self, parts=None):
        for p in self._each() if parts is None else parts:
            v = self.view(self.cross, p)
            self.links.arrived(v, self.base + 3 * p, tensor=self.cross)
            self.links.copy(v, v, self.base + 3 * p + 2, tensor=self.sib).start()

    def wait_diag(self, parts=None):
        for p in self._each() if parts is None else parts:
            self.links.arrived(self.view(self.diag, p), self.base + 3 * p + 2, tensor=self.sib)

    def finish(self):
        for p in self._each():
            v = self.view(self.t, p)
            self.links.copy(v, v, self.base + 3 * p, tensor=self.cross).wait_send()
            self.links.copy(v, v, self.base + 3 * p + 1, tensor=self.sib).wait_send()
            v = self.view(self.cross, p)
            self.links.copy(v, v, self.base + 3 * p + 2, tensor=self.sib).wait_send()


class Reduce:
    def __init__(self, links, part, pre, near, far, t, parts):
        self.links, self.part, self.t, self.parts = links, part, t, parts
        self.pre, self.near, self.far = pre, near, far
        self.sib, self.cross, self.diag = flipped(t, 0, 1), flipped(t, 1, 0), flipped(t, 1, 1)
        self.base = links.take(3 * len(parts))

    def _copy(self, kind, p):
        slot, box, peer = (
            (self.diag, self.pre, self.sib),
            (self.sib, self.near, self.sib),
            (self.cross, self.far, self.cross),
        )[kind]
        rows = pl.ds(*self.parts[p])
        return self.links.copy(
            self.part.at[slot, rows], box.at[rows], self.base + 3 * p + kind, tensor=peer
        )

    def _each(self, parts):
        return range(len(self.parts)) if parts is None else parts

    def send_diag(self, parts=None):
        for p in self._each(parts):
            self._copy(0, p).start()

    def send_sib(self):
        for p in self._each(None):
            self._copy(1, p).start()

    def send_cross(self, parts=None):
        for p in self._each(parts):
            self._copy(0, p).wait_recv()
            rows = pl.ds(*self.parts[p])
            self.part[self.cross, rows] = (
                self.part[self.cross, rows].astype(wide) + self.pre[rows].astype(wide)
            ).astype(low)
            self._copy(2, p).start()

    def result(self, p):
        self._copy(1, p).wait_recv()
        self._copy(2, p).wait_recv()
        rows = pl.ds(*self.parts[p])
        return (
            self.part[self.t, rows].astype(wide)
            + self.near[rows].astype(wide)
            + self.far[rows].astype(wide)
        )

    def finish(self):
        for p in self._each(None):
            for kind in range(3):
                self._copy(kind, p).wait_send()


class DataReduce:
    def __init__(self, links, held, whole, out, box, box_at, first, rows, d, count):
        self.links, self.held, self.whole, self.out, self.d = links, held, whole, out, d
        bits = count.bit_length() - 1
        assert count == 1 << bits and bits >= 3
        self.extra = list(range(3, bits))
        self.region = (first, rows, 0, held.shape[1])
        self.trail, self.sent, self.boxes = [], [], []
        for tall, broad in self.sizes(rows, held.shape[1], count)[0]:
            self.boxes.append(box.at[pl.ds(box_at, tall), pl.ds(0, broad)])
            box_at += tall
        self.base = links.take(9 + len(self.extra))
        self.plan()

    @classmethod
    def sizes(cls, rows, columns, count):
        found = cls.boxes_of(rows, columns)
        found += found[-1:] * (count.bit_length() - 1 - 3)
        return found, sum(size[0] for size in found)

    def _bit(self, b):
        return self.d // (1 << b) % 2

    def _peer(self, b):
        return self.d + (1 - 2 * self._bit(b)) * (1 << b)

    def _send(self, src, dst, at, peer):
        copy = self.links.copy(src, dst, self.base + at, dp=peer)
        copy.start()
        self.sent.append(copy)

    def _wait(self, dst, at, peer):
        self.links.arrived(dst, self.base + at, dp=peer)

    @staticmethod
    def _view(ref, region):
        row, rows, column, columns = region
        if columns == ref.shape[1]:
            return ref.at[pl.ds(row, rows)]
        return ref.at[pl.ds(row, rows), pl.ds(column, columns)]

    @staticmethod
    def _part(region, bit):
        row, rows, column, columns = region
        if rows % 32 == 0:
            return (pl.multiple_of(row + bit * (rows // 2), 16), rows // 2, column, columns)
        return (row, rows, pl.multiple_of(column + bit * (columns // 2), 128), columns // 2)

    def _give_half(self, b, box, at):
        bit = self._bit(b)
        self.trail.append(self.region)
        self._send(self._view(self.held, self._part(self.region, 1 - bit)), self.boxes[box], at, self._peer(b))
        self.region = self._part(self.region, bit)

    def _add(self, boxes, last):
        view = self._view(self.held, self.region)
        total = view[...].astype(wide)
        for box in boxes:
            total += self.boxes[box][...].astype(wide)
        if last:
            view = self._view(self.whole, self.region)
        view[...] = total.astype(low)
        if last:
            self._swap()

    def _swap(self):
        view = self._view(self.whole, self.region)
        for k, b in enumerate(self.extra):
            box, at = self.boxes[k - len(self.extra)], 9 + k
            copy = self.links.copy(view, box, self.base + at, dp=self._peer(b))
            copy.start()
            self._wait(box, at, self._peer(b))
            copy.wait_send()
            view[...] = (view[...].astype(wide) + box[...].astype(wide)).astype(low)

    def _give_whole(self, b, at):
        view = self._view(self.whole, self.region)
        self._send(view, view, at, self._peer(b))

    def _take_half(self, b, at):
        outer = self.trail.pop()
        view = self._view(self.whole, self._part(outer, 1 - self._bit(b)))
        self._wait(view, at, self._peer(b))
        self.region = outer

    def _leave(self):
        rows = pl.ds(self.region[0], self.region[1])
        self.left = pltpu.make_async_copy(
            self.whole.at[rows], self.out.at[rows], self.links.send.at[self.base + 8]
        )
        self.left.start()

    def step(self):
        if self.steps:
            self.steps.pop(0)()

    def finish(self):
        assert not self.steps
        self.left.wait()
        for copy in self.sent:
            copy.wait_send()


class Halves(DataReduce):
    order = (1, 0, 2)

    @staticmethod
    def boxes_of(rows, columns):
        found = []
        for _ in range(3):
            if rows % 32 == 0:
                rows //= 2
            else:
                columns //= 2
            found.append((rows, columns))
        return found

    def plan(self):
        low_bit, x, high = self.order
        self.steps = [
            lambda: self._give_half(low_bit, 0, 0),
            lambda: (self._wait_box(low_bit, 0), self._add((0,), False), self._give_half(x, 1, 1)),
            lambda: (self._wait_box(x, 1), self._add((1,), False), self._give_half(high, 2, 2)),
            lambda: (self._wait_box(high, 2), self._add((2,), True), self._give_whole(high, 3)),
            lambda: (self._take_half(high, 3), self._give_whole(x, 4)),
            lambda: (self._take_half(x, 4), self._give_whole(low_bit, 5)),
            lambda: (self._take_half(low_bit, 5), self._leave()),
        ]

    def _wait_box(self, b, box):
        self._wait(self.boxes[box], box, self._peer(b))


class Quarters(DataReduce):
    @staticmethod
    def boxes_of(rows, columns):
        tall, broad = rows // 8, columns
        if tall % 16:
            tall, broad = rows // 4, columns // 2
        return [(rows // 2, columns)] + [(tall, broad)] * 3

    def plan(self):
        self.steps = [
            lambda: self._give_half(0, 0, 0),
            lambda: (self._wait(self.boxes[0], 0, self._peer(0)), self._add((0,), False), self._give_quarters()),
            lambda: (self._take_boxes(), self._add((1, 2, 3), True), self._give_quarter()),
            lambda: (self._take_quarters(), self._give_whole(0, 7)),
            lambda: (self._take_half(0, 7), self._leave()),
        ]

    def _z(self, j):
        low_bit = (self._bit(1) + j % 2) % 2
        high = (self._bit(2) + j // 2) % 2
        return low_bit, high, self.d // 8 * 8 + high * 4 + low_bit * 2 + self._bit(0)

    def _quarter(self, j):
        low_bit, high, peer = self._z(j)
        return self._part(self._part(self.trail[-1], high), low_bit), peer

    def _give_quarters(self):
        self.trail.append(self.region)
        for j in (1, 2, 3):
            part, peer = self._quarter(j)
            self._send(self._view(self.held, part), self.boxes[j], j, peer)
        self.region = self._quarter(0)[0]

    def _take_boxes(self):
        for j in (1, 2, 3):
            self._wait(self.boxes[j], j, self._z(j)[2])

    def _give_quarter(self):
        view = self._view(self.whole, self.region)
        for j in (1, 2, 3):
            self._send(view, view, 3 + j, self._z(j)[2])

    def _take_quarters(self):
        for j in (1, 2, 3):
            part, peer = self._quarter(j)
            self._wait(self._view(self.whole, part), 3 + j, peer)
        self.region = self.trail.pop()


class Pipeline:
    def __init__(self, plan):
        self.plan, self.members = plan, []

    def add(self, member):
        self.members.append(member)
        member.step()

    def at(self, place):
        for number in self.plan[place]:
            self.members[number].step()

    def finish(self):
        self.at("end")
        for m in self.members:
            while m.steps:
                m.step()
            m.finish()


PLAN = dict(
    waiting=(),
    shared=(0,),
    arriving=(1,),
    h0p0=(),
    h0p2=(3, 2),
    h0=(1,),
    h1p0=(2, 4, 1),
    h1p2=(2, 3),
    h1=(0,),
    h2p0=(1,),
    h2p2=(5, 4, 2),
    h2=(1, 3),
    led=(5, 0),
    crossing=(1, 6, 7, 5, 4),
    told=(6, 7, 3),
    end=(2, 6, 5, 7, 0, 4, 6, 2, 7),
)


class Everyone:
    def __init__(self, links, buf, me, count, device):
        self.links, self.buf, self.me, self.count, self.device = links, buf, me, count, device
        self.base = links.take(count)

    def _copy(self, j):
        slot = self.buf.at[self.me]
        peer = self.device(lax.rem(self.me + j, self.count))
        return self.links.copy(slot, slot, self.base + j, dp=peer)

    def _loop(self, act):
        def one(j, carry):
            act(j)
            return carry

        lax.fori_loop(1, self.count, one, 0)

    def start(self, values):
        self.buf[self.me] = values
        self._loop(lambda j: self._copy(j).start())

    def _hear(self, j):
        peer = lax.rem(self.me + self.count - j, self.count)
        self.links.arrived(self.buf.at[peer], self.base + j, dp=self.device(peer))

    def result(self):
        self._loop(self._hear)
        return lax.fori_loop(1, self.count, lambda j, acc: acc + self.buf[j], self.buf[0])

    def finish(self):
        self._loop(lambda j: self._copy(j).wait_send())


def greet(axis, me, count):
    barrier = pltpu.get_barrier_semaphore()

    def one(j, carry):
        pl.semaphore_signal(
            barrier, inc=1, device_id={axis: lax.rem(me + j, count)}, device_id_type=MESH
        )
        return carry

    lax.fori_loop(1, count, one, 0)


def await_greetings(amount):
    pl.semaphore_wait(pltpu.get_barrier_semaphore(), amount)


def halves(rows):
    first = round_up(rows // 2, 16)
    return ((0, first), (first, rows - first))


def head_masks(shape, local_heads):
    lane = lax.broadcasted_iota(jnp.int32, shape, 1)
    return [
        jnp.where((lane >= h * HEAD_DIM) & (lane < (h + 1) * HEAD_DIM), 1.0, 0.0)
        for h in range(local_heads)
    ], lane


def kernel(n, S):
    links = Links(S.send, S.recv)
    t = lax.axis_index("tensor")
    d = lax.axis_index("dp")
    greet("tensor", t, 4)
    greet("dp", d, n.dp)
    R, own, W, H, D, K = n.R, n.own, n.W, n.H, n.D, n.K
    split = halves(R)
    vector = lambda ref: ref[...].reshape(1, D)

    fetch = pltpu.make_async_copy(S.cot, S.gt, S.local)
    fetch.start()
    S.a1[t] = jnp.zeros((R, D), low)
    S.cot4[t] = jnp.zeros((R, D), low)
    S.a24[t] = jnp.zeros((R, D), low)
    S.hl4[t] = jnp.zeros((R, D), low)
    unit, _ = standardize(S.x[...].astype(wide))
    S.a1[t, 0:own, :] = (unit * vector(S.g1) + vector(S.b1)).astype(low)
    fetch.wait()
    S.cot4[t, 0:own, :] = S.gt[...].astype(low)
    S.ow4[t] = S.ow[...]
    await_greetings(3 + n.dp - 1)
    rows_in = Gather(links, S.a1, t, halves(R))
    cot_in = Gather(links, S.cot4, t, halves(R))
    ow_in = Gather(links, S.ow4, t, ((0, W),))
    rows_in.start()
    S.gw[0:D, :] = jnp.transpose(S.wup[...])
    S.gw[D:, :] = jnp.transpose(S.wdn[...])
    S.v[4 * R :, :] = jnp.zeros((K - 4 * R, H), low)
    length = S.lengths[0]

    chip = t // 2

    def project(i, carry):
        s = flipped(t, i // 2, i % 2)

        @pl.when(i == 1)
        def _():
            rows_in.wait_sib()

        @pl.when(i == 2)
        def _():
            rows_in.forward()
            ow_in.start()

        @pl.when(i == 3)
        def _():
            rows_in.wait_diag()

        slab = S.a1[s]
        lane = lax.broadcasted_iota(jnp.int32, (R, H - W), 1)
        row = lax.broadcasted_iota(jnp.int32, (R, H - W), 0)
        absent = (row >= own) | (row + s * own >= length)
        at = pl.ds(pl.multiple_of(s * R, 16), R)
        out = dot_rows(slab, S.wqkv[0]) + S.bq[0:1, :]
        S.q[s, :, :W] = (out.astype(low).astype(wide) * HEAD_DIM**-0.5).astype(low)
        S.q[s, :, W:] = jnp.where(lane == 0, HEAD_DIM**-0.5, 0.0).astype(low)
        S.k[at, :W] = dot_rows(slab, S.wqkv[1]).astype(low)
        S.k[at, W:] = jnp.where((lane == 0) & absent, -8e30, 0.0).astype(low)
        S.v[at, :W] = (dot_rows(slab, S.wqkv[2]) + S.bq[1:2, :]).astype(low)
        S.v[at, W:] = jnp.where(lane < 2, 1.0, 0.0).astype(low)
        return carry

    lax.fori_loop(0, 4, project, 0)
    if K > 4 * R:
        lane = lax.broadcasted_iota(jnp.int32, (K - 4 * R, H), 1)
        S.k[4 * R :, :] = jnp.where(lane == W, -8e30, 0.0).astype(low)
    S.kt[...] = jnp.transpose(S.k[...])
    S.vt[...] = jnp.transpose(S.v[...])

    masks, lane = head_masks((1, H), n.heads)
    mix_base = links.take(3)

    peers = [flipped(t, 1, 0), flipped(t, 1, 1), flipped(t, 0, 1)]

    def attend(i, carry):
        s = flipped(t, 1 - i // 2, (i + i // 2) % 2)
        query = S.q[s]
        mixed = jnp.zeros((R, H), wide)
        inverse = jnp.zeros((R, 128), wide)
        first = lax.broadcasted_iota(jnp.int32, (1, 128), 1)

        def score(h):
            here = jnp.where(lane == W, 1.0, masks[h]).astype(low)
            return dot(query * here, S.kt[...])

        ready = score(0)
        for h in range(n.heads):
            scores = ready
            if h + 1 < n.heads:
                ready = score(h + 1)
            terms = jnp.exp(scores - jnp.max(scores, -1, keepdims=True)).astype(low)
            S.e[h, s] = terms
            part = dot(terms, S.v[...])
            scale = 1.0 / part[:, W : W + 1]
            mixed += part * (scale * masks[h])
            inverse = jnp.where(first == h, scale, inverse)
        S.o[s] = mixed
        S.inv[s] = inverse
        S.mix[s] = mixed[:, :W].astype(low)

        @pl.when(i < 3)
        def _():
            links.copy(S.mix.at[s], S.mix4.at[t], mix_base + i, tensor=s).start()

        @pl.when(i == 1)
        def _():
            cot_in.start()

        @pl.when(i == 2)
        def _():
            ow_in.wait_sib()
            ow_in.forward()

        return carry

    lax.fori_loop(0, 4, attend, 0)
    ow_in.wait_diag()
    S.mix4[t] = S.mix[t]
    for j, s in enumerate(peers):
        links.arrived(S.mix4.at[s], mix_base + j, tensor=s)

    total = dot(S.mix4[0], S.ow4[0])
    for j in range(1, 4):
        total += dot(S.mix4[j], S.ow4[j])
    total = S.x[...].astype(wide) + (total[:own] + vector(S.ob))
    S.hid[...] = total
    unit, _ = standardize(total)
    S.a24[t, 0:own, :] = (unit * vector(S.g2) + vector(S.b2)).astype(low)
    next_in = Gather(links, S.a24, t, halves(R))
    next_in.start()
    back = Reduce(links, S.part, S.pre1, S.near1, S.far1, t, split)
    ahead = Reduce(links, S.fop, S.pre2, S.near2, S.far2, t, split)
    S.gub[...] = jnp.zeros_like(S.gub)

    def feed(s, start, size):
        rows = pl.ds(start, size)
        up = dot(S.a24[s, rows], S.wup[...]) + vector(S.bup)
        square = up * up
        c = 0.7978845608028654
        bend = jnp.tanh(c * up * (1.0 + 0.044715 * square))
        half = 0.5 * (1.0 + bend)
        slope = half + 0.5 * up * (1.0 - bend * bend) * (c + (3 * 0.044715 * c) * square)
        active = (up * half).astype(low)
        S.pool[s, rows, 0:D] = active
        grad = (dot(S.cot4[s, rows], S.gw[D:, :]) * slope).astype(low)
        S.gup[s, rows] = grad
        S.part[s, rows] = dot(grad, S.gw[0:D, :]).astype(low)
        S.gub[...] += jnp.sum(grad.astype(wide), 0, keepdims=True)

    def lead_out(s, start, size):
        rows = pl.ds(start, size)
        S.fop[s, rows] = dot(S.pool[s, rows, 0:D], S.wdn[...]).astype(low)

    def feed_here(i, carry):
        s = flipped(t, 0, i)

        @pl.when(i == 1)
        def _():
            next_in.wait_sib()
            cot_in.wait_sib()

        feed(s, 0, R)

        @pl.when(i == 1)
        def _():
            back.send_sib()

        lead_out(s, 0, R)
        return carry

    lax.fori_loop(0, 2, feed_here, 0)
    ahead.send_sib()
    for p in (0, 1):

        def feed_there(i, carry, p=p):
            @pl.when(i == 0)
            def _():
                cot_in.forward([p])
                next_in.forward([p])

            @pl.when(i == 1)
            def _():
                cot_in.wait_diag([p])
                next_in.wait_diag([p])

            feed(flipped(t, 1, i), *split[p])
            if p == 1:

                @pl.when(i == 0)
                def _():
                    back.send_cross([0])

            return carry

        lax.fori_loop(0, 2, feed_there, 0)
        back.send_diag([p])
    for i in (0, 1):
        lead_out(flipped(t, 1, i), 0, R)
    back.send_cross([1])
    ahead.send_diag()

    sums = Pipeline(PLAN)
    tile = D // 2
    box_at = 0

    def sum_over_dp(kind, held, whole, out, first, rows):
        nonlocal box_at
        sums.add(kind(links, held, whole, out, S.box, box_at, first, rows, d, n.dp))
        box_at += kind.sizes(rows, D, n.dp)[1]

    for left, right, first in ((S.a24, S.gup, 0), (S.pool, S.cot4, D)):
        rows = left[:, :, 0:D].reshape(4 * R, D)
        S.gw[first : first + D, :] = dot_columns(rows, flat(right)).astype(low)
        for at in (first, first + tile):
            kind = Quarters if at in (0, D + tile) else Halves
            sum_over_dp(kind, S.gw, S.sum1, S.whole1, at, tile)

    sums.at("waiting")
    S.small[...] = jnp.zeros_like(S.small)
    gm_base = links.take(6)
    shared = lambda s, p, j: links.copy(
        S.mix4.at[s, pl.ds(*split[p])], S.gm4.at[t, pl.ds(*split[p])], gm_base + 3 * p + j, tensor=peers[j]
    )
    for p, (start, size) in enumerate(split):
        real = min(size, own - start)
        rows = pl.ds(start, real)
        grad = back.result(p)[:real]
        unit, inverse = standardize(S.hid[rows])
        S.small[2:3, :] += jnp.sum(grad * unit, 0, keepdims=True)
        S.small[3:4, :] += jnp.sum(grad, 0, keepdims=True)
        S.gt[rows] += norm_back(grad, unit, inverse, vector(S.g2))
        S.hl4[t, rows] = S.gt[rows].astype(low)
        rows = pl.ds(start, size)
        for j, s in enumerate(peers + [t]):
            product = dot_rows(S.hl4[t, rows], S.ow4[s]).astype(low)
            if j < 3:
                S.mix4[s, rows] = product
                shared(s, p, j).start()
            else:
                S.gm4[t, rows] = product
    S.small[4:5, :] = jnp.sum(S.hl4[t].astype(wide), 0, keepdims=True)
    S.small[5:6, :] = jnp.sum(S.cot4[t].astype(wide), 0, keepdims=True)
    S.small[6:7, :] = S.gub[...]
    hl_in = Gather(links, S.hl4, t, halves(R))

    next_in.finish()
    S.do[...] = jnp.zeros_like(S.do)
    S.qt[...] = jnp.transpose(flat(S.q))
    sums.at("shared")

    def prepare(i, s):
        if i > 0:
            j = (None, 2, 0, 1)[i]
            for p in (0, 1):
                rows = pl.ds(*split[p])
                links.arrived(S.gm4.at[s, rows], gm_base + 3 * p + j, tensor=peers[j])
        S.do[:, :W] = S.gm4[s].astype(wide)
        inverse = sum(S.inv[s, :, h : h + 1] * masks[h] for h in range(n.heads))
        scaled = (S.do[...] * inverse).astype(low)
        S.v[pl.ds(pl.multiple_of(s * R, 16), R), :] = scaled
        scaled = scaled.astype(wide)
        product = scaled * S.o[s]
        for h in range(n.heads):
            inner = -jnp.sum(product * masks[h], -1, keepdims=True)
            upper = inner.astype(low).astype(wide)
            S.a24[s, :, h * H : (h + 1) * H] = (
                scaled * masks[h]
                + jnp.where(lane == W, upper, 0.0)
                + jnp.where(lane == W + 1, inner - upper, 0.0)
            ).astype(low)

    def pull(h, p):
        grad_p = dot(pair(S.a24.at[:, :, h * H : (h + 1) * H], p), S.vt[...])
        grad_s = (pair(S.e.at[h], p).astype(wide) * grad_p).astype(low)
        set_pair(S.pool, p, grad_s)
        dq = dot(grad_s, S.k[...]) * (masks[h] * HEAD_DIM**-0.5)
        if h > 0:
            dq += pair(S.gup.at[:, :, 0:H], p).astype(wide)
        S.gup[pl.ds(2 * p, 2), :, 0:H] = dq.astype(low).reshape(2, R, H)

    def weights(h):
        at = slice(h * HEAD_DIM, (h + 1) * HEAD_DIM)
        tile = h * HEAD_DIM // 128 * 128
        dqt = jnp.transpose(flat(S.gup.at[:, :, tile : tile + 128]))
        left = jnp.concatenate(
            [dqt[h * HEAD_DIM - tile : (h + 1) * HEAD_DIM - tile], S.qt[at, :], S.kt[at, : 4 * R]], 0
        )
        S.gw2[h * W : (h + 1) * W, :] = dot(left, flat(S.a1)).astype(low)
        sum_over_dp(Quarters, S.gw2, S.sum2, S.whole2, h * W, W)

    for h in range(n.heads):
        for i in (0, 2):
            if (h, i) == (0, 2):
                sums.at("arriving")
            if h == 0:
                prepare(i, flipped(t, i // 2, 0))
                prepare(i + 1, flipped(t, i // 2, 1))
            if (h, i) == (0, 2):
                hl_in.start()
            pull(h, (chip + i // 2) % 2)
            sums.at(f"h{h}p{i}")
            if (h, i) == (1, 0):
                hl_in.wait_sib()
                hl_in.forward()
                ahead.send_cross()
            elif (h, i) == (1, 2):
                hl_in.wait_diag()
                S.gw2[3 * W :, :] = dot_columns(flat(S.mix), flat(S.hl4)).astype(low)
                sum_over_dp(Quarters, S.gw2, S.sum2, S.whole2, 3 * W, W)
        if h == 0:
            S.v[4 * R :, :] = jnp.zeros((K - 4 * R, H), low)
            S.kt[...] = jnp.transpose(S.v[...])
        at = slice(h * HEAD_DIM, (h + 1) * HEAD_DIM)
        S.qt[at, :] = dot(S.qt[at, :], flat(S.pool))[:, : 4 * R].astype(low)
        S.kt[at, : 4 * R] = dot(S.kt[at, : 4 * R], flat(S.e.at[h]))[:, : 4 * R].astype(low)
        if h + 1 < n.heads:
            weights(h)
        sums.at(f"h{h}")

    pad = jnp.zeros((R, H - W), low)
    for part, grad_t in ((1, S.qt), (2, S.kt)):
        rows = jnp.transpose(grad_t[:W, : 4 * R])
        for s in range(4):
            S.gup[s, :, part * H : part * H + W] = rows[s * R : (s + 1) * R]
            S.gup[s, :, part * H + W : (part + 1) * H] = pad

    back.finish()
    down = Reduce(links, S.part, S.pre1, S.near1, S.far1, t, split)

    def lead(s, start, size):
        rows = pl.ds(start, size)
        out = dot(S.gup[s, rows, 0:W], S.wqkv[0])
        out += dot(S.gup[s, rows, H : H + W], S.wqkv[1])
        out += dot(S.gup[s, rows, 2 * H : 2 * H + W], S.wqkv[2])
        S.part[s, rows] = out.astype(low)

    cross, diag, sib = peers
    lead(diag, *split[0])
    down.send_diag([0])
    lead(cross, *split[0])
    weights(n.heads - 1)
    down.send_cross([0])
    lead(diag, *split[1])
    down.send_diag([1])
    lead(cross, *split[1])
    down.send_cross([1])
    lead(sib, 0, R)
    down.send_sib()
    lead(t, 0, R)
    sums.at("led")
    S.small[7:8, 0:H] = jnp.sum(flat(S.gup.at[:, :, 0:H]).astype(wide), 0, keepdims=True)
    S.small[7:8, H : 2 * H] = jnp.sum(
        flat(S.gup.at[:, :, 2 * H : 3 * H]).astype(wide), 0, keepdims=True
    )
    result = jnp.concatenate([ahead.result(0), ahead.result(1)], 0)
    S.output[...] = (S.hid[...] + (result[:own] + vector(S.db))).astype(low)
    sums.at("crossing")

    unit, inverse = standardize(S.x[...].astype(wide))
    grad = jnp.concatenate([down.result(0), down.result(1)], 0)[:own]
    S.small[0:1, :] = jnp.sum(grad * unit, 0, keepdims=True)
    S.small[1:2, :] = jnp.sum(grad, 0, keepdims=True)
    S.small4[t] = S.small[...]
    base3 = links.take(3)
    for j in range(3):
        peer = lax.rem(t + j + 1, 4)
        links.start(S.small4.at[t], S.small4.at[t], base3 + j, tensor=peer)
    S.gt[...] += norm_back(grad, unit, inverse, vector(S.g1))
    sums.at("told")
    for j in range(3):
        peer = lax.rem(t + 3 - j, 4)
        links.arrived(S.small4.at[peer], base3 + j, tensor=peer)
    over = S.small4[0] + S.small4[1] + S.small4[2] + S.small4[3]
    row = lax.broadcasted_iota(jnp.int32, over.shape, 0)
    near = min(8, n.dp)
    inner = Everyone(links, S.smalls, d % near, near, lambda j: d // near * near + j)
    inner.start(jnp.where(row < 6, over, S.small[...]))
    sums.finish()
    total = inner.result()
    inner.finish()
    if n.dp > near:
        outer = Everyone(links, S.smalls2, d // near, n.dp // near, lambda j: j * near + d % near)
        outer.start(total)
        total = outer.result()
        outer.finish()
    S.small_sum[...] = total
    for j, s in enumerate(peers):
        links.copy(S.mix.at[s], S.mix4.at[t], mix_base + j, tensor=s).wait_send()
        for p in (0, 1):
            shared(s, p, j).wait_send()
    for transfer in (rows_in, cot_in, ow_in, hl_in, ahead, down):
        transfer.finish()
    links.finish()


SMALL = ("gain1", "shift1", "gain2", "shift2", "bias_out", "bias_down", "bias_up", "bias_qv")


def finish(n, output, gt, small, whole1, whole2):
    D, W, H = n.D, n.W, n.H
    steps = n.heads
    rows1 = D // steps

    def spread(output, gt, small, up, down, head, out, *refs):
        to_output, to_gt, to_up, to_down, to_qkv, to_out = refs[:6]
        vectors, sems = refs[6:14], refs[14]
        i = pl.program_id(0)
        held = refs[15:]
        come = [pltpu.make_async_copy(a, b, sems.at[j]) for j, (a, b) in enumerate(zip((output, gt), held))]
        go = [
            pltpu.make_async_copy(a, b, sems.at[2 + j])
            for j, (a, b) in enumerate(zip(held, (to_output, to_gt)))
        ]

        @pl.when(i == 0)
        def _():
            for copy in come:
                copy.start()
            for j in range(7):
                vectors[j][...] = small[j : j + 1, :].reshape(D)
            vectors[7][0:1, :] = small[7:8, :W]
            vectors[7][1:2, :] = small[7:8, H : H + W]

        to_up[...] = up[...].astype(wide)
        to_down[...] = down[...].astype(wide)
        for j in range(3):
            to_qkv[j] = head[j * HEAD_DIM : (j + 1) * HEAD_DIM, :].astype(wide)
        to_out[...] = out[...].astype(wide)

        @pl.when(i == 1)
        def _():
            for first, second in zip(come, go):
                first.wait()
                second.start()

        @pl.when(i == steps - 1)
        def _():
            for copy in go:
                copy.wait()

    hbm = pl.BlockSpec(memory_space=pl.ANY)
    whole = pl.BlockSpec(memory_space=pltpu.VMEM)
    at_row = lambda rows, index: pl.BlockSpec((rows, D), lambda i: (index(i), 0))
    shape = jax.ShapeDtypeStruct
    return pl.pallas_call(
        spread,
        grid=(steps,),
        out_shape=[shape(output.shape, low), shape(gt.shape, wide)]
        + [shape((D, D), wide)] * 2
        + [shape((3, W, D), wide), shape((W, D), wide)]
        + [shape((D,), wide)] * 7
        + [shape((2, W), wide)],
        in_specs=[hbm, hbm, whole, at_row(rows1, lambda i: i), at_row(rows1, lambda i: i + steps)]
        + [at_row(W, lambda i: i), at_row(HEAD_DIM, lambda i: 3 * steps + i)],
        out_specs=[hbm, hbm]
        + [at_row(rows1, lambda i: i)] * 2
        + [pl.BlockSpec((3, HEAD_DIM, D), lambda i: (0, i, 0)), at_row(HEAD_DIM, lambda i: i)]
        + [whole] * 8,
        scratch_shapes=[
            pltpu.SemaphoreType.DMA((4,)),
            pltpu.VMEM(output.shape, low),
            pltpu.VMEM(gt.shape, wide),
        ],
    )(output, gt, small, whole1, whole1, whole2, whole2)


def body(
    tokens,
    lengths,
    ln1_gain,
    ln1_shift,
    qkv_weight,
    qv_bias,
    out_weight,
    out_bias,
    ln2_gain,
    ln2_shift,
    up_weight,
    up_bias,
    down_weight,
    down_bias,
    cotangent,
):
    own, D = tokens.shape
    W = qkv_weight.shape[2]
    F = up_weight.shape[1]
    dp = lax.axis_size("dp")
    assert lax.axis_size("tensor") == 4 and lengths.shape[0] == 1 and F == D and 4 * W == D and 3 * round_up(W + 2, 128) == D
    R = round_up(own, 16)
    H = round_up(W + 2, 128)
    K = round_up(4 * R, 256)
    heads = W // HEAD_DIM
    extra = dp.bit_length() - 1 - 3
    n = types.SimpleNamespace(
        own=own, D=D, W=W, R=R, H=H, K=K, dp=dp, heads=heads, extra=extra
    )
    given = dict(
        x=tokens, lengths=lengths, g1=ln1_gain, b1=ln1_shift,
        wqkv=jnp.transpose(qkv_weight, (1, 2, 0)), bq=qv_bias, ow=out_weight, ob=out_bias,
        g2=ln2_gain, b2=ln2_shift, wup=up_weight, bup=up_bias, wdn=down_weight, db=down_bias,
        cot=cotangent,
    )
    outs = dict(
        output=((own, D), low), gt=((own, D), wide), small_sum=((8, D), wide),
        whole1=((2 * D, D), low), whole2=((D, D), low),
    )
    rows4 = ((4, R, D), low)
    slab = ((R, D), low)
    chunks = [(Quarters, D // 2), (Halves, D // 2)] * 2 + [(Quarters, W)] * 4
    scratch = dict(
        a1=rows4, cot4=rows4, ow4=((4, W, D), low), q=((4, R, H), low), k=((K, H), low),
        v=((K, H), low), kt=((H, K), low), vt=((H, K), low), e=((heads, 4, R, K), low),
        o=((4, R, H), wide), inv=((4, R, 128), wide), mix=((4, R, W), low), mix4=((4, R, W), low),
        hid=((own, D), wide),
        a24=rows4, pool=((4, R, K), low), gup=rows4, part=rows4,
        fop=rows4, pre1=slab, near1=slab, far1=slab, pre2=slab, near2=slab, far2=slab,
        gw=((2 * D, D), low), gub=((1, D), wide),
        small=((8, D), wide), hl4=rows4,
        gm4=((4, R, W), low), qt=((H, 4 * R), low), do=((R, H), wide),
        gw2=((D, D), low),
        small4=((4, 8, D), wide), smalls=((min(8, dp), 8, D), wide),
        box=((sum(kind.sizes(r, D, dp)[1] for kind, r in chunks), D), low),
        sum1=((2 * D, D), low), sum2=((D, D), low),
    )
    if dp > 8:
        scratch["smalls2"] = ((dp // 8, 8, D), wide)
    sems = 170 + dp + 8 * extra
    names = list(given) + list(outs) + list(scratch) + ["local", "send", "recv"]
    vmem = pl.BlockSpec(memory_space=pltpu.VMEM)
    smem = pl.BlockSpec(memory_space=pltpu.SMEM)
    hbm = pl.BlockSpec(memory_space=pl.ANY)
    output, gt, small, whole1, whole2 = pl.pallas_call(
        lambda *refs: kernel(n, types.SimpleNamespace(**dict(zip(names, refs)))),
        out_shape=tuple(jax.ShapeDtypeStruct(*spec) for spec in outs.values()),
        in_specs=[dict(lengths=smem, cot=hbm).get(name, vmem) for name in given],
        out_specs=tuple(hbm if name in ("whole1", "whole2") else vmem for name in outs),
        scratch_shapes=[pltpu.VMEM(*spec) for spec in scratch.values()]
        + [pltpu.SemaphoreType.DMA] + [pltpu.SemaphoreType.DMA((sems,))] * 2,
        compiler_params=pltpu.CompilerParams(
            collective_id=0, has_side_effects=True, vmem_limit_bytes=VMEM_BYTES
        ),
    )(*given.values())
    finished = finish(n, output, gt, small, whole1, whole2)
    small_rows = dict(zip(SMALL, finished[6:]))
    return (
        finished[0],
        finished[1],
        small_rows["gain1"],
        small_rows["shift1"],
        jnp.transpose(finished[4], (2, 0, 1)),
        small_rows["bias_qv"],
        finished[5],
        small_rows["bias_out"],
        small_rows["gain2"],
        small_rows["shift2"],
        finished[2],
        small_rows["bias_up"],
        finished[3],
        small_rows["bias_down"],
    )


def solution(mesh):
    placed = (
        P(("dp", "tensor"), None),
        P("dp"),
        P(),
        P(),
        P(None, None, "tensor"),
        P(None, "tensor"),
        P("tensor", None),
        P(),
        P(),
        P(),
        P(None, "tensor"),
        P("tensor"),
        P("tensor", None),
        P(),
        P(("dp", "tensor"), None),
    )
    return jax.shard_map(
        body,
        mesh=mesh,
        in_specs=placed,
        out_specs=(
            P(("dp", "tensor"), None),
            P(("dp", "tensor"), None),
            P(),
            P(),
            P(None, None, "tensor"),
            P(None, "tensor"),
            P("tensor", None),
            P(),
            P(),
            P(),
            P(None, "tensor"),
            P("tensor"),
            P("tensor", None),
            P(),
        ),
        check_vma=False,
    )
```

```python
import types

import jax
import jax.numpy as jnp
from jax import lax
from jax.experimental import pallas as pl
from jax.experimental.pallas import tpu as pltpu
from jax.sharding import PartitionSpec as P

HEAD_DIM = 64
MESH = pl.DeviceIdType.MESH
VMEM_BYTES = 62 * 2**20

epsilon = 1e-06
low = jnp.bfloat16
wide = jnp.float32


def round_up(amount, unit):
    return -(-amount // unit) * unit


def flipped(t, flip_chip, flip_core):
    return (t // 2 + flip_chip) % 2 * 2 + (t % 2 + flip_core) % 2


def dot(left, right):
    return jnp.dot(left, right, preferred_element_type=wide)


def dot_rows(left, right):
    return lax.dot_general(left, right, (((1,), (1,)), ((), ())), preferred_element_type=wide)


def dot_columns(left, right):
    return lax.dot_general(left, right, (((0,), (0,)), ((), ())), preferred_element_type=wide)


def standardize(values):
    center = values - jnp.mean(values, -1, keepdims=True)
    inverse = lax.rsqrt(jnp.mean(center * center, -1, keepdims=True) + epsilon)
    return center * inverse, inverse


def norm_back(grad, unit, inverse, gain):
    scaled = grad * gain
    return inverse * (
        scaled
        - jnp.mean(scaled, -1, keepdims=True)
        - unit * jnp.mean(scaled * unit, -1, keepdims=True)
    )


def pair(ref, p):
    _, rows, columns = ref.shape
    return ref[pl.ds(2 * p, 2)].reshape(2 * rows, columns)


def set_pair(ref, p, values):
    ref[pl.ds(2 * p, 2)] = values.reshape(2, -1, values.shape[1])


def flat(ref):
    a, b, c = ref.shape
    return ref[...].reshape(a * b, c)


class Links:
    def __init__(self, send, recv):
        self.send, self.recv, self.used, self.pending = send, recv, 0, []

    def take(self, amount=1):
        base = self.used
        self.used += amount
        assert self.used <= self.send.shape[0]
        return base

    def copy(self, src, dst, at, **where):
        return pltpu.make_async_remote_copy(
            src_ref=src,
            dst_ref=dst,
            send_sem=self.send.at[at],
            recv_sem=self.recv.at[at],
            device_id=where,
            device_id_type=MESH,
        )

    def start(self, src, dst, at, **where):
        copy = self.copy(src, dst, at, **where)
        copy.start()
        self.pending.append(copy)

    def arrived(self, dst, at, **where):
        self.copy(dst, dst, at, **where).wait_recv()

    def finish(self):
        for copy in self.pending:
            copy.wait_send()
        self.pending = []


class Gather:
    def __init__(self, links, buf, t, parts):
        self.links, self.buf, self.t, self.parts = links, buf, t, parts
        self.sib, self.cross, self.diag = flipped(t, 0, 1), flipped(t, 1, 0), flipped(t, 1, 1)
        self.base = links.take(3 * len(parts))

    def view(self, slot, part):
        start, size = self.parts[part]
        return self.buf.at[slot, pl.ds(start, size)]

    def _each(self):
        return range(len(self.parts))

    def start(self):
        for p in self._each():
            v = self.view(self.t, p)
            self.links.copy(v, v, self.base + 3 * p, tensor=self.cross).start()
        for p in self._each():
            v = self.view(self.t, p)
            self.links.copy(v, v, self.base + 3 * p + 1, tensor=self.sib).start()

    def wait_sib(self):
        for p in self._each():
            self.links.arrived(self.view(self.sib, p), self.base + 3 * p + 1, tensor=self.sib)

    def forward(self, parts=None):
        for p in self._each() if parts is None else parts:
            v = self.view(self.cross, p)
            self.links.arrived(v, self.base + 3 * p, tensor=self.cross)
            self.links.copy(v, v, self.base + 3 * p + 2, tensor=self.sib).start()

    def wait_diag(self, parts=None):
        for p in self._each() if parts is None else parts:
            self.links.arrived(self.view(self.diag, p), self.base + 3 * p + 2, tensor=self.sib)

    def finish(self):
        for p in self._each():
            v = self.view(self.t, p)
            self.links.copy(v, v, self.base + 3 * p, tensor=self.cross).wait_send()
            self.links.copy(v, v, self.base + 3 * p + 1, tensor=self.sib).wait_send()
            v = self.view(self.cross, p)
            self.links.copy(v, v, self.base + 3 * p + 2, tensor=self.sib).wait_send()


class Reduce:
    def __init__(self, links, part, pre, near, far, t, parts):
        self.links, self.part, self.t, self.parts = links, part, t, parts
        self.pre, self.near, self.far = pre, near, far
        self.sib, self.cross, self.diag = flipped(t, 0, 1), flipped(t, 1, 0), flipped(t, 1, 1)
        self.base = links.take(3 * len(parts))

    def _copy(self, kind, p):
        slot, box, peer = (
            (self.diag, self.pre, self.sib),
            (self.sib, self.near, self.sib),
            (self.cross, self.far, self.cross),
        )[kind]
        rows = pl.ds(*self.parts[p])
        return self.links.copy(
            self.part.at[slot, rows], box.at[rows], self.base + 3 * p + kind, tensor=peer
        )

    def _each(self, parts):
        return range(len(self.parts)) if parts is None else parts

    def send_diag(self, parts=None):
        for p in self._each(parts):
            self._copy(0, p).start()

    def send_sib(self):
        for p in self._each(None):
            self._copy(1, p).start()

    def send_cross(self, parts=None):
        for p in self._each(parts):
            self._copy(0, p).wait_recv()
            rows = pl.ds(*self.parts[p])
            self.part[self.cross, rows] = (
                self.part[self.cross, rows].astype(wide) + self.pre[rows].astype(wide)
            ).astype(low)
            self._copy(2, p).start()

    def result(self, p):
        self._copy(1, p).wait_recv()
        self._copy(2, p).wait_recv()
        rows = pl.ds(*self.parts[p])
        return (
            self.part[self.t, rows].astype(wide)
            + self.near[rows].astype(wide)
            + self.far[rows].astype(wide)
        )

    def finish(self):
        for p in self._each(None):
            for kind in range(3):
                self._copy(kind, p).wait_send()


class DataReduce:
    def __init__(self, links, held, whole, out, box, box_at, first, rows, d, count):
        self.links, self.held, self.whole, self.out, self.d = links, held, whole, out, d
        bits = count.bit_length() - 1
        assert count == 1 << bits and bits >= 3
        self.extra = list(range(3, bits))
        self.region = (first, rows, 0, held.shape[1])
        self.trail, self.sent, self.boxes = [], [], []
        for tall, broad in self.sizes(rows, held.shape[1], count)[0]:
            self.boxes.append(box.at[pl.ds(box_at, tall), pl.ds(0, broad)])
            box_at += tall
        self.base = links.take(9 + len(self.extra))
        self.plan()

    @classmethod
    def sizes(cls, rows, columns, count):
        found = cls.boxes_of(rows, columns)
        found += found[-1:] * (count.bit_length() - 1 - 3)
        return found, sum(size[0] for size in found)

    def _bit(self, b):
        return self.d // (1 << b) % 2

    def _peer(self, b):
        return self.d + (1 - 2 * self._bit(b)) * (1 << b)

    def _send(self, src, dst, at, peer):
        copy = self.links.copy(src, dst, self.base + at, dp=peer)
        copy.start()
        self.sent.append(copy)

    def _wait(self, dst, at, peer):
        self.links.arrived(dst, self.base + at, dp=peer)

    @staticmethod
    def _view(ref, region):
        row, rows, column, columns = region
        if columns == ref.shape[1]:
            return ref.at[pl.ds(row, rows)]
        return ref.at[pl.ds(row, rows), pl.ds(column, columns)]

    @staticmethod
    def _part(region, bit):
        row, rows, column, columns = region
        if rows % 32 == 0:
            return (pl.multiple_of(row + bit * (rows // 2), 16), rows // 2, column, columns)
        return (row, rows, pl.multiple_of(column + bit * (columns // 2), 128), columns // 2)

    def _give_half(self, b, box, at):
        bit = self._bit(b)
        self.trail.append(self.region)
        self._send(self._view(self.held, self._part(self.region, 1 - bit)), self.boxes[box], at, self._peer(b))
        self.region = self._part(self.region, bit)

    def _add(self, boxes, last):
        view = self._view(self.held, self.region)
        total = view[...].astype(wide)
        for box in boxes:
            total += self.boxes[box][...].astype(wide)
        if last:
            view = self._view(self.whole, self.region)
        view[...] = total.astype(low)
        if last:
            self._swap()

    def _swap(self):
        view = self._view(self.whole, self.region)
        for k, b in enumerate(self.extra):
            box, at = self.boxes[k - len(self.extra)], 9 + k
            copy = self.links.copy(view, box, self.base + at, dp=self._peer(b))
            copy.start()
            self._wait(box, at, self._peer(b))
            copy.wait_send()
            view[...] = (view[...].astype(wide) + box[...].astype(wide)).astype(low)

    def _give_whole(self, b, at):
        view = self._view(self.whole, self.region)
        self._send(view, view, at, self._peer(b))

    def _take_half(self, b, at):
        outer = self.trail.pop()
        view = self._view(self.whole, self._part(outer, 1 - self._bit(b)))
        self._wait(view, at, self._peer(b))
        self.region = outer

    def _leave(self):
        rows = pl.ds(self.region[0], self.region[1])
        self.left = pltpu.make_async_copy(
            self.whole.at[rows], self.out.at[rows], self.links.send.at[self.base + 8]
        )
        self.left.start()

    def step(self):
        if self.steps:
            self.steps.pop(0)()

    def finish(self):
        assert not self.steps
        self.left.wait()
        for copy in self.sent:
            copy.wait_send()


class Halves(DataReduce):
    order = (1, 0, 2)

    @staticmethod
    def boxes_of(rows, columns):
        found = []
        for _ in range(3):
            if rows % 32 == 0:
                rows //= 2
            else:
                columns //= 2
            found.append((rows, columns))
        return found

    def plan(self):
        low_bit, x, high = self.order
        self.steps = [
            lambda: self._give_half(low_bit, 0, 0),
            lambda: (self._wait_box(low_bit, 0), self._add((0,), False), self._give_half(x, 1, 1)),
            lambda: (self._wait_box(x, 1), self._add((1,), False), self._give_half(high, 2, 2)),
            lambda: (self._wait_box(high, 2), self._add((2,), True), self._give_whole(high, 3)),
            lambda: (self._take_half(high, 3), self._give_whole(x, 4)),
            lambda: (self._take_half(x, 4), self._give_whole(low_bit, 5)),
            lambda: (self._take_half(low_bit, 5), self._leave()),
        ]

    def _wait_box(self, b, box):
        self._wait(self.boxes[box], box, self._peer(b))


class Quarters(DataReduce):
    @staticmethod
    def boxes_of(rows, columns):
        tall, broad = rows // 8, columns
        if tall % 16:
            tall, broad = rows // 4, columns // 2
        return [(rows // 2, columns)] + [(tall, broad)] * 3

    def plan(self):
        self.steps = [
            lambda: self._give_half(0, 0, 0),
            lambda: (self._wait(self.boxes[0], 0, self._peer(0)), self._add((0,), False), self._give_quarters()),
            lambda: (self._take_boxes(), self._add((1, 2, 3), True), self._give_quarter()),
            lambda: (self._take_quarters(), self._give_whole(0, 7)),
            lambda: (self._take_half(0, 7), self._leave()),
        ]

    def _z(self, j):
        low_bit = (self._bit(1) + j % 2) % 2
        high = (self._bit(2) + j // 2) % 2
        return low_bit, high, self.d // 8 * 8 + high * 4 + low_bit * 2 + self._bit(0)

    def _quarter(self, j):
        low_bit, high, peer = self._z(j)
        return self._part(self._part(self.trail[-1], high), low_bit), peer

    def _give_quarters(self):
        self.trail.append(self.region)
        for j in (1, 2, 3):
            part, peer = self._quarter(j)
            self._send(self._view(self.held, part), self.boxes[j], j, peer)
        self.region = self._quarter(0)[0]

    def _take_boxes(self):
        for j in (1, 2, 3):
            self._wait(self.boxes[j], j, self._z(j)[2])

    def _give_quarter(self):
        view = self._view(self.whole, self.region)
        for j in (1, 2, 3):
            self._send(view, view, 3 + j, self._z(j)[2])

    def _take_quarters(self):
        for j in (1, 2, 3):
            part, peer = self._quarter(j)
            self._wait(self._view(self.whole, part), 3 + j, peer)
        self.region = self.trail.pop()


class Pipeline:
    def __init__(self, plan):
        self.plan, self.members = plan, []

    def add(self, member):
        self.members.append(member)
        member.step()

    def at(self, place):
        for number in self.plan[place]:
            self.members[number].step()

    def finish(self):
        self.at("end")
        for m in self.members:
            while m.steps:
                m.step()
            m.finish()


PLAN = dict(
    waiting=(),
    shared=(0,),
    arriving=(1,),
    h0p0=(),
    h0p2=(3, 2),
    h0=(1,),
    h1p0=(2, 4, 1),
    h1p2=(2, 3),
    h1=(0,),
    h2p0=(1,),
    h2p2=(5, 4, 2),
    h2=(1, 3),
    led=(5, 0),
    crossing=(1, 6, 7, 5, 4),
    told=(6, 7, 3),
    end=(2, 6, 5, 7, 0, 4, 6, 2, 7),
)


class Everyone:
    def __init__(self, links, buf, me, count, device):
        self.links, self.buf, self.me, self.count, self.device = links, buf, me, count, device
        self.base = links.take(count)

    def _copy(self, j):
        slot = self.buf.at[self.me]
        peer = self.device(lax.rem(self.me + j, self.count))
        return self.links.copy(slot, slot, self.base + j, dp=peer)

    def _loop(self, act):
        def one(j, carry):
            act(j)
            return carry

        lax.fori_loop(1, self.count, one, 0)

    def start(self, values):
        self.buf[self.me] = values
        self._loop(lambda j: self._copy(j).start())

    def _hear(self, j):
        peer = lax.rem(self.me + self.count - j, self.count)
        self.links.arrived(self.buf.at[peer], self.base + j, dp=self.device(peer))

    def result(self):
        self._loop(self._hear)
        return lax.fori_loop(1, self.count, lambda j, acc: acc + self.buf[j], self.buf[0])

    def finish(self):
        self._loop(lambda j: self._copy(j).wait_send())


def greet(axis, me, count):
    barrier = pltpu.get_barrier_semaphore()

    def one(j, carry):
        pl.semaphore_signal(
            barrier, inc=1, device_id={axis: lax.rem(me + j, count)}, device_id_type=MESH
        )
        return carry

    lax.fori_loop(1, count, one, 0)


def await_greetings(amount):
    pl.semaphore_wait(pltpu.get_barrier_semaphore(), amount)


def halves(rows):
    first = round_up(rows // 2, 16)
    return ((0, first), (first, rows - first))


def head_masks(shape, local_heads):
    lane = lax.broadcasted_iota(jnp.int32, shape, 1)
    return [
        jnp.where((lane >= h * HEAD_DIM) & (lane < (h + 1) * HEAD_DIM), 1.0, 0.0)
        for h in range(local_heads)
    ], lane


def kernel(n, S):
    links = Links(S.send, S.recv)
    t = lax.axis_index("tensor")
    d = lax.axis_index("dp")
    greet("tensor", t, 4)
    greet("dp", d, n.dp)
    R, own, W, H, D, K = n.R, n.own, n.W, n.H, n.D, n.K
    split = halves(R)
    vector = lambda ref: ref[...].reshape(1, D)

    fetch = pltpu.make_async_copy(S.cot, S.gt, S.local)
    fetch.start()
    S.a1[t] = jnp.zeros((R, D), low)
    S.cot4[t] = jnp.zeros((R, D), low)
    S.a24[t] = jnp.zeros((R, D), low)
    S.hl4[t] = jnp.zeros((R, D), low)
    unit, _ = standardize(S.x[...].astype(wide))
    S.a1[t, 0:own, :] = (unit * vector(S.g1) + vector(S.b1)).astype(low)
    fetch.wait()
    S.cot4[t, 0:own, :] = S.gt[...].astype(low)
    S.ow4[t] = S.ow[...]
    await_greetings(3 + n.dp - 1)
    rows_in = Gather(links, S.a1, t, halves(R))
    cot_in = Gather(links, S.cot4, t, halves(R))
    ow_in = Gather(links, S.ow4, t, ((0, W),))
    rows_in.start()
    S.gw[0:D, :] = jnp.transpose(S.wup[...])
    S.gw[D:, :] = jnp.transpose(S.wdn[...])
    S.v[4 * R :, :] = jnp.zeros((K - 4 * R, H), low)
    length = S.lengths[0]

    chip = t // 2

    def project(i, carry):
        s = flipped(t, i // 2, i % 2)

        @pl.when(i == 1)
        def _():
            rows_in.wait_sib()

        @pl.when(i == 2)
        def _():
            rows_in.forward()
            ow_in.start()

        @pl.when(i == 3)
        def _():
            rows_in.wait_diag()

        slab = S.a1[s]
        lane = lax.broadcasted_iota(jnp.int32, (R, H - W), 1)
        row = lax.broadcasted_iota(jnp.int32, (R, H - W), 0)
        absent = (row >= own) | (row + s * own >= length)
        at = pl.ds(pl.multiple_of(s * R, 16), R)
        out = dot_rows(slab, S.wqkv[0]) + S.bq[0:1, :]
        S.q[s, :, :W] = (out.astype(low).astype(wide) * HEAD_DIM**-0.5).astype(low)
        S.q[s, :, W:] = jnp.where(lane == 0, HEAD_DIM**-0.5, 0.0).astype(low)
        S.k[at, :W] = dot_rows(slab, S.wqkv[1]).astype(low)
        S.k[at, W:] = jnp.where((lane == 0) & absent, -8e30, 0.0).astype(low)
        S.v[at, :W] = (dot_rows(slab, S.wqkv[2]) + S.bq[1:2, :]).astype(low)
        S.v[at, W:] = jnp.where(lane < 2, 1.0, 0.0).astype(low)
        return carry

    lax.fori_loop(0, 4, project, 0)
    if K > 4 * R:
        lane = lax.broadcasted_iota(jnp.int32, (K - 4 * R, H), 1)
        S.k[4 * R :, :] = jnp.where(lane == W, -8e30, 0.0).astype(low)
    S.kt[...] = jnp.transpose(S.k[...])
    S.vt[...] = jnp.transpose(S.v[...])

    masks, lane = head_masks((1, H), n.heads)
    mix_base = links.take(3)

    peers = [flipped(t, 1, 0), flipped(t, 1, 1), flipped(t, 0, 1)]

    def attend(i, carry):
        s = flipped(t, 1 - i // 2, (i + i // 2) % 2)
        query = S.q[s]
        mixed = jnp.zeros((R, H), wide)
        inverse = jnp.zeros((R, 128), wide)
        first = lax.broadcasted_iota(jnp.int32, (1, 128), 1)

        def score(h):
            here = jnp.where(lane == W, 1.0, masks[h]).astype(low)
            return dot(query * here, S.kt[...])

        ready = score(0)
        for h in range(n.heads):
            scores = ready
            if h + 1 < n.heads:
                ready = score(h + 1)
            terms = jnp.exp(scores - jnp.max(scores, -1, keepdims=True)).astype(low)
            S.e[h, s] = terms
            part = dot(terms, S.v[...])
            scale = 1.0 / part[:, W : W + 1]
            mixed += part * (scale * masks[h])
            inverse = jnp.where(first == h, scale, inverse)
        S.o[s] = mixed
        S.inv[s] = inverse
        S.mix[s] = mixed[:, :W].astype(low)

        @pl.when(i < 3)
        def _():
            links.copy(S.mix.at[s], S.mix4.at[t], mix_base + i, tensor=s).start()

        @pl.when(i == 1)
        def _():
            cot_in.start()

        @pl.when(i == 2)
        def _():
            ow_in.wait_sib()
            ow_in.forward()

        return carry

    lax.fori_loop(0, 4, attend, 0)
    ow_in.wait_diag()
    S.mix4[t] = S.mix[t]
    for j, s in enumerate(peers):
        links.arrived(S.mix4.at[s], mix_base + j, tensor=s)

    total = dot(S.mix4[0], S.ow4[0])
    for j in range(1, 4):
        total += dot(S.mix4[j], S.ow4[j])
    total = S.x[...].astype(wide) + (total[:own] + vector(S.ob))
    S.hid[...] = total
    unit, _ = standardize(total)
    S.a24[t, 0:own, :] = (unit * vector(S.g2) + vector(S.b2)).astype(low)
    next_in = Gather(links, S.a24, t, halves(R))
    next_in.start()
    back = Reduce(links, S.part, S.pre1, S.near1, S.far1, t, split)
    ahead = Reduce(links, S.fop, S.pre2, S.near2, S.far2, t, split)
    S.gub[...] = jnp.zeros_like(S.gub)

    def feed(s, start, size):
        rows = pl.ds(start, size)
        up = dot(S.a24[s, rows], S.wup[...]) + vector(S.bup)
        square = up * up
        c = 0.7978845608028654
        bend = jnp.tanh(c * up * (1.0 + 0.044715 * square))
        half = 0.5 * (1.0 + bend)
        slope = half + 0.5 * up * (1.0 - bend * bend) * (c + (3 * 0.044715 * c) * square)
        active = (up * half).astype(low)
        S.pool[s, rows, 0:D] = active
        grad = (dot(S.cot4[s, rows], S.gw[D:, :]) * slope).astype(low)
        S.gup[s, rows] = grad
        S.part[s, rows] = dot(grad, S.gw[0:D, :]).astype(low)
        S.gub[...] += jnp.sum(grad.astype(wide), 0, keepdims=True)

    def lead_out(s, start, size):
        rows = pl.ds(start, size)
        S.fop[s, rows] = dot(S.pool[s, rows, 0:D], S.wdn[...]).astype(low)

    def feed_here(i, carry):
        s = flipped(t, 0, i)

        @pl.when(i == 1)
        def _():
            next_in.wait_sib()
            cot_in.wait_sib()

        feed(s, 0, R)

        @pl.when(i == 1)
        def _():
            back.send_sib()

        lead_out(s, 0, R)
        return carry

    lax.fori_loop(0, 2, feed_here, 0)
    ahead.send_sib()
    for p in (0, 1):

        def feed_there(i, carry, p=p):
            @pl.when(i == 0)
            def _():
                cot_in.forward([p])
                next_in.forward([p])

            @pl.when(i == 1)
            def _():
                cot_in.wait_diag([p])
                next_in.wait_diag([p])

            feed(flipped(t, 1, i), *split[p])
            if p == 1:

                @pl.when(i == 0)
                def _():
                    back.send_cross([0])

            return carry

        lax.fori_loop(0, 2, feed_there, 0)
        back.send_diag([p])
    for i in (0, 1):
        lead_out(flipped(t, 1, i), 0, R)
    back.send_cross([1])
    ahead.send_diag()

    sums = Pipeline(PLAN)
    tile = D // 2
    box_at = 0

    def sum_over_dp(kind, held, whole, out, first, rows):
        nonlocal box_at
        sums.add(kind(links, held, whole, out, S.box, box_at, first, rows, d, n.dp))
        box_at += kind.sizes(rows, D, n.dp)[1]

    for left, right, first in ((S.a24, S.gup, 0), (S.pool, S.cot4, D)):
        rows = left[:, :, 0:D].reshape(4 * R, D)
        S.gw[first : first + D, :] = dot_columns(rows, flat(right)).astype(low)
        for at in (first, first + tile):
            kind = Quarters if at in (0, D + tile) else Halves
            sum_over_dp(kind, S.gw, S.sum1, S.whole1, at, tile)

    sums.at("waiting")
    S.small[...] = jnp.zeros_like(S.small)
    gm_base = links.take(6)
    shared = lambda s, p, j: links.copy(
        S.mix4.at[s, pl.ds(*split[p])], S.gm4.at[t, pl.ds(*split[p])], gm_base + 3 * p + j, tensor=peers[j]
    )
    for p, (start, size) in enumerate(split):
        real = min(size, own - start)
        rows = pl.ds(start, real)
        grad = back.result(p)[:real]
        unit, inverse = standardize(S.hid[rows])
        S.small[2:3, :] += jnp.sum(grad * unit, 0, keepdims=True)
        S.small[3:4, :] += jnp.sum(grad, 0, keepdims=True)
        S.gt[rows] += norm_back(grad, unit, inverse, vector(S.g2))
        S.hl4[t, rows] = S.gt[rows].astype(low)
        rows = pl.ds(start, size)
        for j, s in enumerate(peers + [t]):
            product = dot_rows(S.hl4[t, rows], S.ow4[s]).astype(low)
            if j < 3:
                S.mix4[s, rows] = product
                shared(s, p, j).start()
            else:
                S.gm4[t, rows] = product
    S.small[4:5, :] = jnp.sum(S.hl4[t].astype(wide), 0, keepdims=True)
    S.small[5:6, :] = jnp.sum(S.cot4[t].astype(wide), 0, keepdims=True)
    S.small[6:7, :] = S.gub[...]
    hl_in = Gather(links, S.hl4, t, halves(R))

    next_in.finish()
    S.do[...] = jnp.zeros_like(S.do)
    S.qt[...] = jnp.transpose(flat(S.q))
    sums.at("shared")

    def prepare(i, s):
        if i > 0:
            j = (None, 2, 0, 1)[i]
            for p in (0, 1):
                rows = pl.ds(*split[p])
                links.arrived(S.gm4.at[s, rows], gm_base + 3 * p + j, tensor=peers[j])
        S.do[:, :W] = S.gm4[s].astype(wide)
        inverse = sum(S.inv[s, :, h : h + 1] * masks[h] for h in range(n.heads))
        scaled = (S.do[...] * inverse).astype(low)
        S.v[pl.ds(pl.multiple_of(s * R, 16), R), :] = scaled
        scaled = scaled.astype(wide)
        product = scaled * S.o[s]
        for h in range(n.heads):
            inner = -jnp.sum(product * masks[h], -1, keepdims=True)
            upper = inner.astype(low).astype(wide)
            S.a24[s, :, h * H : (h + 1) * H] = (
                scaled * masks[h]
                + jnp.where(lane == W, upper, 0.0)
                + jnp.where(lane == W + 1, inner - upper, 0.0)
            ).astype(low)

    def pull(h, p):
        grad_p = dot(pair(S.a24.at[:, :, h * H : (h + 1) * H], p), S.vt[...])
        grad_s = pair(S.e.at[h], p) * grad_p.astype(low)
        set_pair(S.pool, p, grad_s)
        dq = dot(grad_s, S.k[...]) * (masks[h] * HEAD_DIM**-0.5)
        if h > 0:
            dq += pair(S.gup.at[:, :, 0:H], p).astype(wide)
        S.gup[pl.ds(2 * p, 2), :, 0:H] = dq.astype(low).reshape(2, R, H)

    def weights(h):
        at = slice(h * HEAD_DIM, (h + 1) * HEAD_DIM)
        tile = h * HEAD_DIM // 128 * 128
        dqt = jnp.transpose(flat(S.gup.at[:, :, tile : tile + 128]))
        left = jnp.concatenate(
            [dqt[h * HEAD_DIM - tile : (h + 1) * HEAD_DIM - tile], S.qt[at, :], S.kt[at, : 4 * R]], 0
        )
        S.gw2[h * W : (h + 1) * W, :] = dot(left, flat(S.a1)).astype(low)
        sum_over_dp(Quarters, S.gw2, S.sum2, S.whole2, h * W, W)

    for h in range(n.heads):
        for i in (0, 2):
            if (h, i) == (0, 2):
                sums.at("arriving")
            if h == 0:
                prepare(i, flipped(t, i // 2, 0))
                prepare(i + 1, flipped(t, i // 2, 1))
            if (h, i) == (0, 2):
                hl_in.start()
            pull(h, (chip + i // 2) % 2)
            sums.at(f"h{h}p{i}")
            if (h, i) == (1, 0):
                hl_in.wait_sib()
                hl_in.forward()
                ahead.send_cross()
            elif (h, i) == (1, 2):
                hl_in.wait_diag()
                S.gw2[3 * W :, :] = dot_columns(flat(S.mix), flat(S.hl4)).astype(low)
                sum_over_dp(Quarters, S.gw2, S.sum2, S.whole2, 3 * W, W)
        if h == 0:
            S.v[4 * R :, :] = jnp.zeros((K - 4 * R, H), low)
            S.kt[...] = jnp.transpose(S.v[...])
        at = slice(h * HEAD_DIM, (h + 1) * HEAD_DIM)
        S.qt[at, :] = dot(S.qt[at, :], flat(S.pool))[:, : 4 * R].astype(low)
        S.kt[at, : 4 * R] = dot(S.kt[at, : 4 * R], flat(S.e.at[h]))[:, : 4 * R].astype(low)
        if h + 1 < n.heads:
            weights(h)
        sums.at(f"h{h}")

    pad = jnp.zeros((R, H - W), low)
    for part, grad_t in ((1, S.qt), (2, S.kt)):
        rows = jnp.transpose(grad_t[:W, : 4 * R])
        for s in range(4):
            S.gup[s, :, part * H : part * H + W] = rows[s * R : (s + 1) * R]
            S.gup[s, :, part * H + W : (part + 1) * H] = pad

    back.finish()
    down = Reduce(links, S.part, S.pre1, S.near1, S.far1, t, split)

    def lead(s, start, size):
        rows = pl.ds(start, size)
        out = dot(S.gup[s, rows, 0:W], S.wqkv[0])
        out += dot(S.gup[s, rows, H : H + W], S.wqkv[1])
        out += dot(S.gup[s, rows, 2 * H : 2 * H + W], S.wqkv[2])
        S.part[s, rows] = out.astype(low)
        S.small[0:1, :] += jnp.sum(out * S.a1[s, rows].astype(wide), 0, keepdims=True)
        S.small[1:2, :] += jnp.sum(out, 0, keepdims=True)

    cross, diag, sib = peers
    lead(diag, *split[0])
    down.send_diag([0])
    lead(cross, *split[0])
    weights(n.heads - 1)
    down.send_cross([0])
    lead(diag, *split[1])
    down.send_diag([1])
    lead(cross, *split[1])
    down.send_cross([1])
    lead(sib, 0, R)
    down.send_sib()
    lead(t, 0, R)
    S.small[7:8, 0:H] = jnp.sum(flat(S.gup.at[:, :, 0:H]).astype(wide), 0, keepdims=True)
    S.small[7:8, H : 2 * H] = jnp.sum(
        flat(S.gup.at[:, :, 2 * H : 3 * H]).astype(wide), 0, keepdims=True
    )

    S.small4[t] = S.small[...]
    base3 = links.take(3)
    for j in range(3):
        peer = lax.rem(t + j + 1, 4)
        links.start(S.small4.at[t], S.small4.at[t], base3 + j, tensor=peer)
    sums.at("led")
    result = jnp.concatenate([ahead.result(0), ahead.result(1)], 0)
    S.output[...] = (S.hid[...] + (result[:own] + vector(S.db))).astype(low)
    for j in range(3):
        peer = lax.rem(t + 3 - j, 4)
        links.arrived(S.small4.at[peer], base3 + j, tensor=peer)
    over = S.small4[0] + S.small4[1] + S.small4[2] + S.small4[3]
    row = lax.broadcasted_iota(jnp.int32, over.shape, 0)
    near = min(8, n.dp)
    inner = Everyone(links, S.smalls, d % near, near, lambda j: d // near * near + j)
    inner.start(jnp.where(row < 6, over, S.small[...]))
    sums.at("crossing")

    unit, inverse = standardize(S.x[...].astype(wide))
    grad = jnp.concatenate([down.result(0), down.result(1)], 0)[:own]
    S.gt[...] += norm_back(grad, unit, inverse, vector(S.g1))
    sums.at("told")
    sums.finish()
    total = inner.result()
    inner.finish()
    if n.dp > near:
        outer = Everyone(links, S.smalls2, d // near, n.dp // near, lambda j: j * near + d % near)
        outer.start(total)
        total = outer.result()
        outer.finish()
    S.small_sum[...] = total
    S.small_sum[0:1, :] = (total[0:1, :] - vector(S.b1) * total[1:2, :]) / vector(S.g1)
    for j, s in enumerate(peers):
        links.copy(S.mix.at[s], S.mix4.at[t], mix_base + j, tensor=s).wait_send()
        for p in (0, 1):
            shared(s, p, j).wait_send()
    for transfer in (rows_in, cot_in, ow_in, hl_in, ahead, down):
        transfer.finish()
    links.finish()


SMALL = ("gain1", "shift1", "gain2", "shift2", "bias_out", "bias_down", "bias_up", "bias_qv")


def finish(n, output, gt, small, whole1, whole2):
    D, W, H = n.D, n.W, n.H
    steps = n.heads
    rows1 = D // steps

    def spread(output, gt, small, up, down, head, out, *refs):
        to_output, to_gt, to_up, to_down, to_qkv, to_out = refs[:6]
        vectors, sems = refs[6:14], refs[14]
        i = pl.program_id(0)
        held = refs[15:]
        come = [pltpu.make_async_copy(a, b, sems.at[j]) for j, (a, b) in enumerate(zip((output, gt), held))]
        go = [
            pltpu.make_async_copy(a, b, sems.at[2 + j])
            for j, (a, b) in enumerate(zip(held, (to_output, to_gt)))
        ]

        @pl.when(i == 0)
        def _():
            for copy in come:
                copy.start()
            for j in range(7):
                vectors[j][...] = small[j : j + 1, :].reshape(D)
            vectors[7][0:1, :] = small[7:8, :W]
            vectors[7][1:2, :] = small[7:8, H : H + W]

        to_up[...] = up[...].astype(wide)
        to_down[...] = down[...].astype(wide)
        for j in range(3):
            to_qkv[j] = head[j * HEAD_DIM : (j + 1) * HEAD_DIM, :].astype(wide)
        to_out[...] = out[...].astype(wide)

        @pl.when(i == 1)
        def _():
            for first, second in zip(come, go):
                first.wait()
                second.start()

        @pl.when(i == steps - 1)
        def _():
            for copy in go:
                copy.wait()

    hbm = pl.BlockSpec(memory_space=pl.ANY)
    whole = pl.BlockSpec(memory_space=pltpu.VMEM)
    at_row = lambda rows, index: pl.BlockSpec((rows, D), lambda i: (index(i), 0))
    shape = jax.ShapeDtypeStruct
    return pl.pallas_call(
        spread,
        grid=(steps,),
        out_shape=[shape(output.shape, low), shape(gt.shape, wide)]
        + [shape((D, D), wide)] * 2
        + [shape((3, W, D), wide), shape((W, D), wide)]
        + [shape((D,), wide)] * 7
        + [shape((2, W), wide)],
        in_specs=[hbm, hbm, whole, at_row(rows1, lambda i: i), at_row(rows1, lambda i: i + steps)]
        + [at_row(W, lambda i: i), at_row(HEAD_DIM, lambda i: 3 * steps + i)],
        out_specs=[hbm, hbm]
        + [at_row(rows1, lambda i: i)] * 2
        + [pl.BlockSpec((3, HEAD_DIM, D), lambda i: (0, i, 0)), at_row(HEAD_DIM, lambda i: i)]
        + [whole] * 8,
        scratch_shapes=[
            pltpu.SemaphoreType.DMA((4,)),
            pltpu.VMEM(output.shape, low),
            pltpu.VMEM(gt.shape, wide),
        ],
    )(output, gt, small, whole1, whole1, whole2, whole2)


def body(
    tokens,
    lengths,
    ln1_gain,
    ln1_shift,
    qkv_weight,
    qv_bias,
    out_weight,
    out_bias,
    ln2_gain,
    ln2_shift,
    up_weight,
    up_bias,
    down_weight,
    down_bias,
    cotangent,
):
    own, D = tokens.shape
    W = qkv_weight.shape[2]
    F = up_weight.shape[1]
    dp = lax.axis_size("dp")
    assert lax.axis_size("tensor") == 4 and lengths.shape[0] == 1 and F == D and 4 * W == D and 3 * round_up(W + 2, 128) == D
    R = round_up(own, 16)
    H = round_up(W + 2, 128)
    K = round_up(4 * R, 256)
    heads = W // HEAD_DIM
    extra = dp.bit_length() - 1 - 3
    n = types.SimpleNamespace(
        own=own, D=D, W=W, R=R, H=H, K=K, dp=dp, heads=heads, extra=extra
    )
    given = dict(
        x=tokens, lengths=lengths, g1=ln1_gain, b1=ln1_shift,
        wqkv=jnp.transpose(qkv_weight, (1, 2, 0)), bq=qv_bias, ow=out_weight, ob=out_bias,
        g2=ln2_gain, b2=ln2_shift, wup=up_weight, bup=up_bias, wdn=down_weight, db=down_bias,
        cot=cotangent,
    )
    outs = dict(
        output=((own, D), low), gt=((own, D), wide), small_sum=((8, D), wide),
        whole1=((2 * D, D), low), whole2=((D, D), low),
    )
    rows4 = ((4, R, D), low)
    slab = ((R, D), low)
    chunks = [(Quarters, D // 2), (Halves, D // 2)] * 2 + [(Quarters, W)] * 4
    scratch = dict(
        a1=rows4, cot4=rows4, ow4=((4, W, D), low), q=((4, R, H), low), k=((K, H), low),
        v=((K, H), low), kt=((H, K), low), vt=((H, K), low), e=((heads, 4, R, K), low),
        o=((4, R, H), wide), inv=((4, R, 128), wide), mix=((4, R, W), low), mix4=((4, R, W), low),
        hid=((own, D), wide),
        a24=rows4, pool=((4, R, K), low), gup=rows4, part=rows4,
        fop=rows4, pre1=slab, near1=slab, far1=slab, pre2=slab, near2=slab, far2=slab,
        gw=((2 * D, D), low), gub=((1, D), wide),
        small=((8, D), wide), hl4=rows4,
        gm4=((4, R, W), low), qt=((H, 4 * R), low), do=((R, H), wide),
        gw2=((D, D), low),
        small4=((4, 8, D), wide), smalls=((min(8, dp), 8, D), wide),
        box=((sum(kind.sizes(r, D, dp)[1] for kind, r in chunks), D), low),
        sum1=((2 * D, D), low), sum2=((D, D), low),
    )
    if dp > 8:
        scratch["smalls2"] = ((dp // 8, 8, D), wide)
    sems = 170 + dp + 8 * extra
    names = list(given) + list(outs) + list(scratch) + ["local", "send", "recv"]
    vmem = pl.BlockSpec(memory_space=pltpu.VMEM)
    smem = pl.BlockSpec(memory_space=pltpu.SMEM)
    hbm = pl.BlockSpec(memory_space=pl.ANY)
    output, gt, small, whole1, whole2 = pl.pallas_call(
        lambda *refs: kernel(n, types.SimpleNamespace(**dict(zip(names, refs)))),
        out_shape=tuple(jax.ShapeDtypeStruct(*spec) for spec in outs.values()),
        in_specs=[dict(lengths=smem, cot=hbm).get(name, vmem) for name in given],
        out_specs=tuple(hbm if name in ("whole1", "whole2") else vmem for name in outs),
        scratch_shapes=[pltpu.VMEM(*spec) for spec in scratch.values()]
        + [pltpu.SemaphoreType.DMA] + [pltpu.SemaphoreType.DMA((sems,))] * 2,
        compiler_params=pltpu.CompilerParams(
            collective_id=0, has_side_effects=True, vmem_limit_bytes=VMEM_BYTES
        ),
    )(*given.values())
    finished = finish(n, output, gt, small, whole1, whole2)
    small_rows = dict(zip(SMALL, finished[6:]))
    return (
        finished[0],
        finished[1],
        small_rows["gain1"],
        small_rows["shift1"],
        jnp.transpose(finished[4], (2, 0, 1)),
        small_rows["bias_qv"],
        finished[5],
        small_rows["bias_out"],
        small_rows["gain2"],
        small_rows["shift2"],
        finished[2],
        small_rows["bias_up"],
        finished[3],
        small_rows["bias_down"],
    )


def solution(mesh):
    placed = (
        P(("dp", "tensor"), None),
        P("dp"),
        P(),
        P(),
        P(None, None, "tensor"),
        P(None, "tensor"),
        P("tensor", None),
        P(),
        P(),
        P(),
        P(None, "tensor"),
        P("tensor"),
        P("tensor", None),
        P(),
        P(("dp", "tensor"), None),
    )
    return jax.shard_map(
        body,
        mesh=mesh,
        in_specs=placed,
        out_specs=(
            P(("dp", "tensor"), None),
            P(("dp", "tensor"), None),
            P(),
            P(),
            P(None, None, "tensor"),
            P(None, "tensor"),
            P("tensor", None),
            P(),
            P(),
            P(),
            P(None, "tensor"),
            P("tensor"),
            P("tensor", None),
            P(),
        ),
        check_vma=False,
    )
```

```python
import types

import jax
import jax.numpy as jnp
from jax import lax
from jax.experimental import pallas as pl
from jax.experimental.pallas import tpu as pltpu
from jax.sharding import PartitionSpec as P

HEAD_DIM = 64
MESH = pl.DeviceIdType.MESH
VMEM_BYTES = 62 * 2**20

epsilon = 1e-06
low = jnp.bfloat16
wide = jnp.float32


def round_up(amount, unit):
    return -(-amount // unit) * unit


def flipped(t, flip_chip, flip_core):
    return (t // 2 + flip_chip) % 2 * 2 + (t % 2 + flip_core) % 2


def dot(left, right):
    return jnp.dot(left, right, preferred_element_type=wide)


def dot_rows(left, right):
    return lax.dot_general(left, right, (((1,), (1,)), ((), ())), preferred_element_type=wide)


def dot_columns(left, right):
    return lax.dot_general(left, right, (((0,), (0,)), ((), ())), preferred_element_type=wide)


def standardize(values):
    center = values - jnp.mean(values, -1, keepdims=True)
    inverse = lax.rsqrt(jnp.mean(center * center, -1, keepdims=True) + epsilon)
    return center * inverse, inverse


def norm_back(grad, unit, inverse, gain):
    scaled = grad * gain
    return inverse * (
        scaled
        - jnp.mean(scaled, -1, keepdims=True)
        - unit * jnp.mean(scaled * unit, -1, keepdims=True)
    )


def pair(ref, p):
    _, rows, columns = ref.shape
    return ref[pl.ds(2 * p, 2)].reshape(2 * rows, columns)


def set_pair(ref, p, values):
    ref[pl.ds(2 * p, 2)] = values.reshape(2, -1, values.shape[1])


def flat(ref):
    a, b, c = ref.shape
    return ref[...].reshape(a * b, c)


class Links:
    def __init__(self, send, recv):
        self.send, self.recv, self.used, self.pending = send, recv, 0, []

    def take(self, amount=1):
        base = self.used
        self.used += amount
        assert self.used <= self.send.shape[0]
        return base

    def copy(self, src, dst, at, **where):
        return pltpu.make_async_remote_copy(
            src_ref=src,
            dst_ref=dst,
            send_sem=self.send.at[at],
            recv_sem=self.recv.at[at],
            device_id=where,
            device_id_type=MESH,
        )

    def start(self, src, dst, at, **where):
        copy = self.copy(src, dst, at, **where)
        copy.start()
        self.pending.append(copy)

    def arrived(self, dst, at, **where):
        self.copy(dst, dst, at, **where).wait_recv()

    def finish(self):
        for copy in self.pending:
            copy.wait_send()
        self.pending = []


class Gather:
    def __init__(self, links, buf, t, parts):
        self.links, self.buf, self.t, self.parts = links, buf, t, parts
        self.sib, self.cross, self.diag = flipped(t, 0, 1), flipped(t, 1, 0), flipped(t, 1, 1)
        self.base = links.take(3 * len(parts))

    def view(self, slot, part):
        start, size = self.parts[part]
        return self.buf.at[slot, pl.ds(start, size)]

    def _each(self):
        return range(len(self.parts))

    def start(self):
        for p in self._each():
            v = self.view(self.t, p)
            self.links.copy(v, v, self.base + 3 * p, tensor=self.cross).start()
        for p in self._each():
            v = self.view(self.t, p)
            self.links.copy(v, v, self.base + 3 * p + 1, tensor=self.sib).start()

    def wait_sib(self):
        for p in self._each():
            self.links.arrived(self.view(self.sib, p), self.base + 3 * p + 1, tensor=self.sib)

    def forward(self, parts=None):
        for p in self._each() if parts is None else parts:
            v = self.view(self.cross, p)
            self.links.arrived(v, self.base + 3 * p, tensor=self.cross)
            self.links.copy(v, v, self.base + 3 * p + 2, tensor=self.sib).start()

    def wait_diag(self, parts=None):
        for p in self._each() if parts is None else parts:
            self.links.arrived(self.view(self.diag, p), self.base + 3 * p + 2, tensor=self.sib)

    def finish(self):
        for p in self._each():
            v = self.view(self.t, p)
            self.links.copy(v, v, self.base + 3 * p, tensor=self.cross).wait_send()
            self.links.copy(v, v, self.base + 3 * p + 1, tensor=self.sib).wait_send()
            v = self.view(self.cross, p)
            self.links.copy(v, v, self.base + 3 * p + 2, tensor=self.sib).wait_send()


class Reduce:
    def __init__(self, links, part, pre, near, far, t, parts):
        self.links, self.part, self.t, self.parts = links, part, t, parts
        self.pre, self.near, self.far = pre, near, far
        self.sib, self.cross, self.diag = flipped(t, 0, 1), flipped(t, 1, 0), flipped(t, 1, 1)
        self.base = links.take(3 * len(parts))

    def _copy(self, kind, p):
        slot, box, peer = (
            (self.diag, self.pre, self.sib),
            (self.sib, self.near, self.sib),
            (self.cross, self.far, self.cross),
        )[kind]
        rows = pl.ds(*self.parts[p])
        return self.links.copy(
            self.part.at[slot, rows], box.at[rows], self.base + 3 * p + kind, tensor=peer
        )

    def _each(self, parts):
        return range(len(self.parts)) if parts is None else parts

    def send_diag(self, parts=None):
        for p in self._each(parts):
            self._copy(0, p).start()

    def send_sib(self):
        for p in self._each(None):
            self._copy(1, p).start()

    def send_cross(self, parts=None):
        for p in self._each(parts):
            self._copy(0, p).wait_recv()
            rows = pl.ds(*self.parts[p])
            self.part[self.cross, rows] = (
                self.part[self.cross, rows].astype(wide) + self.pre[rows].astype(wide)
            ).astype(low)
            self._copy(2, p).start()

    def result(self, p):
        self._copy(1, p).wait_recv()
        self._copy(2, p).wait_recv()
        rows = pl.ds(*self.parts[p])
        return (
            self.part[self.t, rows].astype(wide)
            + self.near[rows].astype(wide)
            + self.far[rows].astype(wide)
        )

    def finish(self):
        for p in self._each(None):
            for kind in range(3):
                self._copy(kind, p).wait_send()


class DataReduce:
    def __init__(self, links, held, whole, out, box, box_at, first, rows, d, count):
        self.links, self.held, self.whole, self.out, self.d = links, held, whole, out, d
        bits = count.bit_length() - 1
        assert count == 1 << bits and bits >= 3
        self.extra = list(range(3, bits))
        self.region = (first, rows, 0, held.shape[1])
        self.trail, self.sent, self.boxes = [], [], []
        for tall, broad in self.sizes(rows, held.shape[1], count)[0]:
            self.boxes.append(box.at[pl.ds(box_at, tall), pl.ds(0, broad)])
            box_at += tall
        self.base = links.take(9 + len(self.extra))
        self.plan()

    @classmethod
    def sizes(cls, rows, columns, count):
        found = cls.boxes_of(rows, columns)
        found += found[-1:] * (count.bit_length() - 1 - 3)
        return found, sum(size[0] for size in found)

    def _bit(self, b):
        return self.d // (1 << b) % 2

    def _peer(self, b):
        return self.d + (1 - 2 * self._bit(b)) * (1 << b)

    def _send(self, src, dst, at, peer):
        copy = self.links.copy(src, dst, self.base + at, dp=peer)
        copy.start()
        self.sent.append(copy)

    def _wait(self, dst, at, peer):
        self.links.arrived(dst, self.base + at, dp=peer)

    @staticmethod
    def _view(ref, region):
        row, rows, column, columns = region
        if columns == ref.shape[1]:
            return ref.at[pl.ds(row, rows)]
        return ref.at[pl.ds(row, rows), pl.ds(column, columns)]

    @staticmethod
    def _part(region, bit):
        row, rows, column, columns = region
        if rows % 32 == 0:
            return (pl.multiple_of(row + bit * (rows // 2), 16), rows // 2, column, columns)
        return (row, rows, pl.multiple_of(column + bit * (columns // 2), 128), columns // 2)

    def _give_half(self, b, box, at):
        bit = self._bit(b)
        self.trail.append(self.region)
        self._send(self._view(self.held, self._part(self.region, 1 - bit)), self.boxes[box], at, self._peer(b))
        self.region = self._part(self.region, bit)

    def _add(self, boxes, last):
        view = self._view(self.held, self.region)
        total = view[...].astype(wide)
        for box in boxes:
            total += self.boxes[box][...].astype(wide)
        if last:
            view = self._view(self.whole, self.region)
        view[...] = total.astype(low)
        if last:
            self._swap()

    def _swap(self):
        view = self._view(self.whole, self.region)
        for k, b in enumerate(self.extra):
            box, at = self.boxes[k - len(self.extra)], 9 + k
            copy = self.links.copy(view, box, self.base + at, dp=self._peer(b))
            copy.start()
            self._wait(box, at, self._peer(b))
            copy.wait_send()
            view[...] = (view[...].astype(wide) + box[...].astype(wide)).astype(low)

    def _give_whole(self, b, at):
        view = self._view(self.whole, self.region)
        self._send(view, view, at, self._peer(b))

    def _take_half(self, b, at):
        outer = self.trail.pop()
        view = self._view(self.whole, self._part(outer, 1 - self._bit(b)))
        self._wait(view, at, self._peer(b))
        self.region = outer

    def _leave(self):
        rows = pl.ds(self.region[0], self.region[1])
        self.left = pltpu.make_async_copy(
            self.whole.at[rows], self.out.at[rows], self.links.send.at[self.base + 8]
        )
        self.left.start()

    def step(self):
        if self.steps:
            self.steps.pop(0)()

    def finish(self):
        assert not self.steps
        self.left.wait()
        for copy in self.sent:
            copy.wait_send()


class Halves(DataReduce):
    order = (1, 0, 2)

    @staticmethod
    def boxes_of(rows, columns):
        found = []
        for _ in range(3):
            if rows % 32 == 0:
                rows //= 2
            else:
                columns //= 2
            found.append((rows, columns))
        return found

    def plan(self):
        low_bit, x, high = self.order
        self.steps = [
            lambda: self._give_half(low_bit, 0, 0),
            lambda: (self._wait_box(low_bit, 0), self._add((0,), False), self._give_half(x, 1, 1)),
            lambda: (self._wait_box(x, 1), self._add((1,), False), self._give_half(high, 2, 2)),
            lambda: (self._wait_box(high, 2), self._add((2,), True), self._give_whole(high, 3)),
            lambda: (self._take_half(high, 3), self._give_whole(x, 4)),
            lambda: (self._take_half(x, 4), self._give_whole(low_bit, 5)),
            lambda: (self._take_half(low_bit, 5), self._leave()),
        ]

    def _wait_box(self, b, box):
        self._wait(self.boxes[box], box, self._peer(b))


class Quarters(DataReduce):
    @staticmethod
    def boxes_of(rows, columns):
        tall, broad = rows // 8, columns
        if tall % 16:
            tall, broad = rows // 4, columns // 2
        return [(rows // 2, columns)] + [(tall, broad)] * 3

    def plan(self):
        self.steps = [
            lambda: self._give_half(0, 0, 0),
            lambda: (self._wait(self.boxes[0], 0, self._peer(0)), self._add((0,), False), self._give_quarters()),
            lambda: (self._take_boxes(), self._add((1, 2, 3), True), self._give_quarter()),
            lambda: (self._take_quarters(), self._give_whole(0, 7)),
            lambda: (self._take_half(0, 7), self._leave()),
        ]

    def _z(self, j):
        low_bit = (self._bit(1) + j % 2) % 2
        high = (self._bit(2) + j // 2) % 2
        return low_bit, high, self.d // 8 * 8 + high * 4 + low_bit * 2 + self._bit(0)

    def _quarter(self, j):
        low_bit, high, peer = self._z(j)
        return self._part(self._part(self.trail[-1], high), low_bit), peer

    def _give_quarters(self):
        self.trail.append(self.region)
        for j in (1, 2, 3):
            part, peer = self._quarter(j)
            self._send(self._view(self.held, part), self.boxes[j], j, peer)
        self.region = self._quarter(0)[0]

    def _take_boxes(self):
        for j in (1, 2, 3):
            self._wait(self.boxes[j], j, self._z(j)[2])

    def _give_quarter(self):
        view = self._view(self.whole, self.region)
        for j in (1, 2, 3):
            self._send(view, view, 3 + j, self._z(j)[2])

    def _take_quarters(self):
        for j in (1, 2, 3):
            part, peer = self._quarter(j)
            self._wait(self._view(self.whole, part), 3 + j, peer)
        self.region = self.trail.pop()


class Pipeline:
    def __init__(self, plan):
        self.plan, self.members = plan, []

    def add(self, member):
        self.members.append(member)
        member.step()

    def at(self, place):
        for number in self.plan[place]:
            self.members[number].step()

    def finish(self):
        self.at("end")
        for m in self.members:
            while m.steps:
                m.step()
            m.finish()


PLAN = dict(
    waiting=(),
    shared=(0,),
    arriving=(1,),
    h0p0=(),
    h0p2=(3, 2),
    h0=(1,),
    h1p0=(2, 4, 1),
    h1p2=(2, 3),
    h1=(0,),
    h2p0=(1,),
    h2p2=(5, 4, 2),
    h2=(1, 3),
    led=(5, 0),
    crossing=(1, 6, 7, 5, 4),
    told=(6, 7, 3),
    end=(2, 6, 5, 7, 0, 4, 6, 2, 7),
)


class Everyone:
    def __init__(self, links, buf, me, count, device):
        self.links, self.buf, self.me, self.count, self.device = links, buf, me, count, device
        self.base = links.take(count)

    def _copy(self, j):
        slot = self.buf.at[self.me]
        peer = self.device(lax.rem(self.me + j, self.count))
        return self.links.copy(slot, slot, self.base + j, dp=peer)

    def _loop(self, act):
        def one(j, carry):
            act(j)
            return carry

        lax.fori_loop(1, self.count, one, 0)

    def start(self, values):
        self.buf[self.me] = values
        self._loop(lambda j: self._copy(j).start())

    def _hear(self, j):
        peer = lax.rem(self.me + self.count - j, self.count)
        self.links.arrived(self.buf.at[peer], self.base + j, dp=self.device(peer))

    def result(self):
        self._loop(self._hear)
        return lax.fori_loop(1, self.count, lambda j, acc: acc + self.buf[j], self.buf[0])

    def finish(self):
        self._loop(lambda j: self._copy(j).wait_send())


def greet(axis, me, count):
    barrier = pltpu.get_barrier_semaphore()

    def one(j, carry):
        pl.semaphore_signal(
            barrier, inc=1, device_id={axis: lax.rem(me + j, count)}, device_id_type=MESH
        )
        return carry

    lax.fori_loop(1, count, one, 0)


def await_greetings(amount):
    pl.semaphore_wait(pltpu.get_barrier_semaphore(), amount)


def halves(rows):
    first = round_up(rows // 2, 16)
    return ((0, first), (first, rows - first))


def head_masks(shape, local_heads):
    lane = lax.broadcasted_iota(jnp.int32, shape, 1)
    return [
        jnp.where((lane >= h * HEAD_DIM) & (lane < (h + 1) * HEAD_DIM), 1.0, 0.0)
        for h in range(local_heads)
    ], lane


def kernel(n, S):
    links = Links(S.send, S.recv)
    t = lax.axis_index("tensor")
    d = lax.axis_index("dp")
    greet("tensor", t, 4)
    greet("dp", d, n.dp)
    R, own, W, H, D, K = n.R, n.own, n.W, n.H, n.D, n.K
    split = halves(R)
    vector = lambda ref: ref[...].reshape(1, D)

    fetch = pltpu.make_async_copy(S.cot, S.gt, S.local)
    fetch.start()
    S.a1[t] = jnp.zeros((R, D), low)
    S.cot4[t] = jnp.zeros((R, D), low)
    S.a24[t] = jnp.zeros((R, D), low)
    S.hl4[t] = jnp.zeros((R, D), low)
    unit, _ = standardize(S.x[...].astype(wide))
    S.a1[t, 0:own, :] = (unit * vector(S.g1) + vector(S.b1)).astype(low)
    fetch.wait()
    S.cot4[t, 0:own, :] = S.gt[...].astype(low)
    S.ow4[t] = S.ow[...]
    await_greetings(3 + n.dp - 1)
    rows_in = Gather(links, S.a1, t, halves(R))
    cot_in = Gather(links, S.cot4, t, halves(R))
    ow_in = Gather(links, S.ow4, t, ((0, W),))
    rows_in.start()
    S.gw[0:D, :] = jnp.transpose(S.wup[...])
    S.gw[D:, :] = jnp.transpose(S.wdn[...])
    S.v[4 * R :, :] = jnp.zeros((K - 4 * R, H), low)
    length = S.lengths[0]

    chip = t // 2

    def project(i, carry):
        s = flipped(t, i // 2, i % 2)

        @pl.when(i == 1)
        def _():
            rows_in.wait_sib()

        @pl.when(i == 2)
        def _():
            rows_in.forward()
            ow_in.start()

        @pl.when(i == 3)
        def _():
            rows_in.wait_diag()

        slab = S.a1[s]
        lane = lax.broadcasted_iota(jnp.int32, (R, H - W), 1)
        row = lax.broadcasted_iota(jnp.int32, (R, H - W), 0)
        absent = (row >= own) | (row + s * own >= length)
        at = pl.ds(pl.multiple_of(s * R, 16), R)
        out = dot_rows(slab, S.wqkv[0]) + S.bq[0:1, :]
        S.q[s, :, :W] = (out.astype(low).astype(wide) * HEAD_DIM**-0.5).astype(low)
        S.q[s, :, W:] = jnp.where(lane == 0, HEAD_DIM**-0.5, 0.0).astype(low)
        S.k[at, :W] = dot_rows(slab, S.wqkv[1]).astype(low)
        S.k[at, W:] = jnp.where((lane == 0) & absent, -8e30, 0.0).astype(low)
        S.v[at, :W] = (dot_rows(slab, S.wqkv[2]) + S.bq[1:2, :]).astype(low)
        S.v[at, W:] = jnp.where(lane < 2, 1.0, 0.0).astype(low)
        return carry

    lax.fori_loop(0, 4, project, 0)
    if K > 4 * R:
        lane = lax.broadcasted_iota(jnp.int32, (K - 4 * R, H), 1)
        S.k[4 * R :, :] = jnp.where(lane == W, -8e30, 0.0).astype(low)
    S.kt[...] = jnp.transpose(S.k[...])
    S.vt[...] = jnp.transpose(S.v[...])

    masks, lane = head_masks((1, H), n.heads)
    mix_base = links.take(3)

    peers = [flipped(t, 1, 0), flipped(t, 1, 1), flipped(t, 0, 1)]

    def attend(i, carry):
        s = flipped(t, 1 - i // 2, (i + i // 2) % 2)
        query = S.q[s]
        mixed = jnp.zeros((R, H), wide)
        inverse = jnp.zeros((R, 128), wide)
        first = lax.broadcasted_iota(jnp.int32, (1, 128), 1)

        def score(h):
            here = jnp.where(lane == W, 1.0, masks[h]).astype(low)
            return dot(query * here, S.kt[...])

        ready = score(0)
        for h in range(n.heads):
            scores = ready
            if h + 1 < n.heads:
                ready = score(h + 1)
            terms = jnp.exp(scores - jnp.max(scores, -1, keepdims=True)).astype(low)
            S.e[h, s] = terms
            part = dot(terms, S.v[...])
            scale = 1.0 / part[:, W : W + 1]
            mixed += part * (scale * masks[h])
            inverse = jnp.where(first == h, scale, inverse)
        S.o[s] = mixed
        S.inv[s] = inverse
        S.mix[s] = mixed[:, :W].astype(low)

        @pl.when(i < 3)
        def _():
            links.copy(S.mix.at[s], S.mix4.at[t], mix_base + i, tensor=s).start()

        @pl.when(i == 1)
        def _():
            cot_in.start()

        @pl.when(i == 2)
        def _():
            ow_in.wait_sib()
            ow_in.forward()

        return carry

    lax.fori_loop(0, 4, attend, 0)
    ow_in.wait_diag()
    S.mix4[t] = S.mix[t]
    for j, s in enumerate(peers):
        links.arrived(S.mix4.at[s], mix_base + j, tensor=s)

    total = dot(S.mix4[0], S.ow4[0])
    for j in range(1, 4):
        total += dot(S.mix4[j], S.ow4[j])
    total = S.x[...].astype(wide) + (total[:own] + vector(S.ob))
    S.hid[...] = total
    unit, _ = standardize(total)
    S.a24[t, 0:own, :] = (unit * vector(S.g2) + vector(S.b2)).astype(low)
    next_in = Gather(links, S.a24, t, halves(R))
    next_in.start()
    back = Reduce(links, S.part, S.pre1, S.near1, S.far1, t, split)
    ahead = Reduce(links, S.fop, S.pre2, S.near2, S.far2, t, split)
    S.gub[...] = jnp.zeros_like(S.gub)

    def feed(s, start, size):
        rows = pl.ds(start, size)
        up = dot(S.a24[s, rows], S.wup[...]) + vector(S.bup)
        square = up * up
        c = 0.7978845608028654
        bend = jnp.tanh(c * up * (1.0 + 0.044715 * square))
        half = 0.5 * (1.0 + bend)
        slope = half + 0.5 * up * (1.0 - bend * bend) * (c + (3 * 0.044715 * c) * square)
        active = (up * half).astype(low)
        S.pool[s, rows, 0:D] = active
        grad = (dot(S.cot4[s, rows], S.gw[D:, :]) * slope).astype(low)
        S.gup[s, rows] = grad
        S.part[s, rows] = dot(grad, S.gw[0:D, :]).astype(low)
        S.gub[...] += jnp.sum(grad.astype(wide), 0, keepdims=True)

    def lead_out(s, start, size):
        rows = pl.ds(start, size)
        S.fop[s, rows] = dot(S.pool[s, rows, 0:D], S.wdn[...]).astype(low)

    def feed_here(i, carry):
        s = flipped(t, 0, i)

        @pl.when(i == 1)
        def _():
            next_in.wait_sib()
            cot_in.wait_sib()

        feed(s, 0, R)

        @pl.when(i == 1)
        def _():
            back.send_sib()

        lead_out(s, 0, R)
        return carry

    lax.fori_loop(0, 2, feed_here, 0)
    ahead.send_sib()
    for p in (0, 1):

        def feed_there(i, carry, p=p):
            @pl.when(i == 0)
            def _():
                cot_in.forward([p])
                next_in.forward([p])

            @pl.when(i == 1)
            def _():
                cot_in.wait_diag([p])
                next_in.wait_diag([p])

            feed(flipped(t, 1, i), *split[p])
            if p == 1:

                @pl.when(i == 0)
                def _():
                    back.send_cross([0])

            return carry

        lax.fori_loop(0, 2, feed_there, 0)
        back.send_diag([p])
    for i in (0, 1):
        lead_out(flipped(t, 1, i), 0, R)
    back.send_cross([1])
    ahead.send_diag()

    sums = Pipeline(PLAN)
    tile = D // 2
    box_at = 0

    def sum_over_dp(kind, held, whole, out, first, rows):
        nonlocal box_at
        sums.add(kind(links, held, whole, out, S.box, box_at, first, rows, d, n.dp))
        box_at += kind.sizes(rows, D, n.dp)[1]

    for left, right, first in ((S.a24, S.gup, 0), (S.pool, S.cot4, D)):
        rows = left[:, :, 0:D].reshape(4 * R, D)
        S.gw[first : first + D, :] = dot_columns(rows, flat(right)).astype(low)
        for at in (first, first + tile):
            kind = Quarters if at in (0, D + tile) else Halves
            sum_over_dp(kind, S.gw, S.sum1, S.whole1, at, tile)

    sums.at("waiting")
    S.small[...] = jnp.zeros_like(S.small)
    gm_base = links.take(6)
    shared = lambda s, p, j: links.copy(
        S.mix4.at[s, pl.ds(*split[p])], S.gm4.at[t, pl.ds(*split[p])], gm_base + 3 * p + j, tensor=peers[j]
    )
    for p, (start, size) in enumerate(split):
        real = min(size, own - start)
        rows = pl.ds(start, real)
        grad = back.result(p)[:real]
        unit, inverse = standardize(S.hid[rows])
        S.small[2:3, :] += jnp.sum(grad * unit, 0, keepdims=True)
        S.small[3:4, :] += jnp.sum(grad, 0, keepdims=True)
        S.gt[rows] += norm_back(grad, unit, inverse, vector(S.g2))
        S.hl4[t, rows] = S.gt[rows].astype(low)
        rows = pl.ds(start, size)
        for j, s in enumerate(peers + [t]):
            product = dot_rows(S.hl4[t, rows], S.ow4[s]).astype(low)
            if j < 3:
                S.mix4[s, rows] = product
                shared(s, p, j).start()
            else:
                S.gm4[t, rows] = product
    S.small[4:5, :] = jnp.sum(S.hl4[t].astype(wide), 0, keepdims=True)
    S.small[5:6, :] = jnp.sum(S.cot4[t].astype(wide), 0, keepdims=True)
    S.small[6:7, :] = S.gub[...]
    hl_in = Gather(links, S.hl4, t, halves(R))

    next_in.finish()
    S.do[...] = jnp.zeros_like(S.do)
    S.qt[...] = jnp.transpose(flat(S.q))
    sums.at("shared")

    def prepare(i, s):
        if i > 0:
            j = (None, 2, 0, 1)[i]
            for p in (0, 1):
                rows = pl.ds(*split[p])
                links.arrived(S.gm4.at[s, rows], gm_base + 3 * p + j, tensor=peers[j])
        S.do[:, :W] = S.gm4[s].astype(wide)
        inverse = sum(S.inv[s, :, h : h + 1] * masks[h] for h in range(n.heads))
        scaled = (S.do[...] * inverse).astype(low)
        S.v[pl.ds(pl.multiple_of(s * R, 16), R), :] = scaled
        scaled = scaled.astype(wide)
        product = scaled * S.o[s]
        for h in range(n.heads):
            inner = -jnp.sum(product * masks[h], -1, keepdims=True)
            upper = inner.astype(low).astype(wide)
            S.a24[s, :, h * H : (h + 1) * H] = (
                scaled * masks[h]
                + jnp.where(lane == W, upper, 0.0)
                + jnp.where(lane == W + 1, inner - upper, 0.0)
            ).astype(low)

    def pull(h, p):
        grad_p = dot(pair(S.a24.at[:, :, h * H : (h + 1) * H], p), S.vt[...])
        grad_s = (pair(S.e.at[h], p).astype(wide) * grad_p).astype(low)
        set_pair(S.pool, p, grad_s)
        dq = dot(grad_s, S.k[...]) * (masks[h] * HEAD_DIM**-0.5)
        if h > 0:
            dq += pair(S.gup.at[:, :, 0:H], p).astype(wide)
        S.gup[pl.ds(2 * p, 2), :, 0:H] = dq.astype(low).reshape(2, R, H)

    def weights(h):
        at = slice(h * HEAD_DIM, (h + 1) * HEAD_DIM)
        tile = h * HEAD_DIM // 128 * 128
        dqt = jnp.transpose(flat(S.gup.at[:, :, tile : tile + 128]))
        left = jnp.concatenate(
            [dqt[h * HEAD_DIM - tile : (h + 1) * HEAD_DIM - tile], S.qt[at, :], S.kt[at, : 4 * R]], 0
        )
        out = dot(left, flat(S.a1))
        S.gw2[h * W : (h + 1) * W, :] = out.astype(low)
        for c in range(3):
            product = out[c * HEAD_DIM : (c + 1) * HEAD_DIM] * S.wqkv[c, at, :].astype(wide)
            S.small[0:1, :] += jnp.sum(product, 0, keepdims=True)
        sum_over_dp(Quarters, S.gw2, S.sum2, S.whole2, h * W, W)

    for h in range(n.heads):
        for i in (0, 2):
            if (h, i) == (0, 2):
                sums.at("arriving")
            if h == 0:
                prepare(i, flipped(t, i // 2, 0))
                prepare(i + 1, flipped(t, i // 2, 1))
            if (h, i) == (0, 2):
                hl_in.start()
            pull(h, (chip + i // 2) % 2)
            sums.at(f"h{h}p{i}")
            if (h, i) == (1, 0):
                hl_in.wait_sib()
                hl_in.forward()
                ahead.send_cross()
            elif (h, i) == (1, 2):
                hl_in.wait_diag()
                S.gw2[3 * W :, :] = dot_columns(flat(S.mix), flat(S.hl4)).astype(low)
                sum_over_dp(Quarters, S.gw2, S.sum2, S.whole2, 3 * W, W)
        if h == 0:
            S.v[4 * R :, :] = jnp.zeros((K - 4 * R, H), low)
            S.kt[...] = jnp.transpose(S.v[...])
        at = slice(h * HEAD_DIM, (h + 1) * HEAD_DIM)
        S.qt[at, :] = dot(S.qt[at, :], flat(S.pool))[:, : 4 * R].astype(low)
        S.kt[at, : 4 * R] = dot(S.kt[at, : 4 * R], flat(S.e.at[h]))[:, : 4 * R].astype(low)
        if h + 1 < n.heads:
            weights(h)
        sums.at(f"h{h}")

    pad = jnp.zeros((R, H - W), low)
    for part, grad_t in ((1, S.qt), (2, S.kt)):
        rows = jnp.transpose(grad_t[:W, : 4 * R])
        for s in range(4):
            S.gup[s, :, part * H : part * H + W] = rows[s * R : (s + 1) * R]
            S.gup[s, :, part * H + W : (part + 1) * H] = pad

    back.finish()
    down = Reduce(links, S.part, S.pre1, S.near1, S.far1, t, split)

    def lead(s, start, size):
        rows = pl.ds(start, size)
        out = dot(S.gup[s, rows, 0:W], S.wqkv[0])
        out += dot(S.gup[s, rows, H : H + W], S.wqkv[1])
        out += dot(S.gup[s, rows, 2 * H : 2 * H + W], S.wqkv[2])
        S.part[s, rows] = out.astype(low)

    cross, diag, sib = peers
    lead(diag, *split[0])
    down.send_diag([0])
    lead(cross, *split[0])
    weights(n.heads - 1)
    down.send_cross([0])
    lead(diag, *split[1])
    down.send_diag([1])
    lead(cross, *split[1])
    down.send_cross([1])
    lead(sib, 0, R)
    down.send_sib()
    lead(t, 0, R)
    columns = jnp.sum(flat(S.gup).astype(wide), 0, keepdims=True)
    S.small[7:8, 0:H] = columns[:, 0:H]
    S.small[7:8, H : 2 * H] = columns[:, 2 * H :]
    upper = columns.astype(low)
    both = jnp.concatenate([upper.astype(wide), columns - upper.astype(wide)], 0).astype(low)
    for c in range(3):
        product = dot(both[:, c * H : c * H + W], S.wqkv[c])
        S.small[1:2, :] += jnp.sum(product, 0, keepdims=True)

    S.small4[t] = S.small[...]
    base3 = links.take(3)
    for j in range(3):
        peer = lax.rem(t + j + 1, 4)
        links.start(S.small4.at[t], S.small4.at[t], base3 + j, tensor=peer)
    sums.at("led")
    result = jnp.concatenate([ahead.result(0), ahead.result(1)], 0)
    S.output[...] = (S.hid[...] + (result[:own] + vector(S.db))).astype(low)
    for j in range(3):
        peer = lax.rem(t + 3 - j, 4)
        links.arrived(S.small4.at[peer], base3 + j, tensor=peer)
    over = S.small4[0] + S.small4[1] + S.small4[2] + S.small4[3]
    row = lax.broadcasted_iota(jnp.int32, over.shape, 0)
    near = min(8, n.dp)
    inner = Everyone(links, S.smalls, d % near, near, lambda j: d // near * near + j)
    inner.start(jnp.where(row < 6, over, S.small[...]))
    sums.at("crossing")

    unit, inverse = standardize(S.x[...].astype(wide))
    grad = jnp.concatenate([down.result(0), down.result(1)], 0)[:own]
    S.gt[...] += norm_back(grad, unit, inverse, vector(S.g1))
    sums.at("told")
    sums.finish()
    total = inner.result()
    inner.finish()
    if n.dp > near:
        outer = Everyone(links, S.smalls2, d // near, n.dp // near, lambda j: j * near + d % near)
        outer.start(total)
        total = outer.result()
        outer.finish()
    S.small_sum[...] = total
    S.small_sum[0:1, :] = (total[0:1, :] - vector(S.b1) * total[1:2, :]) / vector(S.g1)
    for j, s in enumerate(peers):
        links.copy(S.mix.at[s], S.mix4.at[t], mix_base + j, tensor=s).wait_send()
        for p in (0, 1):
            shared(s, p, j).wait_send()
    for transfer in (rows_in, cot_in, ow_in, hl_in, ahead, down):
        transfer.finish()
    links.finish()


SMALL = ("gain1", "shift1", "gain2", "shift2", "bias_out", "bias_down", "bias_up", "bias_qv")


def finish(n, output, gt, small, whole1, whole2):
    D, W, H = n.D, n.W, n.H
    steps = n.heads
    rows1 = D // steps

    def spread(output, gt, small, up, down, head, out, *refs):
        to_output, to_gt, to_up, to_down, to_qkv, to_out = refs[:6]
        vectors, sems = refs[6:14], refs[14]
        i = pl.program_id(0)
        held = refs[15:]
        come = [pltpu.make_async_copy(a, b, sems.at[j]) for j, (a, b) in enumerate(zip((output, gt), held))]
        go = [
            pltpu.make_async_copy(a, b, sems.at[2 + j])
            for j, (a, b) in enumerate(zip(held, (to_output, to_gt)))
        ]

        @pl.when(i == 0)
        def _():
            for copy in come:
                copy.start()
            for j in range(7):
                vectors[j][...] = small[j : j + 1, :].reshape(D)
            vectors[7][0:1, :] = small[7:8, :W]
            vectors[7][1:2, :] = small[7:8, H : H + W]

        to_up[...] = up[...].astype(wide)
        to_down[...] = down[...].astype(wide)
        for j in range(3):
            to_qkv[j] = head[j * HEAD_DIM : (j + 1) * HEAD_DIM, :].astype(wide)
        to_out[...] = out[...].astype(wide)

        @pl.when(i == 1)
        def _():
            for first, second in zip(come, go):
                first.wait()
                second.start()

        @pl.when(i == steps - 1)
        def _():
            for copy in go:
                copy.wait()

    hbm = pl.BlockSpec(memory_space=pl.ANY)
    whole = pl.BlockSpec(memory_space=pltpu.VMEM)
    at_row = lambda rows, index: pl.BlockSpec((rows, D), lambda i: (index(i), 0))
    shape = jax.ShapeDtypeStruct
    return pl.pallas_call(
        spread,
        grid=(steps,),
        out_shape=[shape(output.shape, low), shape(gt.shape, wide)]
        + [shape((D, D), wide)] * 2
        + [shape((3, W, D), wide), shape((W, D), wide)]
        + [shape((D,), wide)] * 7
        + [shape((2, W), wide)],
        in_specs=[hbm, hbm, whole, at_row(rows1, lambda i: i), at_row(rows1, lambda i: i + steps)]
        + [at_row(W, lambda i: i), at_row(HEAD_DIM, lambda i: 3 * steps + i)],
        out_specs=[hbm, hbm]
        + [at_row(rows1, lambda i: i)] * 2
        + [pl.BlockSpec((3, HEAD_DIM, D), lambda i: (0, i, 0)), at_row(HEAD_DIM, lambda i: i)]
        + [whole] * 8,
        scratch_shapes=[
            pltpu.SemaphoreType.DMA((4,)),
            pltpu.VMEM(output.shape, low),
            pltpu.VMEM(gt.shape, wide),
        ],
    )(output, gt, small, whole1, whole1, whole2, whole2)


def body(
    tokens,
    lengths,
    ln1_gain,
    ln1_shift,
    qkv_weight,
    qv_bias,
    out_weight,
    out_bias,
    ln2_gain,
    ln2_shift,
    up_weight,
    up_bias,
    down_weight,
    down_bias,
    cotangent,
):
    own, D = tokens.shape
    W = qkv_weight.shape[2]
    F = up_weight.shape[1]
    dp = lax.axis_size("dp")
    assert lax.axis_size("tensor") == 4 and lengths.shape[0] == 1 and F == D and 4 * W == D and 3 * round_up(W + 2, 128) == D
    R = round_up(own, 16)
    H = round_up(W + 2, 128)
    K = round_up(4 * R, 256)
    heads = W // HEAD_DIM
    extra = dp.bit_length() - 1 - 3
    n = types.SimpleNamespace(
        own=own, D=D, W=W, R=R, H=H, K=K, dp=dp, heads=heads, extra=extra
    )
    given = dict(
        x=tokens, lengths=lengths, g1=ln1_gain, b1=ln1_shift,
        wqkv=jnp.transpose(qkv_weight, (1, 2, 0)), bq=qv_bias, ow=out_weight, ob=out_bias,
        g2=ln2_gain, b2=ln2_shift, wup=up_weight, bup=up_bias, wdn=down_weight, db=down_bias,
        cot=cotangent,
    )
    outs = dict(
        output=((own, D), low), gt=((own, D), wide), small_sum=((8, D), wide),
        whole1=((2 * D, D), low), whole2=((D, D), low),
    )
    rows4 = ((4, R, D), low)
    slab = ((R, D), low)
    chunks = [(Quarters, D // 2), (Halves, D // 2)] * 2 + [(Quarters, W)] * 4
    scratch = dict(
        a1=rows4, cot4=rows4, ow4=((4, W, D), low), q=((4, R, H), low), k=((K, H), low),
        v=((K, H), low), kt=((H, K), low), vt=((H, K), low), e=((heads, 4, R, K), low),
        o=((4, R, H), wide), inv=((4, R, 128), wide), mix=((4, R, W), low), mix4=((4, R, W), low),
        hid=((own, D), wide),
        a24=rows4, pool=((4, R, K), low), gup=rows4, part=rows4,
        fop=rows4, pre1=slab, near1=slab, far1=slab, pre2=slab, near2=slab, far2=slab,
        gw=((2 * D, D), low), gub=((1, D), wide),
        small=((8, D), wide), hl4=rows4,
        gm4=((4, R, W), low), qt=((H, 4 * R), low), do=((R, H), wide),
        gw2=((D, D), low),
        small4=((4, 8, D), wide), smalls=((min(8, dp), 8, D), wide),
        box=((sum(kind.sizes(r, D, dp)[1] for kind, r in chunks), D), low),
        sum1=((2 * D, D), low), sum2=((D, D), low),
    )
    if dp > 8:
        scratch["smalls2"] = ((dp // 8, 8, D), wide)
    sems = 170 + dp + 8 * extra
    names = list(given) + list(outs) + list(scratch) + ["local", "send", "recv"]
    vmem = pl.BlockSpec(memory_space=pltpu.VMEM)
    smem = pl.BlockSpec(memory_space=pltpu.SMEM)
    hbm = pl.BlockSpec(memory_space=pl.ANY)
    output, gt, small, whole1, whole2 = pl.pallas_call(
        lambda *refs: kernel(n, types.SimpleNamespace(**dict(zip(names, refs)))),
        out_shape=tuple(jax.ShapeDtypeStruct(*spec) for spec in outs.values()),
        in_specs=[dict(lengths=smem, cot=hbm).get(name, vmem) for name in given],
        out_specs=tuple(hbm if name in ("whole1", "whole2") else vmem for name in outs),
        scratch_shapes=[pltpu.VMEM(*spec) for spec in scratch.values()]
        + [pltpu.SemaphoreType.DMA] + [pltpu.SemaphoreType.DMA((sems,))] * 2,
        compiler_params=pltpu.CompilerParams(
            collective_id=0, has_side_effects=True, vmem_limit_bytes=VMEM_BYTES
        ),
    )(*given.values())
    finished = finish(n, output, gt, small, whole1, whole2)
    small_rows = dict(zip(SMALL, finished[6:]))
    return (
        finished[0],
        finished[1],
        small_rows["gain1"],
        small_rows["shift1"],
        jnp.transpose(finished[4], (2, 0, 1)),
        small_rows["bias_qv"],
        finished[5],
        small_rows["bias_out"],
        small_rows["gain2"],
        small_rows["shift2"],
        finished[2],
        small_rows["bias_up"],
        finished[3],
        small_rows["bias_down"],
    )


def solution(mesh):
    placed = (
        P(("dp", "tensor"), None),
        P("dp"),
        P(),
        P(),
        P(None, None, "tensor"),
        P(None, "tensor"),
        P("tensor", None),
        P(),
        P(),
        P(),
        P(None, "tensor"),
        P("tensor"),
        P("tensor", None),
        P(),
        P(("dp", "tensor"), None),
    )
    return jax.shard_map(
        body,
        mesh=mesh,
        in_specs=placed,
        out_specs=(
            P(("dp", "tensor"), None),
            P(("dp", "tensor"), None),
            P(),
            P(),
            P(None, None, "tensor"),
            P(None, "tensor"),
            P("tensor", None),
            P(),
            P(),
            P(),
            P(None, "tensor"),
            P("tensor"),
            P("tensor", None),
            P(),
        ),
        check_vma=False,
    )
```

```python
import types

import jax
import jax.numpy as jnp
from jax import lax
from jax.experimental import pallas as pl
from jax.experimental.pallas import tpu as pltpu
from jax.sharding import PartitionSpec as P

HEAD_DIM = 64
MESH = pl.DeviceIdType.MESH
VMEM_BYTES = 62 * 2**20

epsilon = 1e-06
low = jnp.bfloat16
wide = jnp.float32


def round_up(amount, unit):
    return -(-amount // unit) * unit


def flipped(t, flip_chip, flip_core):
    return (t // 2 + flip_chip) % 2 * 2 + (t % 2 + flip_core) % 2


def dot(left, right):
    return jnp.dot(left, right, preferred_element_type=wide)


def dot_rows(left, right):
    return lax.dot_general(left, right, (((1,), (1,)), ((), ())), preferred_element_type=wide)


def dot_columns(left, right):
    return lax.dot_general(left, right, (((0,), (0,)), ((), ())), preferred_element_type=wide)


def standardize(values):
    center = values - jnp.mean(values, -1, keepdims=True)
    inverse = lax.rsqrt(jnp.mean(center * center, -1, keepdims=True) + epsilon)
    return center * inverse, inverse


def norm_back(grad, unit, inverse, gain):
    scaled = grad * gain
    return inverse * (
        scaled
        - jnp.mean(scaled, -1, keepdims=True)
        - unit * jnp.mean(scaled * unit, -1, keepdims=True)
    )


def pair(ref, p):
    _, rows, columns = ref.shape
    return ref[pl.ds(2 * p, 2)].reshape(2 * rows, columns)


def set_pair(ref, p, values):
    ref[pl.ds(2 * p, 2)] = values.reshape(2, -1, values.shape[1])


def flat(ref):
    a, b, c = ref.shape
    return ref[...].reshape(a * b, c)


class Links:
    def __init__(self, send, recv):
        self.send, self.recv, self.used, self.pending = send, recv, 0, []

    def take(self, amount=1):
        base = self.used
        self.used += amount
        assert self.used <= self.send.shape[0]
        return base

    def copy(self, src, dst, at, **where):
        return pltpu.make_async_remote_copy(
            src_ref=src,
            dst_ref=dst,
            send_sem=self.send.at[at],
            recv_sem=self.recv.at[at],
            device_id=where,
            device_id_type=MESH,
        )

    def start(self, src, dst, at, **where):
        copy = self.copy(src, dst, at, **where)
        copy.start()
        self.pending.append(copy)

    def arrived(self, dst, at, **where):
        self.copy(dst, dst, at, **where).wait_recv()

    def finish(self):
        for copy in self.pending:
            copy.wait_send()
        self.pending = []


class Gather:
    def __init__(self, links, buf, t, parts):
        self.links, self.buf, self.t, self.parts = links, buf, t, parts
        self.sib, self.cross, self.diag = flipped(t, 0, 1), flipped(t, 1, 0), flipped(t, 1, 1)
        self.base = links.take(3 * len(parts))

    def view(self, slot, part):
        start, size = self.parts[part]
        return self.buf.at[slot, pl.ds(start, size)]

    def _each(self):
        return range(len(self.parts))

    def start(self, parts=None):
        parts = self._each() if parts is None else parts
        for p in parts:
            v = self.view(self.t, p)
            self.links.copy(v, v, self.base + 3 * p, tensor=self.cross).start()
        for p in parts:
            v = self.view(self.t, p)
            self.links.copy(v, v, self.base + 3 * p + 1, tensor=self.sib).start()

    def wait_sib(self):
        for p in self._each():
            self.links.arrived(self.view(self.sib, p), self.base + 3 * p + 1, tensor=self.sib)

    def forward(self, parts=None):
        for p in self._each() if parts is None else parts:
            v = self.view(self.cross, p)
            self.links.arrived(v, self.base + 3 * p, tensor=self.cross)
            self.links.copy(v, v, self.base + 3 * p + 2, tensor=self.sib).start()

    def wait_diag(self, parts=None):
        for p in self._each() if parts is None else parts:
            self.links.arrived(self.view(self.diag, p), self.base + 3 * p + 2, tensor=self.sib)

    def finish(self):
        for p in self._each():
            v = self.view(self.t, p)
            self.links.copy(v, v, self.base + 3 * p, tensor=self.cross).wait_send()
            self.links.copy(v, v, self.base + 3 * p + 1, tensor=self.sib).wait_send()
            v = self.view(self.cross, p)
            self.links.copy(v, v, self.base + 3 * p + 2, tensor=self.sib).wait_send()


class Reduce:
    def __init__(self, links, part, pre, near, far, t, parts):
        self.links, self.part, self.t, self.parts = links, part, t, parts
        self.pre, self.near, self.far = pre, near, far
        self.sib, self.cross, self.diag = flipped(t, 0, 1), flipped(t, 1, 0), flipped(t, 1, 1)
        self.base = links.take(3 * len(parts))

    def _copy(self, kind, p):
        slot, box, peer = (
            (self.diag, self.pre, self.sib),
            (self.sib, self.near, self.sib),
            (self.cross, self.far, self.cross),
        )[kind]
        rows = pl.ds(*self.parts[p])
        return self.links.copy(
            self.part.at[slot, rows], box.at[rows], self.base + 3 * p + kind, tensor=peer
        )

    def _each(self, parts):
        return range(len(self.parts)) if parts is None else parts

    def send_diag(self, parts=None):
        for p in self._each(parts):
            self._copy(0, p).start()

    def send_sib(self):
        for p in self._each(None):
            self._copy(1, p).start()

    def send_cross(self, parts=None):
        for p in self._each(parts):
            self._copy(0, p).wait_recv()
            rows = pl.ds(*self.parts[p])
            self.part[self.cross, rows] = (
                self.part[self.cross, rows].astype(wide) + self.pre[rows].astype(wide)
            ).astype(low)
            self._copy(2, p).start()

    def result(self, p):
        self._copy(1, p).wait_recv()
        self._copy(2, p).wait_recv()
        rows = pl.ds(*self.parts[p])
        return (
            self.part[self.t, rows].astype(wide)
            + self.near[rows].astype(wide)
            + self.far[rows].astype(wide)
        )

    def finish(self):
        for p in self._each(None):
            for kind in range(3):
                self._copy(kind, p).wait_send()


class DataReduce:
    def __init__(self, links, held, whole, out, box, box_at, first, rows, d, count):
        self.links, self.held, self.whole, self.out, self.d = links, held, whole, out, d
        bits = count.bit_length() - 1
        assert count == 1 << bits and bits >= 3
        self.extra = list(range(3, bits))
        self.region = (first, rows, 0, held.shape[1])
        self.trail, self.sent, self.boxes = [], [], []
        for tall, broad in self.sizes(rows, held.shape[1], count)[0]:
            self.boxes.append(box.at[pl.ds(box_at, tall), pl.ds(0, broad)])
            box_at += tall
        self.base = links.take(9 + len(self.extra))
        self.plan()

    @classmethod
    def sizes(cls, rows, columns, count):
        found = cls.boxes_of(rows, columns)
        found += found[-1:] * (count.bit_length() - 1 - 3)
        return found, sum(size[0] for size in found)

    def _bit(self, b):
        return self.d // (1 << b) % 2

    def _peer(self, b):
        return self.d + (1 - 2 * self._bit(b)) * (1 << b)

    def _send(self, src, dst, at, peer):
        copy = self.links.copy(src, dst, self.base + at, dp=peer)
        copy.start()
        self.sent.append(copy)

    def _wait(self, dst, at, peer):
        self.links.arrived(dst, self.base + at, dp=peer)

    @staticmethod
    def _view(ref, region):
        row, rows, column, columns = region
        if columns == ref.shape[1]:
            return ref.at[pl.ds(row, rows)]
        return ref.at[pl.ds(row, rows), pl.ds(column, columns)]

    @staticmethod
    def _part(region, bit):
        row, rows, column, columns = region
        if rows % 32 == 0:
            return (pl.multiple_of(row + bit * (rows // 2), 16), rows // 2, column, columns)
        return (row, rows, pl.multiple_of(column + bit * (columns // 2), 128), columns // 2)

    def _give_half(self, b, box, at):
        bit = self._bit(b)
        self.trail.append(self.region)
        self._send(self._view(self.held, self._part(self.region, 1 - bit)), self.boxes[box], at, self._peer(b))
        self.region = self._part(self.region, bit)

    def _add(self, boxes, last):
        view = self._view(self.held, self.region)
        total = view[...].astype(wide)
        for box in boxes:
            total += self.boxes[box][...].astype(wide)
        if last:
            view = self._view(self.whole, self.region)
        view[...] = total.astype(low)
        if last:
            self._swap()

    def _swap(self):
        view = self._view(self.whole, self.region)
        for k, b in enumerate(self.extra):
            box, at = self.boxes[k - len(self.extra)], 9 + k
            copy = self.links.copy(view, box, self.base + at, dp=self._peer(b))
            copy.start()
            self._wait(box, at, self._peer(b))
            copy.wait_send()
            view[...] = (view[...].astype(wide) + box[...].astype(wide)).astype(low)

    def _give_whole(self, b, at):
        view = self._view(self.whole, self.region)
        self._send(view, view, at, self._peer(b))

    def _take_half(self, b, at):
        outer = self.trail.pop()
        view = self._view(self.whole, self._part(outer, 1 - self._bit(b)))
        self._wait(view, at, self._peer(b))
        self.region = outer

    def _leave(self):
        rows = pl.ds(self.region[0], self.region[1])
        self.left = pltpu.make_async_copy(
            self.whole.at[rows], self.out.at[rows], self.links.send.at[self.base + 8]
        )
        self.left.start()

    def step(self):
        if self.steps:
            self.steps.pop(0)()

    def finish(self):
        assert not self.steps
        self.left.wait()
        for copy in self.sent:
            copy.wait_send()


class Halves(DataReduce):
    order = (1, 0, 2)

    @staticmethod
    def boxes_of(rows, columns):
        found = []
        for _ in range(3):
            if rows % 32 == 0:
                rows //= 2
            else:
                columns //= 2
            found.append((rows, columns))
        return found

    def plan(self):
        low_bit, x, high = self.order
        self.steps = [
            lambda: self._give_half(low_bit, 0, 0),
            lambda: (self._wait_box(low_bit, 0), self._add((0,), False), self._give_half(x, 1, 1)),
            lambda: (self._wait_box(x, 1), self._add((1,), False), self._give_half(high, 2, 2)),
            lambda: (self._wait_box(high, 2), self._add((2,), True), self._give_whole(high, 3)),
            lambda: (self._take_half(high, 3), self._give_whole(x, 4)),
            lambda: (self._take_half(x, 4), self._give_whole(low_bit, 5)),
            lambda: (self._take_half(low_bit, 5), self._leave()),
        ]

    def _wait_box(self, b, box):
        self._wait(self.boxes[box], box, self._peer(b))


class Quarters(DataReduce):
    @staticmethod
    def boxes_of(rows, columns):
        tall, broad = rows // 8, columns
        if tall % 16:
            tall, broad = rows // 4, columns // 2
        return [(rows // 2, columns)] + [(tall, broad)] * 3

    def plan(self):
        self.steps = [
            lambda: self._give_half(0, 0, 0),
            lambda: (self._wait(self.boxes[0], 0, self._peer(0)), self._add((0,), False), self._give_quarters()),
            lambda: (self._take_boxes(), self._add((1, 2, 3), True), self._give_quarter()),
            lambda: (self._take_quarters(), self._give_whole(0, 7)),
            lambda: (self._take_half(0, 7), self._leave()),
        ]

    def _z(self, j):
        low_bit = (self._bit(1) + j % 2) % 2
        high = (self._bit(2) + j // 2) % 2
        return low_bit, high, self.d // 8 * 8 + high * 4 + low_bit * 2 + self._bit(0)

    def _quarter(self, j):
        low_bit, high, peer = self._z(j)
        return self._part(self._part(self.trail[-1], high), low_bit), peer

    def _give_quarters(self):
        self.trail.append(self.region)
        for j in (1, 2, 3):
            part, peer = self._quarter(j)
            self._send(self._view(self.held, part), self.boxes[j], j, peer)
        self.region = self._quarter(0)[0]

    def _take_boxes(self):
        for j in (1, 2, 3):
            self._wait(self.boxes[j], j, self._z(j)[2])

    def _give_quarter(self):
        view = self._view(self.whole, self.region)
        for j in (1, 2, 3):
            self._send(view, view, 3 + j, self._z(j)[2])

    def _take_quarters(self):
        for j in (1, 2, 3):
            part, peer = self._quarter(j)
            self._wait(self._view(self.whole, part), 3 + j, peer)
        self.region = self.trail.pop()


class Pipeline:
    def __init__(self, plan):
        self.plan, self.members = plan, []

    def add(self, member):
        self.members.append(member)
        member.step()

    def at(self, place):
        for number in self.plan[place]:
            self.members[number].step()

    def finish(self):
        self.at("end")
        for m in self.members:
            while m.steps:
                m.step()
            m.finish()


PLAN = dict(
    waiting=(),
    shared=(0,),
    arriving=(1,),
    h0p0=(),
    h0p2=(3, 2),
    h0=(1,),
    h1p0=(2, 4, 1),
    h1p2=(2, 3),
    h1=(0,),
    h2p0=(1,),
    h2p2=(5, 4, 2),
    h2=(1, 3),
    led=(5, 0),
    crossing=(1, 6, 7, 5, 4),
    told=(6, 7, 3),
    end=(2, 6, 5, 7, 0, 4, 6, 2, 7),
)


class Everyone:
    def __init__(self, links, buf, me, count, device):
        self.links, self.buf, self.me, self.count, self.device = links, buf, me, count, device
        self.base = links.take(count)

    def _copy(self, j):
        slot = self.buf.at[self.me]
        peer = self.device(lax.rem(self.me + j, self.count))
        return self.links.copy(slot, slot, self.base + j, dp=peer)

    def _loop(self, act):
        def one(j, carry):
            act(j)
            return carry

        lax.fori_loop(1, self.count, one, 0)

    def start(self, values):
        self.buf[self.me] = values
        self._loop(lambda j: self._copy(j).start())

    def _hear(self, j):
        peer = lax.rem(self.me + self.count - j, self.count)
        self.links.arrived(self.buf.at[peer], self.base + j, dp=self.device(peer))

    def result(self):
        self._loop(self._hear)
        return lax.fori_loop(1, self.count, lambda j, acc: acc + self.buf[j], self.buf[0])

    def finish(self):
        self._loop(lambda j: self._copy(j).wait_send())


def greet(axis, me, count):
    barrier = pltpu.get_barrier_semaphore()

    def one(j, carry):
        pl.semaphore_signal(
            barrier, inc=1, device_id={axis: lax.rem(me + j, count)}, device_id_type=MESH
        )
        return carry

    lax.fori_loop(1, count, one, 0)


def await_greetings(amount):
    pl.semaphore_wait(pltpu.get_barrier_semaphore(), amount)


def halves(rows):
    first = round_up(rows // 2, 16)
    return ((0, first), (first, rows - first))


def head_masks(shape, local_heads):
    lane = lax.broadcasted_iota(jnp.int32, shape, 1)
    return [
        jnp.where((lane >= h * HEAD_DIM) & (lane < (h + 1) * HEAD_DIM), 1.0, 0.0)
        for h in range(local_heads)
    ], lane


def kernel(n, S):
    links = Links(S.send, S.recv)
    t = lax.axis_index("tensor")
    d = lax.axis_index("dp")
    greet("tensor", t, 4)
    greet("dp", d, n.dp)
    R, own, W, H, D, K = n.R, n.own, n.W, n.H, n.D, n.K
    split = halves(R)
    vector = lambda ref: ref[...].reshape(1, D)

    fetch = pltpu.make_async_copy(S.cot, S.gt, S.local)
    fetch.start()
    S.a1[t] = jnp.zeros((R, D), low)
    S.cot4[t] = jnp.zeros((R, D), low)
    S.a24[t] = jnp.zeros((R, D), low)
    S.hl4[t] = jnp.zeros((R, D), low)
    unit, _ = standardize(S.x[...].astype(wide))
    S.a1[t, 0:own, :] = (unit * vector(S.g1) + vector(S.b1)).astype(low)
    fetch.wait()
    S.cot4[t, 0:own, :] = S.gt[...].astype(low)
    S.ow4[t] = S.ow[...]
    await_greetings(3 + n.dp - 1)
    rows_in = Gather(links, S.a1, t, halves(R))
    cot_in = Gather(links, S.cot4, t, halves(R))
    ow_in = Gather(links, S.ow4, t, ((0, W),))
    rows_in.start()
    ow_in.start()
    cot_in.start([0])
    S.gw[0:D, :] = jnp.transpose(S.wup[...])
    S.gw[D:, :] = jnp.transpose(S.wdn[...])
    S.v[4 * R :, :] = jnp.zeros((K - 4 * R, H), low)
    length = S.lengths[0]

    chip = t // 2

    def project(i, carry):
        s = flipped(t, i // 2, i % 2)

        @pl.when(i == 1)
        def _():
            rows_in.wait_sib()

        @pl.when(i == 2)
        def _():
            rows_in.forward()

        @pl.when(i == 3)
        def _():
            rows_in.wait_diag()

        slab = S.a1[s]
        lane = lax.broadcasted_iota(jnp.int32, (R, H - W), 1)
        row = lax.broadcasted_iota(jnp.int32, (R, H - W), 0)
        absent = (row >= own) | (row + s * own >= length)
        at = pl.ds(pl.multiple_of(s * R, 16), R)
        out = dot_rows(slab, S.wqkv[0]) + S.bq[0:1, :]
        S.q[s, :, :W] = (out.astype(low).astype(wide) * HEAD_DIM**-0.5).astype(low)
        S.q[s, :, W:] = jnp.where(lane == 0, HEAD_DIM**-0.5, 0.0).astype(low)
        S.k[at, :W] = dot_rows(slab, S.wqkv[1]).astype(low)
        S.k[at, W:] = jnp.where((lane == 0) & absent, -8e30, 0.0).astype(low)
        S.v[at, :W] = (dot_rows(slab, S.wqkv[2]) + S.bq[1:2, :]).astype(low)
        S.v[at, W:] = jnp.where(lane < 2, 1.0, 0.0).astype(low)
        return carry

    lax.fori_loop(0, 4, project, 0)
    if K > 4 * R:
        lane = lax.broadcasted_iota(jnp.int32, (K - 4 * R, H), 1)
        S.k[4 * R :, :] = jnp.where(lane == W, -8e30, 0.0).astype(low)
    S.kt[...] = jnp.transpose(S.k[...])
    S.vt[...] = jnp.transpose(S.v[...])

    masks, lane = head_masks((1, H), n.heads)
    mix_base = links.take(3)

    peers = [flipped(t, 1, 0), flipped(t, 1, 1), flipped(t, 0, 1)]

    def attend(i, carry):
        s = flipped(t, 1 - i // 2, (i + i // 2) % 2)
        query = S.q[s]
        mixed = jnp.zeros((R, H), wide)
        inverse = jnp.zeros((R, 128), wide)
        first = lax.broadcasted_iota(jnp.int32, (1, 128), 1)

        def score(h):
            here = jnp.where(lane == W, 1.0, masks[h]).astype(low)
            return dot(query * here, S.kt[...])

        ready = score(0)
        for h in range(n.heads):
            scores = ready
            if h + 1 < n.heads:
                ready = score(h + 1)
            terms = jnp.exp(scores - jnp.max(scores, -1, keepdims=True)).astype(low)
            S.e[h, s] = terms
            part = dot(terms, S.v[...])
            scale = 1.0 / part[:, W : W + 1]
            mixed += part * (scale * masks[h])
            inverse = jnp.where(first == h, scale, inverse)
        S.o[s] = mixed
        S.inv[s] = inverse
        S.mix[s] = mixed[:, :W].astype(low)

        @pl.when(i < 3)
        def _():
            links.copy(S.mix.at[s], S.mix4.at[t], mix_base + i, tensor=s).start()

        @pl.when(i == 1)
        def _():
            cot_in.start([1])

        @pl.when(i == 2)
        def _():
            ow_in.wait_sib()
            ow_in.forward()

        return carry

    lax.fori_loop(0, 4, attend, 0)
    ow_in.wait_diag()
    S.mix4[t] = S.mix[t]
    for j, s in enumerate(peers):
        links.arrived(S.mix4.at[s], mix_base + j, tensor=s)

    total = dot(S.mix4[0], S.ow4[0])
    for j in range(1, 4):
        total += dot(S.mix4[j], S.ow4[j])
    total = S.x[...].astype(wide) + (total[:own] + vector(S.ob))
    S.hid[...] = total
    unit, _ = standardize(total)
    S.a24[t, 0:own, :] = (unit * vector(S.g2) + vector(S.b2)).astype(low)
    next_in = Gather(links, S.a24, t, halves(R))
    next_in.start()
    back = Reduce(links, S.part, S.pre1, S.near1, S.far1, t, split)
    ahead = Reduce(links, S.fop, S.pre2, S.near2, S.far2, t, split)
    S.gub[...] = jnp.zeros_like(S.gub)

    def feed(s, start, size):
        rows = pl.ds(start, size)
        up = dot(S.a24[s, rows], S.wup[...]) + vector(S.bup)
        square = up * up
        c = 0.7978845608028654
        bend = jnp.tanh(c * up * (1.0 + 0.044715 * square))
        half = 0.5 * (1.0 + bend)
        slope = half + 0.5 * up * (1.0 - bend * bend) * (c + (3 * 0.044715 * c) * square)
        active = (up * half).astype(low)
        S.pool[s, rows, 0:D] = active
        grad = (dot(S.cot4[s, rows], S.gw[D:, :]) * slope).astype(low)
        S.gup[s, rows] = grad
        S.part[s, rows] = dot(grad, S.gw[0:D, :]).astype(low)
        S.gub[...] += jnp.sum(grad.astype(wide), 0, keepdims=True)

    def lead_out(s, start, size):
        rows = pl.ds(start, size)
        S.fop[s, rows] = dot(S.pool[s, rows, 0:D], S.wdn[...]).astype(low)

    def feed_here(i, carry):
        s = flipped(t, 0, i)

        @pl.when(i == 1)
        def _():
            next_in.wait_sib()
            cot_in.wait_sib()

        feed(s, 0, R)

        @pl.when(i == 1)
        def _():
            back.send_sib()

        lead_out(s, 0, R)
        return carry

    lax.fori_loop(0, 2, feed_here, 0)
    ahead.send_sib()
    for p in (0, 1):

        def feed_there(i, carry, p=p):
            @pl.when(i == 0)
            def _():
                cot_in.forward([p])
                next_in.forward([p])

            @pl.when(i == 1)
            def _():
                cot_in.wait_diag([p])
                next_in.wait_diag([p])

            feed(flipped(t, 1, i), *split[p])
            if p == 1:

                @pl.when(i == 0)
                def _():
                    back.send_cross([0])

            return carry

        lax.fori_loop(0, 2, feed_there, 0)
        back.send_diag([p])
    for i in (0, 1):
        lead_out(flipped(t, 1, i), 0, R)
    back.send_cross([1])
    ahead.send_diag()

    sums = Pipeline(PLAN)
    tile = D // 2
    box_at = 0

    def sum_over_dp(kind, held, whole, out, first, rows):
        nonlocal box_at
        sums.add(kind(links, held, whole, out, S.box, box_at, first, rows, d, n.dp))
        box_at += kind.sizes(rows, D, n.dp)[1]

    for left, right, first in ((S.a24, S.gup, 0), (S.pool, S.cot4, D)):
        rows = left[:, :, 0:D].reshape(4 * R, D)
        S.gw[first : first + D, :] = dot_columns(rows, flat(right)).astype(low)
        for at in (first, first + tile):
            kind = Quarters if at in (0, D + tile) else Halves
            sum_over_dp(kind, S.gw, S.sum1, S.whole1, at, tile)

    sums.at("waiting")
    S.small[...] = jnp.zeros_like(S.small)
    gm_base = links.take(6)
    shared = lambda s, p, j: links.copy(
        S.mix4.at[s, pl.ds(*split[p])], S.gm4.at[t, pl.ds(*split[p])], gm_base + 3 * p + j, tensor=peers[j]
    )
    for p, (start, size) in enumerate(split):
        real = min(size, own - start)
        rows = pl.ds(start, real)
        grad = back.result(p)[:real]
        unit, inverse = standardize(S.hid[rows])
        S.small[2:3, :] += jnp.sum(grad * unit, 0, keepdims=True)
        S.small[3:4, :] += jnp.sum(grad, 0, keepdims=True)
        S.gt[rows] += norm_back(grad, unit, inverse, vector(S.g2))
        S.hl4[t, rows] = S.gt[rows].astype(low)
        rows = pl.ds(start, size)
        for j, s in enumerate(peers + [t]):
            product = dot_rows(S.hl4[t, rows], S.ow4[s]).astype(low)
            if j < 3:
                S.mix4[s, rows] = product
                shared(s, p, j).start()
            else:
                S.gm4[t, rows] = product
    S.small[4:5, :] = jnp.sum(S.hl4[t].astype(wide), 0, keepdims=True)
    S.small[5:6, :] = jnp.sum(S.cot4[t].astype(wide), 0, keepdims=True)
    S.small[6:7, :] = S.gub[...]
    hl_in = Gather(links, S.hl4, t, halves(R))

    next_in.finish()
    S.do[...] = jnp.zeros_like(S.do)
    S.qt[...] = jnp.transpose(flat(S.q))
    sums.at("shared")

    def prepare(i, s):
        if i > 0:
            j = (None, 2, 0, 1)[i]
            for p in (0, 1):
                rows = pl.ds(*split[p])
                links.arrived(S.gm4.at[s, rows], gm_base + 3 * p + j, tensor=peers[j])
        S.do[:, :W] = S.gm4[s].astype(wide)
        inverse = sum(S.inv[s, :, h : h + 1] * masks[h] for h in range(n.heads))
        scaled = (S.do[...] * inverse).astype(low)
        S.v[pl.ds(pl.multiple_of(s * R, 16), R), :] = scaled
        scaled = scaled.astype(wide)
        product = scaled * S.o[s]
        for h in range(n.heads):
            inner = -jnp.sum(product * masks[h], -1, keepdims=True)
            upper = inner.astype(low).astype(wide)
            S.a24[s, :, h * H : (h + 1) * H] = (
                scaled * masks[h]
                + jnp.where(lane == W, upper, 0.0)
                + jnp.where(lane == W + 1, inner - upper, 0.0)
            ).astype(low)

    def pull(h, p):
        grad_p = dot(pair(S.a24.at[:, :, h * H : (h + 1) * H], p), S.vt[...])
        grad_s = (pair(S.e.at[h], p).astype(wide) * grad_p).astype(low)
        set_pair(S.pool, p, grad_s)
        dq = dot(grad_s, S.k[...]) * (masks[h] * HEAD_DIM**-0.5)
        if h > 0:
            dq += pair(S.gup.at[:, :, 0:H], p).astype(wide)
        S.gup[pl.ds(2 * p, 2), :, 0:H] = dq.astype(low).reshape(2, R, H)

    def weights(h):
        at = slice(h * HEAD_DIM, (h + 1) * HEAD_DIM)
        tile = h * HEAD_DIM // 128 * 128
        dqt = jnp.transpose(flat(S.gup.at[:, :, tile : tile + 128]))
        left = jnp.concatenate(
            [dqt[h * HEAD_DIM - tile : (h + 1) * HEAD_DIM - tile], S.qt[at, :], S.kt[at, : 4 * R]], 0
        )
        out = dot(left, flat(S.a1))
        S.gw2[h * W : (h + 1) * W, :] = out.astype(low)
        for c in range(3):
            product = out[c * HEAD_DIM : (c + 1) * HEAD_DIM] * S.wqkv[c, at, :].astype(wide)
            S.small[0:1, :] += jnp.sum(product, 0, keepdims=True)
        sum_over_dp(Quarters, S.gw2, S.sum2, S.whole2, h * W, W)

    for h in range(n.heads):
        for i in (0, 2):
            if (h, i) == (0, 2):
                sums.at("arriving")
            if h == 0:
                prepare(i, flipped(t, i // 2, 0))
                prepare(i + 1, flipped(t, i // 2, 1))
            if (h, i) == (0, 2):
                hl_in.start()
            pull(h, (chip + i // 2) % 2)
            sums.at(f"h{h}p{i}")
            if (h, i) == (1, 0):
                hl_in.wait_sib()
                hl_in.forward()
                ahead.send_cross()
            elif (h, i) == (1, 2):
                hl_in.wait_diag()
                S.gw2[3 * W :, :] = dot_columns(flat(S.mix), flat(S.hl4)).astype(low)
                sum_over_dp(Quarters, S.gw2, S.sum2, S.whole2, 3 * W, W)
        if h == 0:
            S.v[4 * R :, :] = jnp.zeros((K - 4 * R, H), low)
            S.kt[...] = jnp.transpose(S.v[...])
        at = slice(h * HEAD_DIM, (h + 1) * HEAD_DIM)
        S.qt[at, :] = dot(S.qt[at, :], flat(S.pool))[:, : 4 * R].astype(low)
        S.kt[at, : 4 * R] = dot(S.kt[at, : 4 * R], flat(S.e.at[h]))[:, : 4 * R].astype(low)
        if h + 1 < n.heads:
            weights(h)
        sums.at(f"h{h}")

    pad = jnp.zeros((R, H - W), low)
    for part, grad_t in ((1, S.qt), (2, S.kt)):
        rows = jnp.transpose(grad_t[:W, : 4 * R])
        for s in range(4):
            S.gup[s, :, part * H : part * H + W] = rows[s * R : (s + 1) * R]
            S.gup[s, :, part * H + W : (part + 1) * H] = pad

    back.finish()
    down = Reduce(links, S.part, S.pre1, S.near1, S.far1, t, split)

    def lead(s, start, size):
        rows = pl.ds(start, size)
        out = dot(S.gup[s, rows, 0:W], S.wqkv[0])
        out += dot(S.gup[s, rows, H : H + W], S.wqkv[1])
        out += dot(S.gup[s, rows, 2 * H : 2 * H + W], S.wqkv[2])
        S.part[s, rows] = out.astype(low)

    cross, diag, sib = peers
    lead(diag, *split[0])
    down.send_diag([0])
    lead(cross, *split[0])
    weights(n.heads - 1)
    down.send_cross([0])
    lead(diag, *split[1])
    down.send_diag([1])
    lead(cross, *split[1])
    down.send_cross([1])
    lead(sib, 0, R)
    down.send_sib()
    lead(t, 0, R)
    columns = jnp.sum(flat(S.gup).astype(wide), 0, keepdims=True)
    S.small[7:8, 0:H] = columns[:, 0:H]
    S.small[7:8, H : 2 * H] = columns[:, 2 * H :]
    upper = columns.astype(low)
    both = jnp.concatenate([upper.astype(wide), columns - upper.astype(wide)], 0).astype(low)
    for c in range(3):
        product = dot(both[:, c * H : c * H + W], S.wqkv[c])
        S.small[1:2, :] += jnp.sum(product, 0, keepdims=True)

    S.small4[t] = S.small[...]
    base3 = links.take(3)
    for j in range(3):
        peer = lax.rem(t + j + 1, 4)
        links.start(S.small4.at[t], S.small4.at[t], base3 + j, tensor=peer)
    sums.at("led")
    result = jnp.concatenate([ahead.result(0), ahead.result(1)], 0)
    S.output[...] = (S.hid[...] + (result[:own] + vector(S.db))).astype(low)
    sums.at("crossing")

    unit, inverse = standardize(S.x[...].astype(wide))
    grad = jnp.concatenate([down.result(0), down.result(1)], 0)[:own]
    for j in range(3):
        peer = lax.rem(t + 3 - j, 4)
        links.arrived(S.small4.at[peer], base3 + j, tensor=peer)
    over = S.small4[0] + S.small4[1] + S.small4[2] + S.small4[3]
    row = lax.broadcasted_iota(jnp.int32, over.shape, 0)
    near = min(8, n.dp)
    inner = Everyone(links, S.smalls, d % near, near, lambda j: d // near * near + j)
    inner.start(jnp.where(row < 6, over, S.small[...]))
    S.gt[...] += norm_back(grad, unit, inverse, vector(S.g1))
    sums.at("told")
    sums.finish()
    total = inner.result()
    inner.finish()
    if n.dp > near:
        outer = Everyone(links, S.smalls2, d // near, n.dp // near, lambda j: j * near + d % near)
        outer.start(total)
        total = outer.result()
        outer.finish()
    S.small_sum[...] = total
    S.small_sum[0:1, :] = (total[0:1, :] - vector(S.b1) * total[1:2, :]) / vector(S.g1)
    for j, s in enumerate(peers):
        links.copy(S.mix.at[s], S.mix4.at[t], mix_base + j, tensor=s).wait_send()
        for p in (0, 1):
            shared(s, p, j).wait_send()
    for transfer in (rows_in, cot_in, ow_in, hl_in, ahead, down):
        transfer.finish()
    links.finish()


SMALL = ("gain1", "shift1", "gain2", "shift2", "bias_out", "bias_down", "bias_up", "bias_qv")


def finish(n, output, gt, small, whole1, whole2):
    D, W, H = n.D, n.W, n.H
    steps = n.heads
    rows1 = D // steps

    def spread(output, gt, small, up, down, head, out, *refs):
        to_output, to_gt, to_up, to_down, to_qkv, to_out = refs[:6]
        vectors, sems = refs[6:14], refs[14]
        i = pl.program_id(0)
        held = refs[15:]
        come = [pltpu.make_async_copy(a, b, sems.at[j]) for j, (a, b) in enumerate(zip((output, gt), held))]
        go = [
            pltpu.make_async_copy(a, b, sems.at[2 + j])
            for j, (a, b) in enumerate(zip(held, (to_output, to_gt)))
        ]

        @pl.when(i == 0)
        def _():
            for copy in come:
                copy.start()
            for j in range(7):
                vectors[j][...] = small[j : j + 1, :].reshape(D)
            vectors[7][0:1, :] = small[7:8, :W]
            vectors[7][1:2, :] = small[7:8, H : H + W]

        to_up[...] = up[...].astype(wide)
        to_down[...] = down[...].astype(wide)
        for j in range(3):
            to_qkv[j] = head[j * HEAD_DIM : (j + 1) * HEAD_DIM, :].astype(wide)
        to_out[...] = out[...].astype(wide)

        @pl.when(i == 1)
        def _():
            for first, second in zip(come, go):
                first.wait()
                second.start()

        @pl.when(i == steps - 1)
        def _():
            for copy in go:
                copy.wait()

    hbm = pl.BlockSpec(memory_space=pl.ANY)
    whole = pl.BlockSpec(memory_space=pltpu.VMEM)
    at_row = lambda rows, index: pl.BlockSpec((rows, D), lambda i: (index(i), 0))
    shape = jax.ShapeDtypeStruct
    return pl.pallas_call(
        spread,
        grid=(steps,),
        out_shape=[shape(output.shape, low), shape(gt.shape, wide)]
        + [shape((D, D), wide)] * 2
        + [shape((3, W, D), wide), shape((W, D), wide)]
        + [shape((D,), wide)] * 7
        + [shape((2, W), wide)],
        in_specs=[hbm, hbm, whole, at_row(rows1, lambda i: i), at_row(rows1, lambda i: i + steps)]
        + [at_row(W, lambda i: i), at_row(HEAD_DIM, lambda i: 3 * steps + i)],
        out_specs=[hbm, hbm]
        + [at_row(rows1, lambda i: i)] * 2
        + [pl.BlockSpec((3, HEAD_DIM, D), lambda i: (0, i, 0)), at_row(HEAD_DIM, lambda i: i)]
        + [whole] * 8,
        scratch_shapes=[
            pltpu.SemaphoreType.DMA((4,)),
            pltpu.VMEM(output.shape, low),
            pltpu.VMEM(gt.shape, wide),
        ],
    )(output, gt, small, whole1, whole1, whole2, whole2)


def body(
    tokens,
    lengths,
    ln1_gain,
    ln1_shift,
    qkv_weight,
    qv_bias,
    out_weight,
    out_bias,
    ln2_gain,
    ln2_shift,
    up_weight,
    up_bias,
    down_weight,
    down_bias,
    cotangent,
):
    own, D = tokens.shape
    W = qkv_weight.shape[2]
    F = up_weight.shape[1]
    dp = lax.axis_size("dp")
    assert lax.axis_size("tensor") == 4 and lengths.shape[0] == 1 and F == D and 4 * W == D and 3 * round_up(W + 2, 128) == D
    R = round_up(own, 16)
    H = round_up(W + 2, 128)
    K = round_up(4 * R, 256)
    heads = W // HEAD_DIM
    extra = dp.bit_length() - 1 - 3
    n = types.SimpleNamespace(
        own=own, D=D, W=W, R=R, H=H, K=K, dp=dp, heads=heads, extra=extra
    )
    given = dict(
        x=tokens, lengths=lengths, g1=ln1_gain, b1=ln1_shift,
        wqkv=jnp.transpose(qkv_weight, (1, 2, 0)), bq=qv_bias, ow=out_weight, ob=out_bias,
        g2=ln2_gain, b2=ln2_shift, wup=up_weight, bup=up_bias, wdn=down_weight, db=down_bias,
        cot=cotangent,
    )
    outs = dict(
        output=((own, D), low), gt=((own, D), wide), small_sum=((8, D), wide),
        whole1=((2 * D, D), low), whole2=((D, D), low),
    )
    rows4 = ((4, R, D), low)
    slab = ((R, D), low)
    chunks = [(Quarters, D // 2), (Halves, D // 2)] * 2 + [(Quarters, W)] * 4
    scratch = dict(
        a1=rows4, cot4=rows4, ow4=((4, W, D), low), q=((4, R, H), low), k=((K, H), low),
        v=((K, H), low), kt=((H, K), low), vt=((H, K), low), e=((heads, 4, R, K), low),
        o=((4, R, H), wide), inv=((4, R, 128), wide), mix=((4, R, W), low), mix4=((4, R, W), low),
        hid=((own, D), wide),
        a24=rows4, pool=((4, R, K), low), gup=rows4, part=rows4,
        fop=rows4, pre1=slab, near1=slab, far1=slab, pre2=slab, near2=slab, far2=slab,
        gw=((2 * D, D), low), gub=((1, D), wide),
        small=((8, D), wide), hl4=rows4,
        gm4=((4, R, W), low), qt=((H, 4 * R), low), do=((R, H), wide),
        gw2=((D, D), low),
        small4=((4, 8, D), wide), smalls=((min(8, dp), 8, D), wide),
        box=((sum(kind.sizes(r, D, dp)[1] for kind, r in chunks), D), low),
        sum1=((2 * D, D), low), sum2=((D, D), low),
    )
    if dp > 8:
        scratch["smalls2"] = ((dp // 8, 8, D), wide)
    sems = 170 + dp + 8 * extra
    names = list(given) + list(outs) + list(scratch) + ["local", "send", "recv"]
    vmem = pl.BlockSpec(memory_space=pltpu.VMEM)
    smem = pl.BlockSpec(memory_space=pltpu.SMEM)
    hbm = pl.BlockSpec(memory_space=pl.ANY)
    output, gt, small, whole1, whole2 = pl.pallas_call(
        lambda *refs: kernel(n, types.SimpleNamespace(**dict(zip(names, refs)))),
        out_shape=tuple(jax.ShapeDtypeStruct(*spec) for spec in outs.values()),
        in_specs=[dict(lengths=smem, cot=hbm).get(name, vmem) for name in given],
        out_specs=tuple(hbm if name in ("whole1", "whole2") else vmem for name in outs),
        scratch_shapes=[pltpu.VMEM(*spec) for spec in scratch.values()]
        + [pltpu.SemaphoreType.DMA] + [pltpu.SemaphoreType.DMA((sems,))] * 2,
        compiler_params=pltpu.CompilerParams(
            collective_id=0, has_side_effects=True, vmem_limit_bytes=VMEM_BYTES
        ),
    )(*given.values())
    finished = finish(n, output, gt, small, whole1, whole2)
    small_rows = dict(zip(SMALL, finished[6:]))
    return (
        finished[0],
        finished[1],
        small_rows["gain1"],
        small_rows["shift1"],
        jnp.transpose(finished[4], (2, 0, 1)),
        small_rows["bias_qv"],
        finished[5],
        small_rows["bias_out"],
        small_rows["gain2"],
        small_rows["shift2"],
        finished[2],
        small_rows["bias_up"],
        finished[3],
        small_rows["bias_down"],
    )


def solution(mesh):
    placed = (
        P(("dp", "tensor"), None),
        P("dp"),
        P(),
        P(),
        P(None, None, "tensor"),
        P(None, "tensor"),
        P("tensor", None),
        P(),
        P(),
        P(),
        P(None, "tensor"),
        P("tensor"),
        P("tensor", None),
        P(),
        P(("dp", "tensor"), None),
    )
    return jax.shard_map(
        body,
        mesh=mesh,
        in_specs=placed,
        out_specs=(
            P(("dp", "tensor"), None),
            P(("dp", "tensor"), None),
            P(),
            P(),
            P(None, None, "tensor"),
            P(None, "tensor"),
            P("tensor", None),
            P(),
            P(),
            P(),
            P(None, "tensor"),
            P("tensor"),
            P("tensor", None),
            P(),
        ),
        check_vma=False,
    )
```

```python
import types

import jax
import jax.numpy as jnp
from jax import lax
from jax.experimental import pallas as pl
from jax.experimental.pallas import tpu as pltpu
from jax.sharding import PartitionSpec as P

HEAD_DIM = 64
MESH = pl.DeviceIdType.MESH
VMEM_BYTES = 62 * 2**20

epsilon = 1e-06
low = jnp.bfloat16
wide = jnp.float32


def round_up(amount, unit):
    return -(-amount // unit) * unit


def flipped(t, flip_chip, flip_core):
    return (t // 2 + flip_chip) % 2 * 2 + (t % 2 + flip_core) % 2


def dot(left, right):
    return jnp.dot(left, right, preferred_element_type=wide)


def dot_rows(left, right):
    return lax.dot_general(left, right, (((1,), (1,)), ((), ())), preferred_element_type=wide)


def dot_columns(left, right):
    return lax.dot_general(left, right, (((0,), (0,)), ((), ())), preferred_element_type=wide)


def standardize(values):
    center = values - jnp.mean(values, -1, keepdims=True)
    inverse = lax.rsqrt(jnp.mean(center * center, -1, keepdims=True) + epsilon)
    return center * inverse, inverse


def norm_back(grad, unit, inverse, gain):
    scaled = grad * gain
    return inverse * (
        scaled
        - jnp.mean(scaled, -1, keepdims=True)
        - unit * jnp.mean(scaled * unit, -1, keepdims=True)
    )


def pair(ref, p):
    _, rows, columns = ref.shape
    return ref[pl.ds(2 * p, 2)].reshape(2 * rows, columns)


def set_pair(ref, p, values):
    ref[pl.ds(2 * p, 2)] = values.reshape(2, -1, values.shape[1])


def flat(ref):
    a, b, c = ref.shape
    return ref[...].reshape(a * b, c)


class Links:
    def __init__(self, send, recv):
        self.send, self.recv, self.used, self.pending = send, recv, 0, []

    def take(self, amount=1):
        base = self.used
        self.used += amount
        assert self.used <= self.send.shape[0]
        return base

    def copy(self, src, dst, at, **where):
        return pltpu.make_async_remote_copy(
            src_ref=src,
            dst_ref=dst,
            send_sem=self.send.at[at],
            recv_sem=self.recv.at[at],
            device_id=where,
            device_id_type=MESH,
        )

    def start(self, src, dst, at, **where):
        copy = self.copy(src, dst, at, **where)
        copy.start()
        self.pending.append(copy)

    def arrived(self, dst, at, **where):
        self.copy(dst, dst, at, **where).wait_recv()

    def finish(self):
        for copy in self.pending:
            copy.wait_send()
        self.pending = []


class Gather:
    def __init__(self, links, buf, t, parts):
        self.links, self.buf, self.t, self.parts = links, buf, t, parts
        self.sib, self.cross, self.diag = flipped(t, 0, 1), flipped(t, 1, 0), flipped(t, 1, 1)
        self.base = links.take(3 * len(parts))

    def view(self, slot, part):
        start, size = self.parts[part]
        return self.buf.at[slot, pl.ds(start, size)]

    def _each(self):
        return range(len(self.parts))

    def start(self, parts=None):
        parts = self._each() if parts is None else parts
        for p in parts:
            v = self.view(self.t, p)
            self.links.copy(v, v, self.base + 3 * p, tensor=self.cross).start()
        for p in parts:
            v = self.view(self.t, p)
            self.links.copy(v, v, self.base + 3 * p + 1, tensor=self.sib).start()

    def wait_sib(self):
        for p in self._each():
            self.links.arrived(self.view(self.sib, p), self.base + 3 * p + 1, tensor=self.sib)

    def forward(self, parts=None):
        for p in self._each() if parts is None else parts:
            v = self.view(self.cross, p)
            self.links.arrived(v, self.base + 3 * p, tensor=self.cross)
            self.links.copy(v, v, self.base + 3 * p + 2, tensor=self.sib).start()

    def wait_diag(self, parts=None):
        for p in self._each() if parts is None else parts:
            self.links.arrived(self.view(self.diag, p), self.base + 3 * p + 2, tensor=self.sib)

    def finish(self):
        for p in self._each():
            v = self.view(self.t, p)
            self.links.copy(v, v, self.base + 3 * p, tensor=self.cross).wait_send()
            self.links.copy(v, v, self.base + 3 * p + 1, tensor=self.sib).wait_send()
            v = self.view(self.cross, p)
            self.links.copy(v, v, self.base + 3 * p + 2, tensor=self.sib).wait_send()


class Reduce:
    def __init__(self, links, part, pre, near, far, t, parts):
        self.links, self.part, self.t, self.parts = links, part, t, parts
        self.pre, self.near, self.far = pre, near, far
        self.sib, self.cross, self.diag = flipped(t, 0, 1), flipped(t, 1, 0), flipped(t, 1, 1)
        self.base = links.take(3 * len(parts))

    def _copy(self, kind, p):
        slot, box, peer = (
            (self.diag, self.pre, self.sib),
            (self.sib, self.near, self.sib),
            (self.cross, self.far, self.cross),
        )[kind]
        rows = pl.ds(*self.parts[p])
        return self.links.copy(
            self.part.at[slot, rows], box.at[rows], self.base + 3 * p + kind, tensor=peer
        )

    def _each(self, parts):
        return range(len(self.parts)) if parts is None else parts

    def send_diag(self, parts=None):
        for p in self._each(parts):
            self._copy(0, p).start()

    def send_sib(self):
        for p in self._each(None):
            self._copy(1, p).start()

    def send_cross(self, parts=None):
        for p in self._each(parts):
            self._copy(0, p).wait_recv()
            rows = pl.ds(*self.parts[p])
            self.part[self.cross, rows] = (
                self.part[self.cross, rows].astype(wide) + self.pre[rows].astype(wide)
            ).astype(low)
            self._copy(2, p).start()

    def result(self, p):
        self._copy(1, p).wait_recv()
        self._copy(2, p).wait_recv()
        rows = pl.ds(*self.parts[p])
        return (
            self.part[self.t, rows].astype(wide)
            + self.near[rows].astype(wide)
            + self.far[rows].astype(wide)
        )

    def finish(self):
        for p in self._each(None):
            for kind in range(3):
                self._copy(kind, p).wait_send()


class DataReduce:
    def __init__(self, links, held, whole, out, box, box_at, first, rows, d, count):
        self.links, self.held, self.whole, self.out, self.d = links, held, whole, out, d
        bits = count.bit_length() - 1
        assert count == 1 << bits and bits >= 3
        self.extra = list(range(3, bits))
        self.region = (first, rows, 0, held.shape[1])
        self.trail, self.sent, self.boxes = [], [], []
        for tall, broad in self.sizes(rows, held.shape[1], count)[0]:
            self.boxes.append(box.at[pl.ds(box_at, tall), pl.ds(0, broad)])
            box_at += tall
        self.base = links.take(9 + len(self.extra))
        self.plan()

    @classmethod
    def sizes(cls, rows, columns, count):
        found = cls.boxes_of(rows, columns)
        found += found[-1:] * (count.bit_length() - 1 - 3)
        return found, sum(size[0] for size in found)

    def _bit(self, b):
        return self.d // (1 << b) % 2

    def _peer(self, b):
        return self.d + (1 - 2 * self._bit(b)) * (1 << b)

    def _send(self, src, dst, at, peer):
        copy = self.links.copy(src, dst, self.base + at, dp=peer)
        copy.start()
        self.sent.append(copy)

    def _wait(self, dst, at, peer):
        self.links.arrived(dst, self.base + at, dp=peer)

    @staticmethod
    def _view(ref, region):
        row, rows, column, columns = region
        if columns == ref.shape[1]:
            return ref.at[pl.ds(row, rows)]
        return ref.at[pl.ds(row, rows), pl.ds(column, columns)]

    @staticmethod
    def _part(region, bit):
        row, rows, column, columns = region
        if rows % 32 == 0:
            return (pl.multiple_of(row + bit * (rows // 2), 16), rows // 2, column, columns)
        return (row, rows, pl.multiple_of(column + bit * (columns // 2), 128), columns // 2)

    def _give_half(self, b, box, at):
        bit = self._bit(b)
        self.trail.append(self.region)
        self._send(self._view(self.held, self._part(self.region, 1 - bit)), self.boxes[box], at, self._peer(b))
        self.region = self._part(self.region, bit)

    def _add(self, boxes, last):
        view = self._view(self.held, self.region)
        total = view[...].astype(wide)
        for box in boxes:
            total += self.boxes[box][...].astype(wide)
        if last:
            view = self._view(self.whole, self.region)
        view[...] = total.astype(low)
        if last:
            self._swap()

    def _swap(self):
        view = self._view(self.whole, self.region)
        for k, b in enumerate(self.extra):
            box, at = self.boxes[k - len(self.extra)], 9 + k
            copy = self.links.copy(view, box, self.base + at, dp=self._peer(b))
            copy.start()
            self._wait(box, at, self._peer(b))
            copy.wait_send()
            view[...] = (view[...].astype(wide) + box[...].astype(wide)).astype(low)

    def _give_whole(self, b, at):
        view = self._view(self.whole, self.region)
        self._send(view, view, at, self._peer(b))

    def _take_half(self, b, at):
        outer = self.trail.pop()
        view = self._view(self.whole, self._part(outer, 1 - self._bit(b)))
        self._wait(view, at, self._peer(b))
        self.region = outer

    def _leave(self):
        rows = pl.ds(self.region[0], self.region[1])
        self.left = pltpu.make_async_copy(
            self.whole.at[rows], self.out.at[rows], self.links.send.at[self.base + 8]
        )
        self.left.start()

    def step(self):
        if self.steps:
            self.steps.pop(0)()

    def finish(self):
        assert not self.steps
        self.left.wait()
        for copy in self.sent:
            copy.wait_send()


class Halves(DataReduce):
    order = (1, 0, 2)

    @staticmethod
    def boxes_of(rows, columns):
        found = []
        for _ in range(3):
            if rows % 32 == 0:
                rows //= 2
            else:
                columns //= 2
            found.append((rows, columns))
        return found

    def plan(self):
        low_bit, x, high = self.order
        self.steps = [
            lambda: self._give_half(low_bit, 0, 0),
            lambda: (self._wait_box(low_bit, 0), self._add((0,), False), self._give_half(x, 1, 1)),
            lambda: (self._wait_box(x, 1), self._add((1,), False), self._give_half(high, 2, 2)),
            lambda: (self._wait_box(high, 2), self._add((2,), True), self._give_whole(high, 3)),
            lambda: (self._take_half(high, 3), self._give_whole(x, 4)),
            lambda: (self._take_half(x, 4), self._give_whole(low_bit, 5)),
            lambda: (self._take_half(low_bit, 5), self._leave()),
        ]

    def _wait_box(self, b, box):
        self._wait(self.boxes[box], box, self._peer(b))


class Quarters(DataReduce):
    @staticmethod
    def boxes_of(rows, columns):
        tall, broad = rows // 8, columns
        if tall % 16:
            tall, broad = rows // 4, columns // 2
        return [(rows // 2, columns)] + [(tall, broad)] * 3

    def plan(self):
        self.steps = [
            lambda: self._give_half(0, 0, 0),
            lambda: (self._wait(self.boxes[0], 0, self._peer(0)), self._add((0,), False), self._give_quarters()),
            lambda: (self._take_boxes(), self._add((1, 2, 3), True), self._give_quarter()),
            lambda: (self._take_quarters(), self._give_whole(0, 7)),
            lambda: (self._take_half(0, 7), self._leave()),
        ]

    def _z(self, j):
        low_bit = (self._bit(1) + j % 2) % 2
        high = (self._bit(2) + j // 2) % 2
        return low_bit, high, self.d // 8 * 8 + high * 4 + low_bit * 2 + self._bit(0)

    def _quarter(self, j):
        low_bit, high, peer = self._z(j)
        return self._part(self._part(self.trail[-1], high), low_bit), peer

    def _give_quarters(self):
        self.trail.append(self.region)
        for j in (1, 2, 3):
            part, peer = self._quarter(j)
            self._send(self._view(self.held, part), self.boxes[j], j, peer)
        self.region = self._quarter(0)[0]

    def _take_boxes(self):
        for j in (1, 2, 3):
            self._wait(self.boxes[j], j, self._z(j)[2])

    def _give_quarter(self):
        view = self._view(self.whole, self.region)
        for j in (1, 2, 3):
            self._send(view, view, 3 + j, self._z(j)[2])

    def _take_quarters(self):
        for j in (1, 2, 3):
            part, peer = self._quarter(j)
            self._wait(self._view(self.whole, part), 3 + j, peer)
        self.region = self.trail.pop()


class Pipeline:
    def __init__(self, plan):
        self.plan, self.members = plan, []

    def add(self, member):
        self.members.append(member)
        member.step()

    def at(self, place):
        for number in self.plan[place]:
            self.members[number].step()

    def finish(self):
        self.at("end")
        for m in self.members:
            while m.steps:
                m.step()
            m.finish()


PLAN = dict(
    waiting=(),
    shared=(0, 1),
    arriving=(),
    h0p0=(3,),
    h0p2=(2, 1),
    h0=(),
    h1p0=(2, 1, 0, 4),
    h1p2=(2,),
    h1=(1, 3),
    h2p0=(5, 0),
    h2p2=(4, 6),
    h2=(1, 2),
    led=(5, 3, 7, 1, 2),
    crossing=(0, 4, 6, 5),
    told=(7, 2, 6, 5),
    end=(4, 7, 3, 6, 7),
)


class Everyone:
    def __init__(self, links, buf, me, count, device):
        self.links, self.buf, self.me, self.count, self.device = links, buf, me, count, device
        self.base = links.take(count)

    def _copy(self, j):
        slot = self.buf.at[self.me]
        peer = self.device(lax.rem(self.me + j, self.count))
        return self.links.copy(slot, slot, self.base + j, dp=peer)

    def _loop(self, act):
        def one(j, carry):
            act(j)
            return carry

        lax.fori_loop(1, self.count, one, 0)

    def start(self, values):
        self.buf[self.me] = values
        self._loop(lambda j: self._copy(j).start())

    def _hear(self, j):
        peer = lax.rem(self.me + self.count - j, self.count)
        self.links.arrived(self.buf.at[peer], self.base + j, dp=self.device(peer))

    def result(self):
        self._loop(self._hear)
        return lax.fori_loop(1, self.count, lambda j, acc: acc + self.buf[j], self.buf[0])

    def finish(self):
        self._loop(lambda j: self._copy(j).wait_send())


def greet(axis, me, count):
    barrier = pltpu.get_barrier_semaphore()

    def one(j, carry):
        pl.semaphore_signal(
            barrier, inc=1, device_id={axis: lax.rem(me + j, count)}, device_id_type=MESH
        )
        return carry

    lax.fori_loop(1, count, one, 0)


def await_greetings(amount):
    pl.semaphore_wait(pltpu.get_barrier_semaphore(), amount)


def halves(rows):
    first = round_up(rows // 2, 16)
    return ((0, first), (first, rows - first))


def head_masks(shape, local_heads):
    lane = lax.broadcasted_iota(jnp.int32, shape, 1)
    return [
        jnp.where((lane >= h * HEAD_DIM) & (lane < (h + 1) * HEAD_DIM), 1.0, 0.0)
        for h in range(local_heads)
    ], lane


def kernel(n, S):
    links = Links(S.send, S.recv)
    t = lax.axis_index("tensor")
    d = lax.axis_index("dp")
    greet("tensor", t, 4)
    greet("dp", d, n.dp)
    R, own, W, H, D, K = n.R, n.own, n.W, n.H, n.D, n.K
    split = halves(R)
    vector = lambda ref: ref[...].reshape(1, D)

    fetch = pltpu.make_async_copy(S.cot, S.gt, S.local.at[0])
    load = [
        pltpu.make_async_copy(getattr(S, name + "_far"), getattr(S, name), S.local.at[1 + j])
        for j, name in enumerate(LOADED)
    ]
    fetch.start()
    for copy in load:
        copy.start()
    S.a1[t] = jnp.zeros((R, D), low)
    S.cot4[t] = jnp.zeros((R, D), low)
    S.a24[t] = jnp.zeros((R, D), low)
    S.hl4[t] = jnp.zeros((R, D), low)
    rows_in = Gather(links, S.a1, t, split)
    cot_in = Gather(links, S.cot4, t, split)
    ow_in = Gather(links, S.ow4, t, ((0, W),))
    for p, (start, size) in enumerate(split):
        rows = pl.ds(start, min(size, own - start))
        unit, _ = standardize(S.x[rows, :].astype(wide))
        S.a1[t, rows, :] = (unit * vector(S.g1) + vector(S.b1)).astype(low)
        if p == 0:
            await_greetings(3 + n.dp - 1)
        rows_in.start([p])
    load[0].wait()
    S.ow4[t] = S.ow[...]
    ow_in.start()
    fetch.wait()
    S.cot4[t, 0:own, :] = S.gt[...].astype(low)
    cot_in.start([0])
    load[2].wait()
    load[3].wait()
    S.gw[0:D, :] = jnp.transpose(S.wup[...])
    S.gw[D:, :] = jnp.transpose(S.wdn[...])
    load[1].wait()
    S.v[4 * R :, :] = jnp.zeros((K - 4 * R, H), low)
    length = S.lengths[0]

    chip = t // 2

    def project(i, carry):
        s = flipped(t, i // 2, i % 2)

        @pl.when(i == 1)
        def _():
            rows_in.wait_sib()

        @pl.when(i == 2)
        def _():
            rows_in.forward()

        @pl.when(i == 3)
        def _():
            rows_in.wait_diag()

        slab = S.a1[s]
        lane = lax.broadcasted_iota(jnp.int32, (R, H - W), 1)
        row = lax.broadcasted_iota(jnp.int32, (R, H - W), 0)
        absent = (row >= own) | (row + s * own >= length)
        at = pl.ds(pl.multiple_of(s * R, 16), R)
        out = dot_rows(slab, S.wqkv[0]) + S.bq[0:1, :]
        S.q[s, :, :W] = (out.astype(low).astype(wide) * HEAD_DIM**-0.5).astype(low)
        S.q[s, :, W:] = jnp.where(lane == 0, HEAD_DIM**-0.5, 0.0).astype(low)
        S.k[at, :W] = dot_rows(slab, S.wqkv[1]).astype(low)
        S.k[at, W:] = jnp.where((lane == 0) & absent, -8e30, 0.0).astype(low)
        S.v[at, :W] = (dot_rows(slab, S.wqkv[2]) + S.bq[1:2, :]).astype(low)
        S.v[at, W:] = jnp.where(lane < 2, 1.0, 0.0).astype(low)
        return carry

    lax.fori_loop(0, 4, project, 0)
    if K > 4 * R:
        lane = lax.broadcasted_iota(jnp.int32, (K - 4 * R, H), 1)
        S.k[4 * R :, :] = jnp.where(lane == W, -8e30, 0.0).astype(low)
    S.kt[...] = jnp.transpose(S.k[...])
    S.vt[...] = jnp.transpose(S.v[...])

    masks, lane = head_masks((1, H), n.heads)
    mix_base = links.take(3)

    peers = [flipped(t, 1, 0), flipped(t, 1, 1), flipped(t, 0, 1)]

    def attend(i, carry):
        s = flipped(t, 1 - i // 2, (i + i // 2) % 2)
        query = S.q[s]
        mixed = jnp.zeros((R, H), wide)
        inverse = jnp.zeros((R, 128), wide)
        first = lax.broadcasted_iota(jnp.int32, (1, 128), 1)

        def score(h):
            here = jnp.where(lane == W, 1.0, masks[h]).astype(low)
            return dot(query * here, S.kt[...])

        ready = score(0)
        for h in range(n.heads):
            scores = ready
            if h + 1 < n.heads:
                ready = score(h + 1)
            terms = jnp.exp(scores - jnp.max(scores, -1, keepdims=True)).astype(low)
            S.e[h, s] = terms
            part = dot(terms, S.v[...])
            scale = 1.0 / part[:, W : W + 1]
            mixed += part * (scale * masks[h])
            inverse = jnp.where(first == h, scale, inverse)
        S.o[s] = mixed
        S.inv[s] = inverse
        S.mix[s] = mixed[:, :W].astype(low)

        @pl.when(i < 3)
        def _():
            links.copy(S.mix.at[s], S.mix4.at[t], mix_base + i, tensor=s).start()

        @pl.when(i == 1)
        def _():
            cot_in.start([1])

        @pl.when(i == 2)
        def _():
            ow_in.wait_sib()
            ow_in.forward()

        return carry

    lax.fori_loop(0, 4, attend, 0)
    ow_in.wait_diag()
    S.mix4[t] = S.mix[t]
    for j, s in enumerate(peers):
        links.arrived(S.mix4.at[s], mix_base + j, tensor=s)

    total = dot(S.mix4[0], S.ow4[0])
    for j in range(1, 4):
        total += dot(S.mix4[j], S.ow4[j])
    total = S.x[...].astype(wide) + (total[:own] + vector(S.ob))
    S.hid[...] = total
    unit, _ = standardize(total)
    S.a24[t, 0:own, :] = (unit * vector(S.g2) + vector(S.b2)).astype(low)
    next_in = Gather(links, S.a24, t, halves(R))
    next_in.start()
    back = Reduce(links, S.part, S.pre1, S.near1, S.far1, t, split)
    ahead = Reduce(links, S.fop, S.pre2, S.near2, S.far2, t, split)
    S.gub[...] = jnp.zeros_like(S.gub)

    def feed(s, start, size):
        rows = pl.ds(start, size)
        up = dot(S.a24[s, rows], S.wup[...]) + vector(S.bup)
        square = up * up
        c = 0.7978845608028654
        bend = jnp.tanh(c * up * (1.0 + 0.044715 * square))
        half = 0.5 * (1.0 + bend)
        slope = half + 0.5 * up * (1.0 - bend * bend) * (c + (3 * 0.044715 * c) * square)
        active = (up * half).astype(low)
        S.pool[s, rows, 0:D] = active
        grad = (dot(S.cot4[s, rows], S.gw[D:, :]) * slope).astype(low)
        S.gup[s, rows] = grad
        S.part[s, rows] = dot(grad, S.gw[0:D, :]).astype(low)
        S.gub[...] += jnp.sum(grad.astype(wide), 0, keepdims=True)

    def lead_out(s, start, size):
        rows = pl.ds(start, size)
        S.fop[s, rows] = dot(S.pool[s, rows, 0:D], S.wdn[...]).astype(low)

    def feed_here(i, carry):
        s = flipped(t, 0, i)

        @pl.when(i == 1)
        def _():
            next_in.wait_sib()
            cot_in.wait_sib()

        feed(s, 0, R)

        @pl.when(i == 1)
        def _():
            back.send_sib()

        lead_out(s, 0, R)
        return carry

    lax.fori_loop(0, 2, feed_here, 0)
    ahead.send_sib()
    for p in (0, 1):

        def feed_there(i, carry, p=p):
            @pl.when(i == 0)
            def _():
                cot_in.forward([p])
                next_in.forward([p])

            @pl.when(i == 1)
            def _():
                cot_in.wait_diag([p])
                next_in.wait_diag([p])

            feed(flipped(t, 1, i), *split[p])
            if p == 1:

                @pl.when(i == 0)
                def _():
                    back.send_cross([0])

            return carry

        lax.fori_loop(0, 2, feed_there, 0)
        back.send_diag([p])
    for i in (0, 1):
        lead_out(flipped(t, 1, i), 0, R)
    back.send_cross([1])
    ahead.send_diag()

    sums = Pipeline(PLAN)
    tile = D // 2
    box_at = 0

    def sum_over_dp(kind, held, whole, out, first, rows):
        nonlocal box_at
        sums.add(kind(links, held, whole, out, S.box, box_at, first, rows, d, n.dp))
        box_at += kind.sizes(rows, D, n.dp)[1]

    for left, right, first in ((S.a24, S.gup, 0), (S.pool, S.cot4, D)):
        rows = left[:, :, 0:D].reshape(4 * R, D)
        S.gw[first : first + D, :] = dot_columns(rows, flat(right)).astype(low)
        for at in (first, first + tile):
            kind = Quarters if at in (0, D + tile) else Halves
            sum_over_dp(kind, S.gw, S.sum1, S.whole1, at, tile)

    sums.at("waiting")
    S.small[...] = jnp.zeros_like(S.small)
    gm_base = links.take(6)
    shared = lambda s, p, j: links.copy(
        S.mix4.at[s, pl.ds(*split[p])], S.gm4.at[t, pl.ds(*split[p])], gm_base + 3 * p + j, tensor=peers[j]
    )
    for p, (start, size) in enumerate(split):
        real = min(size, own - start)
        rows = pl.ds(start, real)
        grad = back.result(p)[:real]
        unit, inverse = standardize(S.hid[rows])
        S.small[2:3, :] += jnp.sum(grad * unit, 0, keepdims=True)
        S.small[3:4, :] += jnp.sum(grad, 0, keepdims=True)
        S.gt[rows] += norm_back(grad, unit, inverse, vector(S.g2))
        S.hl4[t, rows] = S.gt[rows].astype(low)
        rows = pl.ds(start, size)
        for j, s in enumerate(peers + [t]):
            product = dot_rows(S.hl4[t, rows], S.ow4[s]).astype(low)
            if j < 3:
                S.mix4[s, rows] = product
                shared(s, p, j).start()
            else:
                S.gm4[t, rows] = product
    S.small[4:5, :] = jnp.sum(S.hl4[t].astype(wide), 0, keepdims=True)
    S.small[5:6, :] = jnp.sum(S.cot4[t].astype(wide), 0, keepdims=True)
    S.small[6:7, :] = S.gub[...]
    hl_in = Gather(links, S.hl4, t, halves(R))

    next_in.finish()
    S.do[...] = jnp.zeros_like(S.do)
    S.qt[...] = jnp.transpose(flat(S.q))
    sums.at("shared")

    def prepare(i, s):
        if i > 0:
            j = (None, 2, 0, 1)[i]
            for p in (0, 1):
                rows = pl.ds(*split[p])
                links.arrived(S.gm4.at[s, rows], gm_base + 3 * p + j, tensor=peers[j])
        S.do[:, :W] = S.gm4[s].astype(wide)
        inverse = sum(S.inv[s, :, h : h + 1] * masks[h] for h in range(n.heads))
        scaled = (S.do[...] * inverse).astype(low)
        S.v[pl.ds(pl.multiple_of(s * R, 16), R), :] = scaled
        scaled = scaled.astype(wide)
        product = scaled * S.o[s]
        for h in range(n.heads):
            inner = -jnp.sum(product * masks[h], -1, keepdims=True)
            upper = inner.astype(low).astype(wide)
            S.a24[s, :, h * H : (h + 1) * H] = (
                scaled * masks[h]
                + jnp.where(lane == W, upper, 0.0)
                + jnp.where(lane == W + 1, inner - upper, 0.0)
            ).astype(low)

    def pull(h, p):
        grad_p = dot(pair(S.a24.at[:, :, h * H : (h + 1) * H], p), S.vt[...])
        grad_s = (pair(S.e.at[h], p).astype(wide) * grad_p).astype(low)
        set_pair(S.pool, p, grad_s)
        dq = dot(grad_s, S.k[...]) * (masks[h] * HEAD_DIM**-0.5)
        if h > 0:
            dq += pair(S.gup.at[:, :, 0:H], p).astype(wide)
        S.gup[pl.ds(2 * p, 2), :, 0:H] = dq.astype(low).reshape(2, R, H)

    def weights(h):
        at = slice(h * HEAD_DIM, (h + 1) * HEAD_DIM)
        tile = h * HEAD_DIM // 128 * 128
        dqt = jnp.transpose(flat(S.gup.at[:, :, tile : tile + 128]))
        left = jnp.concatenate(
            [dqt[h * HEAD_DIM - tile : (h + 1) * HEAD_DIM - tile], S.qt[at, :], S.kt[at, : 4 * R]], 0
        )
        out = dot(left, flat(S.a1))
        S.gw2[h * W : (h + 1) * W, :] = out.astype(low)
        for c in range(3):
            product = out[c * HEAD_DIM : (c + 1) * HEAD_DIM] * S.wqkv[c, at, :].astype(wide)
            S.small[0:1, :] += jnp.sum(product, 0, keepdims=True)
        sum_over_dp(Quarters, S.gw2, S.sum2, S.whole2, h * W, W)

    for h in range(n.heads):
        for i in (0, 2):
            if (h, i) == (0, 2):
                sums.at("arriving")
            if h == 0:
                prepare(i, flipped(t, i // 2, 0))
                prepare(i + 1, flipped(t, i // 2, 1))
            if (h, i) == (0, 2):
                hl_in.start()
            pull(h, (chip + i // 2) % 2)
            sums.at(f"h{h}p{i}")
            if (h, i) == (1, 0):
                hl_in.wait_sib()
                hl_in.forward()
                ahead.send_cross()
            elif (h, i) == (1, 2):
                hl_in.wait_diag()
                S.gw2[3 * W :, :] = dot_columns(flat(S.mix), flat(S.hl4)).astype(low)
                sum_over_dp(Quarters, S.gw2, S.sum2, S.whole2, 3 * W, W)
        if h == 0:
            S.v[4 * R :, :] = jnp.zeros((K - 4 * R, H), low)
            S.kt[...] = jnp.transpose(S.v[...])
        at = slice(h * HEAD_DIM, (h + 1) * HEAD_DIM)
        S.qt[at, :] = dot(S.qt[at, :], flat(S.pool))[:, : 4 * R].astype(low)
        S.kt[at, : 4 * R] = dot(S.kt[at, : 4 * R], flat(S.e.at[h]))[:, : 4 * R].astype(low)
        if h + 1 < n.heads:
            weights(h)
        sums.at(f"h{h}")

    pad = jnp.zeros((R, H - W), low)
    for part, grad_t in ((1, S.qt), (2, S.kt)):
        rows = jnp.transpose(grad_t[:W, : 4 * R])
        for s in range(4):
            S.gup[s, :, part * H : part * H + W] = rows[s * R : (s + 1) * R]
            S.gup[s, :, part * H + W : (part + 1) * H] = pad

    back.finish()
    down = Reduce(links, S.part, S.pre1, S.near1, S.far1, t, split)

    def lead(s, start, size):
        rows = pl.ds(start, size)
        out = dot(S.gup[s, rows, 0:W], S.wqkv[0])
        out += dot(S.gup[s, rows, H : H + W], S.wqkv[1])
        out += dot(S.gup[s, rows, 2 * H : 2 * H + W], S.wqkv[2])
        S.part[s, rows] = out.astype(low)

    cross, diag, sib = peers
    lead(diag, *split[0])
    down.send_diag([0])
    lead(cross, *split[0])
    weights(n.heads - 1)
    down.send_cross([0])
    lead(diag, *split[1])
    down.send_diag([1])
    lead(cross, *split[1])
    down.send_cross([1])
    lead(sib, 0, R)
    down.send_sib()
    lead(t, 0, R)
    columns = jnp.sum(flat(S.gup).astype(wide), 0, keepdims=True)
    S.small[7:8, 0:H] = columns[:, 0:H]
    S.small[7:8, H : 2 * H] = columns[:, 2 * H :]
    upper = columns.astype(low)
    both = jnp.concatenate([upper.astype(wide), columns - upper.astype(wide)], 0).astype(low)
    for c in range(3):
        product = dot(both[:, c * H : c * H + W], S.wqkv[c])
        S.small[1:2, :] += jnp.sum(product, 0, keepdims=True)

    S.small4[t] = S.small[...]
    base3 = links.take(3)
    for j in range(3):
        peer = lax.rem(t + j + 1, 4)
        links.start(S.small4.at[t], S.small4.at[t], base3 + j, tensor=peer)
    sums.at("led")
    result = jnp.concatenate([ahead.result(0), ahead.result(1)], 0)
    S.output[...] = (S.hid[...] + (result[:own] + vector(S.db))).astype(low)
    sums.at("crossing")

    unit, inverse = standardize(S.x[...].astype(wide))
    grad = jnp.concatenate([down.result(0), down.result(1)], 0)[:own]
    for j in range(3):
        peer = lax.rem(t + 3 - j, 4)
        links.arrived(S.small4.at[peer], base3 + j, tensor=peer)
    over = S.small4[0] + S.small4[1] + S.small4[2] + S.small4[3]
    row = lax.broadcasted_iota(jnp.int32, over.shape, 0)
    near = min(8, n.dp)
    inner = Everyone(links, S.smalls, d % near, near, lambda j: d // near * near + j)
    inner.start(jnp.where(row < 6, over, S.small[...]))
    S.gt[...] += norm_back(grad, unit, inverse, vector(S.g1))
    sums.at("told")
    sums.finish()
    total = inner.result()
    inner.finish()
    if n.dp > near:
        outer = Everyone(links, S.smalls2, d // near, n.dp // near, lambda j: j * near + d % near)
        outer.start(total)
        total = outer.result()
        outer.finish()
    S.small_sum[...] = total
    S.small_sum[0:1, :] = (total[0:1, :] - vector(S.b1) * total[1:2, :]) / vector(S.g1)
    for j, s in enumerate(peers):
        links.copy(S.mix.at[s], S.mix4.at[t], mix_base + j, tensor=s).wait_send()
        for p in (0, 1):
            shared(s, p, j).wait_send()
    for transfer in (rows_in, cot_in, ow_in, hl_in, ahead, down):
        transfer.finish()
    links.finish()


LOADED = ("ow", "wqkv", "wup", "wdn")
SMALL = ("gain1", "shift1", "gain2", "shift2", "bias_out", "bias_down", "bias_up", "bias_qv")


def finish(n, output, gt, small, whole1, whole2):
    D, W, H = n.D, n.W, n.H
    steps = n.heads
    rows1 = D // steps

    def spread(output, gt, small, up, down, head, out, *refs):
        to_output, to_gt, to_up, to_down, to_qkv, to_out = refs[:6]
        vectors, sems = refs[6:14], refs[14]
        i = pl.program_id(0)
        held = refs[15:]
        come = [pltpu.make_async_copy(a, b, sems.at[j]) for j, (a, b) in enumerate(zip((output, gt), held))]
        go = [
            pltpu.make_async_copy(a, b, sems.at[2 + j])
            for j, (a, b) in enumerate(zip(held, (to_output, to_gt)))
        ]

        @pl.when(i == 0)
        def _():
            for copy in come:
                copy.start()
            for j in range(7):
                vectors[j][...] = small[j : j + 1, :].reshape(D)
            vectors[7][0:1, :] = small[7:8, :W]
            vectors[7][1:2, :] = small[7:8, H : H + W]

        to_up[...] = up[...].astype(wide)
        to_down[...] = down[...].astype(wide)
        for j in range(3):
            to_qkv[j] = head[j * HEAD_DIM : (j + 1) * HEAD_DIM, :].astype(wide)
        to_out[...] = out[...].astype(wide)

        @pl.when(i == 1)
        def _():
            for first, second in zip(come, go):
                first.wait()
                second.start()

        @pl.when(i == steps - 1)
        def _():
            for copy in go:
                copy.wait()

    hbm = pl.BlockSpec(memory_space=pl.ANY)
    whole = pl.BlockSpec(memory_space=pltpu.VMEM)
    at_row = lambda rows, index: pl.BlockSpec((rows, D), lambda i: (index(i), 0))
    shape = jax.ShapeDtypeStruct
    return pl.pallas_call(
        spread,
        grid=(steps,),
        out_shape=[shape(output.shape, low), shape(gt.shape, wide)]
        + [shape((D, D), wide)] * 2
        + [shape((3, W, D), wide), shape((W, D), wide)]
        + [shape((D,), wide)] * 7
        + [shape((2, W), wide)],
        in_specs=[hbm, hbm, whole, at_row(rows1, lambda i: i), at_row(rows1, lambda i: i + steps)]
        + [at_row(W, lambda i: i), at_row(HEAD_DIM, lambda i: 3 * steps + i)],
        out_specs=[hbm, hbm]
        + [at_row(rows1, lambda i: i)] * 2
        + [pl.BlockSpec((3, HEAD_DIM, D), lambda i: (0, i, 0)), at_row(HEAD_DIM, lambda i: i)]
        + [whole] * 8,
        scratch_shapes=[
            pltpu.SemaphoreType.DMA((4,)),
            pltpu.VMEM(output.shape, low),
            pltpu.VMEM(gt.shape, wide),
        ],
    )(output, gt, small, whole1, whole1, whole2, whole2)


def body(
    tokens,
    lengths,
    ln1_gain,
    ln1_shift,
    qkv_weight,
    qv_bias,
    out_weight,
    out_bias,
    ln2_gain,
    ln2_shift,
    up_weight,
    up_bias,
    down_weight,
    down_bias,
    cotangent,
):
    own, D = tokens.shape
    W = qkv_weight.shape[2]
    F = up_weight.shape[1]
    dp = lax.axis_size("dp")
    assert lax.axis_size("tensor") == 4 and lengths.shape[0] == 1 and F == D and 4 * W == D and 3 * round_up(W + 2, 128) == D
    R = round_up(own, 16)
    H = round_up(W + 2, 128)
    K = round_up(4 * R, 256)
    heads = W // HEAD_DIM
    extra = dp.bit_length() - 1 - 3
    n = types.SimpleNamespace(
        own=own, D=D, W=W, R=R, H=H, K=K, dp=dp, heads=heads, extra=extra
    )
    weights = dict(ow=out_weight, wqkv=jnp.transpose(qkv_weight, (1, 2, 0)), wup=up_weight, wdn=down_weight)
    given = dict(
        x=tokens, lengths=lengths, g1=ln1_gain, b1=ln1_shift,
        bq=qv_bias, ob=out_bias, g2=ln2_gain, b2=ln2_shift, bup=up_bias, db=down_bias,
        cot=cotangent,
    )
    given.update({name + "_far": weights[name] for name in LOADED})
    outs = dict(
        output=((own, D), low), gt=((own, D), wide), small_sum=((8, D), wide),
        whole1=((2 * D, D), low), whole2=((D, D), low),
    )
    rows4 = ((4, R, D), low)
    slab = ((R, D), low)
    chunks = [(Quarters, D // 2), (Halves, D // 2)] * 2 + [(Quarters, W)] * 4
    scratch = dict(
        a1=rows4, cot4=rows4, ow4=((4, W, D), low), q=((4, R, H), low), k=((K, H), low),
        v=((K, H), low), kt=((H, K), low), vt=((H, K), low), e=((heads, 4, R, K), low),
        o=((4, R, H), wide), inv=((4, R, 128), wide), mix=((4, R, W), low), mix4=((4, R, W), low),
        hid=((own, D), wide),
        a24=rows4, pool=((4, R, K), low), gup=rows4, part=rows4,
        fop=rows4, pre1=slab, near1=slab, far1=slab, pre2=slab, near2=slab, far2=slab,
        gw=((2 * D, D), low), gub=((1, D), wide),
        small=((8, D), wide), hl4=rows4,
        gm4=((4, R, W), low), qt=((H, 4 * R), low), do=((R, H), wide),
        gw2=((D, D), low),
        small4=((4, 8, D), wide), smalls=((min(8, dp), 8, D), wide),
        box=((sum(kind.sizes(r, D, dp)[1] for kind, r in chunks), D), low),
        sum1=((2 * D, D), low), sum2=((D, D), low),
    )
    scratch.update({name: (weights[name].shape, low) for name in LOADED})
    if dp > 8:
        scratch["smalls2"] = ((dp // 8, 8, D), wide)
    sems = 170 + dp + 8 * extra
    names = list(given) + list(outs) + list(scratch) + ["local", "send", "recv"]
    vmem = pl.BlockSpec(memory_space=pltpu.VMEM)
    smem = pl.BlockSpec(memory_space=pltpu.SMEM)
    hbm = pl.BlockSpec(memory_space=pl.ANY)
    output, gt, small, whole1, whole2 = pl.pallas_call(
        lambda *refs: kernel(n, types.SimpleNamespace(**dict(zip(names, refs)))),
        out_shape=tuple(jax.ShapeDtypeStruct(*spec) for spec in outs.values()),
        in_specs=[
            hbm if name.endswith("_far") else dict(lengths=smem, cot=hbm).get(name, vmem) for name in given
        ],
        out_specs=tuple(hbm if name in ("whole1", "whole2") else vmem for name in outs),
        scratch_shapes=[pltpu.VMEM(*spec) for spec in scratch.values()]
        + [pltpu.SemaphoreType.DMA((5,))] + [pltpu.SemaphoreType.DMA((sems,))] * 2,
        compiler_params=pltpu.CompilerParams(
            collective_id=0, has_side_effects=True, vmem_limit_bytes=VMEM_BYTES
        ),
    )(*given.values())
    finished = finish(n, output, gt, small, whole1, whole2)
    small_rows = dict(zip(SMALL, finished[6:]))
    return (
        finished[0],
        finished[1],
        small_rows["gain1"],
        small_rows["shift1"],
        jnp.transpose(finished[4], (2, 0, 1)),
        small_rows["bias_qv"],
        finished[5],
        small_rows["bias_out"],
        small_rows["gain2"],
        small_rows["shift2"],
        finished[2],
        small_rows["bias_up"],
        finished[3],
        small_rows["bias_down"],
    )


def solution(mesh):
    placed = (
        P(("dp", "tensor"), None),
        P("dp"),
        P(),
        P(),
        P(None, None, "tensor"),
        P(None, "tensor"),
        P("tensor", None),
        P(),
        P(),
        P(),
        P(None, "tensor"),
        P("tensor"),
        P("tensor", None),
        P(),
        P(("dp", "tensor"), None),
    )
    return jax.shard_map(
        body,
        mesh=mesh,
        in_specs=placed,
        out_specs=(
            P(("dp", "tensor"), None),
            P(("dp", "tensor"), None),
            P(),
            P(),
            P(None, None, "tensor"),
            P(None, "tensor"),
            P("tensor", None),
            P(),
            P(),
            P(),
            P(None, "tensor"),
            P("tensor"),
            P("tensor", None),
            P(),
        ),
        check_vma=False,
    )
```

```python
import types

import jax
import jax.numpy as jnp
from jax import lax
from jax.experimental import pallas as pl
from jax.experimental.pallas import tpu as pltpu
from jax.sharding import PartitionSpec as P

HEAD_DIM = 64
LOGICAL = pl.DeviceIdType.LOGICAL
VMEM_BYTES = 62 * 2**20

epsilon = 1e-06
low = jnp.bfloat16
wide = jnp.float32


def round_up(amount, unit):
    return -(-amount // unit) * unit


class Here:
    def __init__(self, dp, tensor):
        self.dp, self.tensor = dp, tensor
        self.d, self.t = lax.axis_index("dp"), lax.axis_index("tensor")
        self.me = self.d * tensor + self.t
        self.chip = lax.div(self.t, 2)
        self.core = self.t - 2 * self.chip
        self.bits, rest = [], self.d
        for _ in range(dp.bit_length() - 1):
            half = lax.div(rest, 2)
            self.bits.append(rest - 2 * half)
            rest = half
        low_bits = sum(bit * (1 << b) for b, bit in enumerate(self.bits[:3]))
        self.near, self.group = low_bits, self.d - low_bits

    def logical(self, dp=None, tensor=None):
        if dp is not None:
            return self.me + (dp - self.d) * self.tensor
        return self.me + (tensor - self.t)

    def bit_flipped(self, b):
        return self.d + (1 - 2 * self.bits[b]) * (1 << b)


def flipped(here, flip_chip, flip_core):
    chip = here.chip + flip_chip - 2 * here.chip * flip_chip
    return 2 * chip + here.core + flip_core - 2 * here.core * flip_core


def two_bits(i):
    high = jnp.where(i >= 2, 1, 0)
    return high, i - 2 * high


def dot(left, right):
    return jnp.dot(left, right, preferred_element_type=wide)


def dot_rows(left, right):
    return lax.dot_general(left, right, (((1,), (1,)), ((), ())), preferred_element_type=wide)


def dot_columns(left, right):
    return lax.dot_general(left, right, (((0,), (0,)), ((), ())), preferred_element_type=wide)


def standardize(values):
    center = values - jnp.mean(values, -1, keepdims=True)
    inverse = lax.rsqrt(jnp.mean(center * center, -1, keepdims=True) + epsilon)
    return center * inverse, inverse


def norm_back(grad, unit, inverse, gain):
    scaled = grad * gain
    return inverse * (
        scaled
        - jnp.mean(scaled, -1, keepdims=True)
        - unit * jnp.mean(scaled * unit, -1, keepdims=True)
    )


def pair(ref, p):
    _, rows, columns = ref.shape
    return ref[pl.ds(2 * p, 2)].reshape(2 * rows, columns)


def set_pair(ref, p, values):
    ref[pl.ds(2 * p, 2)] = values.reshape(2, -1, values.shape[1])


def flat(ref):
    a, b, c = ref.shape
    return ref[...].reshape(a * b, c)


class Links:
    def __init__(self, here, send, recv):
        self.here, self.send, self.recv, self.used, self.pending = here, send, recv, 0, []

    def take(self, amount=1):
        base = self.used
        self.used += amount
        assert self.used <= self.send.shape[0]
        return base

    def copy(self, src, dst, at, **where):
        return pltpu.make_async_remote_copy(
            src_ref=src,
            dst_ref=dst,
            send_sem=self.send.at[at],
            recv_sem=self.recv.at[at],
            device_id=self.here.logical(**where),
            device_id_type=LOGICAL,
        )

    def start(self, src, dst, at, **where):
        copy = self.copy(src, dst, at, **where)
        copy.start()
        self.pending.append(copy)

    def arrived(self, dst, at, **where):
        self.copy(dst, dst, at, **where).wait_recv()

    def finish(self):
        for copy in self.pending:
            copy.wait_send()
        self.pending = []


class Gather:
    def __init__(self, links, buf, here, parts):
        self.links, self.buf, self.t, self.parts = links, buf, here.t, parts
        self.cross, self.diag, self.sib = here.peers
        self.base = links.take(3 * len(parts))

    def view(self, slot, part):
        start, size = self.parts[part]
        return self.buf.at[slot, pl.ds(start, size)]

    def _each(self):
        return range(len(self.parts))

    def start(self, parts=None):
        parts = self._each() if parts is None else parts
        for p in parts:
            v = self.view(self.t, p)
            self.links.copy(v, v, self.base + 3 * p, tensor=self.cross).start()
        for p in parts:
            v = self.view(self.t, p)
            self.links.copy(v, v, self.base + 3 * p + 1, tensor=self.sib).start()

    def wait_sib(self):
        for p in self._each():
            self.links.arrived(self.view(self.sib, p), self.base + 3 * p + 1, tensor=self.sib)

    def forward(self, parts=None):
        for p in self._each() if parts is None else parts:
            v = self.view(self.cross, p)
            self.links.arrived(v, self.base + 3 * p, tensor=self.cross)
            self.links.copy(v, v, self.base + 3 * p + 2, tensor=self.sib).start()

    def wait_diag(self, parts=None):
        for p in self._each() if parts is None else parts:
            self.links.arrived(self.view(self.diag, p), self.base + 3 * p + 2, tensor=self.sib)

    def finish(self):
        for p in self._each():
            v = self.view(self.t, p)
            self.links.copy(v, v, self.base + 3 * p, tensor=self.cross).wait_send()
            self.links.copy(v, v, self.base + 3 * p + 1, tensor=self.sib).wait_send()
            v = self.view(self.cross, p)
            self.links.copy(v, v, self.base + 3 * p + 2, tensor=self.sib).wait_send()


class Reduce:
    def __init__(self, links, part, pre, near, far, here, parts):
        self.links, self.part, self.t, self.parts = links, part, here.t, parts
        self.pre, self.near, self.far = pre, near, far
        self.cross, self.diag, self.sib = here.peers
        self.base = links.take(3 * len(parts))

    def _copy(self, kind, p):
        slot, box, peer = (
            (self.diag, self.pre, self.sib),
            (self.sib, self.near, self.sib),
            (self.cross, self.far, self.cross),
        )[kind]
        rows = pl.ds(*self.parts[p])
        return self.links.copy(
            self.part.at[slot, rows], box.at[rows], self.base + 3 * p + kind, tensor=peer
        )

    def _each(self, parts):
        return range(len(self.parts)) if parts is None else parts

    def send_diag(self, parts=None):
        for p in self._each(parts):
            self._copy(0, p).start()

    def send_sib(self):
        for p in self._each(None):
            self._copy(1, p).start()

    def send_cross(self, parts=None):
        for p in self._each(parts):
            self._copy(0, p).wait_recv()
            rows = pl.ds(*self.parts[p])
            self.part[self.cross, rows] = (
                self.part[self.cross, rows].astype(wide) + self.pre[rows].astype(wide)
            ).astype(low)
            self._copy(2, p).start()

    def result(self, p):
        self._copy(1, p).wait_recv()
        self._copy(2, p).wait_recv()
        rows = pl.ds(*self.parts[p])
        return (
            self.part[self.t, rows].astype(wide)
            + self.near[rows].astype(wide)
            + self.far[rows].astype(wide)
        )

    def finish(self):
        for p in self._each(None):
            for kind in range(3):
                self._copy(kind, p).wait_send()


class DataReduce:
    def __init__(self, links, held, whole, out, box, box_at, first, rows):
        self.links, self.held, self.whole, self.out, self.here = links, held, whole, out, links.here
        count = self.here.dp
        bits = count.bit_length() - 1
        assert count == 1 << bits and bits >= 3
        self.extra = list(range(3, bits))
        self.region = (first, rows, 0, held.shape[1])
        self.trail, self.sent, self.boxes = [], [], []
        for tall, broad in self.sizes(rows, held.shape[1], count)[0]:
            self.boxes.append(box.at[pl.ds(box_at, tall), pl.ds(0, broad)])
            box_at += tall
        self.base = links.take(9 + len(self.extra))
        self.plan()

    @classmethod
    def sizes(cls, rows, columns, count):
        found = cls.boxes_of(rows, columns)
        found += found[-1:] * (count.bit_length() - 1 - 3)
        return found, sum(size[0] for size in found)

    def _bit(self, b):
        return self.here.bits[b]

    def _peer(self, b):
        return self.here.bit_flipped(b)

    def _send(self, src, dst, at, peer):
        copy = self.links.copy(src, dst, self.base + at, dp=peer)
        copy.start()
        self.sent.append(copy)

    def _wait(self, dst, at, peer):
        self.links.arrived(dst, self.base + at, dp=peer)

    @staticmethod
    def _view(ref, region):
        row, rows, column, columns = region
        if columns == ref.shape[1]:
            return ref.at[pl.ds(row, rows)]
        return ref.at[pl.ds(row, rows), pl.ds(column, columns)]

    @staticmethod
    def _part(region, bit):
        row, rows, column, columns = region
        if rows % 32 == 0:
            return (pl.multiple_of(row + bit * (rows // 2), 16), rows // 2, column, columns)
        return (row, rows, pl.multiple_of(column + bit * (columns // 2), 128), columns // 2)

    def _give_half(self, b, box, at):
        bit = self._bit(b)
        self.trail.append(self.region)
        self._send(self._view(self.held, self._part(self.region, 1 - bit)), self.boxes[box], at, self._peer(b))
        self.region = self._part(self.region, bit)

    def _add(self, boxes, last):
        view = self._view(self.held, self.region)
        total = view[...].astype(wide)
        for box in boxes:
            total += self.boxes[box][...].astype(wide)
        if last:
            view = self._view(self.whole, self.region)
        view[...] = total.astype(low)
        if last:
            self._swap()

    def _swap(self):
        view = self._view(self.whole, self.region)
        for k, b in enumerate(self.extra):
            box, at = self.boxes[k - len(self.extra)], 9 + k
            copy = self.links.copy(view, box, self.base + at, dp=self._peer(b))
            copy.start()
            self._wait(box, at, self._peer(b))
            copy.wait_send()
            view[...] = (view[...].astype(wide) + box[...].astype(wide)).astype(low)

    def _give_whole(self, b, at):
        view = self._view(self.whole, self.region)
        self._send(view, view, at, self._peer(b))

    def _take_half(self, b, at):
        outer = self.trail.pop()
        view = self._view(self.whole, self._part(outer, 1 - self._bit(b)))
        self._wait(view, at, self._peer(b))
        self.region = outer

    def _leave(self):
        rows = pl.ds(self.region[0], self.region[1])
        self.left = pltpu.make_async_copy(
            self.whole.at[rows], self.out.at[rows], self.links.send.at[self.base + 8]
        )
        self.left.start()

    def step(self):
        if self.steps:
            self.steps.pop(0)()

    def finish(self):
        assert not self.steps
        self.left.wait()
        for copy in self.sent:
            copy.wait_send()


class Halves(DataReduce):
    order = (1, 0, 2)

    @staticmethod
    def boxes_of(rows, columns):
        found = []
        for _ in range(3):
            if rows % 32 == 0:
                rows //= 2
            else:
                columns //= 2
            found.append((rows, columns))
        return found

    def plan(self):
        low_bit, x, high = self.order
        self.steps = [
            lambda: self._give_half(low_bit, 0, 0),
            lambda: (self._wait_box(low_bit, 0), self._add((0,), False), self._give_half(x, 1, 1)),
            lambda: (self._wait_box(x, 1), self._add((1,), False), self._give_half(high, 2, 2)),
            lambda: (self._wait_box(high, 2), self._add((2,), True), self._give_whole(high, 3)),
            lambda: (self._take_half(high, 3), self._give_whole(x, 4)),
            lambda: (self._take_half(x, 4), self._give_whole(low_bit, 5)),
            lambda: (self._take_half(low_bit, 5), self._leave()),
        ]

    def _wait_box(self, b, box):
        self._wait(self.boxes[box], box, self._peer(b))


class Quarters(DataReduce):
    @staticmethod
    def boxes_of(rows, columns):
        tall, broad = rows // 8, columns
        if tall % 16:
            tall, broad = rows // 4, columns // 2
        return [(rows // 2, columns)] + [(tall, broad)] * 3

    def plan(self):
        self.steps = [
            lambda: self._give_half(0, 0, 0),
            lambda: (self._wait(self.boxes[0], 0, self._peer(0)), self._add((0,), False), self._give_quarters()),
            lambda: (self._take_boxes(), self._add((1, 2, 3), True), self._give_quarter()),
            lambda: (self._take_quarters(), self._give_whole(0, 7)),
            lambda: (self._take_half(0, 7), self._leave()),
        ]

    def _z(self, j):
        low_bit = 1 - self._bit(1) if j % 2 else self._bit(1)
        high = 1 - self._bit(2) if j // 2 else self._bit(2)
        return low_bit, high, self.here.group + high * 4 + low_bit * 2 + self._bit(0)

    def _quarter(self, j):
        low_bit, high, peer = self._z(j)
        return self._part(self._part(self.trail[-1], high), low_bit), peer

    def _give_quarters(self):
        self.trail.append(self.region)
        for j in (1, 2, 3):
            part, peer = self._quarter(j)
            self._send(self._view(self.held, part), self.boxes[j], j, peer)
        self.region = self._quarter(0)[0]

    def _take_boxes(self):
        for j in (1, 2, 3):
            self._wait(self.boxes[j], j, self._z(j)[2])

    def _give_quarter(self):
        view = self._view(self.whole, self.region)
        for j in (1, 2, 3):
            self._send(view, view, 3 + j, self._z(j)[2])

    def _take_quarters(self):
        for j in (1, 2, 3):
            part, peer = self._quarter(j)
            self._wait(self._view(self.whole, part), 3 + j, peer)
        self.region = self.trail.pop()


class Pipeline:
    def __init__(self, plan):
        self.plan, self.members = plan, []

    def add(self, member):
        self.members.append(member)
        member.step()

    def at(self, place):
        for number in self.plan[place]:
            self.members[number].step()

    def finish(self):
        self.at("end")
        for m in self.members:
            while m.steps:
                m.step()
            m.finish()


PLAN = dict(
    waiting=(),
    shared=(0, 1),
    arriving=(),
    h0p0=(3,),
    h0p2=(2, 1),
    h0=(),
    h1p0=(2, 1, 0, 4),
    h1p2=(2,),
    h1=(1, 3),
    h2p0=(5, 0),
    h2p2=(4, 6),
    h2=(1, 2),
    led=(5, 3, 7, 1, 2),
    crossing=(0, 4, 6, 5),
    told=(7, 2, 6, 5),
    end=(4, 7, 3, 6, 7),
)


class Everyone:
    def __init__(self, links, buf, me, count, device):
        self.links, self.buf, self.me, self.count, self.device = links, buf, me, count, device
        self.base = links.take(count)

    def _copy(self, j):
        slot = self.buf.at[self.me]
        peer = self.me + j
        peer = self.device(jnp.where(peer >= self.count, peer - self.count, peer))
        return self.links.copy(slot, slot, self.base + j, dp=peer)

    def _loop(self, act):
        def one(j, carry):
            act(j)
            return carry

        lax.fori_loop(1, self.count, one, 0)

    def start(self, values):
        self.buf[self.me] = values
        self._loop(lambda j: self._copy(j).start())

    def _hear(self, j):
        peer = self.me - j
        peer = jnp.where(peer < 0, peer + self.count, peer)
        self.links.arrived(self.buf.at[peer], self.base + j, dp=self.device(peer))

    def result(self):
        self._loop(self._hear)
        return lax.fori_loop(1, self.count, lambda j, acc: acc + self.buf[j], self.buf[0])

    def finish(self):
        self._loop(lambda j: self._copy(j).wait_send())


def greet(here):
    barrier = pltpu.get_barrier_semaphore()
    for axis, me, count in (("tensor", here.t, here.tensor), ("dp", here.d, here.dp)):

        def one(j, carry, axis=axis, me=me, count=count):
            peer = me + j
            peer = here.logical(**{axis: jnp.where(peer >= count, peer - count, peer)})
            pl.semaphore_signal(barrier, inc=1, device_id=peer, device_id_type=LOGICAL)
            return carry

        lax.fori_loop(1, count, one, 0)


def await_greetings(amount):
    pl.semaphore_wait(pltpu.get_barrier_semaphore(), amount)


def halves(rows):
    first = round_up(rows // 2, 16)
    return ((0, first), (first, rows - first))


def head_masks(shape, local_heads):
    lane = lax.broadcasted_iota(jnp.int32, shape, 1)
    return [
        jnp.where((lane >= h * HEAD_DIM) & (lane < (h + 1) * HEAD_DIM), 1.0, 0.0)
        for h in range(local_heads)
    ], lane


def kernel(n, S):
    here = Here(n.dp, 4)
    t, d = here.t, here.d
    here.peers = peers = [flipped(here, 1, 0), flipped(here, 1, 1), flipped(here, 0, 1)]
    links = Links(here, S.send, S.recv)
    greet(here)
    R, own, W, H, D, K = n.R, n.own, n.W, n.H, n.D, n.K
    split = halves(R)
    vector = lambda ref: ref[...].reshape(1, D)

    fetch = pltpu.make_async_copy(S.cot, S.gt, S.local.at[0])
    load = [
        pltpu.make_async_copy(getattr(S, name + "_far"), getattr(S, name), S.local.at[1 + j])
        for j, name in enumerate(LOADED)
    ]
    fetch.start()
    for copy in load:
        copy.start()
    S.a1[t] = jnp.zeros((R, D), low)
    S.cot4[t] = jnp.zeros((R, D), low)
    S.a24[t] = jnp.zeros((R, D), low)
    S.hl4[t] = jnp.zeros((R, D), low)
    rows_in = Gather(links, S.a1, here, split)
    cot_in = Gather(links, S.cot4, here, split)
    ow_in = Gather(links, S.ow4, here, ((0, W),))
    for p, (start, size) in enumerate(split):
        rows = pl.ds(start, min(size, own - start))
        unit, _ = standardize(S.x[rows, :].astype(wide))
        S.a1[t, rows, :] = (unit * vector(S.g1) + vector(S.b1)).astype(low)
        if p == 0:
            await_greetings(3 + n.dp - 1)
        rows_in.start([p])
    load[0].wait()
    S.ow4[t] = S.ow[...]
    ow_in.start()
    fetch.wait()
    S.cot4[t, 0:own, :] = S.gt[...].astype(low)
    cot_in.start([0])
    load[2].wait()
    load[3].wait()
    S.gw[0:D, :] = jnp.transpose(S.wup[...])
    S.gw[D:, :] = jnp.transpose(S.wdn[...])
    load[1].wait()
    S.v[4 * R :, :] = jnp.zeros((K - 4 * R, H), low)
    length = S.lengths[0]

    chip = here.chip

    def project(i, carry):
        s = flipped(here, *two_bits(i))

        @pl.when(i == 1)
        def _():
            rows_in.wait_sib()

        @pl.when(i == 2)
        def _():
            rows_in.forward()

        @pl.when(i == 3)
        def _():
            rows_in.wait_diag()

        slab = S.a1[s]
        lane = lax.broadcasted_iota(jnp.int32, (R, H - W), 1)
        row = lax.broadcasted_iota(jnp.int32, (R, H - W), 0)
        absent = (row >= own) | (row + s * own >= length)
        at = pl.ds(pl.multiple_of(s * R, 16), R)
        out = dot_rows(slab, S.wqkv[0]) + S.bq[0:1, :]
        S.q[s, :, :W] = (out.astype(low).astype(wide) * HEAD_DIM**-0.5).astype(low)
        S.q[s, :, W:] = jnp.where(lane == 0, HEAD_DIM**-0.5, 0.0).astype(low)
        S.k[at, :W] = dot_rows(slab, S.wqkv[1]).astype(low)
        S.k[at, W:] = jnp.where((lane == 0) & absent, -8e30, 0.0).astype(low)
        S.v[at, :W] = (dot_rows(slab, S.wqkv[2]) + S.bq[1:2, :]).astype(low)
        S.v[at, W:] = jnp.where(lane < 2, 1.0, 0.0).astype(low)
        return carry

    lax.fori_loop(0, 4, project, 0)
    if K > 4 * R:
        lane = lax.broadcasted_iota(jnp.int32, (K - 4 * R, H), 1)
        S.k[4 * R :, :] = jnp.where(lane == W, -8e30, 0.0).astype(low)
    S.kt[...] = jnp.transpose(S.k[...])
    S.vt[...] = jnp.transpose(S.v[...])

    masks, lane = head_masks((1, H), n.heads)
    mix_base = links.take(3)


    def attend(i, carry):
        high, low_bit = two_bits(i)
        s = flipped(here, 1 - high, low_bit + high - 2 * low_bit * high)
        query = S.q[s]
        mixed = jnp.zeros((R, H), wide)
        inverse = jnp.zeros((R, 128), wide)
        first = lax.broadcasted_iota(jnp.int32, (1, 128), 1)

        def score(h):
            here = jnp.where(lane == W, 1.0, masks[h]).astype(low)
            return dot(query * here, S.kt[...])

        ready = score(0)
        for h in range(n.heads):
            scores = ready
            if h + 1 < n.heads:
                ready = score(h + 1)
            terms = jnp.exp(scores - jnp.max(scores, -1, keepdims=True)).astype(low)
            S.e[h, s] = terms
            part = dot(terms, S.v[...])
            scale = 1.0 / part[:, W : W + 1]
            mixed += part * (scale * masks[h])
            inverse = jnp.where(first == h, scale, inverse)
        S.o[s] = mixed
        S.inv[s] = inverse
        S.mix[s] = mixed[:, :W].astype(low)

        @pl.when(i < 3)
        def _():
            links.copy(S.mix.at[s], S.mix4.at[t], mix_base + i, tensor=s).start()

        @pl.when(i == 1)
        def _():
            cot_in.start([1])

        @pl.when(i == 2)
        def _():
            ow_in.wait_sib()
            ow_in.forward()

        return carry

    lax.fori_loop(0, 4, attend, 0)
    ow_in.wait_diag()
    S.mix4[t] = S.mix[t]
    for j, s in enumerate(peers):
        links.arrived(S.mix4.at[s], mix_base + j, tensor=s)

    total = dot(S.mix4[0], S.ow4[0])
    for j in range(1, 4):
        total += dot(S.mix4[j], S.ow4[j])
    total = S.x[...].astype(wide) + (total[:own] + vector(S.ob))
    S.hid[...] = total
    unit, _ = standardize(total)
    S.a24[t, 0:own, :] = (unit * vector(S.g2) + vector(S.b2)).astype(low)
    next_in = Gather(links, S.a24, here, halves(R))
    next_in.start()
    back = Reduce(links, S.part, S.pre1, S.near1, S.far1, here, split)
    ahead = Reduce(links, S.fop, S.pre2, S.near2, S.far2, here, split)
    S.gub[...] = jnp.zeros_like(S.gub)

    def feed(s, start, size):
        rows = pl.ds(start, size)
        up = dot(S.a24[s, rows], S.wup[...]) + vector(S.bup)
        square = up * up
        c = 0.7978845608028654
        bend = jnp.tanh(c * up * (1.0 + 0.044715 * square))
        half = 0.5 * (1.0 + bend)
        slope = half + 0.5 * up * (1.0 - bend * bend) * (c + (3 * 0.044715 * c) * square)
        active = (up * half).astype(low)
        S.pool[s, rows, 0:D] = active
        grad = (dot(S.cot4[s, rows], S.gw[D:, :]) * slope).astype(low)
        S.gup[s, rows] = grad
        S.part[s, rows] = dot(grad, S.gw[0:D, :]).astype(low)
        S.gub[...] += jnp.sum(grad.astype(wide), 0, keepdims=True)

    def lead_out(s, start, size):
        rows = pl.ds(start, size)
        S.fop[s, rows] = dot(S.pool[s, rows, 0:D], S.wdn[...]).astype(low)

    def feed_here(i, carry):
        s = flipped(here, 0, i)

        @pl.when(i == 1)
        def _():
            next_in.wait_sib()
            cot_in.wait_sib()

        feed(s, 0, R)

        @pl.when(i == 1)
        def _():
            back.send_sib()

        lead_out(s, 0, R)
        return carry

    lax.fori_loop(0, 2, feed_here, 0)
    ahead.send_sib()
    for p in (0, 1):

        def feed_there(i, carry, p=p):
            @pl.when(i == 0)
            def _():
                cot_in.forward([p])
                next_in.forward([p])

            @pl.when(i == 1)
            def _():
                cot_in.wait_diag([p])
                next_in.wait_diag([p])

            feed(flipped(here, 1, i), *split[p])
            if p == 1:

                @pl.when(i == 0)
                def _():
                    back.send_cross([0])

            return carry

        lax.fori_loop(0, 2, feed_there, 0)
        back.send_diag([p])
    for i in (0, 1):
        lead_out(flipped(here, 1, i), 0, R)
    back.send_cross([1])
    ahead.send_diag()

    sums = Pipeline(PLAN)
    tile = D // 2
    box_at = 0

    def sum_over_dp(kind, held, whole, out, first, rows):
        nonlocal box_at
        sums.add(kind(links, held, whole, out, S.box, box_at, first, rows))
        box_at += kind.sizes(rows, D, n.dp)[1]

    for left, right, first in ((S.a24, S.gup, 0), (S.pool, S.cot4, D)):
        rows = left[:, :, 0:D].reshape(4 * R, D)
        S.gw[first : first + D, :] = dot_columns(rows, flat(right)).astype(low)
        for at in (first, first + tile):
            kind = Quarters if at in (0, D + tile) else Halves
            sum_over_dp(kind, S.gw, S.sum1, S.whole1, at, tile)

    sums.at("waiting")
    S.small[...] = jnp.zeros_like(S.small)
    gm_base = links.take(6)
    shared = lambda s, p, j: links.copy(
        S.mix4.at[s, pl.ds(*split[p])], S.gm4.at[t, pl.ds(*split[p])], gm_base + 3 * p + j, tensor=peers[j]
    )
    for p, (start, size) in enumerate(split):
        real = min(size, own - start)
        rows = pl.ds(start, real)
        grad = back.result(p)[:real]
        unit, inverse = standardize(S.hid[rows])
        S.small[2:3, :] += jnp.sum(grad * unit, 0, keepdims=True)
        S.small[3:4, :] += jnp.sum(grad, 0, keepdims=True)
        S.gt[rows] += norm_back(grad, unit, inverse, vector(S.g2))
        S.hl4[t, rows] = S.gt[rows].astype(low)
        rows = pl.ds(start, size)
        for j, s in enumerate(peers + [t]):
            product = dot_rows(S.hl4[t, rows], S.ow4[s]).astype(low)
            if j < 3:
                S.mix4[s, rows] = product
                shared(s, p, j).start()
            else:
                S.gm4[t, rows] = product
    S.small[4:5, :] = jnp.sum(S.hl4[t].astype(wide), 0, keepdims=True)
    S.small[5:6, :] = jnp.sum(S.cot4[t].astype(wide), 0, keepdims=True)
    S.small[6:7, :] = S.gub[...]
    hl_in = Gather(links, S.hl4, here, halves(R))

    next_in.finish()
    S.do[...] = jnp.zeros_like(S.do)
    S.qt[...] = jnp.transpose(flat(S.q))
    sums.at("shared")

    def prepare(i, s):
        if i > 0:
            j = (None, 2, 0, 1)[i]
            for p in (0, 1):
                rows = pl.ds(*split[p])
                links.arrived(S.gm4.at[s, rows], gm_base + 3 * p + j, tensor=peers[j])
        S.do[:, :W] = S.gm4[s].astype(wide)
        inverse = sum(S.inv[s, :, h : h + 1] * masks[h] for h in range(n.heads))
        scaled = (S.do[...] * inverse).astype(low)
        S.v[pl.ds(pl.multiple_of(s * R, 16), R), :] = scaled
        scaled = scaled.astype(wide)
        product = scaled * S.o[s]
        for h in range(n.heads):
            inner = -jnp.sum(product * masks[h], -1, keepdims=True)
            upper = inner.astype(low).astype(wide)
            S.a24[s, :, h * H : (h + 1) * H] = (
                scaled * masks[h]
                + jnp.where(lane == W, upper, 0.0)
                + jnp.where(lane == W + 1, inner - upper, 0.0)
            ).astype(low)

    def pull(h, p):
        grad_p = dot(pair(S.a24.at[:, :, h * H : (h + 1) * H], p), S.vt[...])
        grad_s = (pair(S.e.at[h], p).astype(wide) * grad_p).astype(low)
        set_pair(S.pool, p, grad_s)
        dq = dot(grad_s, S.k[...]) * (masks[h] * HEAD_DIM**-0.5)
        if h > 0:
            dq += pair(S.gup.at[:, :, 0:H], p).astype(wide)
        S.gup[pl.ds(2 * p, 2), :, 0:H] = dq.astype(low).reshape(2, R, H)

    def weights(h):
        at = slice(h * HEAD_DIM, (h + 1) * HEAD_DIM)
        tile = h * HEAD_DIM // 128 * 128
        dqt = jnp.transpose(flat(S.gup.at[:, :, tile : tile + 128]))
        left = jnp.concatenate(
            [dqt[h * HEAD_DIM - tile : (h + 1) * HEAD_DIM - tile], S.qt[at, :], S.kt[at, : 4 * R]], 0
        )
        out = dot(left, flat(S.a1))
        S.gw2[h * W : (h + 1) * W, :] = out.astype(low)
        for c in range(3):
            product = out[c * HEAD_DIM : (c + 1) * HEAD_DIM] * S.wqkv[c, at, :].astype(wide)
            S.small[0:1, :] += jnp.sum(product, 0, keepdims=True)
        sum_over_dp(Quarters, S.gw2, S.sum2, S.whole2, h * W, W)

    for h in range(n.heads):
        for i in (0, 2):
            if (h, i) == (0, 2):
                sums.at("arriving")
            if h == 0:
                prepare(i, flipped(here, i // 2, 0))
                prepare(i + 1, flipped(here, i // 2, 1))
            if (h, i) == (0, 2):
                hl_in.start()
            pull(h, chip if i == 0 else 1 - chip)
            sums.at(f"h{h}p{i}")
            if (h, i) == (1, 0):
                hl_in.wait_sib()
                hl_in.forward()
                ahead.send_cross()
            elif (h, i) == (1, 2):
                hl_in.wait_diag()
                S.gw2[3 * W :, :] = dot_columns(flat(S.mix), flat(S.hl4)).astype(low)
                sum_over_dp(Quarters, S.gw2, S.sum2, S.whole2, 3 * W, W)
        if h == 0:
            S.v[4 * R :, :] = jnp.zeros((K - 4 * R, H), low)
            S.kt[...] = jnp.transpose(S.v[...])
        at = slice(h * HEAD_DIM, (h + 1) * HEAD_DIM)
        S.qt[at, :] = dot(S.qt[at, :], flat(S.pool))[:, : 4 * R].astype(low)
        S.kt[at, : 4 * R] = dot(S.kt[at, : 4 * R], flat(S.e.at[h]))[:, : 4 * R].astype(low)
        if h + 1 < n.heads:
            weights(h)
        sums.at(f"h{h}")

    pad = jnp.zeros((R, H - W), low)
    for part, grad_t in ((1, S.qt), (2, S.kt)):
        rows = jnp.transpose(grad_t[:W, : 4 * R])
        for s in range(4):
            S.gup[s, :, part * H : part * H + W] = rows[s * R : (s + 1) * R]
            S.gup[s, :, part * H + W : (part + 1) * H] = pad

    back.finish()
    down = Reduce(links, S.part, S.pre1, S.near1, S.far1, here, split)

    def lead(s, start, size):
        rows = pl.ds(start, size)
        out = dot(S.gup[s, rows, 0:W], S.wqkv[0])
        out += dot(S.gup[s, rows, H : H + W], S.wqkv[1])
        out += dot(S.gup[s, rows, 2 * H : 2 * H + W], S.wqkv[2])
        S.part[s, rows] = out.astype(low)

    cross, diag, sib = peers
    lead(diag, *split[0])
    down.send_diag([0])
    lead(cross, *split[0])
    weights(n.heads - 1)
    down.send_cross([0])
    lead(diag, *split[1])
    down.send_diag([1])
    lead(cross, *split[1])
    down.send_cross([1])
    lead(sib, 0, R)
    down.send_sib()
    lead(t, 0, R)
    columns = jnp.sum(flat(S.gup).astype(wide), 0, keepdims=True)
    S.small[7:8, 0:H] = columns[:, 0:H]
    S.small[7:8, H : 2 * H] = columns[:, 2 * H :]
    upper = columns.astype(low)
    both = jnp.concatenate([upper.astype(wide), columns - upper.astype(wide)], 0).astype(low)
    for c in range(3):
        product = dot(both[:, c * H : c * H + W], S.wqkv[c])
        S.small[1:2, :] += jnp.sum(product, 0, keepdims=True)

    S.small4[t] = S.small[...]
    base3 = links.take(3)
    for j in range(3):
        links.start(S.small4.at[t], S.small4.at[t], base3 + j, tensor=peers[j])
    sums.at("led")
    result = jnp.concatenate([ahead.result(0), ahead.result(1)], 0)
    S.output[...] = (S.hid[...] + (result[:own] + vector(S.db))).astype(low)
    sums.at("crossing")

    unit, inverse = standardize(S.x[...].astype(wide))
    grad = jnp.concatenate([down.result(0), down.result(1)], 0)[:own]
    for j in range(3):
        links.arrived(S.small4.at[peers[j]], base3 + j, tensor=peers[j])
    over = S.small4[0] + S.small4[1] + S.small4[2] + S.small4[3]
    row = lax.broadcasted_iota(jnp.int32, over.shape, 0)
    near = min(8, n.dp)
    inner = Everyone(links, S.smalls, here.near, near, lambda j: here.group + j)
    inner.start(jnp.where(row < 6, over, S.small[...]))
    S.gt[...] += norm_back(grad, unit, inverse, vector(S.g1))
    sums.at("told")
    sums.finish()
    total = inner.result()
    inner.finish()
    if n.dp > near:
        outer = Everyone(links, S.smalls2, lax.div(here.group, near), n.dp // near, lambda j: j * near + here.near)
        outer.start(total)
        total = outer.result()
        outer.finish()
    S.small_sum[...] = total
    S.small_sum[0:1, :] = (total[0:1, :] - vector(S.b1) * total[1:2, :]) / vector(S.g1)
    for j, s in enumerate(peers):
        links.copy(S.mix.at[s], S.mix4.at[t], mix_base + j, tensor=s).wait_send()
        for p in (0, 1):
            shared(s, p, j).wait_send()
    for transfer in (rows_in, cot_in, ow_in, hl_in, ahead, down):
        transfer.finish()
    links.finish()


LOADED = ("ow", "wqkv", "wup", "wdn")
SMALL = ("gain1", "shift1", "gain2", "shift2", "bias_out", "bias_down", "bias_up", "bias_qv")


def finish(n, output, gt, small, whole1, whole2):
    D, W, H = n.D, n.W, n.H
    steps = n.heads
    rows1 = D // steps

    def spread(output, gt, small, up, down, head, out, *refs):
        to_output, to_gt, to_up, to_down, to_qkv, to_out = refs[:6]
        vectors, sems = refs[6:14], refs[14]
        i = pl.program_id(0)
        held = refs[15:]
        come = [pltpu.make_async_copy(a, b, sems.at[j]) for j, (a, b) in enumerate(zip((output, gt), held))]
        go = [
            pltpu.make_async_copy(a, b, sems.at[2 + j])
            for j, (a, b) in enumerate(zip(held, (to_output, to_gt)))
        ]

        @pl.when(i == 0)
        def _():
            for copy in come:
                copy.start()
            for j in range(7):
                vectors[j][...] = small[j : j + 1, :].reshape(D)
            vectors[7][0:1, :] = small[7:8, :W]
            vectors[7][1:2, :] = small[7:8, H : H + W]

        to_up[...] = up[...].astype(wide)
        to_down[...] = down[...].astype(wide)
        for j in range(3):
            to_qkv[j] = head[j * HEAD_DIM : (j + 1) * HEAD_DIM, :].astype(wide)
        to_out[...] = out[...].astype(wide)

        @pl.when(i == 1)
        def _():
            for first, second in zip(come, go):
                first.wait()
                second.start()

        @pl.when(i == steps - 1)
        def _():
            for copy in go:
                copy.wait()

    hbm = pl.BlockSpec(memory_space=pl.ANY)
    whole = pl.BlockSpec(memory_space=pltpu.VMEM)
    at_row = lambda rows, index: pl.BlockSpec((rows, D), lambda i: (index(i), 0))
    shape = jax.ShapeDtypeStruct
    return pl.pallas_call(
        spread,
        grid=(steps,),
        out_shape=[shape(output.shape, low), shape(gt.shape, wide)]
        + [shape((D, D), wide)] * 2
        + [shape((3, W, D), wide), shape((W, D), wide)]
        + [shape((D,), wide)] * 7
        + [shape((2, W), wide)],
        in_specs=[hbm, hbm, whole, at_row(rows1, lambda i: i), at_row(rows1, lambda i: i + steps)]
        + [at_row(W, lambda i: i), at_row(HEAD_DIM, lambda i: 3 * steps + i)],
        out_specs=[hbm, hbm]
        + [at_row(rows1, lambda i: i)] * 2
        + [pl.BlockSpec((3, HEAD_DIM, D), lambda i: (0, i, 0)), at_row(HEAD_DIM, lambda i: i)]
        + [whole] * 8,
        scratch_shapes=[
            pltpu.SemaphoreType.DMA((4,)),
            pltpu.VMEM(output.shape, low),
            pltpu.VMEM(gt.shape, wide),
        ],
    )(output, gt, small, whole1, whole1, whole2, whole2)


def body(
    tokens,
    lengths,
    ln1_gain,
    ln1_shift,
    qkv_weight,
    qv_bias,
    out_weight,
    out_bias,
    ln2_gain,
    ln2_shift,
    up_weight,
    up_bias,
    down_weight,
    down_bias,
    cotangent,
):
    own, D = tokens.shape
    W = qkv_weight.shape[2]
    F = up_weight.shape[1]
    dp = lax.axis_size("dp")
    assert lax.axis_size("tensor") == 4 and lengths.shape[0] == 1 and F == D and 4 * W == D and 3 * round_up(W + 2, 128) == D
    R = round_up(own, 16)
    H = round_up(W + 2, 128)
    K = round_up(4 * R, 256)
    heads = W // HEAD_DIM
    extra = dp.bit_length() - 1 - 3
    n = types.SimpleNamespace(
        own=own, D=D, W=W, R=R, H=H, K=K, dp=dp, heads=heads, extra=extra
    )
    weights = dict(ow=out_weight, wqkv=jnp.transpose(qkv_weight, (1, 2, 0)), wup=up_weight, wdn=down_weight)
    given = dict(
        x=tokens, lengths=lengths, g1=ln1_gain, b1=ln1_shift,
        bq=qv_bias, ob=out_bias, g2=ln2_gain, b2=ln2_shift, bup=up_bias, db=down_bias,
        cot=cotangent,
    )
    given.update({name + "_far": weights[name] for name in LOADED})
    outs = dict(
        output=((own, D), low), gt=((own, D), wide), small_sum=((8, D), wide),
        whole1=((2 * D, D), low), whole2=((D, D), low),
    )
    rows4 = ((4, R, D), low)
    slab = ((R, D), low)
    chunks = [(Quarters, D // 2), (Halves, D // 2)] * 2 + [(Quarters, W)] * 4
    scratch = dict(
        a1=rows4, cot4=rows4, ow4=((4, W, D), low), q=((4, R, H), low), k=((K, H), low),
        v=((K, H), low), kt=((H, K), low), vt=((H, K), low), e=((heads, 4, R, K), low),
        o=((4, R, H), wide), inv=((4, R, 128), wide), mix=((4, R, W), low), mix4=((4, R, W), low),
        hid=((own, D), wide),
        a24=rows4, pool=((4, R, K), low), gup=rows4, part=rows4,
        fop=rows4, pre1=slab, near1=slab, far1=slab, pre2=slab, near2=slab, far2=slab,
        gw=((2 * D, D), low), gub=((1, D), wide),
        small=((8, D), wide), hl4=rows4,
        gm4=((4, R, W), low), qt=((H, 4 * R), low), do=((R, H), wide),
        gw2=((D, D), low),
        small4=((4, 8, D), wide), smalls=((min(8, dp), 8, D), wide),
        box=((sum(kind.sizes(r, D, dp)[1] for kind, r in chunks), D), low),
        sum1=((2 * D, D), low), sum2=((D, D), low),
    )
    scratch.update({name: (weights[name].shape, low) for name in LOADED})
    if dp > 8:
        scratch["smalls2"] = ((dp // 8, 8, D), wide)
    sems = 170 + dp + 8 * extra
    names = list(given) + list(outs) + list(scratch) + ["local", "send", "recv"]
    vmem = pl.BlockSpec(memory_space=pltpu.VMEM)
    smem = pl.BlockSpec(memory_space=pltpu.SMEM)
    hbm = pl.BlockSpec(memory_space=pl.ANY)
    output, gt, small, whole1, whole2 = pl.pallas_call(
        lambda *refs: kernel(n, types.SimpleNamespace(**dict(zip(names, refs)))),
        out_shape=tuple(jax.ShapeDtypeStruct(*spec) for spec in outs.values()),
        in_specs=[
            hbm if name.endswith("_far") else dict(lengths=smem, cot=hbm).get(name, vmem) for name in given
        ],
        out_specs=tuple(hbm if name in ("whole1", "whole2") else vmem for name in outs),
        scratch_shapes=[pltpu.VMEM(*spec) for spec in scratch.values()]
        + [pltpu.SemaphoreType.DMA((5,))] + [pltpu.SemaphoreType.DMA((sems,))] * 2,
        compiler_params=pltpu.CompilerParams(
            collective_id=0, has_side_effects=True, vmem_limit_bytes=VMEM_BYTES
        ),
    )(*given.values())
    finished = finish(n, output, gt, small, whole1, whole2)
    small_rows = dict(zip(SMALL, finished[6:]))
    return (
        finished[0],
        finished[1],
        small_rows["gain1"],
        small_rows["shift1"],
        jnp.transpose(finished[4], (2, 0, 1)),
        small_rows["bias_qv"],
        finished[5],
        small_rows["bias_out"],
        small_rows["gain2"],
        small_rows["shift2"],
        finished[2],
        small_rows["bias_up"],
        finished[3],
        small_rows["bias_down"],
    )


def solution(mesh):
    placed = (
        P(("dp", "tensor"), None),
        P("dp"),
        P(),
        P(),
        P(None, None, "tensor"),
        P(None, "tensor"),
        P("tensor", None),
        P(),
        P(),
        P(),
        P(None, "tensor"),
        P("tensor"),
        P("tensor", None),
        P(),
        P(("dp", "tensor"), None),
    )
    return jax.shard_map(
        body,
        mesh=mesh,
        in_specs=placed,
        out_specs=(
            P(("dp", "tensor"), None),
            P(("dp", "tensor"), None),
            P(),
            P(),
            P(None, None, "tensor"),
            P(None, "tensor"),
            P("tensor", None),
            P(),
            P(),
            P(),
            P(None, "tensor"),
            P("tensor"),
            P("tensor", None),
            P(),
        ),
        check_vma=False,
    )
```

```python
import types

import jax
import jax.numpy as jnp
from jax import lax
from jax.experimental import pallas as pl
from jax.experimental.pallas import tpu as pltpu
from jax.sharding import PartitionSpec as P

HEAD_DIM = 64
LOGICAL = pl.DeviceIdType.LOGICAL
VMEM_BYTES = 62 * 2**20

epsilon = 1e-06
low = jnp.bfloat16
wide = jnp.float32


def round_up(amount, unit):
    return -(-amount // unit) * unit


class Here:
    def __init__(self, dp, tensor):
        self.dp, self.tensor = dp, tensor
        self.d, self.t = lax.axis_index("dp"), lax.axis_index("tensor")
        self.me = self.d * tensor + self.t
        self.chip = lax.div(self.t, 2)
        self.core = self.t - 2 * self.chip
        self.bits, rest = [], self.d
        for _ in range(dp.bit_length() - 1):
            half = lax.div(rest, 2)
            self.bits.append(rest - 2 * half)
            rest = half
        low_bits = sum(bit * (1 << b) for b, bit in enumerate(self.bits[:3]))
        self.near, self.group = low_bits, self.d - low_bits

    def logical(self, dp=None, tensor=None):
        if dp is not None:
            return self.me + (dp - self.d) * self.tensor
        return self.me + (tensor - self.t)

    def bit_flipped(self, b):
        return self.d + (1 - 2 * self.bits[b]) * (1 << b)


def flipped(here, flip_chip, flip_core):
    chip = here.chip + flip_chip - 2 * here.chip * flip_chip
    return 2 * chip + here.core + flip_core - 2 * here.core * flip_core


def two_bits(i):
    high = jnp.where(i >= 2, 1, 0)
    return high, i - 2 * high


def dot(left, right):
    return jnp.dot(left, right, preferred_element_type=wide)


def dot_rows(left, right):
    return lax.dot_general(left, right, (((1,), (1,)), ((), ())), preferred_element_type=wide)


def dot_columns(left, right):
    return lax.dot_general(left, right, (((0,), (0,)), ((), ())), preferred_element_type=wide)


def standardize(values):
    center = values - jnp.mean(values, -1, keepdims=True)
    inverse = lax.rsqrt(jnp.mean(center * center, -1, keepdims=True) + epsilon)
    return center * inverse, inverse


def norm_back(grad, unit, inverse, gain):
    scaled = grad * gain
    return inverse * (
        scaled
        - jnp.mean(scaled, -1, keepdims=True)
        - unit * jnp.mean(scaled * unit, -1, keepdims=True)
    )


def pair(ref, p):
    _, rows, columns = ref.shape
    return ref[pl.ds(2 * p, 2)].reshape(2 * rows, columns)


def set_pair(ref, p, values):
    ref[pl.ds(2 * p, 2)] = values.reshape(2, -1, values.shape[1])


def flat(ref):
    a, b, c = ref.shape
    return ref[...].reshape(a * b, c)


class Links:
    def __init__(self, here, send, recv):
        self.here, self.send, self.recv, self.used, self.pending = here, send, recv, 0, []

    def take(self, amount=1):
        base = self.used
        self.used += amount
        assert self.used <= self.send.shape[0]
        return base

    def copy(self, src, dst, at, **where):
        return pltpu.make_async_remote_copy(
            src_ref=src,
            dst_ref=dst,
            send_sem=self.send.at[at],
            recv_sem=self.recv.at[at],
            device_id=self.here.logical(**where),
            device_id_type=LOGICAL,
        )

    def start(self, src, dst, at, **where):
        copy = self.copy(src, dst, at, **where)
        copy.start()
        self.pending.append(copy)

    def arrived(self, dst, at, **where):
        self.copy(dst, dst, at, **where).wait_recv()

    def finish(self):
        for copy in self.pending:
            copy.wait_send()
        self.pending = []


class Gather:
    def __init__(self, links, buf, here, parts):
        self.links, self.buf, self.t, self.parts = links, buf, here.t, parts
        self.cross, self.diag, self.sib = here.peers
        self.base = links.take(3 * len(parts))

    def view(self, slot, part):
        start, size = self.parts[part]
        return self.buf.at[slot, pl.ds(start, size)]

    def _each(self):
        return range(len(self.parts))

    def start(self, parts=None):
        parts = self._each() if parts is None else parts
        for p in parts:
            v = self.view(self.t, p)
            self.links.copy(v, v, self.base + 3 * p, tensor=self.cross).start()
        for p in parts:
            v = self.view(self.t, p)
            self.links.copy(v, v, self.base + 3 * p + 1, tensor=self.sib).start()

    def wait_sib(self):
        for p in self._each():
            self.links.arrived(self.view(self.sib, p), self.base + 3 * p + 1, tensor=self.sib)

    def forward(self, parts=None):
        for p in self._each() if parts is None else parts:
            v = self.view(self.cross, p)
            self.links.arrived(v, self.base + 3 * p, tensor=self.cross)
            self.links.copy(v, v, self.base + 3 * p + 2, tensor=self.sib).start()

    def wait_diag(self, parts=None):
        for p in self._each() if parts is None else parts:
            self.links.arrived(self.view(self.diag, p), self.base + 3 * p + 2, tensor=self.sib)

    def finish(self):
        for p in self._each():
            v = self.view(self.t, p)
            self.links.copy(v, v, self.base + 3 * p, tensor=self.cross).wait_send()
            self.links.copy(v, v, self.base + 3 * p + 1, tensor=self.sib).wait_send()
            v = self.view(self.cross, p)
            self.links.copy(v, v, self.base + 3 * p + 2, tensor=self.sib).wait_send()


class Reduce:
    def __init__(self, links, part, pre, near, far, here, parts):
        self.links, self.part, self.t, self.parts = links, part, here.t, parts
        self.pre, self.near, self.far = pre, near, far
        self.cross, self.diag, self.sib = here.peers
        self.base = links.take(3 * len(parts))

    def _copy(self, kind, p):
        slot, box, peer = (
            (self.diag, self.pre, self.sib),
            (self.sib, self.near, self.sib),
            (self.cross, self.far, self.cross),
        )[kind]
        rows = pl.ds(*self.parts[p])
        return self.links.copy(
            self.part.at[slot, rows], box.at[rows], self.base + 3 * p + kind, tensor=peer
        )

    def _each(self, parts):
        return range(len(self.parts)) if parts is None else parts

    def send_diag(self, parts=None):
        for p in self._each(parts):
            self._copy(0, p).start()

    def send_sib(self):
        for p in self._each(None):
            self._copy(1, p).start()

    def send_cross(self, parts=None):
        for p in self._each(parts):
            self._copy(0, p).wait_recv()
            rows = pl.ds(*self.parts[p])
            self.part[self.cross, rows] = (
                self.part[self.cross, rows].astype(wide) + self.pre[rows].astype(wide)
            ).astype(low)
            self._copy(2, p).start()

    def result(self, p):
        self._copy(1, p).wait_recv()
        self._copy(2, p).wait_recv()
        rows = pl.ds(*self.parts[p])
        return (
            self.part[self.t, rows].astype(wide)
            + self.near[rows].astype(wide)
            + self.far[rows].astype(wide)
        )

    def finish(self):
        for p in self._each(None):
            for kind in range(3):
                self._copy(kind, p).wait_send()


class DataReduce:
    def __init__(self, links, held, whole, out, box, box_at, first, rows):
        self.links, self.held, self.whole, self.out, self.here = links, held, whole, out, links.here
        count = self.here.dp
        bits = count.bit_length() - 1
        assert count == 1 << bits and bits >= 3
        self.extra = list(range(3, bits))
        self.region = (first, rows, 0, held.shape[1])
        self.trail, self.sent, self.boxes = [], [], []
        for tall, broad in self.sizes(rows, held.shape[1], count)[0]:
            self.boxes.append(box.at[pl.ds(box_at, tall), pl.ds(0, broad)])
            box_at += tall
        self.base = links.take(9 + len(self.extra))
        self.plan()

    @classmethod
    def sizes(cls, rows, columns, count):
        found = cls.boxes_of(rows, columns)
        found += found[-1:] * (count.bit_length() - 1 - 3)
        return found, sum(size[0] for size in found)

    def _bit(self, b):
        return self.here.bits[b]

    def _peer(self, b):
        return self.here.bit_flipped(b)

    def _send(self, src, dst, at, peer):
        copy = self.links.copy(src, dst, self.base + at, dp=peer)
        copy.start()
        self.sent.append(copy)

    def _wait(self, dst, at, peer):
        self.links.arrived(dst, self.base + at, dp=peer)

    @staticmethod
    def _view(ref, region):
        row, rows, column, columns = region
        if columns == ref.shape[1]:
            return ref.at[pl.ds(row, rows)]
        return ref.at[pl.ds(row, rows), pl.ds(column, columns)]

    @staticmethod
    def _part(region, bit):
        row, rows, column, columns = region
        if rows % 32 == 0:
            return (pl.multiple_of(row + bit * (rows // 2), 16), rows // 2, column, columns)
        return (row, rows, pl.multiple_of(column + bit * (columns // 2), 128), columns // 2)

    def _give_half(self, b, box, at):
        bit = self._bit(b)
        self.trail.append(self.region)
        self._send(self._view(self.held, self._part(self.region, 1 - bit)), self.boxes[box], at, self._peer(b))
        self.region = self._part(self.region, bit)

    def _add(self, boxes, last):
        view = self._view(self.held, self.region)
        total = view[...].astype(wide)
        for box in boxes:
            total += self.boxes[box][...].astype(wide)
        if last:
            view = self._view(self.whole, self.region)
        view[...] = total.astype(low)
        if last:
            self._swap()

    def _swap(self):
        view = self._view(self.whole, self.region)
        for k, b in enumerate(self.extra):
            box, at = self.boxes[k - len(self.extra)], 9 + k
            copy = self.links.copy(view, box, self.base + at, dp=self._peer(b))
            copy.start()
            self._wait(box, at, self._peer(b))
            copy.wait_send()
            view[...] = (view[...].astype(wide) + box[...].astype(wide)).astype(low)

    def _give_whole(self, b, at):
        view = self._view(self.whole, self.region)
        self._send(view, view, at, self._peer(b))

    def _take_half(self, b, at):
        outer = self.trail.pop()
        view = self._view(self.whole, self._part(outer, 1 - self._bit(b)))
        self._wait(view, at, self._peer(b))
        self.region = outer

    def _leave(self):
        rows = pl.ds(self.region[0], self.region[1])
        self.left = pltpu.make_async_copy(
            self.whole.at[rows], self.out.at[rows], self.links.send.at[self.base + 8]
        )
        self.left.start()

    def step(self):
        if self.steps:
            self.steps.pop(0)()

    def finish(self):
        assert not self.steps
        self.left.wait()
        for copy in self.sent:
            copy.wait_send()


class Halves(DataReduce):
    order = (1, 0, 2)

    @staticmethod
    def boxes_of(rows, columns):
        found = []
        for _ in range(3):
            if rows % 32 == 0:
                rows //= 2
            else:
                columns //= 2
            found.append((rows, columns))
        return found

    def plan(self):
        a, b, c = self.order
        self.steps = [
            lambda: self._give_half(a, 0, 0),
            lambda: (self._wait_box(a, 0), self._add((0,), False), self._give_half(b, 1, 1)),
            lambda: (self._wait_box(b, 1), self._add((1,), False), self._give_half(c, 2, 2)),
            lambda: (self._wait_box(c, 2), self._add((2,), True), self._give_whole(c, 3)),
            lambda: (self._take_half(c, 3), self._give_whole(b, 4)),
            lambda: (self._take_half(b, 4), self._give_whole(a, 5)),
            lambda: (self._take_half(a, 5), self._leave()),
        ]

    def _wait_box(self, b, box):
        self._wait(self.boxes[box], box, self._peer(b))


class HalvesFromX(Halves):
    order = (0, 1, 2)


class Quarters(DataReduce):
    @staticmethod
    def boxes_of(rows, columns):
        tall, broad = rows // 8, columns
        if tall % 16:
            tall, broad = rows // 4, columns // 2
        return [(rows // 2, columns)] + [(tall, broad)] * 3

    def plan(self):
        self.steps = [
            lambda: self._give_half(0, 0, 0),
            lambda: (self._wait(self.boxes[0], 0, self._peer(0)), self._add((0,), False), self._give_quarters()),
            lambda: (self._take_boxes(), self._add((1, 2, 3), True), self._give_quarter()),
            lambda: (self._take_quarters(), self._give_whole(0, 7)),
            lambda: (self._take_half(0, 7), self._leave()),
        ]

    def _z(self, j):
        low_bit = 1 - self._bit(1) if j % 2 else self._bit(1)
        high = 1 - self._bit(2) if j // 2 else self._bit(2)
        return low_bit, high, self.here.group + high * 4 + low_bit * 2 + self._bit(0)

    def _quarter(self, j):
        low_bit, high, peer = self._z(j)
        return self._part(self._part(self.trail[-1], high), low_bit), peer

    def _give_quarters(self):
        self.trail.append(self.region)
        for j in (1, 2, 3):
            part, peer = self._quarter(j)
            self._send(self._view(self.held, part), self.boxes[j], j, peer)
        self.region = self._quarter(0)[0]

    def _take_boxes(self):
        for j in (1, 2, 3):
            self._wait(self.boxes[j], j, self._z(j)[2])

    def _give_quarter(self):
        view = self._view(self.whole, self.region)
        for j in (1, 2, 3):
            self._send(view, view, 3 + j, self._z(j)[2])

    def _take_quarters(self):
        for j in (1, 2, 3):
            part, peer = self._quarter(j)
            self._wait(self._view(self.whole, part), 3 + j, peer)
        self.region = self.trail.pop()


class Pipeline:
    def __init__(self, plan):
        self.plan, self.members = plan, []

    def add(self, member):
        self.members.append(member)
        member.step()

    def at(self, place):
        for number in self.plan[place]:
            self.members[number].step()

    def finish(self):
        self.at("end")
        for m in self.members:
            while m.steps:
                m.step()
            m.finish()


PLAN = dict(
    waiting=(),
    shared=(0, 1),
    arriving=(),
    h0p0=(2, 0),
    h0p2=(2, 3, 0, 1),
    h0=(),
    h1p0=(3, 0),
    h1p2=(1,),
    h1=(3,),
    h2p0=(2, 0, 4),
    h2p2=(3, 1, 5, 6, 2),
    h2=(3, 4),
    led=(2, 5),
    crossing=(7, 3, 4, 6),
    told=(5, 7, 0),
    end=(2, 1, 6, 4, 5, 7, 6, 7, 1),
)


class Everyone:
    def __init__(self, links, buf, me, count, device):
        self.links, self.buf, self.me, self.count, self.device = links, buf, me, count, device
        self.base = links.take(count)

    def _copy(self, j):
        slot = self.buf.at[self.me]
        peer = self.me + j
        peer = self.device(jnp.where(peer >= self.count, peer - self.count, peer))
        return self.links.copy(slot, slot, self.base + j, dp=peer)

    def _loop(self, act):
        def one(j, carry):
            act(j)
            return carry

        lax.fori_loop(1, self.count, one, 0)

    def start(self, values):
        self.buf[self.me] = values
        self._loop(lambda j: self._copy(j).start())

    def _hear(self, j):
        peer = self.me - j
        peer = jnp.where(peer < 0, peer + self.count, peer)
        self.links.arrived(self.buf.at[peer], self.base + j, dp=self.device(peer))

    def result(self):
        self._loop(self._hear)
        return lax.fori_loop(1, self.count, lambda j, acc: acc + self.buf[j], self.buf[0])

    def finish(self):
        self._loop(lambda j: self._copy(j).wait_send())


def greet(here):
    barrier = pltpu.get_barrier_semaphore()
    for axis, me, count in (("tensor", here.t, here.tensor), ("dp", here.d, here.dp)):

        def one(j, carry, axis=axis, me=me, count=count):
            peer = me + j
            peer = here.logical(**{axis: jnp.where(peer >= count, peer - count, peer)})
            pl.semaphore_signal(barrier, inc=1, device_id=peer, device_id_type=LOGICAL)
            return carry

        lax.fori_loop(1, count, one, 0)


def await_greetings(amount):
    pl.semaphore_wait(pltpu.get_barrier_semaphore(), amount)


def halves(rows):
    first = round_up(rows // 2, 16)
    return ((0, first), (first, rows - first))


def head_masks(shape, local_heads):
    lane = lax.broadcasted_iota(jnp.int32, shape, 1)
    return [
        jnp.where((lane >= h * HEAD_DIM) & (lane < (h + 1) * HEAD_DIM), 1.0, 0.0)
        for h in range(local_heads)
    ], lane


def kernel(n, S):
    here = Here(n.dp, 4)
    t, d = here.t, here.d
    here.peers = peers = [flipped(here, 1, 0), flipped(here, 1, 1), flipped(here, 0, 1)]
    links = Links(here, S.send, S.recv)
    greet(here)
    R, own, W, H, D, K = n.R, n.own, n.W, n.H, n.D, n.K
    split = halves(R)
    vector = lambda ref: ref[...].reshape(1, D)

    fetch = pltpu.make_async_copy(S.cot, S.gt, S.local.at[0])
    load = [
        pltpu.make_async_copy(getattr(S, name + "_far"), getattr(S, name), S.local.at[1 + j])
        for j, name in enumerate(LOADED)
    ]
    fetch.start()
    for copy in load:
        copy.start()
    S.a1[t] = jnp.zeros((R, D), low)
    S.cot4[t] = jnp.zeros((R, D), low)
    S.a24[t] = jnp.zeros((R, D), low)
    S.hl4[t] = jnp.zeros((R, D), low)
    rows_in = Gather(links, S.a1, here, split)
    cot_in = Gather(links, S.cot4, here, split)
    ow_in = Gather(links, S.ow4, here, ((0, W),))
    for p, (start, size) in enumerate(split):
        rows = pl.ds(start, min(size, own - start))
        unit, _ = standardize(S.x[rows, :].astype(wide))
        S.a1[t, rows, :] = (unit * vector(S.g1) + vector(S.b1)).astype(low)
        if p == 0:
            await_greetings(3 + n.dp - 1)
        rows_in.start([p])
    load[0].wait()
    S.ow4[t] = S.ow[...]
    ow_in.start()
    fetch.wait()
    S.cot4[t, 0:own, :] = S.gt[...].astype(low)
    cot_in.start([0])
    load[2].wait()
    load[3].wait()
    S.gw[0:D, :] = jnp.transpose(S.wup[...])
    S.gw[D:, :] = jnp.transpose(S.wdn[...])
    load[1].wait()
    S.v[4 * R :, :] = jnp.zeros((K - 4 * R, H), low)
    length = S.lengths[0]

    chip = here.chip

    def project(i, carry):
        s = flipped(here, *two_bits(i))

        @pl.when(i == 1)
        def _():
            rows_in.wait_sib()

        @pl.when(i == 2)
        def _():
            rows_in.forward()

        @pl.when(i == 3)
        def _():
            rows_in.wait_diag()

        slab = S.a1[s]
        lane = lax.broadcasted_iota(jnp.int32, (R, H - W), 1)
        row = lax.broadcasted_iota(jnp.int32, (R, H - W), 0)
        absent = (row >= own) | (row + s * own >= length)
        at = pl.ds(pl.multiple_of(s * R, 16), R)
        out = dot_rows(slab, S.wqkv[0]) + S.bq[0:1, :]
        S.q[s, :, :W] = (out.astype(low).astype(wide) * HEAD_DIM**-0.5).astype(low)
        S.q[s, :, W:] = jnp.where(lane == 0, HEAD_DIM**-0.5, 0.0).astype(low)
        S.k[at, :W] = dot_rows(slab, S.wqkv[1]).astype(low)
        S.k[at, W:] = jnp.where((lane == 0) & absent, -8e30, 0.0).astype(low)
        S.v[at, :W] = (dot_rows(slab, S.wqkv[2]) + S.bq[1:2, :]).astype(low)
        S.v[at, W:] = jnp.where(lane < 2, 1.0, 0.0).astype(low)
        return carry

    lax.fori_loop(0, 4, project, 0)
    if K > 4 * R:
        lane = lax.broadcasted_iota(jnp.int32, (K - 4 * R, H), 1)
        S.k[4 * R :, :] = jnp.where(lane == W, -8e30, 0.0).astype(low)
    S.kt[...] = jnp.transpose(S.k[...])
    S.vt[...] = jnp.transpose(S.v[...])

    masks, lane = head_masks((1, H), n.heads)
    mix_base = links.take(3)


    def attend(i, carry):
        high, low_bit = two_bits(i)
        s = flipped(here, 1 - high, low_bit + high - 2 * low_bit * high)
        query = S.q[s]
        mixed = jnp.zeros((R, H), wide)
        inverse = jnp.zeros((R, 128), wide)
        first = lax.broadcasted_iota(jnp.int32, (1, 128), 1)

        def score(h):
            here = jnp.where(lane == W, 1.0, masks[h]).astype(low)
            return dot(query * here, S.kt[...])

        ready = score(0)
        for h in range(n.heads):
            scores = ready
            if h + 1 < n.heads:
                ready = score(h + 1)
            terms = jnp.exp(scores - jnp.max(scores, -1, keepdims=True)).astype(low)
            S.e[h, s] = terms
            part = dot(terms, S.v[...])
            scale = 1.0 / part[:, W : W + 1]
            mixed += part * (scale * masks[h])
            inverse = jnp.where(first == h, scale, inverse)
        S.o[s] = mixed
        S.inv[s] = inverse
        S.mix[s] = mixed[:, :W].astype(low)

        @pl.when(i < 3)
        def _():
            links.copy(S.mix.at[s], S.mix4.at[t], mix_base + i, tensor=s).start()

        @pl.when(i == 1)
        def _():
            cot_in.start([1])

        @pl.when(i == 2)
        def _():
            ow_in.wait_sib()
            ow_in.forward()

        return carry

    lax.fori_loop(0, 4, attend, 0)
    ow_in.wait_diag()
    S.mix4[t] = S.mix[t]
    for j, s in enumerate(peers):
        links.arrived(S.mix4.at[s], mix_base + j, tensor=s)

    total = dot(S.mix4[0], S.ow4[0])
    for j in range(1, 4):
        total += dot(S.mix4[j], S.ow4[j])
    total = S.x[...].astype(wide) + (total[:own] + vector(S.ob))
    S.hid[...] = total
    unit, _ = standardize(total)
    S.a24[t, 0:own, :] = (unit * vector(S.g2) + vector(S.b2)).astype(low)
    next_in = Gather(links, S.a24, here, halves(R))
    next_in.start()
    back = Reduce(links, S.part, S.pre1, S.near1, S.far1, here, split)
    ahead = Reduce(links, S.fop, S.pre2, S.near2, S.far2, here, split)
    S.gub[...] = jnp.zeros_like(S.gub)

    def feed(s, start, size):
        rows = pl.ds(start, size)
        up = dot(S.a24[s, rows], S.wup[...]) + vector(S.bup)
        square = up * up
        c = 0.7978845608028654
        bend = jnp.tanh(c * up * (1.0 + 0.044715 * square))
        half = 0.5 * (1.0 + bend)
        slope = half + 0.5 * up * (1.0 - bend * bend) * (c + (3 * 0.044715 * c) * square)
        active = (up * half).astype(low)
        S.pool[s, rows, 0:D] = active
        grad = (dot(S.cot4[s, rows], S.gw[D:, :]) * slope).astype(low)
        S.gup[s, rows] = grad
        S.part[s, rows] = dot(grad, S.gw[0:D, :]).astype(low)
        S.gub[...] += jnp.sum(grad.astype(wide), 0, keepdims=True)

    def lead_out(s, start, size):
        rows = pl.ds(start, size)
        S.fop[s, rows] = dot(S.pool[s, rows, 0:D], S.wdn[...]).astype(low)

    def feed_here(i, carry):
        s = flipped(here, 0, i)

        @pl.when(i == 1)
        def _():
            next_in.wait_sib()
            cot_in.wait_sib()

        feed(s, 0, R)

        @pl.when(i == 1)
        def _():
            back.send_sib()

        lead_out(s, 0, R)
        return carry

    lax.fori_loop(0, 2, feed_here, 0)
    ahead.send_sib()
    for p in (0, 1):

        def feed_there(i, carry, p=p):
            @pl.when(i == 0)
            def _():
                cot_in.forward([p])
                next_in.forward([p])

            @pl.when(i == 1)
            def _():
                cot_in.wait_diag([p])
                next_in.wait_diag([p])

            feed(flipped(here, 1, i), *split[p])
            if p == 1:

                @pl.when(i == 0)
                def _():
                    back.send_cross([0])

            return carry

        lax.fori_loop(0, 2, feed_there, 0)
        back.send_diag([p])
    for i in (0, 1):
        lead_out(flipped(here, 1, i), 0, R)
    back.send_cross([1])
    ahead.send_diag()

    sums = Pipeline(PLAN)
    tile = D // 2
    box_at = 0

    def sum_over_dp(kind, held, whole, out, first, rows):
        nonlocal box_at
        sums.add(kind(links, held, whole, out, S.box, box_at, first, rows))
        box_at += kind.sizes(rows, D, n.dp)[1]

    for left, right, first in ((S.a24, S.gup, 0), (S.pool, S.cot4, D)):
        rows = left[:, :, 0:D].reshape(4 * R, D)
        S.gw[first : first + D, :] = dot_columns(rows, flat(right)).astype(low)
        for at in (first, first + tile):
            kind = Halves if at == tile else HalvesFromX
            sum_over_dp(kind, S.gw, S.sum1, S.whole1, at, tile)

    sums.at("waiting")
    S.small[...] = jnp.zeros_like(S.small)
    gm_base = links.take(6)
    shared = lambda s, p, j: links.copy(
        S.mix4.at[s, pl.ds(*split[p])], S.gm4.at[t, pl.ds(*split[p])], gm_base + 3 * p + j, tensor=peers[j]
    )
    for p, (start, size) in enumerate(split):
        real = min(size, own - start)
        rows = pl.ds(start, real)
        grad = back.result(p)[:real]
        unit, inverse = standardize(S.hid[rows])
        S.small[2:3, :] += jnp.sum(grad * unit, 0, keepdims=True)
        S.small[3:4, :] += jnp.sum(grad, 0, keepdims=True)
        S.gt[rows] += norm_back(grad, unit, inverse, vector(S.g2))
        S.hl4[t, rows] = S.gt[rows].astype(low)
        rows = pl.ds(start, size)
        for j, s in enumerate(peers + [t]):
            product = dot_rows(S.hl4[t, rows], S.ow4[s]).astype(low)
            if j < 3:
                S.mix4[s, rows] = product
                shared(s, p, j).start()
            else:
                S.gm4[t, rows] = product
    S.small[4:5, :] = jnp.sum(S.hl4[t].astype(wide), 0, keepdims=True)
    S.small[5:6, :] = jnp.sum(S.cot4[t].astype(wide), 0, keepdims=True)
    S.small[6:7, :] = S.gub[...]
    hl_in = Gather(links, S.hl4, here, halves(R))

    next_in.finish()
    S.do[...] = jnp.zeros_like(S.do)
    S.qt[...] = jnp.transpose(flat(S.q))
    sums.at("shared")

    def prepare(i, s):
        if i > 0:
            j = (None, 2, 0, 1)[i]
            for p in (0, 1):
                rows = pl.ds(*split[p])
                links.arrived(S.gm4.at[s, rows], gm_base + 3 * p + j, tensor=peers[j])
        S.do[:, :W] = S.gm4[s].astype(wide)
        inverse = sum(S.inv[s, :, h : h + 1] * masks[h] for h in range(n.heads))
        scaled = (S.do[...] * inverse).astype(low)
        S.v[pl.ds(pl.multiple_of(s * R, 16), R), :] = scaled
        scaled = scaled.astype(wide)
        product = scaled * S.o[s]
        for h in range(n.heads):
            inner = -jnp.sum(product * masks[h], -1, keepdims=True)
            upper = inner.astype(low).astype(wide)
            S.a24[s, :, h * H : (h + 1) * H] = (
                scaled * masks[h]
                + jnp.where(lane == W, upper, 0.0)
                + jnp.where(lane == W + 1, inner - upper, 0.0)
            ).astype(low)

    def pull(h, p):
        grad_p = dot(pair(S.a24.at[:, :, h * H : (h + 1) * H], p), S.vt[...])
        grad_s = (pair(S.e.at[h], p).astype(wide) * grad_p).astype(low)
        set_pair(S.pool, p, grad_s)
        dq = dot(grad_s, S.k[...]) * (masks[h] * HEAD_DIM**-0.5)
        if h > 0:
            dq += pair(S.gup.at[:, :, 0:H], p).astype(wide)
        S.gup[pl.ds(2 * p, 2), :, 0:H] = dq.astype(low).reshape(2, R, H)

    def weights(h):
        at = slice(h * HEAD_DIM, (h + 1) * HEAD_DIM)
        tile = h * HEAD_DIM // 128 * 128
        dqt = jnp.transpose(flat(S.gup.at[:, :, tile : tile + 128]))
        left = jnp.concatenate(
            [dqt[h * HEAD_DIM - tile : (h + 1) * HEAD_DIM - tile], S.qt[at, :], S.kt[at, : 4 * R]], 0
        )
        out = dot(left, flat(S.a1))
        S.gw2[h * W : (h + 1) * W, :] = out.astype(low)
        for c in range(3):
            product = out[c * HEAD_DIM : (c + 1) * HEAD_DIM] * S.wqkv[c, at, :].astype(wide)
            S.small[0:1, :] += jnp.sum(product, 0, keepdims=True)
        sum_over_dp(Quarters, S.gw2, S.sum2, S.whole2, h * W, W)

    for h in range(n.heads):
        for i in (0, 2):
            if (h, i) == (0, 2):
                sums.at("arriving")
            if h == 0:
                prepare(i, flipped(here, i // 2, 0))
                prepare(i + 1, flipped(here, i // 2, 1))
            if (h, i) == (0, 2):
                hl_in.start()
            pull(h, chip if i == 0 else 1 - chip)
            sums.at(f"h{h}p{i}")
            if (h, i) == (1, 0):
                hl_in.wait_sib()
                hl_in.forward()
                ahead.send_cross()
            elif (h, i) == (1, 2):
                hl_in.wait_diag()
                S.gw2[3 * W :, :] = dot_columns(flat(S.mix), flat(S.hl4)).astype(low)
                sum_over_dp(Quarters, S.gw2, S.sum2, S.whole2, 3 * W, W)
        if h == 0:
            S.v[4 * R :, :] = jnp.zeros((K - 4 * R, H), low)
            S.kt[...] = jnp.transpose(S.v[...])
        at = slice(h * HEAD_DIM, (h + 1) * HEAD_DIM)
        S.qt[at, :] = dot(S.qt[at, :], flat(S.pool))[:, : 4 * R].astype(low)
        S.kt[at, : 4 * R] = dot(S.kt[at, : 4 * R], flat(S.e.at[h]))[:, : 4 * R].astype(low)
        if h + 1 < n.heads:
            weights(h)
        sums.at(f"h{h}")

    pad = jnp.zeros((R, H - W), low)
    for part, grad_t in ((1, S.qt), (2, S.kt)):
        rows = jnp.transpose(grad_t[:W, : 4 * R])
        for s in range(4):
            S.gup[s, :, part * H : part * H + W] = rows[s * R : (s + 1) * R]
            S.gup[s, :, part * H + W : (part + 1) * H] = pad

    back.finish()
    down = Reduce(links, S.part, S.pre1, S.near1, S.far1, here, split)

    def lead(s, start, size):
        rows = pl.ds(start, size)
        out = dot(S.gup[s, rows, 0:W], S.wqkv[0])
        out += dot(S.gup[s, rows, H : H + W], S.wqkv[1])
        out += dot(S.gup[s, rows, 2 * H : 2 * H + W], S.wqkv[2])
        S.part[s, rows] = out.astype(low)

    cross, diag, sib = peers
    lead(diag, *split[0])
    down.send_diag([0])
    lead(cross, *split[0])
    weights(n.heads - 1)
    down.send_cross([0])
    lead(diag, *split[1])
    down.send_diag([1])
    lead(cross, *split[1])
    down.send_cross([1])
    lead(sib, 0, R)
    down.send_sib()
    lead(t, 0, R)
    columns = jnp.sum(flat(S.gup).astype(wide), 0, keepdims=True)
    S.small[7:8, 0:H] = columns[:, 0:H]
    S.small[7:8, H : 2 * H] = columns[:, 2 * H :]
    upper = columns.astype(low)
    both = jnp.concatenate([upper.astype(wide), columns - upper.astype(wide)], 0).astype(low)
    for c in range(3):
        product = dot(both[:, c * H : c * H + W], S.wqkv[c])
        S.small[1:2, :] += jnp.sum(product, 0, keepdims=True)

    S.small4[t] = S.small[...]
    base3 = links.take(3)
    for j in range(3):
        links.start(S.small4.at[t], S.small4.at[t], base3 + j, tensor=peers[j])
    sums.at("led")
    result = jnp.concatenate([ahead.result(0), ahead.result(1)], 0)
    S.output[...] = (S.hid[...] + (result[:own] + vector(S.db))).astype(low)
    sums.at("crossing")

    unit, inverse = standardize(S.x[...].astype(wide))
    grad = jnp.concatenate([down.result(0), down.result(1)], 0)[:own]
    for j in range(3):
        links.arrived(S.small4.at[peers[j]], base3 + j, tensor=peers[j])
    over = S.small4[0] + S.small4[1] + S.small4[2] + S.small4[3]
    row = lax.broadcasted_iota(jnp.int32, over.shape, 0)
    near = min(8, n.dp)
    inner = Everyone(links, S.smalls, here.near, near, lambda j: here.group + j)
    inner.start(jnp.where(row < 6, over, S.small[...]))
    S.gt[...] += norm_back(grad, unit, inverse, vector(S.g1))
    sums.at("told")
    sums.finish()
    total = inner.result()
    inner.finish()
    if n.dp > near:
        outer = Everyone(links, S.smalls2, lax.div(here.group, near), n.dp // near, lambda j: j * near + here.near)
        outer.start(total)
        total = outer.result()
        outer.finish()
    S.small_sum[...] = total
    S.small_sum[0:1, :] = (total[0:1, :] - vector(S.b1) * total[1:2, :]) / vector(S.g1)
    for j, s in enumerate(peers):
        links.copy(S.mix.at[s], S.mix4.at[t], mix_base + j, tensor=s).wait_send()
        for p in (0, 1):
            shared(s, p, j).wait_send()
    for transfer in (rows_in, cot_in, ow_in, hl_in, ahead, down):
        transfer.finish()
    links.finish()


LOADED = ("ow", "wqkv", "wup", "wdn")
SMALL = ("gain1", "shift1", "gain2", "shift2", "bias_out", "bias_down", "bias_up", "bias_qv")


def finish(n, output, gt, small, whole1, whole2):
    D, W, H = n.D, n.W, n.H
    steps = n.heads
    rows1 = D // steps

    def spread(output, gt, small, up, down, head, out, *refs):
        to_output, to_gt, to_up, to_down, to_qkv, to_out = refs[:6]
        vectors, sems = refs[6:14], refs[14]
        i = pl.program_id(0)
        held = refs[15:]
        come = [pltpu.make_async_copy(a, b, sems.at[j]) for j, (a, b) in enumerate(zip((output, gt), held))]
        go = [
            pltpu.make_async_copy(a, b, sems.at[2 + j])
            for j, (a, b) in enumerate(zip(held, (to_output, to_gt)))
        ]

        @pl.when(i == 0)
        def _():
            for copy in come:
                copy.start()
            for j in range(7):
                vectors[j][...] = small[j : j + 1, :].reshape(D)
            vectors[7][0:1, :] = small[7:8, :W]
            vectors[7][1:2, :] = small[7:8, H : H + W]

        to_up[...] = up[...].astype(wide)
        to_down[...] = down[...].astype(wide)
        for j in range(3):
            to_qkv[j] = head[j * HEAD_DIM : (j + 1) * HEAD_DIM, :].astype(wide)
        to_out[...] = out[...].astype(wide)

        @pl.when(i == 1)
        def _():
            for first, second in zip(come, go):
                first.wait()
                second.start()

        @pl.when(i == steps - 1)
        def _():
            for copy in go:
                copy.wait()

    hbm = pl.BlockSpec(memory_space=pl.ANY)
    whole = pl.BlockSpec(memory_space=pltpu.VMEM)
    at_row = lambda rows, index: pl.BlockSpec((rows, D), lambda i: (index(i), 0))
    shape = jax.ShapeDtypeStruct
    return pl.pallas_call(
        spread,
        grid=(steps,),
        out_shape=[shape(output.shape, low), shape(gt.shape, wide)]
        + [shape((D, D), wide)] * 2
        + [shape((3, W, D), wide), shape((W, D), wide)]
        + [shape((D,), wide)] * 7
        + [shape((2, W), wide)],
        in_specs=[hbm, hbm, whole, at_row(rows1, lambda i: i), at_row(rows1, lambda i: i + steps)]
        + [at_row(W, lambda i: i), at_row(HEAD_DIM, lambda i: 3 * steps + i)],
        out_specs=[hbm, hbm]
        + [at_row(rows1, lambda i: i)] * 2
        + [pl.BlockSpec((3, HEAD_DIM, D), lambda i: (0, i, 0)), at_row(HEAD_DIM, lambda i: i)]
        + [whole] * 8,
        scratch_shapes=[
            pltpu.SemaphoreType.DMA((4,)),
            pltpu.VMEM(output.shape, low),
            pltpu.VMEM(gt.shape, wide),
        ],
    )(output, gt, small, whole1, whole1, whole2, whole2)


def body(
    tokens,
    lengths,
    ln1_gain,
    ln1_shift,
    qkv_weight,
    qv_bias,
    out_weight,
    out_bias,
    ln2_gain,
    ln2_shift,
    up_weight,
    up_bias,
    down_weight,
    down_bias,
    cotangent,
):
    own, D = tokens.shape
    W = qkv_weight.shape[2]
    F = up_weight.shape[1]
    dp = lax.axis_size("dp")
    assert lax.axis_size("tensor") == 4 and lengths.shape[0] == 1 and F == D and 4 * W == D and 3 * round_up(W + 2, 128) == D
    R = round_up(own, 16)
    H = round_up(W + 2, 128)
    K = round_up(4 * R, 256)
    heads = W // HEAD_DIM
    extra = dp.bit_length() - 1 - 3
    n = types.SimpleNamespace(
        own=own, D=D, W=W, R=R, H=H, K=K, dp=dp, heads=heads, extra=extra
    )
    weights = dict(ow=out_weight, wqkv=jnp.transpose(qkv_weight, (1, 2, 0)), wup=up_weight, wdn=down_weight)
    given = dict(
        x=tokens, lengths=lengths, g1=ln1_gain, b1=ln1_shift,
        bq=qv_bias, ob=out_bias, g2=ln2_gain, b2=ln2_shift, bup=up_bias, db=down_bias,
        cot=cotangent,
    )
    given.update({name + "_far": weights[name] for name in LOADED})
    outs = dict(
        output=((own, D), low), gt=((own, D), wide), small_sum=((8, D), wide),
        whole1=((2 * D, D), low), whole2=((D, D), low),
    )
    rows4 = ((4, R, D), low)
    slab = ((R, D), low)
    chunks = [(Halves, D // 2)] * 4 + [(Quarters, W)] * 4
    scratch = dict(
        a1=rows4, cot4=rows4, ow4=((4, W, D), low), q=((4, R, H), low), k=((K, H), low),
        v=((K, H), low), kt=((H, K), low), vt=((H, K), low), e=((heads, 4, R, K), low),
        o=((4, R, H), wide), inv=((4, R, 128), wide), mix=((4, R, W), low), mix4=((4, R, W), low),
        hid=((own, D), wide),
        a24=rows4, pool=((4, R, K), low), gup=rows4, part=rows4,
        fop=rows4, pre1=slab, near1=slab, far1=slab, pre2=slab, near2=slab, far2=slab,
        gw=((2 * D, D), low), gub=((1, D), wide),
        small=((8, D), wide), hl4=rows4,
        gm4=((4, R, W), low), qt=((H, 4 * R), low), do=((R, H), wide),
        gw2=((D, D), low),
        small4=((4, 8, D), wide), smalls=((min(8, dp), 8, D), wide),
        box=((sum(kind.sizes(r, D, dp)[1] for kind, r in chunks), D), low),
        sum1=((2 * D, D), low), sum2=((D, D), low),
    )
    scratch.update({name: (weights[name].shape, low) for name in LOADED})
    if dp > 8:
        scratch["smalls2"] = ((dp // 8, 8, D), wide)
    sems = 170 + dp + 8 * extra
    names = list(given) + list(outs) + list(scratch) + ["local", "send", "recv"]
    vmem = pl.BlockSpec(memory_space=pltpu.VMEM)
    smem = pl.BlockSpec(memory_space=pltpu.SMEM)
    hbm = pl.BlockSpec(memory_space=pl.ANY)
    output, gt, small, whole1, whole2 = pl.pallas_call(
        lambda *refs: kernel(n, types.SimpleNamespace(**dict(zip(names, refs)))),
        out_shape=tuple(jax.ShapeDtypeStruct(*spec) for spec in outs.values()),
        in_specs=[
            hbm if name.endswith("_far") else dict(lengths=smem, cot=hbm).get(name, vmem) for name in given
        ],
        out_specs=tuple(hbm if name in ("whole1", "whole2") else vmem for name in outs),
        scratch_shapes=[pltpu.VMEM(*spec) for spec in scratch.values()]
        + [pltpu.SemaphoreType.DMA((5,))] + [pltpu.SemaphoreType.DMA((sems,))] * 2,
        compiler_params=pltpu.CompilerParams(
            collective_id=0, has_side_effects=True, vmem_limit_bytes=VMEM_BYTES
        ),
    )(*given.values())
    finished = finish(n, output, gt, small, whole1, whole2)
    small_rows = dict(zip(SMALL, finished[6:]))
    return (
        finished[0],
        finished[1],
        small_rows["gain1"],
        small_rows["shift1"],
        jnp.transpose(finished[4], (2, 0, 1)),
        small_rows["bias_qv"],
        finished[5],
        small_rows["bias_out"],
        small_rows["gain2"],
        small_rows["shift2"],
        finished[2],
        small_rows["bias_up"],
        finished[3],
        small_rows["bias_down"],
    )


def solution(mesh):
    placed = (
        P(("dp", "tensor"), None),
        P("dp"),
        P(),
        P(),
        P(None, None, "tensor"),
        P(None, "tensor"),
        P("tensor", None),
        P(),
        P(),
        P(),
        P(None, "tensor"),
        P("tensor"),
        P("tensor", None),
        P(),
        P(("dp", "tensor"), None),
    )
    return jax.shard_map(
        body,
        mesh=mesh,
        in_specs=placed,
        out_specs=(
            P(("dp", "tensor"), None),
            P(("dp", "tensor"), None),
            P(),
            P(),
            P(None, None, "tensor"),
            P(None, "tensor"),
            P("tensor", None),
            P(),
            P(),
            P(),
            P(None, "tensor"),
            P("tensor"),
            P("tensor", None),
            P(),
        ),
        check_vma=False,
    )
```

```python
import types

import jax
import jax.numpy as jnp
from jax import lax
from jax.experimental import pallas as pl
from jax.experimental.pallas import tpu as pltpu
from jax.sharding import PartitionSpec as P

HEAD_DIM = 64
LOGICAL = pl.DeviceIdType.LOGICAL
VMEM_BYTES = 62 * 2**20

epsilon = 1e-06
low = jnp.bfloat16
wide = jnp.float32


def round_up(amount, unit):
    return -(-amount // unit) * unit


class Here:
    def __init__(self, dp, tensor):
        self.dp, self.tensor = dp, tensor
        self.d, self.t = lax.axis_index("dp"), lax.axis_index("tensor")
        self.me = self.d * tensor + self.t
        self.chip = lax.div(self.t, 2)
        self.core = self.t - 2 * self.chip
        self.bits, rest = [], self.d
        for _ in range(dp.bit_length() - 1):
            half = lax.div(rest, 2)
            self.bits.append(rest - 2 * half)
            rest = half
        low_bits = sum(bit * (1 << b) for b, bit in enumerate(self.bits[:3]))
        self.near, self.group = low_bits, self.d - low_bits

    def logical(self, dp=None, tensor=None):
        if dp is not None:
            return self.me + (dp - self.d) * self.tensor
        return self.me + (tensor - self.t)

    def bit_flipped(self, b):
        return self.d + (1 - 2 * self.bits[b]) * (1 << b)


def flipped(here, flip_chip, flip_core):
    chip = here.chip + flip_chip - 2 * here.chip * flip_chip
    return 2 * chip + here.core + flip_core - 2 * here.core * flip_core


def two_bits(i):
    high = jnp.where(i >= 2, 1, 0)
    return high, i - 2 * high


def dot(left, right):
    return jnp.dot(left, right, preferred_element_type=wide)


def dot_rows(left, right):
    return lax.dot_general(left, right, (((1,), (1,)), ((), ())), preferred_element_type=wide)


def dot_columns(left, right):
    return lax.dot_general(left, right, (((0,), (0,)), ((), ())), preferred_element_type=wide)


def standardize(values):
    center = values - jnp.mean(values, -1, keepdims=True)
    inverse = lax.rsqrt(jnp.mean(center * center, -1, keepdims=True) + epsilon)
    return center * inverse, inverse


def norm_back(grad, unit, inverse, gain):
    scaled = grad * gain
    return inverse * (
        scaled
        - jnp.mean(scaled, -1, keepdims=True)
        - unit * jnp.mean(scaled * unit, -1, keepdims=True)
    )


def pair(ref, p):
    _, rows, columns = ref.shape
    return ref[pl.ds(2 * p, 2)].reshape(2 * rows, columns)


def set_pair(ref, p, values):
    ref[pl.ds(2 * p, 2)] = values.reshape(2, -1, values.shape[1])


def flat(ref):
    a, b, c = ref.shape
    return ref[...].reshape(a * b, c)


class Links:
    def __init__(self, here, send, recv):
        self.here, self.send, self.recv, self.used, self.pending = here, send, recv, 0, []

    def take(self, amount=1):
        base = self.used
        self.used += amount
        assert self.used <= self.send.shape[0]
        return base

    def copy(self, src, dst, at, **where):
        return pltpu.make_async_remote_copy(
            src_ref=src,
            dst_ref=dst,
            send_sem=self.send.at[at],
            recv_sem=self.recv.at[at],
            device_id=self.here.logical(**where),
            device_id_type=LOGICAL,
        )

    def start(self, src, dst, at, **where):
        copy = self.copy(src, dst, at, **where)
        copy.start()
        self.pending.append(copy)

    def arrived(self, dst, at, **where):
        self.copy(dst, dst, at, **where).wait_recv()

    def finish(self):
        for copy in self.pending:
            copy.wait_send()
        self.pending = []


class Gather:
    def __init__(self, links, buf, here, parts):
        self.links, self.buf, self.t, self.parts = links, buf, here.t, parts
        self.cross, self.diag, self.sib = here.peers
        self.base = links.take(3 * len(parts))

    def view(self, slot, part):
        start, size = self.parts[part]
        return self.buf.at[slot, pl.ds(start, size)]

    def _each(self):
        return range(len(self.parts))

    def start(self, parts=None):
        parts = self._each() if parts is None else parts
        for p in parts:
            v = self.view(self.t, p)
            self.links.copy(v, v, self.base + 3 * p, tensor=self.cross).start()
        for p in parts:
            v = self.view(self.t, p)
            self.links.copy(v, v, self.base + 3 * p + 1, tensor=self.sib).start()

    def wait_sib(self):
        for p in self._each():
            self.links.arrived(self.view(self.sib, p), self.base + 3 * p + 1, tensor=self.sib)

    def forward(self, parts=None):
        for p in self._each() if parts is None else parts:
            v = self.view(self.cross, p)
            self.links.arrived(v, self.base + 3 * p, tensor=self.cross)
            self.links.copy(v, v, self.base + 3 * p + 2, tensor=self.sib).start()

    def wait_diag(self, parts=None):
        for p in self._each() if parts is None else parts:
            self.links.arrived(self.view(self.diag, p), self.base + 3 * p + 2, tensor=self.sib)

    def finish(self):
        for p in self._each():
            v = self.view(self.t, p)
            self.links.copy(v, v, self.base + 3 * p, tensor=self.cross).wait_send()
            self.links.copy(v, v, self.base + 3 * p + 1, tensor=self.sib).wait_send()
            v = self.view(self.cross, p)
            self.links.copy(v, v, self.base + 3 * p + 2, tensor=self.sib).wait_send()


class Reduce:
    def __init__(self, links, part, pre, near, far, here, parts):
        self.links, self.part, self.t, self.parts = links, part, here.t, parts
        self.pre, self.near, self.far = pre, near, far
        self.cross, self.diag, self.sib = here.peers
        self.base = links.take(3 * len(parts))

    def _copy(self, kind, p):
        slot, box, peer = (
            (self.diag, self.pre, self.sib),
            (self.sib, self.near, self.sib),
            (self.cross, self.far, self.cross),
        )[kind]
        rows = pl.ds(*self.parts[p])
        return self.links.copy(
            self.part.at[slot, rows], box.at[rows], self.base + 3 * p + kind, tensor=peer
        )

    def _each(self, parts):
        return range(len(self.parts)) if parts is None else parts

    def send_diag(self, parts=None):
        for p in self._each(parts):
            self._copy(0, p).start()

    def send_sib(self):
        for p in self._each(None):
            self._copy(1, p).start()

    def send_cross(self, parts=None):
        for p in self._each(parts):
            self._copy(0, p).wait_recv()
            rows = pl.ds(*self.parts[p])
            self.part[self.cross, rows] = (
                self.part[self.cross, rows].astype(wide) + self.pre[rows].astype(wide)
            ).astype(low)
            self._copy(2, p).start()

    def result(self, p):
        self._copy(1, p).wait_recv()
        self._copy(2, p).wait_recv()
        rows = pl.ds(*self.parts[p])
        return (
            self.part[self.t, rows].astype(wide)
            + self.near[rows].astype(wide)
            + self.far[rows].astype(wide)
        )

    def finish(self):
        for p in self._each(None):
            for kind in range(3):
                self._copy(kind, p).wait_send()


class DataReduce:
    def __init__(self, links, held, whole, out, box, box_at, first, rows):
        self.links, self.held, self.whole, self.out, self.here = links, held, whole, out, links.here
        count = self.here.dp
        bits = count.bit_length() - 1
        assert count == 1 << bits and bits >= 3
        self.extra = list(range(3, bits))
        self.region = (first, rows, 0, held.shape[1])
        self.trail, self.sent, self.boxes = [], [], []
        for tall, broad in self.sizes(rows, held.shape[1], count)[0]:
            self.boxes.append(box.at[pl.ds(box_at, tall), pl.ds(0, broad)])
            box_at += tall
        self.base = links.take(9 + len(self.extra))
        self.plan()

    @classmethod
    def sizes(cls, rows, columns, count):
        found = cls.boxes_of(rows, columns)
        found += found[-1:] * (count.bit_length() - 1 - 3)
        return found, sum(size[0] for size in found)

    def _bit(self, b):
        return self.here.bits[b]

    def _peer(self, b):
        return self.here.bit_flipped(b)

    def _send(self, src, dst, at, peer):
        copy = self.links.copy(src, dst, self.base + at, dp=peer)
        copy.start()
        self.sent.append(copy)

    def _wait(self, dst, at, peer):
        self.links.arrived(dst, self.base + at, dp=peer)

    @staticmethod
    def _view(ref, region):
        row, rows, column, columns = region
        if columns == ref.shape[1]:
            return ref.at[pl.ds(row, rows)]
        return ref.at[pl.ds(row, rows), pl.ds(column, columns)]

    @staticmethod
    def _part(region, bit):
        row, rows, column, columns = region
        if rows % 32 == 0:
            return (pl.multiple_of(row + bit * (rows // 2), 16), rows // 2, column, columns)
        return (row, rows, pl.multiple_of(column + bit * (columns // 2), 128), columns // 2)

    def _give_half(self, b, box, at):
        bit = self._bit(b)
        self.trail.append(self.region)
        self._send(self._view(self.held, self._part(self.region, 1 - bit)), self.boxes[box], at, self._peer(b))
        self.region = self._part(self.region, bit)

    def _add(self, boxes, last):
        view = self._view(self.held, self.region)
        total = view[...].astype(wide)
        for box in boxes:
            total += self.boxes[box][...].astype(wide)
        if last:
            view = self._view(self.whole, self.region)
        view[...] = total.astype(low)
        if last:
            self._swap()

    def _swap(self):
        view = self._view(self.whole, self.region)
        for k, b in enumerate(self.extra):
            box, at = self.boxes[k - len(self.extra)], 9 + k
            copy = self.links.copy(view, box, self.base + at, dp=self._peer(b))
            copy.start()
            self._wait(box, at, self._peer(b))
            copy.wait_send()
            view[...] = (view[...].astype(wide) + box[...].astype(wide)).astype(low)

    def _give_whole(self, b, at):
        view = self._view(self.whole, self.region)
        self._send(view, view, at, self._peer(b))

    def _take_half(self, b, at):
        outer = self.trail.pop()
        view = self._view(self.whole, self._part(outer, 1 - self._bit(b)))
        self._wait(view, at, self._peer(b))
        self.region = outer

    def _leave(self):
        rows = pl.ds(self.region[0], self.region[1])
        self.left = pltpu.make_async_copy(
            self.whole.at[rows], self.out.at[rows], self.links.send.at[self.base + 8]
        )
        self.left.start()

    def step(self):
        if self.steps:
            self.steps.pop(0)()

    def finish(self):
        assert not self.steps
        self.left.wait()
        for copy in self.sent:
            copy.wait_send()


class Halves(DataReduce):
    order = (1, 0, 2)

    @staticmethod
    def boxes_of(rows, columns):
        found = []
        for _ in range(3):
            if rows % 32 == 0:
                rows //= 2
            else:
                columns //= 2
            found.append((rows, columns))
        return found

    def plan(self):
        a, b, c = self.order
        self.steps = [
            lambda: self._give_half(a, 0, 0),
            lambda: (self._wait_box(a, 0), self._add((0,), False), self._give_half(b, 1, 1)),
            lambda: (self._wait_box(b, 1), self._add((1,), False), self._give_half(c, 2, 2)),
            lambda: (self._wait_box(c, 2), self._add((2,), True), self._give_whole(c, 3)),
            lambda: (self._take_half(c, 3), self._give_whole(b, 4)),
            lambda: (self._take_half(b, 4), self._give_whole(a, 5)),
            lambda: (self._take_half(a, 5), self._leave()),
        ]

    def _wait_box(self, b, box):
        self._wait(self.boxes[box], box, self._peer(b))


class HalvesFromX(Halves):
    order = (0, 1, 2)


class Quarters(DataReduce):
    @staticmethod
    def boxes_of(rows, columns):
        tall, broad = rows // 8, columns
        if tall % 16:
            tall, broad = rows // 4, columns // 2
        return [(rows // 2, columns)] + [(tall, broad)] * 3

    def plan(self):
        self.steps = [
            lambda: self._give_half(0, 0, 0),
            lambda: (self._wait(self.boxes[0], 0, self._peer(0)), self._add((0,), False), self._give_quarters()),
            lambda: (self._take_boxes(), self._add((1, 2, 3), True), self._give_quarter()),
            lambda: (self._take_quarters(), self._give_whole(0, 7)),
            lambda: (self._take_half(0, 7), self._leave()),
        ]

    def _z(self, j):
        low_bit = 1 - self._bit(1) if j % 2 else self._bit(1)
        high = 1 - self._bit(2) if j // 2 else self._bit(2)
        return low_bit, high, self.here.group + high * 4 + low_bit * 2 + self._bit(0)

    def _quarter(self, j):
        low_bit, high, peer = self._z(j)
        return self._part(self._part(self.trail[-1], high), low_bit), peer

    def _give_quarters(self):
        self.trail.append(self.region)
        for j in (1, 2, 3):
            part, peer = self._quarter(j)
            self._send(self._view(self.held, part), self.boxes[j], j, peer)
        self.region = self._quarter(0)[0]

    def _take_boxes(self):
        for j in (1, 2, 3):
            self._wait(self.boxes[j], j, self._z(j)[2])

    def _give_quarter(self):
        view = self._view(self.whole, self.region)
        for j in (1, 2, 3):
            self._send(view, view, 3 + j, self._z(j)[2])

    def _take_quarters(self):
        for j in (1, 2, 3):
            part, peer = self._quarter(j)
            self._wait(self._view(self.whole, part), 3 + j, peer)
        self.region = self.trail.pop()


class Pipeline:
    def __init__(self, plan):
        self.plan, self.members = plan, []

    def add(self, member):
        self.members.append(member)
        member.step()

    def at(self, place):
        for number in self.plan[place]:
            self.members[number].step()

    def finish(self):
        self.at("end")
        for m in self.members:
            while m.steps:
                m.step()
            m.finish()


PLAN = dict(
    waiting=(),
    shared=(1, 0),
    arriving=(),
    h0p0=(2, 1),
    h0p2=(2, 3),
    h0=(1,),
    h1p0=(2, 4),
    h1p2=(3,),
    h1=(4, 2, 6, 3, 0),
    h2p0=(2, 4, 1),
    h2p2=(6, 5),
    h2=(),
    led=(3, 2, 1, 4, 0, 6, 7, 5),
    crossing=(3, 1, 4, 0, 6),
    told=(3, 7, 4, 5),
    end=(0, 6, 7, 5, 6, 7, 0),
)


class Everyone:
    def __init__(self, links, buf, me, count, device):
        self.links, self.buf, self.me, self.count, self.device = links, buf, me, count, device
        self.base = links.take(count)

    def _copy(self, j):
        slot = self.buf.at[self.me]
        peer = self.me + j
        peer = self.device(jnp.where(peer >= self.count, peer - self.count, peer))
        return self.links.copy(slot, slot, self.base + j, dp=peer)

    def _loop(self, act):
        def one(j, carry):
            act(j)
            return carry

        lax.fori_loop(1, self.count, one, 0)

    def start(self, values):
        self.buf[self.me] = values
        self._loop(lambda j: self._copy(j).start())

    def _hear(self, j):
        peer = self.me - j
        peer = jnp.where(peer < 0, peer + self.count, peer)
        self.links.arrived(self.buf.at[peer], self.base + j, dp=self.device(peer))

    def result(self):
        self._loop(self._hear)
        return lax.fori_loop(1, self.count, lambda j, acc: acc + self.buf[j], self.buf[0])

    def finish(self):
        self._loop(lambda j: self._copy(j).wait_send())


def greet(here):
    barrier = pltpu.get_barrier_semaphore()
    for axis, me, count in (("tensor", here.t, here.tensor), ("dp", here.d, here.dp)):

        def one(j, carry, axis=axis, me=me, count=count):
            peer = me + j
            peer = here.logical(**{axis: jnp.where(peer >= count, peer - count, peer)})
            pl.semaphore_signal(barrier, inc=1, device_id=peer, device_id_type=LOGICAL)
            return carry

        lax.fori_loop(1, count, one, 0)


def await_greetings(amount):
    pl.semaphore_wait(pltpu.get_barrier_semaphore(), amount)


def halves(rows):
    first = round_up(rows // 2, 16)
    return ((0, first), (first, rows - first))


def head_masks(shape, local_heads):
    lane = lax.broadcasted_iota(jnp.int32, shape, 1)
    return [
        jnp.where((lane >= h * HEAD_DIM) & (lane < (h + 1) * HEAD_DIM), 1.0, 0.0)
        for h in range(local_heads)
    ], lane


def kernel(n, S):
    here = Here(n.dp, 4)
    t, d = here.t, here.d
    here.peers = peers = [flipped(here, 1, 0), flipped(here, 1, 1), flipped(here, 0, 1)]
    links = Links(here, S.send, S.recv)
    greet(here)
    R, own, W, H, D, K = n.R, n.own, n.W, n.H, n.D, n.K
    split = halves(R)
    vector = lambda ref: ref[...].reshape(1, D)

    fetch = pltpu.make_async_copy(S.cot, S.gt, S.local.at[0])
    load = [
        pltpu.make_async_copy(getattr(S, name + "_far"), getattr(S, name), S.local.at[1 + j])
        for j, name in enumerate(LOADED)
    ]
    fetch.start()
    for copy in load:
        copy.start()
    S.a1[t] = jnp.zeros((R, D), low)
    S.cot4[t] = jnp.zeros((R, D), low)
    S.a24[t] = jnp.zeros((R, D), low)
    S.hl4[t] = jnp.zeros((R, D), low)
    rows_in = Gather(links, S.a1, here, split)
    cot_in = Gather(links, S.cot4, here, split)
    ow_in = Gather(links, S.ow4, here, ((0, W),))
    for p, (start, size) in enumerate(split):
        rows = pl.ds(start, min(size, own - start))
        unit, _ = standardize(S.x[rows, :].astype(wide))
        S.a1[t, rows, :] = (unit * vector(S.g1) + vector(S.b1)).astype(low)
        if p == 0:
            await_greetings(3 + n.dp - 1)
        rows_in.start([p])
    load[0].wait()
    S.ow4[t] = S.ow[...]
    ow_in.start()
    fetch.wait()
    S.cot4[t, 0:own, :] = S.gt[...].astype(low)
    cot_in.start([0])
    load[2].wait()
    load[3].wait()
    S.gw[0:D, :] = jnp.transpose(S.wup[...])
    S.gw[D:, :] = jnp.transpose(S.wdn[...])
    load[1].wait()
    S.v[4 * R :, :] = jnp.zeros((K - 4 * R, H), low)
    length = S.lengths[0]

    chip = here.chip

    def project(i, carry):
        s = flipped(here, *two_bits(i))

        @pl.when(i == 1)
        def _():
            rows_in.wait_sib()

        @pl.when(i == 2)
        def _():
            rows_in.forward()

        @pl.when(i == 3)
        def _():
            rows_in.wait_diag()

        slab = S.a1[s]
        lane = lax.broadcasted_iota(jnp.int32, (R, H - W), 1)
        row = lax.broadcasted_iota(jnp.int32, (R, H - W), 0)
        absent = (row >= own) | (row + s * own >= length)
        at = pl.ds(pl.multiple_of(s * R, 16), R)
        out = dot_rows(slab, S.wqkv[0]) + S.bq[0:1, :]
        S.q[s, :, :W] = (out.astype(low).astype(wide) * HEAD_DIM**-0.5).astype(low)
        S.q[s, :, W:] = jnp.where(lane == 0, HEAD_DIM**-0.5, 0.0).astype(low)
        S.k[at, :W] = dot_rows(slab, S.wqkv[1]).astype(low)
        S.k[at, W:] = jnp.where((lane == 0) & absent, -8e30, 0.0).astype(low)
        S.v[at, :W] = (dot_rows(slab, S.wqkv[2]) + S.bq[1:2, :]).astype(low)
        S.v[at, W:] = jnp.where(lane < 2, 1.0, 0.0).astype(low)
        return carry

    lax.fori_loop(0, 4, project, 0)
    if K > 4 * R:
        lane = lax.broadcasted_iota(jnp.int32, (K - 4 * R, H), 1)
        S.k[4 * R :, :] = jnp.where(lane == W, -8e30, 0.0).astype(low)
    S.kt[...] = jnp.transpose(S.k[...])
    S.vt[...] = jnp.transpose(S.v[...])

    masks, lane = head_masks((1, H), n.heads)
    mix_base = links.take(3)


    def attend(i, carry):
        high, low_bit = two_bits(i)
        s = flipped(here, 1 - high, low_bit + high - 2 * low_bit * high)
        query = S.q[s]
        mixed = jnp.zeros((R, H), wide)
        inverse = jnp.zeros((R, 128), wide)
        first = lax.broadcasted_iota(jnp.int32, (1, 128), 1)

        def score(h):
            here = jnp.where(lane == W, 1.0, masks[h]).astype(low)
            return dot(query * here, S.kt[...])

        ready = score(0)
        for h in range(n.heads):
            scores = ready
            if h + 1 < n.heads:
                ready = score(h + 1)
            terms = jnp.exp(scores - jnp.max(scores, -1, keepdims=True)).astype(low)
            S.e[h, s] = terms
            part = dot(terms, S.v[...])
            scale = 1.0 / part[:, W : W + 1]
            mixed += part * (scale * masks[h])
            inverse = jnp.where(first == h, scale, inverse)
        S.o[s] = mixed
        S.inv[s] = inverse
        S.mix[s] = mixed[:, :W].astype(low)

        @pl.when(i < 3)
        def _():
            links.copy(S.mix.at[s], S.mix4.at[t], mix_base + i, tensor=s).start()

        @pl.when(i == 1)
        def _():
            cot_in.start([1])

        @pl.when(i == 2)
        def _():
            ow_in.wait_sib()
            ow_in.forward()

        return carry

    lax.fori_loop(0, 4, attend, 0)
    ow_in.wait_diag()
    S.mix4[t] = S.mix[t]
    for j, s in enumerate(peers):
        links.arrived(S.mix4.at[s], mix_base + j, tensor=s)

    total = dot(S.mix4[0], S.ow4[0])
    for j in range(1, 4):
        total += dot(S.mix4[j], S.ow4[j])
    total = S.x[...].astype(wide) + (total[:own] + vector(S.ob))
    S.hid[...] = total
    unit, _ = standardize(total)
    S.a24[t, 0:own, :] = (unit * vector(S.g2) + vector(S.b2)).astype(low)
    next_in = Gather(links, S.a24, here, halves(R))
    next_in.start()
    back = Reduce(links, S.part, S.pre1, S.near1, S.far1, here, split)
    ahead = Reduce(links, S.fop, S.pre2, S.near2, S.far2, here, split)
    S.gub[...] = jnp.zeros_like(S.gub)

    def feed(s, start, size):
        rows = pl.ds(start, size)
        up = dot(S.a24[s, rows], S.wup[...]) + vector(S.bup)
        square = up * up
        c = 0.7978845608028654
        bend = jnp.tanh(c * up * (1.0 + 0.044715 * square))
        half = 0.5 * (1.0 + bend)
        slope = half + 0.5 * up * (1.0 - bend * bend) * (c + (3 * 0.044715 * c) * square)
        active = (up * half).astype(low)
        S.pool[s, rows, 0:D] = active
        grad = (dot(S.cot4[s, rows], S.gw[D:, :]) * slope).astype(low)
        S.gup[s, rows] = grad
        S.part[s, rows] = dot(grad, S.gw[0:D, :]).astype(low)
        S.gub[...] += jnp.sum(grad.astype(wide), 0, keepdims=True)

    def lead_out(s, start, size):
        rows = pl.ds(start, size)
        S.fop[s, rows] = dot(S.pool[s, rows, 0:D], S.wdn[...]).astype(low)

    def feed_here(i, carry):
        s = flipped(here, 0, i)

        @pl.when(i == 1)
        def _():
            next_in.wait_sib()
            cot_in.wait_sib()

        feed(s, 0, R)

        @pl.when(i == 1)
        def _():
            back.send_sib()

        lead_out(s, 0, R)
        return carry

    lax.fori_loop(0, 2, feed_here, 0)
    ahead.send_sib()
    for p in (0, 1):

        def feed_there(i, carry, p=p):
            @pl.when(i == 0)
            def _():
                cot_in.forward([p])
                next_in.forward([p])

            @pl.when(i == 1)
            def _():
                cot_in.wait_diag([p])
                next_in.wait_diag([p])

            feed(flipped(here, 1, i), *split[p])
            if p == 1:

                @pl.when(i == 0)
                def _():
                    back.send_cross([0])

            return carry

        lax.fori_loop(0, 2, feed_there, 0)
        back.send_diag([p])
    for i in (0, 1):
        lead_out(flipped(here, 1, i), 0, R)
    back.send_cross([1])
    ahead.send_diag()

    sums = Pipeline(PLAN)
    tile = D // 2
    box_at = 0

    def sum_over_dp(kind, held, whole, out, first, rows):
        nonlocal box_at
        sums.add(kind(links, held, whole, out, S.box, box_at, first, rows))
        box_at += kind.sizes(rows, D, n.dp)[1]

    for left, right, first in ((S.a24, S.gup, 0), (S.pool, S.cot4, D)):
        rows = left[:, :, 0:D].reshape(4 * R, D)
        S.gw[first : first + D, :] = dot_columns(rows, flat(right)).astype(low)
        for at in (first, first + tile):
            kind = Halves if at == 0 else HalvesFromX
            sum_over_dp(kind, S.gw, S.sum1, S.whole1, at, tile)

    sums.at("waiting")
    S.small[...] = jnp.zeros_like(S.small)
    gm_base = links.take(6)
    shared = lambda s, p, j: links.copy(
        S.mix4.at[s, pl.ds(*split[p])], S.gm4.at[t, pl.ds(*split[p])], gm_base + 3 * p + j, tensor=peers[j]
    )
    for p, (start, size) in enumerate(split):
        real = min(size, own - start)
        rows = pl.ds(start, real)
        grad = back.result(p)[:real]
        unit, inverse = standardize(S.hid[rows])
        S.small[2:3, :] += jnp.sum(grad * unit, 0, keepdims=True)
        S.small[3:4, :] += jnp.sum(grad, 0, keepdims=True)
        S.gt[rows] += norm_back(grad, unit, inverse, vector(S.g2))
        S.hl4[t, rows] = S.gt[rows].astype(low)
        rows = pl.ds(start, size)
        for j, s in enumerate(peers + [t]):
            product = dot_rows(S.hl4[t, rows], S.ow4[s]).astype(low)
            if j < 3:
                S.mix4[s, rows] = product
                shared(s, p, j).start()
            else:
                S.gm4[t, rows] = product
    S.small[4:5, :] = jnp.sum(S.hl4[t].astype(wide), 0, keepdims=True)
    S.small[5:6, :] = jnp.sum(S.cot4[t].astype(wide), 0, keepdims=True)
    S.small[6:7, :] = S.gub[...]
    hl_in = Gather(links, S.hl4, here, halves(R))

    next_in.finish()
    S.do[...] = jnp.zeros_like(S.do)
    S.qt[...] = jnp.transpose(flat(S.q))
    sums.at("shared")

    def prepare(i, s):
        if i > 0:
            j = (None, 2, 0, 1)[i]
            for p in (0, 1):
                rows = pl.ds(*split[p])
                links.arrived(S.gm4.at[s, rows], gm_base + 3 * p + j, tensor=peers[j])
        S.do[:, :W] = S.gm4[s].astype(wide)
        inverse = sum(S.inv[s, :, h : h + 1] * masks[h] for h in range(n.heads))
        scaled = (S.do[...] * inverse).astype(low)
        S.v[pl.ds(pl.multiple_of(s * R, 16), R), :] = scaled
        scaled = scaled.astype(wide)
        product = scaled * S.o[s]
        for h in range(n.heads):
            inner = -jnp.sum(product * masks[h], -1, keepdims=True)
            upper = inner.astype(low).astype(wide)
            S.a24[s, :, h * H : (h + 1) * H] = (
                scaled * masks[h]
                + jnp.where(lane == W, upper, 0.0)
                + jnp.where(lane == W + 1, inner - upper, 0.0)
            ).astype(low)

    def pull(h, p):
        grad_p = dot(pair(S.a24.at[:, :, h * H : (h + 1) * H], p), S.vt[...])
        grad_s = (pair(S.e.at[h], p).astype(wide) * grad_p).astype(low)
        set_pair(S.pool, p, grad_s)
        dq = dot(grad_s, S.k[...]) * (masks[h] * HEAD_DIM**-0.5)
        if h > 0:
            dq += pair(S.gup.at[:, :, 0:H], p).astype(wide)
        S.gup[pl.ds(2 * p, 2), :, 0:H] = dq.astype(low).reshape(2, R, H)

    def weights(h):
        at = slice(h * HEAD_DIM, (h + 1) * HEAD_DIM)
        tile = h * HEAD_DIM // 128 * 128
        dqt = jnp.transpose(flat(S.gup.at[:, :, tile : tile + 128]))
        left = jnp.concatenate(
            [dqt[h * HEAD_DIM - tile : (h + 1) * HEAD_DIM - tile], S.qt[at, :], S.kt[at, : 4 * R]], 0
        )
        out = dot(left, flat(S.a1))
        S.gw2[h * W : (h + 1) * W, :] = out.astype(low)
        for c in range(3):
            product = out[c * HEAD_DIM : (c + 1) * HEAD_DIM] * S.wqkv[c, at, :].astype(wide)
            S.small[0:1, :] += jnp.sum(product, 0, keepdims=True)
        kind = HalvesFromX if h + 1 < n.heads else Quarters
        sum_over_dp(kind, S.gw2, S.sum2, S.whole2, h * W, W)

    for h in range(n.heads):
        for i in (0, 2):
            if (h, i) == (0, 2):
                sums.at("arriving")
            if h == 0:
                prepare(i, flipped(here, i // 2, 0))
                prepare(i + 1, flipped(here, i // 2, 1))
            if (h, i) == (0, 2):
                hl_in.start()
            pull(h, chip if i == 0 else 1 - chip)
            sums.at(f"h{h}p{i}")
            if (h, i) == (1, 0):
                hl_in.wait_sib()
                hl_in.forward()
                ahead.send_cross()
            elif (h, i) == (1, 2):
                hl_in.wait_diag()
                S.gw2[3 * W :, :] = dot_columns(flat(S.mix), flat(S.hl4)).astype(low)
                sum_over_dp(Quarters, S.gw2, S.sum2, S.whole2, 3 * W, W)
        if h == 0:
            S.v[4 * R :, :] = jnp.zeros((K - 4 * R, H), low)
            S.kt[...] = jnp.transpose(S.v[...])
        at = slice(h * HEAD_DIM, (h + 1) * HEAD_DIM)
        S.qt[at, :] = dot(S.qt[at, :], flat(S.pool))[:, : 4 * R].astype(low)
        S.kt[at, : 4 * R] = dot(S.kt[at, : 4 * R], flat(S.e.at[h]))[:, : 4 * R].astype(low)
        if h + 1 < n.heads:
            weights(h)
        sums.at(f"h{h}")

    pad = jnp.zeros((R, H - W), low)
    for part, grad_t in ((1, S.qt), (2, S.kt)):
        rows = jnp.transpose(grad_t[:W, : 4 * R])
        for s in range(4):
            S.gup[s, :, part * H : part * H + W] = rows[s * R : (s + 1) * R]
            S.gup[s, :, part * H + W : (part + 1) * H] = pad

    back.finish()
    down = Reduce(links, S.part, S.pre1, S.near1, S.far1, here, split)

    def lead(s, start, size):
        rows = pl.ds(start, size)
        out = dot(S.gup[s, rows, 0:W], S.wqkv[0])
        out += dot(S.gup[s, rows, H : H + W], S.wqkv[1])
        out += dot(S.gup[s, rows, 2 * H : 2 * H + W], S.wqkv[2])
        S.part[s, rows] = out.astype(low)

    cross, diag, sib = peers
    lead(diag, *split[0])
    down.send_diag([0])
    lead(cross, *split[0])
    weights(n.heads - 1)
    down.send_cross([0])
    lead(diag, *split[1])
    down.send_diag([1])
    lead(cross, *split[1])
    down.send_cross([1])
    lead(sib, 0, R)
    down.send_sib()
    lead(t, 0, R)
    columns = jnp.sum(flat(S.gup).astype(wide), 0, keepdims=True)
    S.small[7:8, 0:H] = columns[:, 0:H]
    S.small[7:8, H : 2 * H] = columns[:, 2 * H :]
    upper = columns.astype(low)
    both = jnp.concatenate([upper.astype(wide), columns - upper.astype(wide)], 0).astype(low)
    for c in range(3):
        product = dot(both[:, c * H : c * H + W], S.wqkv[c])
        S.small[1:2, :] += jnp.sum(product, 0, keepdims=True)

    S.small4[t] = S.small[...]
    base3 = links.take(3)
    for j in range(3):
        links.start(S.small4.at[t], S.small4.at[t], base3 + j, tensor=peers[j])
    sums.at("led")
    result = jnp.concatenate([ahead.result(0), ahead.result(1)], 0)
    S.output[...] = (S.hid[...] + (result[:own] + vector(S.db))).astype(low)
    sums.at("crossing")

    unit, inverse = standardize(S.x[...].astype(wide))
    grad = jnp.concatenate([down.result(0), down.result(1)], 0)[:own]
    for j in range(3):
        links.arrived(S.small4.at[peers[j]], base3 + j, tensor=peers[j])
    over = S.small4[0] + S.small4[1] + S.small4[2] + S.small4[3]
    row = lax.broadcasted_iota(jnp.int32, over.shape, 0)
    near = min(8, n.dp)
    inner = Everyone(links, S.smalls, here.near, near, lambda j: here.group + j)
    inner.start(jnp.where(row < 6, over, S.small[...]))
    S.gt[...] += norm_back(grad, unit, inverse, vector(S.g1))
    sums.at("told")
    sums.finish()
    total = inner.result()
    inner.finish()
    if n.dp > near:
        outer = Everyone(links, S.smalls2, lax.div(here.group, near), n.dp // near, lambda j: j * near + here.near)
        outer.start(total)
        total = outer.result()
        outer.finish()
    S.small_sum[...] = total
    S.small_sum[0:1, :] = (total[0:1, :] - vector(S.b1) * total[1:2, :]) / vector(S.g1)
    for j, s in enumerate(peers):
        links.copy(S.mix.at[s], S.mix4.at[t], mix_base + j, tensor=s).wait_send()
        for p in (0, 1):
            shared(s, p, j).wait_send()
    for transfer in (rows_in, cot_in, ow_in, hl_in, ahead, down):
        transfer.finish()
    links.finish()


LOADED = ("ow", "wqkv", "wup", "wdn")
SMALL = ("gain1", "shift1", "gain2", "shift2", "bias_out", "bias_down", "bias_up", "bias_qv")


def finish(n, output, gt, small, whole1, whole2):
    D, W, H = n.D, n.W, n.H
    steps = n.heads
    rows1 = D // steps

    def spread(output, gt, small, up, down, head, out, *refs):
        to_output, to_gt, to_up, to_down, to_qkv, to_out = refs[:6]
        vectors, sems = refs[6:14], refs[14]
        i = pl.program_id(0)
        held = refs[15:]
        come = [pltpu.make_async_copy(a, b, sems.at[j]) for j, (a, b) in enumerate(zip((output, gt), held))]
        go = [
            pltpu.make_async_copy(a, b, sems.at[2 + j])
            for j, (a, b) in enumerate(zip(held, (to_output, to_gt)))
        ]

        @pl.when(i == 0)
        def _():
            for copy in come:
                copy.start()
            for j in range(7):
                vectors[j][...] = small[j : j + 1, :].reshape(D)
            vectors[7][0:1, :] = small[7:8, :W]
            vectors[7][1:2, :] = small[7:8, H : H + W]

        to_up[...] = up[...].astype(wide)
        to_down[...] = down[...].astype(wide)
        for j in range(3):
            to_qkv[j] = head[j * HEAD_DIM : (j + 1) * HEAD_DIM, :].astype(wide)
        to_out[...] = out[...].astype(wide)

        @pl.when(i == 1)
        def _():
            for first, second in zip(come, go):
                first.wait()
                second.start()

        @pl.when(i == steps - 1)
        def _():
            for copy in go:
                copy.wait()

    hbm = pl.BlockSpec(memory_space=pl.ANY)
    whole = pl.BlockSpec(memory_space=pltpu.VMEM)
    at_row = lambda rows, index: pl.BlockSpec((rows, D), lambda i: (index(i), 0))
    shape = jax.ShapeDtypeStruct
    return pl.pallas_call(
        spread,
        grid=(steps,),
        out_shape=[shape(output.shape, low), shape(gt.shape, wide)]
        + [shape((D, D), wide)] * 2
        + [shape((3, W, D), wide), shape((W, D), wide)]
        + [shape((D,), wide)] * 7
        + [shape((2, W), wide)],
        in_specs=[hbm, hbm, whole, at_row(rows1, lambda i: i), at_row(rows1, lambda i: i + steps)]
        + [at_row(W, lambda i: i), at_row(HEAD_DIM, lambda i: 3 * steps + i)],
        out_specs=[hbm, hbm]
        + [at_row(rows1, lambda i: i)] * 2
        + [pl.BlockSpec((3, HEAD_DIM, D), lambda i: (0, i, 0)), at_row(HEAD_DIM, lambda i: i)]
        + [whole] * 8,
        scratch_shapes=[
            pltpu.SemaphoreType.DMA((4,)),
            pltpu.VMEM(output.shape, low),
            pltpu.VMEM(gt.shape, wide),
        ],
    )(output, gt, small, whole1, whole1, whole2, whole2)


def body(
    tokens,
    lengths,
    ln1_gain,
    ln1_shift,
    qkv_weight,
    qv_bias,
    out_weight,
    out_bias,
    ln2_gain,
    ln2_shift,
    up_weight,
    up_bias,
    down_weight,
    down_bias,
    cotangent,
):
    own, D = tokens.shape
    W = qkv_weight.shape[2]
    F = up_weight.shape[1]
    dp = lax.axis_size("dp")
    assert lax.axis_size("tensor") == 4 and lengths.shape[0] == 1 and F == D and 4 * W == D and 3 * round_up(W + 2, 128) == D
    R = round_up(own, 16)
    H = round_up(W + 2, 128)
    K = round_up(4 * R, 256)
    heads = W // HEAD_DIM
    extra = dp.bit_length() - 1 - 3
    n = types.SimpleNamespace(
        own=own, D=D, W=W, R=R, H=H, K=K, dp=dp, heads=heads, extra=extra
    )
    weights = dict(ow=out_weight, wqkv=jnp.transpose(qkv_weight, (1, 2, 0)), wup=up_weight, wdn=down_weight)
    given = dict(
        x=tokens, lengths=lengths, g1=ln1_gain, b1=ln1_shift,
        bq=qv_bias, ob=out_bias, g2=ln2_gain, b2=ln2_shift, bup=up_bias, db=down_bias,
        cot=cotangent,
    )
    given.update({name + "_far": weights[name] for name in LOADED})
    outs = dict(
        output=((own, D), low), gt=((own, D), wide), small_sum=((8, D), wide),
        whole1=((2 * D, D), low), whole2=((D, D), low),
    )
    rows4 = ((4, R, D), low)
    slab = ((R, D), low)
    chunks = [(Halves, D // 2)] * 4 + [(Halves, W)] * 2 + [(Quarters, W)] * 2
    scratch = dict(
        a1=rows4, cot4=rows4, ow4=((4, W, D), low), q=((4, R, H), low), k=((K, H), low),
        v=((K, H), low), kt=((H, K), low), vt=((H, K), low), e=((heads, 4, R, K), low),
        o=((4, R, H), wide), inv=((4, R, 128), wide), mix=((4, R, W), low), mix4=((4, R, W), low),
        hid=((own, D), wide),
        a24=rows4, pool=((4, R, K), low), gup=rows4, part=rows4,
        fop=rows4, pre1=slab, near1=slab, far1=slab, pre2=slab, near2=slab, far2=slab,
        gw=((2 * D, D), low), gub=((1, D), wide),
        small=((8, D), wide), hl4=rows4,
        gm4=((4, R, W), low), qt=((H, 4 * R), low), do=((R, H), wide),
        gw2=((D, D), low),
        small4=((4, 8, D), wide), smalls=((min(8, dp), 8, D), wide),
        box=((sum(kind.sizes(r, D, dp)[1] for kind, r in chunks), D), low),
        sum1=((2 * D, D), low), sum2=((D, D), low),
    )
    scratch.update({name: (weights[name].shape, low) for name in LOADED})
    if dp > 8:
        scratch["smalls2"] = ((dp // 8, 8, D), wide)
    sems = 180 + dp + 8 * extra
    names = list(given) + list(outs) + list(scratch) + ["local", "send", "recv"]
    vmem = pl.BlockSpec(memory_space=pltpu.VMEM)
    smem = pl.BlockSpec(memory_space=pltpu.SMEM)
    hbm = pl.BlockSpec(memory_space=pl.ANY)
    output, gt, small, whole1, whole2 = pl.pallas_call(
        lambda *refs: kernel(n, types.SimpleNamespace(**dict(zip(names, refs)))),
        out_shape=tuple(jax.ShapeDtypeStruct(*spec) for spec in outs.values()),
        in_specs=[
            hbm if name.endswith("_far") else dict(lengths=smem, cot=hbm).get(name, vmem) for name in given
        ],
        out_specs=tuple(hbm if name in ("whole1", "whole2") else vmem for name in outs),
        scratch_shapes=[pltpu.VMEM(*spec) for spec in scratch.values()]
        + [pltpu.SemaphoreType.DMA((5,))] + [pltpu.SemaphoreType.DMA((sems,))] * 2,
        compiler_params=pltpu.CompilerParams(
            collective_id=0, has_side_effects=True, vmem_limit_bytes=VMEM_BYTES
        ),
    )(*given.values())
    finished = finish(n, output, gt, small, whole1, whole2)
    small_rows = dict(zip(SMALL, finished[6:]))
    return (
        finished[0],
        finished[1],
        small_rows["gain1"],
        small_rows["shift1"],
        jnp.transpose(finished[4], (2, 0, 1)),
        small_rows["bias_qv"],
        finished[5],
        small_rows["bias_out"],
        small_rows["gain2"],
        small_rows["shift2"],
        finished[2],
        small_rows["bias_up"],
        finished[3],
        small_rows["bias_down"],
    )


def solution(mesh):
    placed = (
        P(("dp", "tensor"), None),
        P("dp"),
        P(),
        P(),
        P(None, None, "tensor"),
        P(None, "tensor"),
        P("tensor", None),
        P(),
        P(),
        P(),
        P(None, "tensor"),
        P("tensor"),
        P("tensor", None),
        P(),
        P(("dp", "tensor"), None),
    )
    return jax.shard_map(
        body,
        mesh=mesh,
        in_specs=placed,
        out_specs=(
            P(("dp", "tensor"), None),
            P(("dp", "tensor"), None),
            P(),
            P(),
            P(None, None, "tensor"),
            P(None, "tensor"),
            P("tensor", None),
            P(),
            P(),
            P(),
            P(None, "tensor"),
            P("tensor"),
            P("tensor", None),
            P(),
        ),
        check_vma=False,
    )
```

```python
import types

import jax
import jax.numpy as jnp
from jax import lax
from jax.experimental import pallas as pl
from jax.experimental.pallas import tpu as pltpu
from jax.sharding import PartitionSpec as P

HEAD_DIM = 64
LOGICAL = pl.DeviceIdType.LOGICAL
VMEM_BYTES = 62 * 2**20

epsilon = 1e-06
low = jnp.bfloat16
wide = jnp.float32


def round_up(amount, unit):
    return -(-amount // unit) * unit


class Here:
    def __init__(self, dp, tensor):
        self.dp, self.tensor = dp, tensor
        self.d, self.t = lax.axis_index("dp"), lax.axis_index("tensor")
        self.me = self.d * tensor + self.t
        self.chip = lax.div(self.t, 2)
        self.core = self.t - 2 * self.chip
        self.bits, rest = [], self.d
        for _ in range(dp.bit_length() - 1):
            half = lax.div(rest, 2)
            self.bits.append(rest - 2 * half)
            rest = half
        low_bits = sum(bit * (1 << b) for b, bit in enumerate(self.bits[:3]))
        self.near, self.group = low_bits, self.d - low_bits

    def logical(self, dp=None, tensor=None):
        if dp is not None:
            return self.me + (dp - self.d) * self.tensor
        return self.me + (tensor - self.t)

    def bit_flipped(self, b):
        return self.d + (1 - 2 * self.bits[b]) * (1 << b)


def flipped(here, flip_chip, flip_core):
    chip = here.chip + flip_chip - 2 * here.chip * flip_chip
    return 2 * chip + here.core + flip_core - 2 * here.core * flip_core


def two_bits(i):
    high = jnp.where(i >= 2, 1, 0)
    return high, i - 2 * high


def dot(left, right):
    return jnp.dot(left, right, preferred_element_type=wide)


def dot_rows(left, right):
    return lax.dot_general(left, right, (((1,), (1,)), ((), ())), preferred_element_type=wide)


def dot_columns(left, right):
    return lax.dot_general(left, right, (((0,), (0,)), ((), ())), preferred_element_type=wide)


def standardize(values):
    center = values - jnp.mean(values, -1, keepdims=True)
    inverse = lax.rsqrt(jnp.mean(center * center, -1, keepdims=True) + epsilon)
    return center * inverse, inverse


def norm_back(grad, unit, inverse, gain):
    scaled = grad * gain
    return inverse * (
        scaled
        - jnp.mean(scaled, -1, keepdims=True)
        - unit * jnp.mean(scaled * unit, -1, keepdims=True)
    )


def pair(ref, p):
    _, rows, columns = ref.shape
    return ref[pl.ds(2 * p, 2)].reshape(2 * rows, columns)


def set_pair(ref, p, values):
    ref[pl.ds(2 * p, 2)] = values.reshape(2, -1, values.shape[1])


def flat(ref):
    a, b, c = ref.shape
    return ref[...].reshape(a * b, c)


class Links:
    def __init__(self, here, send, recv):
        self.here, self.send, self.recv, self.used, self.pending = here, send, recv, 0, []

    def take(self, amount=1):
        base = self.used
        self.used += amount
        assert self.used <= self.send.shape[0]
        return base

    def copy(self, src, dst, at, **where):
        return pltpu.make_async_remote_copy(
            src_ref=src,
            dst_ref=dst,
            send_sem=self.send.at[at],
            recv_sem=self.recv.at[at],
            device_id=self.here.logical(**where),
            device_id_type=LOGICAL,
        )

    def start(self, src, dst, at, **where):
        copy = self.copy(src, dst, at, **where)
        copy.start()
        self.pending.append(copy)

    def arrived(self, dst, at, **where):
        self.copy(dst, dst, at, **where).wait_recv()

    def finish(self):
        for copy in self.pending:
            copy.wait_send()
        self.pending = []


class Gather:
    def __init__(self, links, buf, here, parts):
        self.links, self.buf, self.t, self.parts = links, buf, here.t, parts
        self.cross, self.diag, self.sib = here.peers
        self.base = links.take(3 * len(parts))

    def view(self, slot, part):
        start, size = self.parts[part]
        return self.buf.at[slot, pl.ds(start, size)]

    def _each(self):
        return range(len(self.parts))

    def start(self, parts=None):
        parts = self._each() if parts is None else parts
        for p in parts:
            v = self.view(self.t, p)
            self.links.copy(v, v, self.base + 3 * p, tensor=self.cross).start()
        for p in parts:
            v = self.view(self.t, p)
            self.links.copy(v, v, self.base + 3 * p + 1, tensor=self.sib).start()

    def wait_sib(self):
        for p in self._each():
            self.links.arrived(self.view(self.sib, p), self.base + 3 * p + 1, tensor=self.sib)

    def forward(self, parts=None):
        for p in self._each() if parts is None else parts:
            v = self.view(self.cross, p)
            self.links.arrived(v, self.base + 3 * p, tensor=self.cross)
            self.links.copy(v, v, self.base + 3 * p + 2, tensor=self.sib).start()

    def wait_diag(self, parts=None):
        for p in self._each() if parts is None else parts:
            self.links.arrived(self.view(self.diag, p), self.base + 3 * p + 2, tensor=self.sib)

    def finish(self):
        for p in self._each():
            v = self.view(self.t, p)
            self.links.copy(v, v, self.base + 3 * p, tensor=self.cross).wait_send()
            self.links.copy(v, v, self.base + 3 * p + 1, tensor=self.sib).wait_send()
            v = self.view(self.cross, p)
            self.links.copy(v, v, self.base + 3 * p + 2, tensor=self.sib).wait_send()


class Reduce:
    def __init__(self, links, part, pre, near, far, here, parts):
        self.links, self.part, self.t, self.parts = links, part, here.t, parts
        self.pre, self.near, self.far = pre, near, far
        self.cross, self.diag, self.sib = here.peers
        self.base = links.take(3 * len(parts))

    def _copy(self, kind, p):
        slot, box, peer = (
            (self.diag, self.pre, self.sib),
            (self.sib, self.near, self.sib),
            (self.cross, self.far, self.cross),
        )[kind]
        rows = pl.ds(*self.parts[p])
        return self.links.copy(
            self.part.at[slot, rows], box.at[rows], self.base + 3 * p + kind, tensor=peer
        )

    def _each(self, parts):
        return range(len(self.parts)) if parts is None else parts

    def send_diag(self, parts=None):
        for p in self._each(parts):
            self._copy(0, p).start()

    def send_sib(self):
        for p in self._each(None):
            self._copy(1, p).start()

    def send_cross(self, parts=None):
        for p in self._each(parts):
            self._copy(0, p).wait_recv()
            rows = pl.ds(*self.parts[p])
            self.part[self.cross, rows] = (
                self.part[self.cross, rows].astype(wide) + self.pre[rows].astype(wide)
            ).astype(low)
            self._copy(2, p).start()

    def result(self, p):
        self._copy(1, p).wait_recv()
        self._copy(2, p).wait_recv()
        rows = pl.ds(*self.parts[p])
        return (
            self.part[self.t, rows].astype(wide)
            + self.near[rows].astype(wide)
            + self.far[rows].astype(wide)
        )

    def finish(self):
        for p in self._each(None):
            for kind in range(3):
                self._copy(kind, p).wait_send()


class DataReduce:
    def __init__(self, links, held, whole, out, box, box_at, first, rows):
        self.links, self.held, self.whole, self.out, self.here = links, held, whole, out, links.here
        count = self.here.dp
        bits = count.bit_length() - 1
        assert count == 1 << bits and bits >= 3
        self.extra = list(range(3, bits))
        self.region = (first, rows, 0, held.shape[1])
        self.trail, self.sent, self.boxes = [], [], []
        for tall, broad in self.sizes(rows, held.shape[1], count)[0]:
            self.boxes.append(box.at[pl.ds(box_at, tall), pl.ds(0, broad)])
            box_at += tall
        self.base = links.take(9 + len(self.extra))
        self.plan()

    @classmethod
    def sizes(cls, rows, columns, count):
        found = cls.boxes_of(rows, columns)
        found += found[-1:] * (count.bit_length() - 1 - 3)
        return found, sum(size[0] for size in found)

    def _bit(self, b):
        return self.here.bits[b]

    def _peer(self, b):
        return self.here.bit_flipped(b)

    def _send(self, src, dst, at, peer):
        copy = self.links.copy(src, dst, self.base + at, dp=peer)
        copy.start()
        self.sent.append(copy)

    def _wait(self, dst, at, peer):
        self.links.arrived(dst, self.base + at, dp=peer)

    @staticmethod
    def _view(ref, region):
        row, rows, column, columns = region
        if columns == ref.shape[1]:
            return ref.at[pl.ds(row, rows)]
        return ref.at[pl.ds(row, rows), pl.ds(column, columns)]

    @staticmethod
    def _part(region, bit):
        row, rows, column, columns = region
        if rows % 32 == 0:
            return (pl.multiple_of(row + bit * (rows // 2), 16), rows // 2, column, columns)
        return (row, rows, pl.multiple_of(column + bit * (columns // 2), 128), columns // 2)

    def _give_half(self, b, box, at):
        bit = self._bit(b)
        self.trail.append(self.region)
        self._send(self._view(self.held, self._part(self.region, 1 - bit)), self.boxes[box], at, self._peer(b))
        self.region = self._part(self.region, bit)

    def _add(self, boxes, last):
        view = self._view(self.held, self.region)
        total = view[...].astype(wide)
        for box in boxes:
            total += self.boxes[box][...].astype(wide)
        if last:
            view = self._view(self.whole, self.region)
        view[...] = total.astype(low)
        if last:
            self._swap()

    def _swap(self):
        view = self._view(self.whole, self.region)
        for k, b in enumerate(self.extra):
            box, at = self.boxes[k - len(self.extra)], 9 + k
            copy = self.links.copy(view, box, self.base + at, dp=self._peer(b))
            copy.start()
            self._wait(box, at, self._peer(b))
            copy.wait_send()
            view[...] = (view[...].astype(wide) + box[...].astype(wide)).astype(low)

    def _give_whole(self, b, at):
        view = self._view(self.whole, self.region)
        self._send(view, view, at, self._peer(b))

    def _take_half(self, b, at):
        outer = self.trail.pop()
        view = self._view(self.whole, self._part(outer, 1 - self._bit(b)))
        self._wait(view, at, self._peer(b))
        self.region = outer

    def _leave(self):
        rows = pl.ds(self.region[0], self.region[1])
        self.left = pltpu.make_async_copy(
            self.whole.at[rows], self.out.at[rows], self.links.send.at[self.base + 8]
        )
        self.left.start()

    def step(self):
        if self.steps:
            self.steps.pop(0)()

    def finish(self):
        assert not self.steps
        self.left.wait()
        for copy in self.sent:
            copy.wait_send()


class Halves(DataReduce):
    order = (1, 0, 2)

    @staticmethod
    def boxes_of(rows, columns):
        found = []
        for _ in range(3):
            if rows % 32 == 0:
                rows //= 2
            else:
                columns //= 2
            found.append((rows, columns))
        return found

    def plan(self):
        a, b, c = self.order
        self.steps = [
            lambda: self._give_half(a, 0, 0),
            lambda: (self._wait_box(a, 0), self._add((0,), False), self._give_half(b, 1, 1)),
            lambda: (self._wait_box(b, 1), self._add((1,), False), self._give_half(c, 2, 2)),
            lambda: (self._wait_box(c, 2), self._add((2,), True), self._give_whole(c, 3)),
            lambda: (self._take_half(c, 3), self._give_whole(b, 4)),
            lambda: (self._take_half(b, 4), self._give_whole(a, 5)),
            lambda: (self._take_half(a, 5), self._leave()),
        ]

    def _wait_box(self, b, box):
        self._wait(self.boxes[box], box, self._peer(b))


class HalvesFromX(Halves):
    order = (0, 1, 2)


class Quarters(DataReduce):
    @staticmethod
    def boxes_of(rows, columns):
        tall, broad = rows // 8, columns
        if tall % 16:
            tall, broad = rows // 4, columns // 2
        return [(rows // 2, columns)] + [(tall, broad)] * 3

    def plan(self):
        self.steps = [
            lambda: self._give_half(0, 0, 0),
            lambda: (self._wait(self.boxes[0], 0, self._peer(0)), self._add((0,), False), self._give_quarters()),
            lambda: (self._take_boxes(), self._add((1, 2, 3), True), self._give_quarter()),
            lambda: (self._take_quarters(), self._give_whole(0, 7)),
            lambda: (self._take_half(0, 7), self._leave()),
        ]

    def _z(self, j):
        low_bit = 1 - self._bit(1) if j % 2 else self._bit(1)
        high = 1 - self._bit(2) if j // 2 else self._bit(2)
        return low_bit, high, self.here.group + high * 4 + low_bit * 2 + self._bit(0)

    def _quarter(self, j):
        low_bit, high, peer = self._z(j)
        return self._part(self._part(self.trail[-1], high), low_bit), peer

    def _give_quarters(self):
        self.trail.append(self.region)
        for j in (1, 2, 3):
            part, peer = self._quarter(j)
            self._send(self._view(self.held, part), self.boxes[j], j, peer)
        self.region = self._quarter(0)[0]

    def _take_boxes(self):
        for j in (1, 2, 3):
            self._wait(self.boxes[j], j, self._z(j)[2])

    def _give_quarter(self):
        view = self._view(self.whole, self.region)
        for j in (1, 2, 3):
            self._send(view, view, 3 + j, self._z(j)[2])

    def _take_quarters(self):
        for j in (1, 2, 3):
            part, peer = self._quarter(j)
            self._wait(self._view(self.whole, part), 3 + j, peer)
        self.region = self.trail.pop()


class Pipeline:
    def __init__(self, plan):
        self.plan, self.members = plan, []

    def add(self, member):
        self.members.append(member)
        member.step()

    def at(self, place):
        for number in self.plan[place]:
            self.members[number].step()

    def finish(self):
        self.at("end")
        for m in self.members:
            while m.steps:
                m.step()
            m.finish()


PLAN = dict(
    waiting=(),
    shared=(0,),
    arriving=(2, 0),
    h0p0=(),
    h0p2=(2, 1, 3, 0),
    h0=(1, 3, 2),
    h1p0=(0,),
    h1p2=(1,),
    h1=(3, 4, 0, 2, 6, 5),
    h2p0=(1,),
    h2p2=(3, 7, 2, 0, 6, 4, 5),
    h2=(3,),
    led=(6, 2, 8, 7, 5, 4),
    crossing=(6, 3, 8),
    told=(1,),
    end=(4, 6, 5, 7, 8, 6, 7, 1, 8),
)


class Everyone:
    def __init__(self, links, buf, me, count, device):
        self.links, self.buf, self.me, self.count, self.device = links, buf, me, count, device
        self.base = links.take(count)

    def _copy(self, j):
        slot = self.buf.at[self.me]
        peer = self.me + j
        peer = self.device(jnp.where(peer >= self.count, peer - self.count, peer))
        return self.links.copy(slot, slot, self.base + j, dp=peer)

    def _loop(self, act):
        def one(j, carry):
            act(j)
            return carry

        lax.fori_loop(1, self.count, one, 0)

    def start(self, values):
        self.buf[self.me] = values
        self._loop(lambda j: self._copy(j).start())

    def _hear(self, j):
        peer = self.me - j
        peer = jnp.where(peer < 0, peer + self.count, peer)
        self.links.arrived(self.buf.at[peer], self.base + j, dp=self.device(peer))

    def result(self):
        self._loop(self._hear)
        return lax.fori_loop(1, self.count, lambda j, acc: acc + self.buf[j], self.buf[0])

    def finish(self):
        self._loop(lambda j: self._copy(j).wait_send())


def greet(here):
    barrier = pltpu.get_barrier_semaphore()
    for axis, me, count in (("tensor", here.t, here.tensor), ("dp", here.d, here.dp)):

        def one(j, carry, axis=axis, me=me, count=count):
            peer = me + j
            peer = here.logical(**{axis: jnp.where(peer >= count, peer - count, peer)})
            pl.semaphore_signal(barrier, inc=1, device_id=peer, device_id_type=LOGICAL)
            return carry

        lax.fori_loop(1, count, one, 0)


def await_greetings(amount):
    pl.semaphore_wait(pltpu.get_barrier_semaphore(), amount)


def halves(rows):
    first = round_up(rows // 2, 16)
    return ((0, first), (first, rows - first))


def head_masks(shape, local_heads):
    lane = lax.broadcasted_iota(jnp.int32, shape, 1)
    return [
        jnp.where((lane >= h * HEAD_DIM) & (lane < (h + 1) * HEAD_DIM), 1.0, 0.0)
        for h in range(local_heads)
    ], lane


def kernel(n, S):
    here = Here(n.dp, 4)
    t, d = here.t, here.d
    here.peers = peers = [flipped(here, 1, 0), flipped(here, 1, 1), flipped(here, 0, 1)]
    links = Links(here, S.send, S.recv)
    greet(here)
    R, own, W, H, D, K = n.R, n.own, n.W, n.H, n.D, n.K
    split = halves(R)
    vector = lambda ref: ref[...].reshape(1, D)

    fetch = pltpu.make_async_copy(S.cot, S.gt, S.local.at[0])
    load = [
        pltpu.make_async_copy(getattr(S, name + "_far"), getattr(S, name), S.local.at[1 + j])
        for j, name in enumerate(LOADED)
    ]
    fetch.start()
    for copy in load:
        copy.start()
    S.a1[t] = jnp.zeros((R, D), low)
    S.cot4[t] = jnp.zeros((R, D), low)
    S.a24[t] = jnp.zeros((R, D), low)
    S.hl4[t] = jnp.zeros((R, D), low)
    rows_in = Gather(links, S.a1, here, split)
    cot_in = Gather(links, S.cot4, here, split)
    ow_in = Gather(links, S.ow4, here, ((0, W),))
    for p, (start, size) in enumerate(split):
        rows = pl.ds(start, min(size, own - start))
        unit, _ = standardize(S.x[rows, :].astype(wide))
        S.a1[t, rows, :] = (unit * vector(S.g1) + vector(S.b1)).astype(low)
        if p == 0:
            await_greetings(3 + n.dp - 1)
        rows_in.start([p])
    load[0].wait()
    S.ow4[t] = S.ow[...]
    ow_in.start()
    fetch.wait()
    S.cot4[t, 0:own, :] = S.gt[...].astype(low)
    cot_in.start([0])
    load[2].wait()
    load[3].wait()
    S.gw[0:D, :] = jnp.transpose(S.wup[...])
    S.gw[D:, :] = jnp.transpose(S.wdn[...])
    load[1].wait()
    S.v[4 * R :, :] = jnp.zeros((K - 4 * R, H), low)
    length = S.lengths[0]

    chip = here.chip

    def project(i, carry):
        s = flipped(here, *two_bits(i))

        @pl.when(i == 1)
        def _():
            rows_in.wait_sib()

        @pl.when(i == 2)
        def _():
            rows_in.forward()

        @pl.when(i == 3)
        def _():
            rows_in.wait_diag()

        slab = S.a1[s]
        lane = lax.broadcasted_iota(jnp.int32, (R, H - W), 1)
        row = lax.broadcasted_iota(jnp.int32, (R, H - W), 0)
        absent = (row >= own) | (row + s * own >= length)
        at = pl.ds(pl.multiple_of(s * R, 16), R)
        out = dot_rows(slab, S.wqkv[0]) + S.bq[0:1, :]
        S.q[s, :, :W] = (out.astype(low).astype(wide) * HEAD_DIM**-0.5).astype(low)
        S.q[s, :, W:] = jnp.where(lane == 0, HEAD_DIM**-0.5, 0.0).astype(low)
        S.k[at, :W] = dot_rows(slab, S.wqkv[1]).astype(low)
        S.k[at, W:] = jnp.where((lane == 0) & absent, -8e30, 0.0).astype(low)
        S.v[at, :W] = (dot_rows(slab, S.wqkv[2]) + S.bq[1:2, :]).astype(low)
        S.v[at, W:] = jnp.where(lane < 2, 1.0, 0.0).astype(low)
        return carry

    lax.fori_loop(0, 4, project, 0)
    if K > 4 * R:
        lane = lax.broadcasted_iota(jnp.int32, (K - 4 * R, H), 1)
        S.k[4 * R :, :] = jnp.where(lane == W, -8e30, 0.0).astype(low)
    S.kt[...] = jnp.transpose(S.k[...])
    S.vt[...] = jnp.transpose(S.v[...])

    masks, lane = head_masks((1, H), n.heads)
    mix_base = links.take(3)


    def attend(i, carry):
        high, low_bit = two_bits(i)
        s = flipped(here, 1 - high, low_bit + high - 2 * low_bit * high)
        query = S.q[s]
        mixed = jnp.zeros((R, H), wide)
        inverse = jnp.zeros((R, 128), wide)
        first = lax.broadcasted_iota(jnp.int32, (1, 128), 1)

        def score(h):
            here = jnp.where(lane == W, 1.0, masks[h]).astype(low)
            return dot(query * here, S.kt[...])

        ready = score(0)
        for h in range(n.heads):
            scores = ready
            if h + 1 < n.heads:
                ready = score(h + 1)
            terms = jnp.exp(scores - jnp.max(scores, -1, keepdims=True)).astype(low)
            S.e[h, s] = terms
            part = dot(terms, S.v[...])
            scale = 1.0 / part[:, W : W + 1]
            mixed += part * (scale * masks[h])
            inverse = jnp.where(first == h, scale, inverse)
        S.o[s] = mixed
        S.inv[s] = inverse
        S.mix[s] = mixed[:, :W].astype(low)

        @pl.when(i < 3)
        def _():
            links.copy(S.mix.at[s], S.mix4.at[t], mix_base + i, tensor=s).start()

        @pl.when(i == 1)
        def _():
            cot_in.start([1])

        @pl.when(i == 2)
        def _():
            ow_in.wait_sib()
            ow_in.forward()

        return carry

    lax.fori_loop(0, 4, attend, 0)
    ow_in.wait_diag()
    S.mix4[t] = S.mix[t]
    for j, s in enumerate(peers):
        links.arrived(S.mix4.at[s], mix_base + j, tensor=s)

    total = dot(S.mix4[0], S.ow4[0])
    for j in range(1, 4):
        total += dot(S.mix4[j], S.ow4[j])
    total = S.x[...].astype(wide) + (total[:own] + vector(S.ob))
    S.hid[...] = total
    unit, _ = standardize(total)
    S.a24[t, 0:own, :] = (unit * vector(S.g2) + vector(S.b2)).astype(low)
    next_in = Gather(links, S.a24, here, halves(R))
    next_in.start()
    back = Reduce(links, S.part, S.pre1, S.near1, S.far1, here, split)
    ahead = Reduce(links, S.fop, S.pre2, S.near2, S.far2, here, split)
    S.gub[...] = jnp.zeros_like(S.gub)

    def feed(s, start, size):
        rows = pl.ds(start, size)
        up = dot(S.a24[s, rows], S.wup[...]) + vector(S.bup)
        square = up * up
        c = 0.7978845608028654
        bend = jnp.tanh(c * up * (1.0 + 0.044715 * square))
        half = 0.5 * (1.0 + bend)
        slope = half + 0.5 * up * (1.0 - bend * bend) * (c + (3 * 0.044715 * c) * square)
        active = (up * half).astype(low)
        S.pool[s, rows, 0:D] = active
        grad = (dot(S.cot4[s, rows], S.gw[D:, :]) * slope).astype(low)
        S.gup[s, rows] = grad
        S.part[s, rows] = dot(grad, S.gw[0:D, :]).astype(low)
        S.gub[...] += jnp.sum(grad.astype(wide), 0, keepdims=True)

    def lead_out(s, start, size):
        rows = pl.ds(start, size)
        S.fop[s, rows] = dot(S.pool[s, rows, 0:D], S.wdn[...]).astype(low)

    def feed_here(i, carry):
        s = flipped(here, 0, i)

        @pl.when(i == 1)
        def _():
            next_in.wait_sib()
            cot_in.wait_sib()

        feed(s, 0, R)

        @pl.when(i == 1)
        def _():
            back.send_sib()

        lead_out(s, 0, R)
        return carry

    lax.fori_loop(0, 2, feed_here, 0)
    ahead.send_sib()
    for p in (0, 1):

        def feed_there(i, carry, p=p):
            @pl.when(i == 0)
            def _():
                cot_in.forward([p])
                next_in.forward([p])

            @pl.when(i == 1)
            def _():
                cot_in.wait_diag([p])
                next_in.wait_diag([p])

            feed(flipped(here, 1, i), *split[p])
            if p == 1:

                @pl.when(i == 0)
                def _():
                    back.send_cross([0])

            return carry

        lax.fori_loop(0, 2, feed_there, 0)
        back.send_diag([p])
    for i in (0, 1):
        lead_out(flipped(here, 1, i), 0, R)
    back.send_cross([1])
    ahead.send_diag()

    sums = Pipeline(PLAN)
    tile = D // 2
    box_at = 0

    def sum_over_dp(kind, held, whole, out, first, rows):
        nonlocal box_at
        sums.add(kind(links, held, whole, out, S.box, box_at, first, rows))
        box_at += kind.sizes(rows, D, n.dp)[1]

    for left, right, first in ((S.a24, S.gup, 0), (S.pool, S.cot4, D)):
        rows = left[:, :, 0:D].reshape(4 * R, D)
        S.gw[first : first + D, :] = dot_columns(rows, flat(right)).astype(low)
        for at in (first, first + tile):
            kind = Halves if at == tile else HalvesFromX
            sum_over_dp(kind, S.gw, S.sum1, S.whole1, at, tile)

    sums.at("waiting")
    S.small[...] = jnp.zeros_like(S.small)
    gm_base = links.take(6)
    shared = lambda s, p, j: links.copy(
        S.mix4.at[s, pl.ds(*split[p])], S.gm4.at[t, pl.ds(*split[p])], gm_base + 3 * p + j, tensor=peers[j]
    )
    for p, (start, size) in enumerate(split):
        real = min(size, own - start)
        rows = pl.ds(start, real)
        grad = back.result(p)[:real]
        unit, inverse = standardize(S.hid[rows])
        S.small[2:3, :] += jnp.sum(grad * unit, 0, keepdims=True)
        S.small[3:4, :] += jnp.sum(grad, 0, keepdims=True)
        S.gt[rows] += norm_back(grad, unit, inverse, vector(S.g2))
        S.hl4[t, rows] = S.gt[rows].astype(low)
        rows = pl.ds(start, size)
        for j, s in enumerate(peers + [t]):
            product = dot_rows(S.hl4[t, rows], S.ow4[s]).astype(low)
            if j < 3:
                S.mix4[s, rows] = product
                shared(s, p, j).start()
            else:
                S.gm4[t, rows] = product
    S.small[4:5, :] = jnp.sum(S.hl4[t].astype(wide), 0, keepdims=True)
    S.small[5:6, :] = jnp.sum(S.cot4[t].astype(wide), 0, keepdims=True)
    S.small[6:7, :] = S.gub[...]
    hl_in = Gather(links, S.hl4, here, halves(R))

    next_in.finish()
    S.do[...] = jnp.zeros_like(S.do)
    S.qt[...] = jnp.transpose(flat(S.q))
    sums.at("shared")

    def prepare(i, s):
        if i > 0:
            j = (None, 2, 0, 1)[i]
            for p in (0, 1):
                rows = pl.ds(*split[p])
                links.arrived(S.gm4.at[s, rows], gm_base + 3 * p + j, tensor=peers[j])
        S.do[:, :W] = S.gm4[s].astype(wide)
        inverse = sum(S.inv[s, :, h : h + 1] * masks[h] for h in range(n.heads))
        scaled = (S.do[...] * inverse).astype(low)
        S.v[pl.ds(pl.multiple_of(s * R, 16), R), :] = scaled
        scaled = scaled.astype(wide)
        product = scaled * S.o[s]
        for h in range(n.heads):
            inner = -jnp.sum(product * masks[h], -1, keepdims=True)
            upper = inner.astype(low).astype(wide)
            S.a24[s, :, h * H : (h + 1) * H] = (
                scaled * masks[h]
                + jnp.where(lane == W, upper, 0.0)
                + jnp.where(lane == W + 1, inner - upper, 0.0)
            ).astype(low)

    def pull(h, p):
        grad_p = dot(pair(S.a24.at[:, :, h * H : (h + 1) * H], p), S.vt[...])
        grad_s = (pair(S.e.at[h], p).astype(wide) * grad_p).astype(low)
        set_pair(S.pool, p, grad_s)
        dq = dot(grad_s, S.k[...]) * (masks[h] * HEAD_DIM**-0.5)
        if h > 0:
            dq += pair(S.gup.at[:, :, 0:H], p).astype(wide)
        S.gup[pl.ds(2 * p, 2), :, 0:H] = dq.astype(low).reshape(2, R, H)

    def keep(out, row, parts):
        S.gw2[row : row + out.shape[0], :] = out.astype(low)
        for j, (c, h) in enumerate(parts):
            product = out[j * HEAD_DIM : (j + 1) * HEAD_DIM]
            product *= S.wqkv[c, h * HEAD_DIM : (h + 1) * HEAD_DIM, :].astype(wide)
            S.small[0:1, :] += jnp.sum(product, 0, keepdims=True)
        sum_over_dp(Quarters, S.gw2, S.sum2, S.whole2, row, out.shape[0])

    def weights(h):
        at = slice(h * HEAD_DIM, (h + 1) * HEAD_DIM)
        tile = h * HEAD_DIM // 128 * 128
        dqt = jnp.transpose(flat(S.gup.at[:, :, tile : tile + 128]))
        left = jnp.concatenate([dqt[h * HEAD_DIM - tile : (h + 1) * HEAD_DIM - tile], S.qt[at, :]], 0)
        keep(dot(left, flat(S.a1)), 2 * h * HEAD_DIM, [(0, h), (1, h)])

    for h in range(n.heads):
        for i in (0, 2):
            if (h, i) == (0, 2):
                sums.at("arriving")
            if h == 0:
                prepare(i, flipped(here, i // 2, 0))
                prepare(i + 1, flipped(here, i // 2, 1))
            if (h, i) == (0, 2):
                hl_in.start()
            pull(h, chip if i == 0 else 1 - chip)
            sums.at(f"h{h}p{i}")
            if (h, i) == (1, 0):
                hl_in.wait_sib()
                hl_in.forward()
                ahead.send_cross()
            elif (h, i) == (1, 2):
                hl_in.wait_diag()
                S.gw2[3 * W :, :] = dot_columns(flat(S.mix), flat(S.hl4)).astype(low)
                sum_over_dp(HalvesFromX, S.gw2, S.sum2, S.whole2, 3 * W, W)
        at = slice(h * HEAD_DIM, (h + 1) * HEAD_DIM)
        if h == 0:
            S.v[4 * R :, :] = jnp.zeros((K - 4 * R, H), low)
            S.kt[...] = jnp.transpose(S.v[...])
            for g in range(n.heads):
                rows = slice(g * HEAD_DIM, (g + 1) * HEAD_DIM)
                S.kt[rows, : 4 * R] = dot(S.kt[rows, : 4 * R], flat(S.e.at[g]))[:, : 4 * R].astype(low)
            keep(dot(S.kt[:W, : 4 * R], flat(S.a1)), 2 * W, [(2, g) for g in range(n.heads)])
        S.qt[at, :] = dot(S.qt[at, :], flat(S.pool))[:, : 4 * R].astype(low)
        if h + 1 < n.heads:
            weights(h)
        sums.at(f"h{h}")

    pad = jnp.zeros((R, H - W), low)
    for part, grad_t in ((1, S.qt), (2, S.kt)):
        rows = jnp.transpose(grad_t[:W, : 4 * R])
        for s in range(4):
            S.gup[s, :, part * H : part * H + W] = rows[s * R : (s + 1) * R]
            S.gup[s, :, part * H + W : (part + 1) * H] = pad

    back.finish()
    down = Reduce(links, S.part, S.pre1, S.near1, S.far1, here, split)

    def lead(s, start, size):
        rows = pl.ds(start, size)
        out = dot(S.gup[s, rows, 0:W], S.wqkv[0])
        out += dot(S.gup[s, rows, H : H + W], S.wqkv[1])
        out += dot(S.gup[s, rows, 2 * H : 2 * H + W], S.wqkv[2])
        S.part[s, rows] = out.astype(low)

    cross, diag, sib = peers
    lead(diag, *split[0])
    down.send_diag([0])
    lead(cross, *split[0])
    weights(n.heads - 1)
    down.send_cross([0])
    lead(diag, *split[1])
    down.send_diag([1])
    lead(cross, *split[1])
    down.send_cross([1])
    lead(sib, 0, R)
    down.send_sib()
    lead(t, 0, R)
    columns = jnp.sum(flat(S.gup).astype(wide), 0, keepdims=True)
    S.small[7:8, 0:H] = columns[:, 0:H]
    S.small[7:8, H : 2 * H] = columns[:, 2 * H :]
    upper = columns.astype(low)
    both = jnp.concatenate([upper.astype(wide), columns - upper.astype(wide)], 0).astype(low)
    for c in range(3):
        product = dot(both[:, c * H : c * H + W], S.wqkv[c])
        S.small[1:2, :] += jnp.sum(product, 0, keepdims=True)

    S.small4[t] = S.small[...]
    base3 = links.take(3)
    for j in range(3):
        links.start(S.small4.at[t], S.small4.at[t], base3 + j, tensor=peers[j])
    sums.at("led")
    result = jnp.concatenate([ahead.result(0), ahead.result(1)], 0)
    S.output[...] = (S.hid[...] + (result[:own] + vector(S.db))).astype(low)
    sums.at("crossing")

    unit, inverse = standardize(S.x[...].astype(wide))
    grad = jnp.concatenate([down.result(0), down.result(1)], 0)[:own]
    for j in range(3):
        links.arrived(S.small4.at[peers[j]], base3 + j, tensor=peers[j])
    over = S.small4[0] + S.small4[1] + S.small4[2] + S.small4[3]
    row = lax.broadcasted_iota(jnp.int32, over.shape, 0)
    near = min(8, n.dp)
    inner = Everyone(links, S.smalls, here.near, near, lambda j: here.group + j)
    inner.start(jnp.where(row < 6, over, S.small[...]))
    S.gt[...] += norm_back(grad, unit, inverse, vector(S.g1))
    sums.at("told")
    sums.finish()
    total = inner.result()
    inner.finish()
    if n.dp > near:
        outer = Everyone(links, S.smalls2, lax.div(here.group, near), n.dp // near, lambda j: j * near + here.near)
        outer.start(total)
        total = outer.result()
        outer.finish()
    S.small_sum[...] = total
    S.small_sum[0:1, :] = (total[0:1, :] - vector(S.b1) * total[1:2, :]) / vector(S.g1)
    for j, s in enumerate(peers):
        links.copy(S.mix.at[s], S.mix4.at[t], mix_base + j, tensor=s).wait_send()
        for p in (0, 1):
            shared(s, p, j).wait_send()
    for transfer in (rows_in, cot_in, ow_in, hl_in, ahead, down):
        transfer.finish()
    links.finish()


LOADED = ("ow", "wqkv", "wup", "wdn")
SMALL = ("gain1", "shift1", "gain2", "shift2", "bias_out", "bias_down", "bias_up", "bias_qv")


def finish(n, output, gt, small, whole1, whole2):
    D, W, H = n.D, n.W, n.H
    steps = n.heads
    rows1 = D // steps

    def spread(output, gt, small, up, down, head, value, out, *refs):
        to_output, to_gt, to_up, to_down, to_qkv, to_out = refs[:6]
        vectors, sems = refs[6:14], refs[14]
        i = pl.program_id(0)
        held = refs[15:]
        come = [pltpu.make_async_copy(a, b, sems.at[j]) for j, (a, b) in enumerate(zip((output, gt), held))]
        go = [
            pltpu.make_async_copy(a, b, sems.at[2 + j])
            for j, (a, b) in enumerate(zip(held, (to_output, to_gt)))
        ]

        @pl.when(i == 0)
        def _():
            for copy in come:
                copy.start()
            for j in range(7):
                vectors[j][...] = small[j : j + 1, :].reshape(D)
            vectors[7][0:1, :] = small[7:8, :W]
            vectors[7][1:2, :] = small[7:8, H : H + W]

        to_up[...] = up[...].astype(wide)
        to_down[...] = down[...].astype(wide)
        to_qkv[0] = head[0:HEAD_DIM, :].astype(wide)
        to_qkv[1] = head[HEAD_DIM:, :].astype(wide)
        to_qkv[2] = value[...].astype(wide)
        to_out[...] = out[...].astype(wide)

        @pl.when(i == 1)
        def _():
            for first, second in zip(come, go):
                first.wait()
                second.start()

        @pl.when(i == steps - 1)
        def _():
            for copy in go:
                copy.wait()

    hbm = pl.BlockSpec(memory_space=pl.ANY)
    whole = pl.BlockSpec(memory_space=pltpu.VMEM)
    at_row = lambda rows, index: pl.BlockSpec((rows, D), lambda i: (index(i), 0))
    shape = jax.ShapeDtypeStruct
    return pl.pallas_call(
        spread,
        grid=(steps,),
        out_shape=[shape(output.shape, low), shape(gt.shape, wide)]
        + [shape((D, D), wide)] * 2
        + [shape((3, W, D), wide), shape((W, D), wide)]
        + [shape((D,), wide)] * 7
        + [shape((2, W), wide)],
        in_specs=[hbm, hbm, whole, at_row(rows1, lambda i: i), at_row(rows1, lambda i: i + steps)]
        + [at_row(2 * HEAD_DIM, lambda i: i)]
        + [at_row(HEAD_DIM, lambda i, j=j: j * steps + i) for j in (2, 3)],
        out_specs=[hbm, hbm]
        + [at_row(rows1, lambda i: i)] * 2
        + [pl.BlockSpec((3, HEAD_DIM, D), lambda i: (0, i, 0)), at_row(HEAD_DIM, lambda i: i)]
        + [whole] * 8,
        scratch_shapes=[
            pltpu.SemaphoreType.DMA((4,)),
            pltpu.VMEM(output.shape, low),
            pltpu.VMEM(gt.shape, wide),
        ],
    )(output, gt, small, whole1, whole1, whole2, whole2, whole2)


def body(
    tokens,
    lengths,
    ln1_gain,
    ln1_shift,
    qkv_weight,
    qv_bias,
    out_weight,
    out_bias,
    ln2_gain,
    ln2_shift,
    up_weight,
    up_bias,
    down_weight,
    down_bias,
    cotangent,
):
    own, D = tokens.shape
    W = qkv_weight.shape[2]
    F = up_weight.shape[1]
    dp = lax.axis_size("dp")
    assert lax.axis_size("tensor") == 4 and lengths.shape[0] == 1 and F == D and 4 * W == D and 3 * round_up(W + 2, 128) == D
    R = round_up(own, 16)
    H = round_up(W + 2, 128)
    K = round_up(4 * R, 256)
    heads = W // HEAD_DIM
    extra = dp.bit_length() - 1 - 3
    n = types.SimpleNamespace(
        own=own, D=D, W=W, R=R, H=H, K=K, dp=dp, heads=heads, extra=extra
    )
    weights = dict(ow=out_weight, wqkv=jnp.transpose(qkv_weight, (1, 2, 0)), wup=up_weight, wdn=down_weight)
    given = dict(
        x=tokens, lengths=lengths, g1=ln1_gain, b1=ln1_shift,
        bq=qv_bias, ob=out_bias, g2=ln2_gain, b2=ln2_shift, bup=up_bias, db=down_bias,
        cot=cotangent,
    )
    given.update({name + "_far": weights[name] for name in LOADED})
    outs = dict(
        output=((own, D), low), gt=((own, D), wide), small_sum=((8, D), wide),
        whole1=((2 * D, D), low), whole2=((D, D), low),
    )
    rows4 = ((4, R, D), low)
    slab = ((R, D), low)
    chunks = [(Halves, D // 2)] * 4 + [(Halves, W), (Quarters, W)] + [(Quarters, 2 * HEAD_DIM)] * heads
    scratch = dict(
        a1=rows4, cot4=rows4, ow4=((4, W, D), low), q=((4, R, H), low), k=((K, H), low),
        v=((K, H), low), kt=((H, K), low), vt=((H, K), low), e=((heads, 4, R, K), low),
        o=((4, R, H), wide), inv=((4, R, 128), wide), mix=((4, R, W), low), mix4=((4, R, W), low),
        hid=((own, D), wide),
        a24=rows4, pool=((4, R, K), low), gup=rows4, part=rows4,
        fop=rows4, pre1=slab, near1=slab, far1=slab, pre2=slab, near2=slab, far2=slab,
        gw=((2 * D, D), low), gub=((1, D), wide),
        small=((8, D), wide), hl4=rows4,
        gm4=((4, R, W), low), qt=((H, 4 * R), low), do=((R, H), wide),
        gw2=((D, D), low),
        small4=((4, 8, D), wide), smalls=((min(8, dp), 8, D), wide),
        box=((sum(kind.sizes(r, D, dp)[1] for kind, r in chunks), D), low),
        sum1=((2 * D, D), low), sum2=((D, D), low),
    )
    scratch.update({name: (weights[name].shape, low) for name in LOADED})
    if dp > 8:
        scratch["smalls2"] = ((dp // 8, 8, D), wide)
    sems = 190 + dp + 9 * extra
    names = list(given) + list(outs) + list(scratch) + ["local", "send", "recv"]
    vmem = pl.BlockSpec(memory_space=pltpu.VMEM)
    smem = pl.BlockSpec(memory_space=pltpu.SMEM)
    hbm = pl.BlockSpec(memory_space=pl.ANY)
    output, gt, small, whole1, whole2 = pl.pallas_call(
        lambda *refs: kernel(n, types.SimpleNamespace(**dict(zip(names, refs)))),
        out_shape=tuple(jax.ShapeDtypeStruct(*spec) for spec in outs.values()),
        in_specs=[
            hbm if name.endswith("_far") else dict(lengths=smem, cot=hbm).get(name, vmem) for name in given
        ],
        out_specs=tuple(hbm if name in ("whole1", "whole2") else vmem for name in outs),
        scratch_shapes=[pltpu.VMEM(*spec) for spec in scratch.values()]
        + [pltpu.SemaphoreType.DMA((5,))] + [pltpu.SemaphoreType.DMA((sems,))] * 2,
        compiler_params=pltpu.CompilerParams(
            collective_id=0, has_side_effects=True, vmem_limit_bytes=VMEM_BYTES
        ),
    )(*given.values())
    finished = finish(n, output, gt, small, whole1, whole2)
    small_rows = dict(zip(SMALL, finished[6:]))
    return (
        finished[0],
        finished[1],
        small_rows["gain1"],
        small_rows["shift1"],
        jnp.transpose(finished[4], (2, 0, 1)),
        small_rows["bias_qv"],
        finished[5],
        small_rows["bias_out"],
        small_rows["gain2"],
        small_rows["shift2"],
        finished[2],
        small_rows["bias_up"],
        finished[3],
        small_rows["bias_down"],
    )


def solution(mesh):
    placed = (
        P(("dp", "tensor"), None),
        P("dp"),
        P(),
        P(),
        P(None, None, "tensor"),
        P(None, "tensor"),
        P("tensor", None),
        P(),
        P(),
        P(),
        P(None, "tensor"),
        P("tensor"),
        P("tensor", None),
        P(),
        P(("dp", "tensor"), None),
    )
    return jax.shard_map(
        body,
        mesh=mesh,
        in_specs=placed,
        out_specs=(
            P(("dp", "tensor"), None),
            P(("dp", "tensor"), None),
            P(),
            P(),
            P(None, None, "tensor"),
            P(None, "tensor"),
            P("tensor", None),
            P(),
            P(),
            P(),
            P(None, "tensor"),
            P("tensor"),
            P("tensor", None),
            P(),
        ),
        check_vma=False,
    )
```

```python
import types

import jax
import jax.numpy as jnp
from jax import lax
from jax.experimental import pallas as pl
from jax.experimental.pallas import tpu as pltpu
from jax.sharding import PartitionSpec as P

HEAD_DIM = 64
LOGICAL = pl.DeviceIdType.LOGICAL
VMEM_BYTES = 62 * 2**20

epsilon = 1e-06
low = jnp.bfloat16
wide = jnp.float32


def round_up(amount, unit):
    return -(-amount // unit) * unit


class Here:
    def __init__(self, dp, tensor):
        self.dp, self.tensor = dp, tensor
        self.d, self.t = lax.axis_index("dp"), lax.axis_index("tensor")
        self.me = self.d * tensor + self.t
        self.chip = lax.div(self.t, 2)
        self.core = self.t - 2 * self.chip
        self.bits, rest = [], self.d
        for _ in range(dp.bit_length() - 1):
            half = lax.div(rest, 2)
            self.bits.append(rest - 2 * half)
            rest = half
        low_bits = sum(bit * (1 << b) for b, bit in enumerate(self.bits[:3]))
        self.near, self.group = low_bits, self.d - low_bits

    def logical(self, dp=None, tensor=None):
        if dp is not None:
            return self.me + (dp - self.d) * self.tensor
        return self.me + (tensor - self.t)

    def bit_flipped(self, b):
        return self.d + (1 - 2 * self.bits[b]) * (1 << b)


def flipped(here, flip_chip, flip_core):
    chip = here.chip + flip_chip - 2 * here.chip * flip_chip
    return 2 * chip + here.core + flip_core - 2 * here.core * flip_core


def two_bits(i):
    high = jnp.where(i >= 2, 1, 0)
    return high, i - 2 * high


def dot(left, right):
    return jnp.dot(left, right, preferred_element_type=wide)


def dot_rows(left, right):
    return lax.dot_general(left, right, (((1,), (1,)), ((), ())), preferred_element_type=wide)


def dot_columns(left, right):
    return lax.dot_general(left, right, (((0,), (0,)), ((), ())), preferred_element_type=wide)


def standardize(values):
    center = values - jnp.mean(values, -1, keepdims=True)
    inverse = lax.rsqrt(jnp.mean(center * center, -1, keepdims=True) + epsilon)
    return center * inverse, inverse


def norm_back(grad, unit, inverse, gain):
    scaled = grad * gain
    return inverse * (
        scaled
        - jnp.mean(scaled, -1, keepdims=True)
        - unit * jnp.mean(scaled * unit, -1, keepdims=True)
    )


def pair(ref, p):
    _, rows, columns = ref.shape
    return ref[pl.ds(2 * p, 2)].reshape(2 * rows, columns)


def set_pair(ref, p, values):
    ref[pl.ds(2 * p, 2)] = values.reshape(2, -1, values.shape[1])


def flat(ref):
    a, b, c = ref.shape
    return ref[...].reshape(a * b, c)


class Links:
    def __init__(self, here, send, recv):
        self.here, self.send, self.recv, self.used, self.pending = here, send, recv, 0, []

    def take(self, amount=1):
        base = self.used
        self.used += amount
        assert self.used <= self.send.shape[0]
        return base

    def copy(self, src, dst, at, **where):
        return pltpu.make_async_remote_copy(
            src_ref=src,
            dst_ref=dst,
            send_sem=self.send.at[at],
            recv_sem=self.recv.at[at],
            device_id=self.here.logical(**where),
            device_id_type=LOGICAL,
        )

    def start(self, src, dst, at, **where):
        copy = self.copy(src, dst, at, **where)
        copy.start()
        self.pending.append(copy)

    def arrived(self, dst, at, **where):
        self.copy(dst, dst, at, **where).wait_recv()

    def finish(self):
        for copy in self.pending:
            copy.wait_send()
        self.pending = []


class Gather:
    def __init__(self, links, buf, here, parts):
        self.links, self.buf, self.t, self.parts = links, buf, here.t, parts
        self.cross, self.diag, self.sib = here.peers
        self.base = links.take(3 * len(parts))

    def view(self, slot, part):
        start, size = self.parts[part]
        return self.buf.at[slot, pl.ds(start, size)]

    def _each(self):
        return range(len(self.parts))

    def start(self, parts=None):
        parts = self._each() if parts is None else parts
        for p in parts:
            v = self.view(self.t, p)
            self.links.copy(v, v, self.base + 3 * p, tensor=self.cross).start()
        for p in parts:
            v = self.view(self.t, p)
            self.links.copy(v, v, self.base + 3 * p + 1, tensor=self.sib).start()

    def wait_sib(self):
        for p in self._each():
            self.links.arrived(self.view(self.sib, p), self.base + 3 * p + 1, tensor=self.sib)

    def forward(self, parts=None):
        for p in self._each() if parts is None else parts:
            v = self.view(self.cross, p)
            self.links.arrived(v, self.base + 3 * p, tensor=self.cross)
            self.links.copy(v, v, self.base + 3 * p + 2, tensor=self.sib).start()

    def wait_diag(self, parts=None):
        for p in self._each() if parts is None else parts:
            self.links.arrived(self.view(self.diag, p), self.base + 3 * p + 2, tensor=self.sib)

    def finish(self):
        for p in self._each():
            v = self.view(self.t, p)
            self.links.copy(v, v, self.base + 3 * p, tensor=self.cross).wait_send()
            self.links.copy(v, v, self.base + 3 * p + 1, tensor=self.sib).wait_send()
            v = self.view(self.cross, p)
            self.links.copy(v, v, self.base + 3 * p + 2, tensor=self.sib).wait_send()


class Reduce:
    def __init__(self, links, part, pre, near, far, here, parts):
        self.links, self.part, self.t, self.parts = links, part, here.t, parts
        self.pre, self.near, self.far = pre, near, far
        self.cross, self.diag, self.sib = here.peers
        self.base = links.take(3 * len(parts))

    def _copy(self, kind, p):
        slot, box, peer = (
            (self.diag, self.pre, self.sib),
            (self.sib, self.near, self.sib),
            (self.cross, self.far, self.cross),
        )[kind]
        rows = pl.ds(*self.parts[p])
        return self.links.copy(
            self.part.at[slot, rows], box.at[rows], self.base + 3 * p + kind, tensor=peer
        )

    def _each(self, parts):
        return range(len(self.parts)) if parts is None else parts

    def send_diag(self, parts=None):
        for p in self._each(parts):
            self._copy(0, p).start()

    def send_sib(self):
        for p in self._each(None):
            self._copy(1, p).start()

    def send_cross(self, parts=None):
        for p in self._each(parts):
            self._copy(0, p).wait_recv()
            rows = pl.ds(*self.parts[p])
            self.part[self.cross, rows] = (
                self.part[self.cross, rows].astype(wide) + self.pre[rows].astype(wide)
            ).astype(low)
            self._copy(2, p).start()

    def result(self, p):
        self._copy(1, p).wait_recv()
        self._copy(2, p).wait_recv()
        rows = pl.ds(*self.parts[p])
        return (
            self.part[self.t, rows].astype(wide)
            + self.near[rows].astype(wide)
            + self.far[rows].astype(wide)
        )

    def finish(self):
        for p in self._each(None):
            for kind in range(3):
                self._copy(kind, p).wait_send()


class DataReduce:
    def __init__(self, links, held, whole, out, box, box_at, first, rows):
        self.links, self.held, self.whole, self.out, self.here = links, held, whole, out, links.here
        count = self.here.dp
        bits = count.bit_length() - 1
        assert count == 1 << bits and bits >= 3
        self.extra = list(range(3, bits))
        self.region = (first, rows, 0, held.shape[1])
        self.trail, self.sent, self.boxes = [], [], []
        for tall, broad in self.sizes(rows, held.shape[1], count)[0]:
            self.boxes.append(box.at[pl.ds(box_at, tall), pl.ds(0, broad)])
            box_at += tall
        self.base = links.take(9 + len(self.extra))
        self.plan()

    @classmethod
    def sizes(cls, rows, columns, count):
        found = cls.boxes_of(rows, columns)
        found += found[-1:] * (count.bit_length() - 1 - 3)
        return found, sum(size[0] for size in found)

    def _bit(self, b):
        return self.here.bits[b]

    def _peer(self, b):
        return self.here.bit_flipped(b)

    def _send(self, src, dst, at, peer):
        copy = self.links.copy(src, dst, self.base + at, dp=peer)
        copy.start()
        self.sent.append(copy)

    def _wait(self, dst, at, peer):
        self.links.arrived(dst, self.base + at, dp=peer)

    @staticmethod
    def _view(ref, region):
        row, rows, column, columns = region
        if columns == ref.shape[1]:
            return ref.at[pl.ds(row, rows)]
        return ref.at[pl.ds(row, rows), pl.ds(column, columns)]

    @staticmethod
    def _part(region, bit):
        row, rows, column, columns = region
        if rows % 32 == 0:
            return (pl.multiple_of(row + bit * (rows // 2), 16), rows // 2, column, columns)
        return (row, rows, pl.multiple_of(column + bit * (columns // 2), 128), columns // 2)

    def _give_half(self, b, box, at):
        bit = self._bit(b)
        self.trail.append(self.region)
        self._send(self._view(self.held, self._part(self.region, 1 - bit)), self.boxes[box], at, self._peer(b))
        self.region = self._part(self.region, bit)

    def _add(self, boxes, last):
        view = self._view(self.held, self.region)
        total = view[...].astype(wide)
        for box in boxes:
            total += self.boxes[box][...].astype(wide)
        if last:
            view = self._view(self.whole, self.region)
        view[...] = total.astype(low)
        if last:
            self._swap()

    def _swap(self):
        view = self._view(self.whole, self.region)
        for k, b in enumerate(self.extra):
            box, at = self.boxes[k - len(self.extra)], 9 + k
            copy = self.links.copy(view, box, self.base + at, dp=self._peer(b))
            copy.start()
            self._wait(box, at, self._peer(b))
            copy.wait_send()
            view[...] = (view[...].astype(wide) + box[...].astype(wide)).astype(low)

    def _give_whole(self, b, at):
        view = self._view(self.whole, self.region)
        self._send(view, view, at, self._peer(b))

    def _take_half(self, b, at):
        outer = self.trail.pop()
        view = self._view(self.whole, self._part(outer, 1 - self._bit(b)))
        self._wait(view, at, self._peer(b))
        self.region = outer

    def _leave(self):
        rows = pl.ds(self.region[0], self.region[1])
        self.left = pltpu.make_async_copy(
            self.whole.at[rows], self.out.at[rows], self.links.send.at[self.base + 8]
        )
        self.left.start()

    def step(self):
        if self.steps:
            self.steps.pop(0)()

    def finish(self):
        assert not self.steps
        self.left.wait()
        for copy in self.sent:
            copy.wait_send()


class Halves(DataReduce):
    order = (1, 0, 2)

    @staticmethod
    def boxes_of(rows, columns):
        found = []
        for _ in range(3):
            if rows % 32 == 0:
                rows //= 2
            else:
                columns //= 2
            found.append((rows, columns))
        return found

    def plan(self):
        a, b, c = self.order
        self.steps = [
            lambda: self._give_half(a, 0, 0),
            lambda: (self._wait_box(a, 0), self._add((0,), False), self._give_half(b, 1, 1)),
            lambda: (self._wait_box(b, 1), self._add((1,), False), self._give_half(c, 2, 2)),
            lambda: (self._wait_box(c, 2), self._add((2,), True), self._give_whole(c, 3)),
            lambda: (self._take_half(c, 3), self._give_whole(b, 4)),
            lambda: (self._take_half(b, 4), self._give_whole(a, 5)),
            lambda: (self._take_half(a, 5), self._leave()),
        ]

    def _wait_box(self, b, box):
        self._wait(self.boxes[box], box, self._peer(b))


class HalvesFromX(Halves):
    order = (0, 1, 2)


class Quarters(DataReduce):
    @staticmethod
    def boxes_of(rows, columns):
        tall, broad = rows // 8, columns
        if tall % 16:
            tall, broad = rows // 4, columns // 2
        return [(rows // 2, columns)] + [(tall, broad)] * 3

    def plan(self):
        self.steps = [
            lambda: self._give_half(0, 0, 0),
            lambda: (self._wait(self.boxes[0], 0, self._peer(0)), self._add((0,), False), self._give_quarters()),
            lambda: (self._take_boxes(), self._add((1, 2, 3), True), self._give_quarter()),
            lambda: (self._take_quarters(), self._give_whole(0, 7)),
            lambda: (self._take_half(0, 7), self._leave()),
        ]

    def _z(self, j):
        low_bit = 1 - self._bit(1) if j % 2 else self._bit(1)
        high = 1 - self._bit(2) if j // 2 else self._bit(2)
        return low_bit, high, self.here.group + high * 4 + low_bit * 2 + self._bit(0)

    def _quarter(self, j):
        low_bit, high, peer = self._z(j)
        return self._part(self._part(self.trail[-1], high), low_bit), peer

    def _give_quarters(self):
        self.trail.append(self.region)
        for j in (1, 2, 3):
            part, peer = self._quarter(j)
            self._send(self._view(self.held, part), self.boxes[j], j, peer)
        self.region = self._quarter(0)[0]

    def _take_boxes(self):
        for j in (1, 2, 3):
            self._wait(self.boxes[j], j, self._z(j)[2])

    def _give_quarter(self):
        view = self._view(self.whole, self.region)
        for j in (1, 2, 3):
            self._send(view, view, 3 + j, self._z(j)[2])

    def _take_quarters(self):
        for j in (1, 2, 3):
            part, peer = self._quarter(j)
            self._wait(self._view(self.whole, part), 3 + j, peer)
        self.region = self.trail.pop()


class Pipeline:
    def __init__(self, plan):
        self.plan, self.members = plan, []

    def add(self, member):
        self.members.append(member)
        member.step()

    def at(self, place):
        for number in self.plan[place]:
            self.members[number].step()

    def finish(self):
        self.at("end")
        for m in self.members:
            while m.steps:
                m.step()
            m.finish()


PLAN = dict(
    waiting=(),
    shared=(0,),
    arriving=(0,),
    h0p0=(2,),
    h0p2=(2, 1, 3, 0),
    h0=(1,),
    h1p0=(0, 3),
    h1p2=(1, 0),
    h1=(3, 2, 4),
    h2p0=(0, 1, 3),
    h2p2=(5, 2, 6, 3),
    h2=(4,),
    led=(7, 2, 3, 5, 6, 4),
    crossing=(7, 1, 2),
    told=(5, 4),
    end=(6, 5, 7, 6, 1, 7),
)


class Everyone:
    def __init__(self, links, buf, me, count, device):
        self.links, self.buf, self.me, self.count, self.device = links, buf, me, count, device
        self.base = links.take(count)

    def _copy(self, j):
        slot = self.buf.at[self.me]
        peer = self.me + j
        peer = self.device(jnp.where(peer >= self.count, peer - self.count, peer))
        return self.links.copy(slot, slot, self.base + j, dp=peer)

    def _loop(self, act):
        def one(j, carry):
            act(j)
            return carry

        lax.fori_loop(1, self.count, one, 0)

    def start(self, values):
        self.buf[self.me] = values
        self._loop(lambda j: self._copy(j).start())

    def _hear(self, j):
        peer = self.me - j
        peer = jnp.where(peer < 0, peer + self.count, peer)
        self.links.arrived(self.buf.at[peer], self.base + j, dp=self.device(peer))

    def result(self):
        self._loop(self._hear)
        return lax.fori_loop(1, self.count, lambda j, acc: acc + self.buf[j], self.buf[0])

    def finish(self):
        self._loop(lambda j: self._copy(j).wait_send())


def greet(here):
    barrier = pltpu.get_barrier_semaphore()
    for axis, me, count in (("tensor", here.t, here.tensor), ("dp", here.d, here.dp)):

        def one(j, carry, axis=axis, me=me, count=count):
            peer = me + j
            peer = here.logical(**{axis: jnp.where(peer >= count, peer - count, peer)})
            pl.semaphore_signal(barrier, inc=1, device_id=peer, device_id_type=LOGICAL)
            return carry

        lax.fori_loop(1, count, one, 0)


def await_greetings(amount):
    pl.semaphore_wait(pltpu.get_barrier_semaphore(), amount)


def halves(rows):
    first = round_up(rows // 2, 16)
    return ((0, first), (first, rows - first))


def head_masks(shape, local_heads):
    lane = lax.broadcasted_iota(jnp.int32, shape, 1)
    return [
        jnp.where((lane >= h * HEAD_DIM) & (lane < (h + 1) * HEAD_DIM), 1.0, 0.0)
        for h in range(local_heads)
    ], lane


def kernel(n, S):
    here = Here(n.dp, 4)
    t, d = here.t, here.d
    here.peers = peers = [flipped(here, 1, 0), flipped(here, 1, 1), flipped(here, 0, 1)]
    links = Links(here, S.send, S.recv)
    greet(here)
    R, own, W, H, D, K = n.R, n.own, n.W, n.H, n.D, n.K
    split = halves(R)
    vector = lambda ref: ref[...].reshape(1, D)

    fetch = pltpu.make_async_copy(S.cot, S.gt, S.local.at[0])
    load = [
        pltpu.make_async_copy(getattr(S, name + "_far"), getattr(S, name), S.local.at[1 + j])
        for j, name in enumerate(LOADED)
    ]
    fetch.start()
    for copy in load:
        copy.start()
    S.a1[t] = jnp.zeros((R, D), low)
    S.cot4[t] = jnp.zeros((R, D), low)
    S.a24[t] = jnp.zeros((R, D), low)
    S.hl4[t] = jnp.zeros((R, D), low)
    rows_in = Gather(links, S.a1, here, split)
    cot_in = Gather(links, S.cot4, here, split)
    ow_in = Gather(links, S.ow4, here, ((0, W),))
    for p, (start, size) in enumerate(split):
        rows = pl.ds(start, min(size, own - start))
        unit, _ = standardize(S.x[rows, :].astype(wide))
        S.a1[t, rows, :] = (unit * vector(S.g1) + vector(S.b1)).astype(low)
        if p == 0:
            await_greetings(3 + n.dp - 1)
        rows_in.start([p])
    load[0].wait()
    S.ow4[t] = S.ow[...]
    ow_in.start()
    fetch.wait()
    S.cot4[t, 0:own, :] = S.gt[...].astype(low)
    cot_in.start([0])
    load[2].wait()
    load[3].wait()
    S.gw[0:D, :] = jnp.transpose(S.wup[...])
    S.gw[D:, :] = jnp.transpose(S.wdn[...])
    load[1].wait()
    S.v[4 * R :, :] = jnp.zeros((K - 4 * R, H), low)
    length = S.lengths[0]

    chip = here.chip

    def project(i, carry):
        s = flipped(here, *two_bits(i))

        @pl.when(i == 1)
        def _():
            rows_in.wait_sib()

        @pl.when(i == 2)
        def _():
            rows_in.forward()

        @pl.when(i == 3)
        def _():
            rows_in.wait_diag()

        slab = S.a1[s]
        lane = lax.broadcasted_iota(jnp.int32, (R, H - W), 1)
        row = lax.broadcasted_iota(jnp.int32, (R, H - W), 0)
        absent = (row >= own) | (row + s * own >= length)
        at = pl.ds(pl.multiple_of(s * R, 16), R)
        out = dot_rows(slab, S.wqkv[0]) + S.bq[0:1, :]
        S.q[s, :, :W] = (out.astype(low).astype(wide) * HEAD_DIM**-0.5).astype(low)
        S.q[s, :, W:] = jnp.where(lane == 0, HEAD_DIM**-0.5, 0.0).astype(low)
        S.k[at, :W] = dot_rows(slab, S.wqkv[1]).astype(low)
        S.k[at, W:] = jnp.where((lane == 0) & absent, -8e30, 0.0).astype(low)
        S.v[at, :W] = (dot_rows(slab, S.wqkv[2]) + S.bq[1:2, :]).astype(low)
        S.v[at, W:] = jnp.where(lane < 2, 1.0, 0.0).astype(low)
        return carry

    lax.fori_loop(0, 4, project, 0)
    if K > 4 * R:
        lane = lax.broadcasted_iota(jnp.int32, (K - 4 * R, H), 1)
        S.k[4 * R :, :] = jnp.where(lane == W, -8e30, 0.0).astype(low)
    S.kt[...] = jnp.transpose(S.k[...])
    S.vt[...] = jnp.transpose(S.v[...])

    masks, lane = head_masks((1, H), n.heads)
    mix_base = links.take(3)


    def attend(i, carry):
        high, low_bit = two_bits(i)
        s = flipped(here, 1 - high, low_bit + high - 2 * low_bit * high)
        query = S.q[s]
        mixed = jnp.zeros((R, H), wide)
        inverse = jnp.zeros((R, 128), wide)
        first = lax.broadcasted_iota(jnp.int32, (1, 128), 1)

        def score(h):
            here = jnp.where(lane == W, 1.0, masks[h]).astype(low)
            return dot(query * here, S.kt[...])

        ready = score(0)
        for h in range(n.heads):
            scores = ready
            if h + 1 < n.heads:
                ready = score(h + 1)
            terms = jnp.exp(scores - jnp.max(scores, -1, keepdims=True)).astype(low)
            S.e[h, s] = terms
            part = dot(terms, S.v[...])
            scale = 1.0 / part[:, W : W + 1]
            mixed += part * (scale * masks[h])
            inverse = jnp.where(first == h, scale, inverse)
        S.o[s] = mixed
        S.inv[s] = inverse
        S.mix[s] = mixed[:, :W].astype(low)

        @pl.when(i < 3)
        def _():
            links.copy(S.mix.at[s], S.mix4.at[t], mix_base + i, tensor=s).start()

        @pl.when(i == 1)
        def _():
            cot_in.start([1])

        @pl.when(i == 2)
        def _():
            ow_in.wait_sib()
            ow_in.forward()

        return carry

    lax.fori_loop(0, 4, attend, 0)
    ow_in.wait_diag()
    S.mix4[t] = S.mix[t]
    for j, s in enumerate(peers):
        links.arrived(S.mix4.at[s], mix_base + j, tensor=s)

    total = dot(S.mix4[0], S.ow4[0])
    for j in range(1, 4):
        total += dot(S.mix4[j], S.ow4[j])
    total = S.x[...].astype(wide) + (total[:own] + vector(S.ob))
    S.hid[...] = total
    unit, _ = standardize(total)
    S.a24[t, 0:own, :] = (unit * vector(S.g2) + vector(S.b2)).astype(low)
    next_in = Gather(links, S.a24, here, halves(R))
    next_in.start()
    back = Reduce(links, S.part, S.pre1, S.near1, S.far1, here, split)
    ahead = Reduce(links, S.fop, S.pre2, S.near2, S.far2, here, split)
    S.gub[...] = jnp.zeros_like(S.gub)

    def feed(s, start, size):
        rows = pl.ds(start, size)
        up = dot(S.a24[s, rows], S.wup[...]) + vector(S.bup)
        square = up * up
        c = 0.7978845608028654
        bend = jnp.tanh(c * up * (1.0 + 0.044715 * square))
        half = 0.5 * (1.0 + bend)
        slope = half + 0.5 * up * (1.0 - bend * bend) * (c + (3 * 0.044715 * c) * square)
        active = (up * half).astype(low)
        S.pool[s, rows, 0:D] = active
        grad = (dot(S.cot4[s, rows], S.gw[D:, :]) * slope).astype(low)
        S.gup[s, rows] = grad
        S.part[s, rows] = dot(grad, S.gw[0:D, :]).astype(low)
        S.gub[...] += jnp.sum(grad.astype(wide), 0, keepdims=True)

    def lead_out(s, start, size):
        rows = pl.ds(start, size)
        S.fop[s, rows] = dot(S.pool[s, rows, 0:D], S.wdn[...]).astype(low)

    def feed_here(i, carry):
        s = flipped(here, 0, i)

        @pl.when(i == 1)
        def _():
            next_in.wait_sib()
            cot_in.wait_sib()

        feed(s, 0, R)

        @pl.when(i == 1)
        def _():
            back.send_sib()

        lead_out(s, 0, R)
        return carry

    lax.fori_loop(0, 2, feed_here, 0)
    ahead.send_sib()
    for p in (0, 1):

        def feed_there(i, carry, p=p):
            @pl.when(i == 0)
            def _():
                cot_in.forward([p])
                next_in.forward([p])

            @pl.when(i == 1)
            def _():
                cot_in.wait_diag([p])
                next_in.wait_diag([p])

            feed(flipped(here, 1, i), *split[p])
            if p == 1:

                @pl.when(i == 0)
                def _():
                    back.send_cross([0])

            return carry

        lax.fori_loop(0, 2, feed_there, 0)
        back.send_diag([p])
    for i in (0, 1):
        lead_out(flipped(here, 1, i), 0, R)
    back.send_cross([1])
    ahead.send_diag()

    sums = Pipeline(PLAN)
    tile = D // 2
    box_at = 0

    def sum_over_dp(kind, held, whole, out, first, rows):
        nonlocal box_at
        sums.add(kind(links, held, whole, out, S.box, box_at, first, rows))
        box_at += kind.sizes(rows, D, n.dp)[1]

    for left, right, first in ((S.a24, S.gup, 0), (S.pool, S.cot4, D)):
        rows = left[:, :, 0:D].reshape(4 * R, D)
        S.gw[first : first + D, :] = dot_columns(rows, flat(right)).astype(low)
        for at in (first, first + tile):
            kind = Halves if at == tile else HalvesFromX
            sum_over_dp(kind, S.gw, S.sum1, S.whole1, at, tile)

    sums.at("waiting")
    S.small[...] = jnp.zeros_like(S.small)
    gm_base = links.take(6)
    shared = lambda s, p, j: links.copy(
        S.mix4.at[s, pl.ds(*split[p])], S.gm4.at[t, pl.ds(*split[p])], gm_base + 3 * p + j, tensor=peers[j]
    )
    for p, (start, size) in enumerate(split):
        real = min(size, own - start)
        rows = pl.ds(start, real)
        grad = back.result(p)[:real]
        unit, inverse = standardize(S.hid[rows])
        S.small[2:3, :] += jnp.sum(grad * unit, 0, keepdims=True)
        S.small[3:4, :] += jnp.sum(grad, 0, keepdims=True)
        S.gt[rows] += norm_back(grad, unit, inverse, vector(S.g2))
        S.hl4[t, rows] = S.gt[rows].astype(low)
        rows = pl.ds(start, size)
        for j, s in enumerate(peers + [t]):
            product = dot_rows(S.hl4[t, rows], S.ow4[s]).astype(low)
            if j < 3:
                S.mix4[s, rows] = product
                shared(s, p, j).start()
            else:
                S.gm4[t, rows] = product
    S.small[4:5, :] = jnp.sum(S.hl4[t].astype(wide), 0, keepdims=True)
    S.small[5:6, :] = jnp.sum(S.cot4[t].astype(wide), 0, keepdims=True)
    S.small[6:7, :] = S.gub[...]
    hl_in = Gather(links, S.hl4, here, halves(R))

    next_in.finish()
    S.do[...] = jnp.zeros_like(S.do)
    S.qt[...] = jnp.transpose(flat(S.q))
    sums.at("shared")

    def prepare(i, s):
        if i > 0:
            j = (None, 2, 0, 1)[i]
            for p in (0, 1):
                rows = pl.ds(*split[p])
                links.arrived(S.gm4.at[s, rows], gm_base + 3 * p + j, tensor=peers[j])
        S.do[:, :W] = S.gm4[s].astype(wide)
        inverse = sum(S.inv[s, :, h : h + 1] * masks[h] for h in range(n.heads))
        scaled = (S.do[...] * inverse).astype(low)
        S.v[pl.ds(pl.multiple_of(s * R, 16), R), :] = scaled
        scaled = scaled.astype(wide)
        product = scaled * S.o[s]
        for h in range(n.heads):
            inner = -jnp.sum(product * masks[h], -1, keepdims=True)
            upper = inner.astype(low).astype(wide)
            S.a24[s, :, h * H : (h + 1) * H] = (
                scaled * masks[h]
                + jnp.where(lane == W, upper, 0.0)
                + jnp.where(lane == W + 1, inner - upper, 0.0)
            ).astype(low)

    def pull(h, p):
        grad_p = dot(pair(S.a24.at[:, :, h * H : (h + 1) * H], p), S.vt[...])
        grad_s = (pair(S.e.at[h], p).astype(wide) * grad_p).astype(low)
        set_pair(S.pool, p, grad_s)
        dq = dot(grad_s, S.k[...]) * (masks[h] * HEAD_DIM**-0.5)
        if h > 0:
            dq += pair(S.gup.at[:, :, 0:H], p).astype(wide)
        S.gup[pl.ds(2 * p, 2), :, 0:H] = dq.astype(low).reshape(2, R, H)

    def weights(h):
        at = slice(h * HEAD_DIM, (h + 1) * HEAD_DIM)
        tile = h * HEAD_DIM // 128 * 128
        dqt = jnp.transpose(flat(S.gup.at[:, :, tile : tile + 128]))
        left = jnp.concatenate(
            [dqt[h * HEAD_DIM - tile : (h + 1) * HEAD_DIM - tile], S.qt[at, :], S.kt[at, : 4 * R]], 0
        )
        out = dot(left, flat(S.a1))
        S.gw2[h * W : (h + 1) * W, :] = out.astype(low)
        for c in range(3):
            product = out[c * HEAD_DIM : (c + 1) * HEAD_DIM] * S.wqkv[c, at, :].astype(wide)
            S.small[0:1, :] += jnp.sum(product, 0, keepdims=True)
        sum_over_dp(Quarters, S.gw2, S.sum2, S.whole2, h * W, W)

    for h in range(n.heads):
        for i in (0, 2):
            if (h, i) == (0, 2):
                sums.at("arriving")
            if h == 0:
                prepare(i, flipped(here, i // 2, 0))
                prepare(i + 1, flipped(here, i // 2, 1))
            if (h, i) == (0, 2):
                hl_in.start()
            pull(h, chip if i == 0 else 1 - chip)
            sums.at(f"h{h}p{i}")
            if (h, i) == (1, 0):
                hl_in.wait_sib()
                hl_in.forward()
                ahead.send_cross()
            elif (h, i) == (1, 2):
                hl_in.wait_diag()
                S.gw2[3 * W :, :] = dot_columns(flat(S.mix), flat(S.hl4)).astype(low)
                sum_over_dp(Quarters, S.gw2, S.sum2, S.whole2, 3 * W, W)
        if h == 0:
            S.v[4 * R :, :] = jnp.zeros((K - 4 * R, H), low)
            S.kt[...] = jnp.transpose(S.v[...])
        at = slice(h * HEAD_DIM, (h + 1) * HEAD_DIM)
        S.qt[at, :] = dot(S.qt[at, :], flat(S.pool))[:, : 4 * R].astype(low)
        S.kt[at, : 4 * R] = dot(S.kt[at, : 4 * R], flat(S.e.at[h]))[:, : 4 * R].astype(low)
        if h + 1 < n.heads:
            weights(h)
        sums.at(f"h{h}")

    pad = jnp.zeros((R, H - W), low)
    for part, grad_t in ((1, S.qt), (2, S.kt)):
        rows = jnp.transpose(grad_t[:W, : 4 * R])
        for s in range(4):
            S.gup[s, :, part * H : part * H + W] = rows[s * R : (s + 1) * R]
            S.gup[s, :, part * H + W : (part + 1) * H] = pad

    back.finish()
    down = Reduce(links, S.part, S.pre1, S.near1, S.far1, here, split)

    def lead(s, start, size):
        rows = pl.ds(start, size)
        out = dot(S.gup[s, rows, 0:W], S.wqkv[0])
        out += dot(S.gup[s, rows, H : H + W], S.wqkv[1])
        out += dot(S.gup[s, rows, 2 * H : 2 * H + W], S.wqkv[2])
        S.part[s, rows] = out.astype(low)

    cross, diag, sib = peers
    lead(diag, *split[0])
    down.send_diag([0])
    lead(cross, *split[0])
    weights(n.heads - 1)
    down.send_cross([0])
    lead(diag, *split[1])
    down.send_diag([1])
    lead(cross, *split[1])
    down.send_cross([1])
    lead(sib, 0, R)
    down.send_sib()
    lead(t, 0, R)
    columns = jnp.sum(flat(S.gup).astype(wide), 0, keepdims=True)
    S.small[7:8, 0:H] = columns[:, 0:H]
    S.small[7:8, H : 2 * H] = columns[:, 2 * H :]
    upper = columns.astype(low)
    both = jnp.concatenate([upper.astype(wide), columns - upper.astype(wide)], 0).astype(low)
    for c in range(3):
        product = dot(both[:, c * H : c * H + W], S.wqkv[c])
        S.small[1:2, :] += jnp.sum(product, 0, keepdims=True)

    S.small4[t] = S.small[...]
    base3 = links.take(3)
    for j in range(3):
        links.start(S.small4.at[t], S.small4.at[t], base3 + j, tensor=peers[j])
    sums.at("led")
    result = jnp.concatenate([ahead.result(0), ahead.result(1)], 0)
    S.output[...] = (S.hid[...] + (result[:own] + vector(S.db))).astype(low)
    sums.at("crossing")

    unit, inverse = standardize(S.x[...].astype(wide))
    grad = jnp.concatenate([down.result(0), down.result(1)], 0)[:own]
    for j in range(3):
        links.arrived(S.small4.at[peers[j]], base3 + j, tensor=peers[j])
    over = S.small4[0] + S.small4[1] + S.small4[2] + S.small4[3]
    row = lax.broadcasted_iota(jnp.int32, over.shape, 0)
    near = min(8, n.dp)
    inner = Everyone(links, S.smalls, here.near, near, lambda j: here.group + j)
    inner.start(jnp.where(row < 6, over, S.small[...]))
    S.gt[...] += norm_back(grad, unit, inverse, vector(S.g1))
    sums.at("told")
    sums.finish()
    total = inner.result()
    inner.finish()
    if n.dp > near:
        outer = Everyone(links, S.smalls2, lax.div(here.group, near), n.dp // near, lambda j: j * near + here.near)
        outer.start(total)
        total = outer.result()
        outer.finish()
    S.small_sum[...] = total
    S.small_sum[0:1, :] = (total[0:1, :] - vector(S.b1) * total[1:2, :]) / vector(S.g1)
    for j, s in enumerate(peers):
        links.copy(S.mix.at[s], S.mix4.at[t], mix_base + j, tensor=s).wait_send()
        for p in (0, 1):
            shared(s, p, j).wait_send()
    for transfer in (rows_in, cot_in, ow_in, hl_in, ahead, down):
        transfer.finish()
    links.finish()


LOADED = ("ow", "wqkv", "wup", "wdn")
SMALL = ("gain1", "shift1", "gain2", "shift2", "bias_out", "bias_down", "bias_up", "bias_qv")


def finish(n, output, gt, small, whole1, whole2):
    D, W, H = n.D, n.W, n.H
    steps = n.heads
    rows1 = D // steps

    def spread(output, gt, small, up, down, head, out, *refs):
        to_output, to_gt, to_up, to_down, to_qkv, to_out = refs[:6]
        vectors, sems = refs[6:14], refs[14]
        i = pl.program_id(0)
        held = refs[15:]
        come = [pltpu.make_async_copy(a, b, sems.at[j]) for j, (a, b) in enumerate(zip((output, gt), held))]
        go = [
            pltpu.make_async_copy(a, b, sems.at[2 + j])
            for j, (a, b) in enumerate(zip(held, (to_output, to_gt)))
        ]

        @pl.when(i == 0)
        def _():
            for copy in come:
                copy.start()
            for j in range(7):
                vectors[j][...] = small[j : j + 1, :].reshape(D)
            vectors[7][0:1, :] = small[7:8, :W]
            vectors[7][1:2, :] = small[7:8, H : H + W]

        to_up[...] = up[...].astype(wide)
        to_down[...] = down[...].astype(wide)
        for j in range(3):
            to_qkv[j] = head[j * HEAD_DIM : (j + 1) * HEAD_DIM, :].astype(wide)
        to_out[...] = out[...].astype(wide)

        @pl.when(i == 1)
        def _():
            for first, second in zip(come, go):
                first.wait()
                second.start()

        @pl.when(i == steps - 1)
        def _():
            for copy in go:
                copy.wait()

    hbm = pl.BlockSpec(memory_space=pl.ANY)
    whole = pl.BlockSpec(memory_space=pltpu.VMEM)
    at_row = lambda rows, index: pl.BlockSpec((rows, D), lambda i: (index(i), 0))
    shape = jax.ShapeDtypeStruct
    return pl.pallas_call(
        spread,
        grid=(steps,),
        out_shape=[shape(output.shape, low), shape(gt.shape, wide)]
        + [shape((D, D), wide)] * 2
        + [shape((3, W, D), wide), shape((W, D), wide)]
        + [shape((D,), wide)] * 7
        + [shape((2, W), wide)],
        in_specs=[hbm, hbm, whole, at_row(rows1, lambda i: i), at_row(rows1, lambda i: i + steps)]
        + [at_row(W, lambda i: i), at_row(HEAD_DIM, lambda i: 3 * steps + i)],
        out_specs=[hbm, hbm]
        + [at_row(rows1, lambda i: i)] * 2
        + [pl.BlockSpec((3, HEAD_DIM, D), lambda i: (0, i, 0)), at_row(HEAD_DIM, lambda i: i)]
        + [whole] * 8,
        scratch_shapes=[
            pltpu.SemaphoreType.DMA((4,)),
            pltpu.VMEM(output.shape, low),
            pltpu.VMEM(gt.shape, wide),
        ],
    )(output, gt, small, whole1, whole1, whole2, whole2)


def body(
    tokens,
    lengths,
    ln1_gain,
    ln1_shift,
    qkv_weight,
    qv_bias,
    out_weight,
    out_bias,
    ln2_gain,
    ln2_shift,
    up_weight,
    up_bias,
    down_weight,
    down_bias,
    cotangent,
):
    own, D = tokens.shape
    W = qkv_weight.shape[2]
    F = up_weight.shape[1]
    dp = lax.axis_size("dp")
    assert lax.axis_size("tensor") == 4 and lengths.shape[0] == 1 and F == D and 4 * W == D and 3 * round_up(W + 2, 128) == D
    R = round_up(own, 16)
    H = round_up(W + 2, 128)
    K = round_up(4 * R, 256)
    heads = W // HEAD_DIM
    extra = dp.bit_length() - 1 - 3
    n = types.SimpleNamespace(
        own=own, D=D, W=W, R=R, H=H, K=K, dp=dp, heads=heads, extra=extra
    )
    weights = dict(ow=out_weight, wqkv=jnp.transpose(qkv_weight, (1, 2, 0)), wup=up_weight, wdn=down_weight)
    given = dict(
        x=tokens, lengths=lengths, g1=ln1_gain, b1=ln1_shift,
        bq=qv_bias, ob=out_bias, g2=ln2_gain, b2=ln2_shift, bup=up_bias, db=down_bias,
        cot=cotangent,
    )
    given.update({name + "_far": weights[name] for name in LOADED})
    outs = dict(
        output=((own, D), low), gt=((own, D), wide), small_sum=((8, D), wide),
        whole1=((2 * D, D), low), whole2=((D, D), low),
    )
    rows4 = ((4, R, D), low)
    slab = ((R, D), low)
    chunks = [(Halves, D // 2)] * 4 + [(Quarters, W)] * 4
    scratch = dict(
        a1=rows4, cot4=rows4, ow4=((4, W, D), low), q=((4, R, H), low), k=((K, H), low),
        v=((K, H), low), kt=((H, K), low), vt=((H, K), low), e=((heads, 4, R, K), low),
        o=((4, R, H), wide), inv=((4, R, 128), wide), mix=((4, R, W), low), mix4=((4, R, W), low),
        hid=((own, D), wide),
        a24=rows4, pool=((4, R, K), low), gup=rows4, part=rows4,
        fop=rows4, pre1=slab, near1=slab, far1=slab, pre2=slab, near2=slab, far2=slab,
        gw=((2 * D, D), low), gub=((1, D), wide),
        small=((8, D), wide), hl4=rows4,
        gm4=((4, R, W), low), qt=((H, 4 * R), low), do=((R, H), wide),
        gw2=((D, D), low),
        small4=((4, 8, D), wide), smalls=((min(8, dp), 8, D), wide),
        box=((sum(kind.sizes(r, D, dp)[1] for kind, r in chunks), D), low),
        sum1=((2 * D, D), low), sum2=((D, D), low),
    )
    scratch.update({name: (weights[name].shape, low) for name in LOADED})
    if dp > 8:
        scratch["smalls2"] = ((dp // 8, 8, D), wide)
    sems = 170 + dp + 8 * extra
    names = list(given) + list(outs) + list(scratch) + ["local", "send", "recv"]
    vmem = pl.BlockSpec(memory_space=pltpu.VMEM)
    smem = pl.BlockSpec(memory_space=pltpu.SMEM)
    hbm = pl.BlockSpec(memory_space=pl.ANY)
    output, gt, small, whole1, whole2 = pl.pallas_call(
        lambda *refs: kernel(n, types.SimpleNamespace(**dict(zip(names, refs)))),
        out_shape=tuple(jax.ShapeDtypeStruct(*spec) for spec in outs.values()),
        in_specs=[
            hbm if name.endswith("_far") else dict(lengths=smem, cot=hbm).get(name, vmem) for name in given
        ],
        out_specs=tuple(hbm if name in ("whole1", "whole2") else vmem for name in outs),
        scratch_shapes=[pltpu.VMEM(*spec) for spec in scratch.values()]
        + [pltpu.SemaphoreType.DMA((5,))] + [pltpu.SemaphoreType.DMA((sems,))] * 2,
        compiler_params=pltpu.CompilerParams(
            collective_id=0, has_side_effects=True, vmem_limit_bytes=VMEM_BYTES
        ),
    )(*given.values())
    finished = finish(n, output, gt, small, whole1, whole2)
    small_rows = dict(zip(SMALL, finished[6:]))
    return (
        finished[0],
        finished[1],
        small_rows["gain1"],
        small_rows["shift1"],
        jnp.transpose(finished[4], (2, 0, 1)),
        small_rows["bias_qv"],
        finished[5],
        small_rows["bias_out"],
        small_rows["gain2"],
        small_rows["shift2"],
        finished[2],
        small_rows["bias_up"],
        finished[3],
        small_rows["bias_down"],
    )


def solution(mesh):
    placed = (
        P(("dp", "tensor"), None),
        P("dp"),
        P(),
        P(),
        P(None, None, "tensor"),
        P(None, "tensor"),
        P("tensor", None),
        P(),
        P(),
        P(),
        P(None, "tensor"),
        P("tensor"),
        P("tensor", None),
        P(),
        P(("dp", "tensor"), None),
    )
    return jax.shard_map(
        body,
        mesh=mesh,
        in_specs=placed,
        out_specs=(
            P(("dp", "tensor"), None),
            P(("dp", "tensor"), None),
            P(),
            P(),
            P(None, None, "tensor"),
            P(None, "tensor"),
            P("tensor", None),
            P(),
            P(),
            P(),
            P(None, "tensor"),
            P("tensor"),
            P("tensor", None),
            P(),
        ),
        check_vma=False,
    )
```
